32 devices in a mesh: gx: 2 (over y), gy: 4 (over z), gz: 4 (over x, core).
Axes of the slice: x: 2, y: 2, z: 4, core: 2. Of those that a mesh axis runs over, the one named last changes fastest.
Arguments:
- pops: float32 [27, 16, 32, 256], P(None, 'gz', 'gy', 'gx')
- solid: int32 [16, 32, 256], P('gz', 'gy', 'gx'), may hold values from 0 to 1, as said below
- profile_table: float32 [8, 16], P(None, 'gz'), as said below
- profile_index: int32 [32], P('gy'), may hold values from 0 to 7
Outputs:
- updated: float32 [27, 16, 32, 256], P(None, 'gz', 'gy', 'gx')
The draws below stay inside these ranges and needn't reach their ends.
Inputs may be any that keep to these rules, and one draw needn't show every extreme that they name: `solid`: buildings are vertical columns on footprints of 4 x 4 cells aligned to multiples of 4; every cell with z index 15 is 0. `profile_table`: every profile's speeds lie in a band of positive values.
All inputs are finite; a program needn't handle non-finite values.
Results may differ from the reference program's by a relative error of at most 0.0003.
Values sent between devices are 32-bit elements; how exact they have to be, the bound alone decides.
No kernel may reach another device: no remote copies, remote signals or barrier semaphores. Data moves between devices by JAX's collectives and lax.ppermute only.
A program may use at most 64 MiB of HBM per device.

```python
import jax
import jax.numpy as jnp
import numpy as np
from jax import lax

STEPS = 2
PROF = 8
NX = 256
NY = 32
NZ = 16
SPONGE = 32


def lattice_drawn():
    velocity = np.array([[cx, cy, cz] for cz in (-1, 0, 1) for cy in (-1, 0, 1) for cx in (-1, 0, 1)])
    lengths_sq = (velocity * velocity).sum(1)
    weights = np.array([8.0 / 27.0, 2.0 / 27.0, 1.0 / 54.0, 1.0 / 216.0])[lengths_sq]
    return (velocity, weights)


def draw_pops(key, part):
    velocity, weights = lattice_drawn()
    keys = jax.random.split(jax.random.fold_in(key, 11), 6)
    shape = (NZ, NY, NX)
    height = (jnp.arange(NZ, dtype=jnp.float32)[:, None, None] + 0.5) / NZ
    rough = jax.random.uniform(keys[0], shape, jnp.float32, 0.5, 1.5)
    noise = jnp.clip(jax.random.normal(keys[4], (27,) + shape, jnp.float32), -2.0, 2.0)
    amplitude = jnp.exp(jax.random.uniform(keys[5], shape, jnp.float32, jnp.log(0.1), jnp.log(0.4)))
    speed_x = 0.12 * (0.2 + 0.8 * height) * rough
    speed_y = 0.04 * jnp.clip(jax.random.normal(keys[1], shape, jnp.float32), -3.0, 3.0)
    speed_z = 0.03 * jnp.clip(jax.random.normal(keys[2], shape, jnp.float32), -3.0, 3.0)
    density = 1.0 + 0.03 * jnp.clip(jax.random.normal(keys[3], shape, jnp.float32), -3.0, 3.0)
    comp_x = jnp.asarray(velocity[:, 0], jnp.float32).reshape(27, 1, 1, 1)
    comp_y = jnp.asarray(velocity[:, 1], jnp.float32).reshape(27, 1, 1, 1)
    comp_z = jnp.asarray(velocity[:, 2], jnp.float32).reshape(27, 1, 1, 1)
    factor = jnp.asarray(weights, jnp.float32).reshape(27, 1, 1, 1)
    along = comp_x * speed_x + comp_y * speed_y + comp_z * speed_z
    square = speed_x * speed_x + speed_y * speed_y + speed_z * speed_z
    balance = factor * density * (1.0 + 3.0 * along + 4.5 * along * along - 1.5 * square)
    return (balance + factor * amplitude[None] * noise).astype(jnp.float32)


def draw_solid(key, part):
    heights = jax.random.randint(jax.random.fold_in(key, 23), (NY // 4, NX // 4), -(NZ - 1), NZ)
    heights = jnp.maximum(heights, 0)
    heights = heights.at[0, 0].set(NZ - 1)
    heights = heights.at[0, 1].set(0)
    heights = jnp.repeat(jnp.repeat(heights, 4, axis=0), 4, axis=1)
    level = jnp.arange(NZ, dtype=jnp.int32)[:, None, None]
    return (level < heights[None]).astype(jnp.int32)


def draw_profile_table(key, part):
    keys = jax.random.split(jax.random.fold_in(key, 37), 3)
    height = (jnp.arange(NZ, dtype=jnp.float32)[None, :] + 0.5) / NZ
    exponent = jnp.exp(jax.random.uniform(keys[0], (PROF, 1), jnp.float32, jnp.log(0.1), jnp.log(0.5)))
    scale = jax.random.uniform(keys[1], (PROF, 1), jnp.float32, 0.1, 0.18)
    rough = jax.random.uniform(keys[2], (PROF, NZ), jnp.float32, 0.7, 1.3)
    return (scale * (0.1 + height ** exponent) * rough).astype(jnp.float32)


def with_ends(values, own_key, smallest, high):
    dims = values.shape
    index_at = [jax.random.randint(jax.random.fold_in(own_key, axis), (), 0, dims[axis]) for axis in range(len(dims))]
    values = values.at[tuple(index_at)].set(smallest)
    longest = dims.index(max(dims))
    index_at[longest] = (index_at[longest] + 1) % dims[longest]
    return values.at[tuple(index_at)].set(high)


def setup_inputs(seed: int = 0) -> dict:
    seeds = jax.random.split(jax.random.key(seed), 5)
    pops = draw_pops(jax.random.fold_in(seeds[4], 71), 0)
    solid = draw_solid(jax.random.fold_in(seeds[4], 71), 0)
    profile_table = draw_profile_table(jax.random.fold_in(seeds[4], 71), 0)
    profile_index = with_ends(jax.random.randint(seeds[3], (NY,), 0, PROF), jax.random.fold_in(seeds[3], 1), 0, PROF - 1).astype(jnp.int32)
    return dict(pops=pops, solid=solid, profile_table=profile_table, profile_index=profile_index)


tau_base = 0.52
smag_const = 0.17

def lattice():
    velocity = np.array([[cx, cy, cz] for cz in (-1, 0, 1) for cy in (-1, 0, 1) for cx in (-1, 0, 1)])
    lengths_sq = (velocity * velocity).sum(1)
    weights = np.array([8.0 / 27.0, 2.0 / 27.0, 1.0 / 54.0, 1.0 / 216.0])[lengths_sq]
    return (velocity, weights)

def mirror_of(number):
    velocity, weights = lattice()
    cx, cy, cz = velocity[number]
    return int((1 - cz) * 9 + (cy + 1) * 3 + (cx + 1))

def equilibrium(density, speed_x, speed_y, speed_z):
    velocity, weights = lattice()
    comp_x = jnp.asarray(velocity[:, 0], jnp.float32).reshape(27, 1, 1, 1)
    comp_y = jnp.asarray(velocity[:, 1], jnp.float32).reshape(27, 1, 1, 1)
    comp_z = jnp.asarray(velocity[:, 2], jnp.float32).reshape(27, 1, 1, 1)
    factor = jnp.asarray(weights, jnp.float32).reshape(27, 1, 1, 1)
    along = comp_x * speed_x + comp_y * speed_y + comp_z * speed_z
    square = speed_x * speed_x + speed_y * speed_y + speed_z * speed_z
    return factor * density * (1.0 + 3.0 * along + 4.5 * along * along - 1.5 * square)

def collide(pops):
    velocity, weights = lattice()
    first_table = np.concatenate([np.ones((27, 1)), velocity], axis=1)
    moments = jnp.einsum('qm,qzyx->mzyx', jnp.asarray(first_table, jnp.float32), pops, precision=lax.Precision.HIGHEST)
    density = moments[0]
    speed_x = moments[1] / density
    speed_y = moments[2] / density
    speed_z = moments[3] / density
    nonequil = pops - equilibrium(density, speed_x, speed_y, speed_z)
    pair_table = np.stack([velocity[:, 0] * velocity[:, 0], velocity[:, 1] * velocity[:, 1], velocity[:, 2] * velocity[:, 2], velocity[:, 0] * velocity[:, 1], velocity[:, 0] * velocity[:, 2], velocity[:, 1] * velocity[:, 2]], axis=1)
    stress = jnp.einsum('qm,qzyx->mzyx', jnp.asarray(pair_table, jnp.float32), nonequil, precision=lax.Precision.HIGHEST)
    strain_sq = stress[0] ** 2 + stress[1] ** 2 + stress[2] ** 2 + 2.0 * (stress[3] ** 2 + stress[4] ** 2 + stress[5] ** 2)
    magnitude = jnp.sqrt(2.0 * strain_sq)
    relax = 0.5 * (tau_base + jnp.sqrt(tau_base * tau_base + 18.0 * math_root_two() * smag_const * smag_const * magnitude / density))
    return (pops - nonequil / relax, density)

def math_root_two():
    return 1.4142135623730951

def reference(pops, solid, profile_table, profile_index):
    velocity, weights = lattice()
    onehot = (profile_index[:, None] == jnp.arange(PROF, dtype=jnp.int32)[None, :]).astype(jnp.float32)
    target = jnp.einsum('yp,pz->zy', onehot, profile_table, precision=lax.Precision.HIGHEST)[:, :, None]
    sponge = (jnp.arange(NX, dtype=jnp.int32) < SPONGE)[None, None, None, :]
    height = jnp.arange(NZ, dtype=jnp.int32)[:, None, None]
    fluid = (solid == 0)[None]
    rest = jnp.asarray(weights, jnp.float32).reshape(27, 1, 1, 1)
    walls = jnp.pad(solid, ((1, 1), (0, 0), (0, 0)))
    for step in range(STEPS):
        post, density = collide(pops)
        zeros = jnp.zeros_like(density)
        pinned = equilibrium(density, target + zeros, zeros, zeros)
        post = jnp.where(sponge, pinned, post)
        padded = jnp.pad(post, ((0, 0), (1, 1), (0, 0), (0, 0)))
        pieces = []
        for number in range(27):
            cx, cy, cz = [int(value) for value in velocity[number]]
            source = jnp.roll(padded[number], (cy, cx), axis=(1, 2))[1 - cz:1 - cz + NZ]
            blocked = jnp.roll(walls, (cy, cx), axis=(1, 2))[1 - cz:1 - cz + NZ] == 1
            bounce = post[26 - number]
            mirror = jnp.roll(post[mirror_of(number)], (cy, cx), axis=(1, 2))
            value = jnp.where(blocked, bounce, source)
            value = jnp.where(height - cz < 0, bounce, value)
            value = jnp.where(height - cz > NZ - 1, mirror, value)
            pieces.append(value)
        pops = jnp.where(fluid, jnp.stack(pieces), rest)
    return pops
```

```python
import jax
import jax.numpy as jnp
import numpy as np
from jax import lax
from jax.experimental import pallas as pl
from jax.experimental.pallas import tpu as pltpu
from jax.sharding import PartitionSpec as P

SPONGE = 32
TAU = 0.52
SMAG = 18.0 * 1.4142135623730951 * 0.17 * 0.17

VEL = [(cx, cy, cz) for cz in (-1, 0, 1) for cy in (-1, 0, 1) for cx in (-1, 0, 1)]
WEIGHT = [
    float(np.array([8.0 / 27.0, 2.0 / 27.0, 1.0 / 54.0, 1.0 / 216.0])[cx * cx + cy * cy + cz * cz])
    for cx, cy, cz in VEL
]
WALL, AIM, CHANNELS = 27, 28, 29
NZ, NY, NX = 4, 8, 128
PITCH = NY + 4
FLAT = (NZ + 4) * PITCH
PAD = 8
ROWS = PAD + FLAT + PAD
UNITS = (NZ + 2) * PITCH // 8

VMEM = pl.BlockSpec(memory_space=pltpu.VMEM)
SMEM = pl.BlockSpec(memory_space=pltpu.SMEM)
F32 = jnp.float32

Y_ROWS = (CHANNELS + 9) * NZ
Z_BLOCKS = CHANNELS + 10
Z_ROWS = -(-Z_BLOCKS * PITCH // 8) * 8


def relaxed(f, sponge, aim):
    quad = {}
    for cz in (-1, 0, 1):
        line = {}
        for cy in (-1, 0, 1):
            base = 9 * (cz + 1) + 3 * (cy + 1)
            both = f[base + 2] + f[base]
            line[cy] = (both + f[base + 1], f[base + 2] - f[base], both)
        s = line[1][0] + line[-1][0]
        sx = line[1][1] + line[-1][1]
        quad[cz] = dict(
            n=s + line[0][0],
            y=line[1][0] - line[-1][0],
            yy=s,
            x=sx + line[0][1],
            xy=line[1][1] - line[-1][1],
            xx=line[1][2] + line[-1][2] + line[0][2],
        )
    up, mid, down = quad[1], quad[0], quad[-1]
    zz = up["n"] + down["n"]
    rho = zz + mid["n"]
    jz = up["n"] - down["n"]
    jy = up["y"] + down["y"] + mid["y"]
    jx = up["x"] + down["x"] + mid["x"]
    inverse = 1.0 / rho
    ux, uy, uz = jx * inverse, jy * inverse, jz * inverse
    third = rho * (1.0 / 3.0)
    pxx = (up["xx"] + down["xx"] + mid["xx"]) - (third + jx * ux)
    pyy = (up["yy"] + down["yy"] + mid["yy"]) - (third + jy * uy)
    pzz = zz - (third + jz * uz)
    pxy = (up["xy"] + down["xy"] + mid["xy"]) - jx * uy
    pxz = (up["x"] - down["x"]) - jx * uz
    pyz = (up["y"] - down["y"]) - jy * uz
    strain = pxx * pxx + pyy * pyy + pzz * pzz + 2.0 * (pxy * pxy + pxz * pxz + pyz * pyz)
    size = jnp.sqrt(2.0 * strain)
    tau = 0.5 * (TAU + jnp.sqrt(TAU * TAU + SMAG * size * inverse))
    omega = 1.0 / tau
    keep = 1.0 - omega
    if sponge is not None:
        keep = jnp.where(sponge, 0.0, keep)
        omega = jnp.where(sponge, 1.0, omega)
        ux = jnp.where(sponge, aim, ux)
        uy = jnp.where(sponge, 0.0, uy)
        uz = jnp.where(sponge, 0.0, uz)
    square = 1.0 - 1.5 * (ux * ux + uy * uy + uz * uz)
    vx, vy, vz = 3.0 * ux, 3.0 * uy, 3.0 * uz
    share = rho * omega
    weighted = {w: share * w for w in sorted(set(WEIGHT))}
    post = [None] * 27
    for q in range(14):
        cx, cy, cz = VEL[q]
        along = None
        for c, v in ((cx, vx), (cy, vy), (cz, vz)):
            if c:
                along = (v if c > 0 else -v) if along is None else (along + v if c > 0 else along - v)
        scale = weighted[WEIGHT[q]]
        if along is None:
            post[q] = keep * f[q] + scale * square
            continue
        even = square + 0.5 * along * along
        post[q] = keep * f[q] + scale * (even + along)
        post[26 - q] = keep * f[26 - q] + scale * (even - along)
    return post


def lane_ids():
    return lax.broadcasted_iota(jnp.int32, (8, 128), 1)


def row_ids():
    return lax.broadcasted_iota(jnp.int32, (8, 128), 0)


def first_kernel(pops, solid, table, index, own, yup, ydown):
    lanes, rows = lane_ids(), row_ids()
    sponge = (lax.axis_index("gx") * NX + lanes) < SPONGE
    for z in range(NZ):
        aim = jnp.zeros((8, 128), F32)
        for y in range(NY):
            aim = jnp.where(rows == y, table[index[y], z], aim)
        post = relaxed([pops[q, z] for q in range(27)], sponge, aim)
        for q in range(27):
            own[pl.ds((q * NZ + z) * 8, 8), :] = post[q]
        own[pl.ds((WALL * NZ + z) * 8, 8), :] = solid[z].astype(F32)
        own[pl.ds((AIM * NZ + z) * 8, 8), :] = aim
    for out, edge, second, part in ((yup, 7, 6, 6), (ydown, 0, 1, 0)):
        out[pl.ds(0, CHANNELS * NZ), :] = own[pl.ds(edge, CHANNELS * NZ, stride=8), :]
        for a in range(3):
            out[pl.ds((CHANNELS + 3 * a) * NZ, 3 * NZ), :] = own[
                pl.ds((9 * a + part) * NZ * 8 + second, 3 * NZ, stride=8), :
            ]


def second_kernel(own, below, above, zup, zdown):
    for out, first, second, part in ((zup, NZ - 1, NZ - 2, 2), (zdown, 0, 1, 0)):
        for k in range(Z_BLOCKS):
            channel, z = (k, first) if k < CHANNELS else (9 * part + k - CHANNELS, second)
            if k == Z_BLOCKS - 1:
                channel = WALL
            out[pl.ds(k * PITCH + 2, 8), :] = own[pl.ds((channel * NZ + z) * 8, 8), :]
        for halo, near, far, group in ((below, 1, 0, 6), (above, PITCH - 2, PITCH - 1, 0)):
            out[pl.ds(near, CHANNELS, stride=PITCH), :] = halo[pl.ds(first, CHANNELS, stride=NZ), :]
            out[pl.ds(CHANNELS * PITCH + near, 9, stride=PITCH), :] = halo[
                pl.ds(9 * part * NZ + second, 9, stride=NZ), :
            ]
            wall_first = halo[pl.ds(WALL * NZ + first, 1), :]
            wall_second = halo[pl.ds(WALL * NZ + second, 1), :]
            out[pl.ds((Z_BLOCKS - 1) * PITCH + near, 1), :] = wall_second
            for a in range(3):
                out[pl.ds((9 * a + group) * PITCH + far, 3, stride=PITCH), :] = halo[
                    pl.ds((CHANNELS + 3 * a) * NZ + first, 3, stride=NZ), :
                ]
            out[pl.ds((CHANNELS + group) * PITCH + far, 3, stride=PITCH), :] = halo[
                pl.ds((CHANNELS + 3 * part) * NZ + second, 3, stride=NZ), :
            ]
            out[pl.ds(WALL * PITCH + far, 1), :] = wall_first
            out[pl.ds((Z_BLOCKS - 1) * PITCH + far, 1), :] = wall_second


def plane_at(z):
    return PAD + (z + 2) * PITCH


def third_kernel(own, below, above, floor, ceiling, full, pack):
    last = lax.axis_size("gz") - 1
    here = lax.axis_index("gz")
    for c in range(CHANNELS):
        for z in range(NZ):
            full[c, pl.ds(plane_at(z) + 2, 8), :] = own[pl.ds((c * NZ + z) * 8, 8), :]
        for halo, near in ((below, 1), (above, PITCH - 2)):
            full[c, pl.ds(plane_at(0) + near, NZ, stride=PITCH), :] = halo[pl.ds(c * NZ, NZ), :]
        full[c, pl.ds(plane_at(-1), PITCH), :] = floor[pl.ds(c * PITCH, PITCH), :]
        full[c, pl.ds(plane_at(NZ), PITCH), :] = ceiling[pl.ds(c * PITCH, PITCH), :]
    for halo, far, group in ((below, 0, 6), (above, PITCH - 1, 0)):
        for k in range(9):
            q = 9 * (k // 3) + group + k % 3
            full[q, pl.ds(plane_at(0) + far, NZ, stride=PITCH), :] = halo[
                pl.ds((CHANNELS + k) * NZ, NZ), :
            ]
        full[WALL, pl.ds(plane_at(0) + far, NZ, stride=PITCH), :] = halo[pl.ds(WALL * NZ, NZ), :]
    for halo, far, group in ((floor, -2, 18), (ceiling, NZ + 1, 0)):
        for k in range(10):
            q = group + k if k < 9 else WALL
            full[q, pl.ds(plane_at(far), PITCH), :] = halo[pl.ds((CHANNELS + k) * PITCH, PITCH), :]

    @pl.when(here == 0)
    def _():
        full[WALL, pl.ds(plane_at(-1), PITCH), :] = jnp.ones((PITCH, 128), F32)

    @pl.when(here == last)
    def _():
        for q in range(9):
            full[q, pl.ds(plane_at(NZ), PITCH), :] = full[q + 18, pl.ds(plane_at(NZ - 1), PITCH), :]

    slot = lane_ids() // 4
    for t in range(FLAT // 8):
        packed = jnp.zeros((8, 128), F32)
        for c in range(CHANNELS):
            moved = pltpu.roll(full[c, pl.ds(PAD + 8 * t, 8), :], (4 * c + 2) % 128, 1)
            packed = jnp.where(slot == c, moved, packed)
        pack[pl.ds(8 * t, 8), :] = packed


def last_kernel(full, mine, left, right, out, post, west, east, turn, walls, back):
    here_x, size_x = lax.axis_index("gx"), lax.axis_size("gx")
    top = lax.axis_index("gz") == lax.axis_size("gz") - 1
    lanes, rows = lane_ids(), row_ids()

    west[pl.ds(PAD, FLAT), :] = left[...]
    east[pl.ds(PAD, FLAT), :] = right[...]

    def edged(value, cx, channel, start):
        if cx == 0:
            return value
        if cx > 0:
            column = pltpu.roll(west[pl.ds(start, 8), :], (128 - 4 * channel - 1) % 128, 1)
            return jnp.where(lanes == 0, column, pltpu.roll(value, 1, 1))
        column = pltpu.roll(east[pl.ds(start, 8), :], (127 - 4 * channel - 2) % 128, 1)
        return jnp.where(lanes == 127, column, pltpu.roll(value, 127, 1))

    for cx in (-1, 0, 1):
        for t in range(FLAT // 8):
            start = PAD + 8 * t
            walls[cx + 1, pl.ds(start, 8), :] = edged(full[WALL, pl.ds(start, 8), :], cx, WALL, start)

    for i, source in enumerate((mine, left, right)):
        block = jnp.concatenate([source[...], jnp.zeros((128 - FLAT, 128), F32)], axis=0)
        turn[i, pl.ds(PAD, 128), :] = block.T
    strip = []
    for c in range(CHANNELS):
        a = turn[1, pl.ds(PAD + 4 * c, 8), :]
        b = turn[0, pl.ds(PAD + 4 * c, 8), :]
        d = turn[0, pl.ds(PAD + 4 * c - 4, 8), :]
        e = turn[2, pl.ds(PAD + 4 * c - 4, 8), :]
        strip.append(jnp.where(rows < 2, a, jnp.where(rows < 4, b, jnp.where(rows < 6, d, e))))

    def shifted(value, q):
        cx, cy, cz = VEL[q]
        if cx:
            value = pltpu.roll(value, cx % 8, 0)
        step = (PITCH * cz + cy) % 128
        return pltpu.roll(value, step, 1) if step else value

    moved = []
    for q in range(27):
        value = shifted(strip[q], q)
        if q != 13:
            value = jnp.where(shifted(strip[WALL], q) != 0.0, strip[26 - q], value)
        moved.append(jnp.where(strip[WALL] != 0.0, WEIGHT[q], value))
    column = here_x * NX + jnp.where(rows < 4, rows - 2, rows + (NX - 6))
    column = lax.rem(column + size_x * NX, size_x * NX)
    sides = relaxed(moved, column < SPONGE, strip[AIM])
    lid = top & (lanes >= (NZ + 2) * PITCH) & (lanes < (NZ + 3) * PITCH)
    for q in range(9):
        sides[q] = jnp.where(lid, pltpu.roll(sides[q + 18], PITCH, 1), sides[q])
    merged = []
    for k in range(9):
        merged.append(jnp.where(rows < 4, sides[3 * k + 2], sides[3 * k]))
    merged = jnp.concatenate(merged + [jnp.zeros((128 - 72, 128), F32)], axis=0)
    back[...] = merged.T

    sponge = (here_x * NX + lanes) < SPONGE
    for u in range(UNITS):
        cell = PAD + PITCH + 8 * u
        f = []
        solid = walls[1, pl.ds(cell, 8), :] != 0.0
        for q in range(27):
            cx, cy, cz = VEL[q]
            start = cell - PITCH * cz - cy
            value = edged(full[q, pl.ds(start, 8), :], cx, q, start)
            if q != 13:
                blocked = walls[cx + 1, pl.ds(start, 8), :] != 0.0
                value = jnp.where(blocked, full[26 - q, pl.ds(cell, 8), :], value)
            f.append(jnp.where(solid, WEIGHT[q], value))
        done = relaxed(f, sponge, full[AIM, pl.ds(cell, 8), :])
        for q in range(27):
            post[q, pl.ds(8 * u, 8), :] = done[q]

    @pl.when(top)
    def _():
        for q in range(9):
            post[q, pl.ds((NZ + 1) * PITCH, PITCH), :] = post[q + 18, pl.ds(NZ * PITCH, PITCH), :]

    for z in range(NZ):
        cell = (z + 1) * PITCH + 2
        solid = walls[1, pl.ds(PAD + PITCH + cell, 8), :] != 0.0
        for q in range(27):
            cx, cy, cz = VEL[q]
            start = cell - PITCH * cz - cy
            value = post[q, pl.ds(start, 8), :]
            if cx:
                lane = 8 * (q // 3) + (1 if cx > 0 else 6)
                edge = 0 if cx > 0 else 127
                side = pltpu.roll(back[pl.ds(PITCH + start, 8), :], (edge - lane) % 128, 1)
                value = jnp.where(lanes == edge, side, pltpu.roll(value, cx % 128, 1))
            if q != 13:
                blocked = walls[cx + 1, pl.ds(PAD + PITCH + start, 8), :] != 0.0
                value = jnp.where(blocked, post[26 - q, pl.ds(cell, 8), :], value)
            out[q, z] = jnp.where(solid, WEIGHT[q], value)


def both_ways(axis, ahead, back, wrap):
    size = lax.axis_size(axis)
    up = [(i, (i + 1) % size) for i in range(size if wrap else size - 1)]
    down = [(j, i) for i, j in up]
    return lax.ppermute(ahead, axis, up), lax.ppermute(back, axis, down)


def shape(*dims):
    return jax.ShapeDtypeStruct(dims, F32)


def shards(pops, solid, profile_table, profile_index):
    own, yup, ydown = pl.pallas_call(
        first_kernel,
        out_shape=[shape(CHANNELS * NZ * 8, 128), shape(Y_ROWS, 128), shape(Y_ROWS, 128)],
        in_specs=[VMEM, VMEM, SMEM, SMEM],
        out_specs=[VMEM] * 3,
        name="collide",
    )(pops, solid, profile_table, profile_index)
    below, above = both_ways("gy", yup, ydown, True)
    zup, zdown = pl.pallas_call(
        second_kernel,
        out_shape=[shape(Z_ROWS, 128)] * 2,
        in_specs=[VMEM] * 3,
        out_specs=[VMEM] * 2,
        name="pack_z",
    )(own, below, above)
    floor, ceiling = both_ways("gz", zup, zdown, False)
    full, pack = pl.pallas_call(
        third_kernel,
        out_shape=[shape(CHANNELS, ROWS, 128), shape(FLAT, 128)],
        in_specs=[VMEM] * 5,
        out_specs=[VMEM] * 2,
        name="pack_x",
    )(own, below, above, floor, ceiling)
    if lax.axis_size("gx") == 2:
        left = lax.ppermute(pack, "gx", [(0, 1), (1, 0)])
        right = left
    else:
        left, right = both_ways("gx", pack, pack, True)
    return pl.pallas_call(
        last_kernel,
        out_shape=shape(27, NZ, NY, NX),
        in_specs=[VMEM] * 4,
        out_specs=VMEM,
        scratch_shapes=[
            pltpu.VMEM((27, UNITS * 8, 128), F32),
            pltpu.VMEM((ROWS, 128), F32),
            pltpu.VMEM((ROWS, 128), F32),
            pltpu.VMEM((3, PAD + 128 + PAD, 128), F32),
            pltpu.VMEM((3, ROWS, 128), F32),
            pltpu.VMEM((128, 128), F32),
        ],
        name="finish",
    )(full, pack, left, right)


def solution(mesh):
    return jax.shard_map(
        shards,
        mesh=mesh,
        in_specs=(P(None, "gz", "gy", "gx"), P("gz", "gy", "gx"), P(None, "gz"), P("gy")),
        out_specs=P(None, "gz", "gy", "gx"),
        check_vma=False,
    )
```

```python
import jax
import jax.numpy as jnp
import numpy as np
from jax import lax
from jax.experimental import pallas as pl
from jax.experimental.pallas import tpu as pltpu
from jax.sharding import PartitionSpec as P

SPONGE = 32
TAU = 0.52
SMAG = 18.0 * 1.4142135623730951 * 0.17 * 0.17

VEL = [(cx, cy, cz) for cz in (-1, 0, 1) for cy in (-1, 0, 1) for cx in (-1, 0, 1)]
WEIGHT = [
    float(np.array([8.0 / 27.0, 2.0 / 27.0, 1.0 / 54.0, 1.0 / 216.0])[cx * cx + cy * cy + cz * cz])
    for cx, cy, cz in VEL
]
WALL, AIM, CHANNELS = 27, 28, 29
NZ, NY, NX = 4, 8, 128
PITCH = NY + 4
FLAT = (NZ + 4) * PITCH
PAD = 8
ROWS = PAD + FLAT + PAD
UNITS = (NZ + 2) * PITCH // 8

PARAMS = pltpu.CompilerParams(vmem_limit_bytes=12 * 2**20)
VMEM = pl.BlockSpec(memory_space=pltpu.VMEM)
SMEM = pl.BlockSpec(memory_space=pltpu.SMEM)
F32 = jnp.float32

Y_ROWS = (CHANNELS + 9) * NZ
Z_BLOCKS = CHANNELS + 10
Z_ROWS = -(-Z_BLOCKS * PITCH // 8) * 8


def relaxed(f, sponge, aim):
    quad = {}
    for cz in (-1, 0, 1):
        line = {}
        for cy in (-1, 0, 1):
            base = 9 * (cz + 1) + 3 * (cy + 1)
            both = f[base + 2] + f[base]
            line[cy] = (both + f[base + 1], f[base + 2] - f[base], both)
        s = line[1][0] + line[-1][0]
        sx = line[1][1] + line[-1][1]
        quad[cz] = dict(
            n=s + line[0][0],
            y=line[1][0] - line[-1][0],
            yy=s,
            x=sx + line[0][1],
            xy=line[1][1] - line[-1][1],
            xx=line[1][2] + line[-1][2] + line[0][2],
        )
    up, mid, down = quad[1], quad[0], quad[-1]
    zz = up["n"] + down["n"]
    rho = zz + mid["n"]
    jz = up["n"] - down["n"]
    jy = up["y"] + down["y"] + mid["y"]
    jx = up["x"] + down["x"] + mid["x"]
    inverse = 1.0 / rho
    ux, uy, uz = jx * inverse, jy * inverse, jz * inverse
    third = rho * (1.0 / 3.0)
    pxx = (up["xx"] + down["xx"] + mid["xx"]) - (third + jx * ux)
    pyy = (up["yy"] + down["yy"] + mid["yy"]) - (third + jy * uy)
    pzz = zz - (third + jz * uz)
    pxy = (up["xy"] + down["xy"] + mid["xy"]) - jx * uy
    pxz = (up["x"] - down["x"]) - jx * uz
    pyz = (up["y"] - down["y"]) - jy * uz
    strain = pxx * pxx + pyy * pyy + pzz * pzz + 2.0 * (pxy * pxy + pxz * pxz + pyz * pyz)
    size = jnp.sqrt(2.0 * strain)
    tau = 0.5 * (TAU + jnp.sqrt(TAU * TAU + SMAG * size * inverse))
    omega = 1.0 / tau
    keep = 1.0 - omega
    if sponge is not None:
        keep = jnp.where(sponge, 0.0, keep)
        omega = jnp.where(sponge, 1.0, omega)
        ux = jnp.where(sponge, aim, ux)
        uy = jnp.where(sponge, 0.0, uy)
        uz = jnp.where(sponge, 0.0, uz)
    square = 1.0 - 1.5 * (ux * ux + uy * uy + uz * uz)
    vx, vy, vz = 3.0 * ux, 3.0 * uy, 3.0 * uz
    share = rho * omega
    weighted = {w: share * w for w in sorted(set(WEIGHT))}
    post = [None] * 27
    for q in range(14):
        cx, cy, cz = VEL[q]
        along = None
        for c, v in ((cx, vx), (cy, vy), (cz, vz)):
            if c:
                along = (v if c > 0 else -v) if along is None else (along + v if c > 0 else along - v)
        scale = weighted[WEIGHT[q]]
        if along is None:
            post[q] = keep * f[q] + scale * square
            continue
        even = square + 0.5 * along * along
        post[q] = keep * f[q] + scale * (even + along)
        post[26 - q] = keep * f[26 - q] + scale * (even - along)
    return post


def lane_ids():
    return lax.broadcasted_iota(jnp.int32, (8, 128), 1)


def row_ids():
    return lax.broadcasted_iota(jnp.int32, (8, 128), 0)


def first_kernel(pops, solid, table, index, own, yup, ydown):
    lanes, rows = lane_ids(), row_ids()
    sponge = (lax.axis_index("gx") * NX + lanes) < SPONGE
    for z in range(NZ):
        aim = jnp.zeros((8, 128), F32)
        for y in range(NY):
            aim = jnp.where(rows == y, table[z, index[y]], aim)
        post = relaxed([pops[q, z] for q in range(27)], sponge, aim)
        for q in range(27):
            own[pl.ds((q * NZ + z) * 8, 8), :] = post[q]
        own[pl.ds((WALL * NZ + z) * 8, 8), :] = solid[z].astype(F32)
        own[pl.ds((AIM * NZ + z) * 8, 8), :] = aim
    for out, edge, second, part in ((yup, 7, 6, 6), (ydown, 0, 1, 0)):
        out[pl.ds(0, CHANNELS * NZ), :] = own[pl.ds(edge, CHANNELS * NZ, stride=8), :]
        for a in range(3):
            out[pl.ds((CHANNELS + 3 * a) * NZ, 3 * NZ), :] = own[
                pl.ds((9 * a + part) * NZ * 8 + second, 3 * NZ, stride=8), :
            ]


def second_kernel(own, below, above, zup, zdown):
    for out, first, second, part in ((zup, NZ - 1, NZ - 2, 2), (zdown, 0, 1, 0)):
        for k in range(Z_BLOCKS):
            channel, z = (k, first) if k < CHANNELS else (9 * part + k - CHANNELS, second)
            if k == Z_BLOCKS - 1:
                channel = WALL
            out[pl.ds(k * PITCH + 2, 8), :] = own[pl.ds((channel * NZ + z) * 8, 8), :]
        for halo, near, far, group in ((below, 1, 0, 6), (above, PITCH - 2, PITCH - 1, 0)):
            out[pl.ds(near, CHANNELS, stride=PITCH), :] = halo[pl.ds(first, CHANNELS, stride=NZ), :]
            out[pl.ds(CHANNELS * PITCH + near, 9, stride=PITCH), :] = halo[
                pl.ds(9 * part * NZ + second, 9, stride=NZ), :
            ]
            wall_first = halo[pl.ds(WALL * NZ + first, 1), :]
            wall_second = halo[pl.ds(WALL * NZ + second, 1), :]
            out[pl.ds((Z_BLOCKS - 1) * PITCH + near, 1), :] = wall_second
            for a in range(3):
                out[pl.ds((9 * a + group) * PITCH + far, 3, stride=PITCH), :] = halo[
                    pl.ds((CHANNELS + 3 * a) * NZ + first, 3, stride=NZ), :
                ]
            out[pl.ds((CHANNELS + group) * PITCH + far, 3, stride=PITCH), :] = halo[
                pl.ds((CHANNELS + 3 * part) * NZ + second, 3, stride=NZ), :
            ]
            out[pl.ds(WALL * PITCH + far, 1), :] = wall_first
            out[pl.ds((Z_BLOCKS - 1) * PITCH + far, 1), :] = wall_second


def plane_at(z):
    return PAD + (z + 2) * PITCH


def third_kernel(own, below, above, floor, ceiling, full, pack):
    last = lax.axis_size("gz") - 1
    here = lax.axis_index("gz")
    for c in range(CHANNELS):
        for z in range(NZ):
            full[c, pl.ds(plane_at(z) + 2, 8), :] = own[pl.ds((c * NZ + z) * 8, 8), :]
        for halo, near in ((below, 1), (above, PITCH - 2)):
            full[c, pl.ds(plane_at(0) + near, NZ, stride=PITCH), :] = halo[pl.ds(c * NZ, NZ), :]
        full[c, pl.ds(plane_at(-1), PITCH), :] = floor[pl.ds(c * PITCH, PITCH), :]
        full[c, pl.ds(plane_at(NZ), PITCH), :] = ceiling[pl.ds(c * PITCH, PITCH), :]
    for halo, far, group in ((below, 0, 6), (above, PITCH - 1, 0)):
        for k in range(9):
            q = 9 * (k // 3) + group + k % 3
            full[q, pl.ds(plane_at(0) + far, NZ, stride=PITCH), :] = halo[
                pl.ds((CHANNELS + k) * NZ, NZ), :
            ]
        full[WALL, pl.ds(plane_at(0) + far, NZ, stride=PITCH), :] = halo[pl.ds(WALL * NZ, NZ), :]
    for halo, far, group in ((floor, -2, 18), (ceiling, NZ + 1, 0)):
        for k in range(10):
            q = group + k if k < 9 else WALL
            full[q, pl.ds(plane_at(far), PITCH), :] = halo[pl.ds((CHANNELS + k) * PITCH, PITCH), :]

    @pl.when(here == 0)
    def _():
        full[WALL, pl.ds(plane_at(-1), PITCH), :] = jnp.ones((PITCH, 128), F32)

    @pl.when(here == last)
    def _():
        for q in range(9):
            full[q, pl.ds(plane_at(NZ), PITCH), :] = full[q + 18, pl.ds(plane_at(NZ - 1), PITCH), :]

    slot = lane_ids() // 4
    for t in range(FLAT // 8):
        packed = jnp.zeros((8, 128), F32)
        for c in range(CHANNELS):
            moved = pltpu.roll(full[c, pl.ds(PAD + 8 * t, 8), :], (4 * c + 2) % 128, 1)
            packed = jnp.where(slot == c, moved, packed)
        pack[pl.ds(8 * t, 8), :] = packed


def last_kernel(full, mine, left, right, out, post, west, east, turn, walls, back):
    here_x, size_x = lax.axis_index("gx"), lax.axis_size("gx")
    top = lax.axis_index("gz") == lax.axis_size("gz") - 1
    lanes, rows = lane_ids(), row_ids()

    west[pl.ds(PAD, FLAT), :] = left[...]
    east[pl.ds(PAD, FLAT), :] = right[...]

    def edged(value, cx, channel, start):
        if cx == 0:
            return value
        if cx > 0:
            column = pltpu.roll(west[pl.ds(start, 8), :], (128 - 4 * channel - 1) % 128, 1)
            return jnp.where(lanes == 0, column, pltpu.roll(value, 1, 1))
        column = pltpu.roll(east[pl.ds(start, 8), :], (127 - 4 * channel - 2) % 128, 1)
        return jnp.where(lanes == 127, column, pltpu.roll(value, 127, 1))

    for cx in (-1, 0, 1):
        for t in range(FLAT // 8):
            start = PAD + 8 * t
            walls[cx + 1, pl.ds(start, 8), :] = edged(full[WALL, pl.ds(start, 8), :], cx, WALL, start)

    for i, source in enumerate((mine, left, right)):
        block = jnp.concatenate([source[...], jnp.zeros((128 - FLAT, 128), F32)], axis=0)
        turn[i, pl.ds(PAD, 128), :] = block.T
    strip = []
    for c in range(CHANNELS):
        a = turn[1, pl.ds(PAD + 4 * c, 8), :]
        b = turn[0, pl.ds(PAD + 4 * c, 8), :]
        d = turn[0, pl.ds(PAD + 4 * c - 4, 8), :]
        e = turn[2, pl.ds(PAD + 4 * c - 4, 8), :]
        strip.append(jnp.where(rows < 2, a, jnp.where(rows < 4, b, jnp.where(rows < 6, d, e))))

    def shifted(value, q):
        cx, cy, cz = VEL[q]
        if cx:
            value = pltpu.roll(value, cx % 8, 0)
        step = (PITCH * cz + cy) % 128
        return pltpu.roll(value, step, 1) if step else value

    moved = []
    for q in range(27):
        value = shifted(strip[q], q)
        if q != 13:
            value = jnp.where(shifted(strip[WALL], q) != 0.0, strip[26 - q], value)
        moved.append(jnp.where(strip[WALL] != 0.0, WEIGHT[q], value))
    column = here_x * NX + jnp.where(rows < 4, rows - 2, rows + (NX - 6))
    column = lax.rem(column + size_x * NX, size_x * NX)
    sides = relaxed(moved, column < SPONGE, strip[AIM])
    lid = top & (lanes >= (NZ + 2) * PITCH) & (lanes < (NZ + 3) * PITCH)
    for q in range(9):
        sides[q] = jnp.where(lid, pltpu.roll(sides[q + 18], PITCH, 1), sides[q])
    merged = []
    for k in range(9):
        merged.append(jnp.where(rows < 4, sides[3 * k + 2], sides[3 * k]))
    merged = jnp.concatenate(merged + [jnp.zeros((128 - 72, 128), F32)], axis=0)
    back[...] = merged.T

    sponge = (here_x * NX + lanes) < SPONGE
    for u in range(UNITS):
        cell = PAD + PITCH + 8 * u
        f = []
        solid = walls[1, pl.ds(cell, 8), :] != 0.0
        for q in range(27):
            cx, cy, cz = VEL[q]
            start = cell - PITCH * cz - cy
            value = edged(full[q, pl.ds(start, 8), :], cx, q, start)
            if q != 13:
                blocked = walls[cx + 1, pl.ds(start, 8), :] != 0.0
                value = jnp.where(blocked, full[26 - q, pl.ds(cell, 8), :], value)
            f.append(jnp.where(solid, WEIGHT[q], value))
        done = relaxed(f, sponge, full[AIM, pl.ds(cell, 8), :])
        for q in range(27):
            post[q, pl.ds(8 * u, 8), :] = done[q]

    @pl.when(top)
    def _():
        for q in range(9):
            post[q, pl.ds((NZ + 1) * PITCH, PITCH), :] = post[q + 18, pl.ds(NZ * PITCH, PITCH), :]

    for z in range(NZ):
        cell = (z + 1) * PITCH + 2
        solid = walls[1, pl.ds(PAD + PITCH + cell, 8), :] != 0.0
        for q in range(27):
            cx, cy, cz = VEL[q]
            start = cell - PITCH * cz - cy
            value = post[q, pl.ds(start, 8), :]
            if cx:
                lane = 8 * (q // 3) + (1 if cx > 0 else 6)
                edge = 0 if cx > 0 else 127
                side = pltpu.roll(back[pl.ds(PITCH + start, 8), :], (edge - lane) % 128, 1)
                value = jnp.where(lanes == edge, side, pltpu.roll(value, cx % 128, 1))
            if q != 13:
                blocked = walls[cx + 1, pl.ds(PAD + PITCH + start, 8), :] != 0.0
                value = jnp.where(blocked, post[26 - q, pl.ds(cell, 8), :], value)
            out[q, z] = jnp.where(solid, WEIGHT[q], value)


def both_ways(axis, ahead, back, wrap):
    size = lax.axis_size(axis)
    up = [(i, (i + 1) % size) for i in range(size if wrap else size - 1)]
    down = [(j, i) for i, j in up]
    return lax.ppermute(ahead, axis, up), lax.ppermute(back, axis, down)


def shape(*dims):
    return jax.ShapeDtypeStruct(dims, F32)


def shards(pops, solid, profile_table, profile_index):
    own, yup, ydown = pl.pallas_call(
        first_kernel,
        out_shape=[shape(CHANNELS * NZ * 8, 128), shape(Y_ROWS, 128), shape(Y_ROWS, 128)],
        in_specs=[VMEM, VMEM, SMEM, SMEM],
        out_specs=[VMEM] * 3,
        compiler_params=PARAMS,
        name="collide",
    )(pops, solid, profile_table.T, profile_index)
    below, above = both_ways("gy", yup, ydown, True)
    zup, zdown = pl.pallas_call(
        second_kernel,
        out_shape=[shape(Z_ROWS, 128)] * 2,
        in_specs=[VMEM] * 3,
        out_specs=[VMEM] * 2,
        compiler_params=PARAMS,
        name="pack_z",
    )(own, below, above)
    floor, ceiling = both_ways("gz", zup, zdown, False)
    full, pack = pl.pallas_call(
        third_kernel,
        out_shape=[shape(CHANNELS, ROWS, 128), shape(FLAT, 128)],
        in_specs=[VMEM] * 5,
        out_specs=[VMEM] * 2,
        compiler_params=PARAMS,
        name="pack_x",
    )(own, below, above, floor, ceiling)
    if lax.axis_size("gx") == 2:
        left = lax.ppermute(pack, "gx", [(0, 1), (1, 0)])
        right = left
    else:
        left, right = both_ways("gx", pack, pack, True)
    return pl.pallas_call(
        last_kernel,
        out_shape=shape(27, NZ, NY, NX),
        in_specs=[VMEM] * 4,
        out_specs=VMEM,
        scratch_shapes=[
            pltpu.VMEM((27, UNITS * 8, 128), F32),
            pltpu.VMEM((ROWS, 128), F32),
            pltpu.VMEM((ROWS, 128), F32),
            pltpu.VMEM((3, PAD + 128 + PAD, 128), F32),
            pltpu.VMEM((3, ROWS, 128), F32),
            pltpu.VMEM((128, 128), F32),
        ],
        compiler_params=PARAMS,
        name="finish",
    )(full, pack, left, right)


def solution(mesh):
    return jax.shard_map(
        shards,
        mesh=mesh,
        in_specs=(P(None, "gz", "gy", "gx"), P("gz", "gy", "gx"), P(None, "gz"), P("gy")),
        out_specs=P(None, "gz", "gy", "gx"),
        check_vma=False,
    )
```

```python
import functools

import jax
import jax.numpy as jnp
import numpy as np
from jax import lax
from jax.experimental import pallas as pl
from jax.experimental.pallas import tpu as pltpu
from jax.sharding import PartitionSpec as P

SPONGE = 32
TAU = 0.52
SMAG = 18.0 * 1.4142135623730951 * 0.17 * 0.17

VEL = [(cx, cy, cz) for cz in (-1, 0, 1) for cy in (-1, 0, 1) for cx in (-1, 0, 1)]
WEIGHT = [
    float(np.array([8.0 / 27.0, 2.0 / 27.0, 1.0 / 54.0, 1.0 / 216.0])[cx * cx + cy * cy + cz * cz])
    for cx, cy, cz in VEL
]
WALL, AIM, CHANNELS = 27, 28, 29
NZ, NY, NX = 4, 8, 128
PITCH = NY + 4
FLAT = (NZ + 4) * PITCH
PAD = 8
ROWS = PAD + FLAT + PAD
UNITS = (NZ + 2) * PITCH // 8

PARAMS = pltpu.CompilerParams(vmem_limit_bytes=12 * 2**20)
VMEM = pl.BlockSpec(memory_space=pltpu.VMEM)
HBM = pl.BlockSpec(memory_space=pltpu.HBM)
F32 = jnp.float32

Y_ROWS = (CHANNELS + 9) * NZ
Z_BLOCKS = CHANNELS + 10
Z_ROWS = -(-Z_BLOCKS * PITCH // 8) * 8


def relaxed(f, sponge, aim):
    quad = {}
    for cz in (-1, 0, 1):
        line = {}
        for cy in (-1, 0, 1):
            base = 9 * (cz + 1) + 3 * (cy + 1)
            both = f[base + 2] + f[base]
            line[cy] = (both + f[base + 1], f[base + 2] - f[base], both)
        s = line[1][0] + line[-1][0]
        sx = line[1][1] + line[-1][1]
        quad[cz] = dict(
            n=s + line[0][0],
            y=line[1][0] - line[-1][0],
            yy=s,
            x=sx + line[0][1],
            xy=line[1][1] - line[-1][1],
            xx=line[1][2] + line[-1][2] + line[0][2],
        )
    up, mid, down = quad[1], quad[0], quad[-1]
    zz = up["n"] + down["n"]
    rho = zz + mid["n"]
    jz = up["n"] - down["n"]
    jy = up["y"] + down["y"] + mid["y"]
    jx = up["x"] + down["x"] + mid["x"]
    inverse = 1.0 / rho
    ux, uy, uz = jx * inverse, jy * inverse, jz * inverse
    third = rho * (1.0 / 3.0)
    pxx = (up["xx"] + down["xx"] + mid["xx"]) - (third + jx * ux)
    pyy = (up["yy"] + down["yy"] + mid["yy"]) - (third + jy * uy)
    pzz = zz - (third + jz * uz)
    pxy = (up["xy"] + down["xy"] + mid["xy"]) - jx * uy
    pxz = (up["x"] - down["x"]) - jx * uz
    pyz = (up["y"] - down["y"]) - jy * uz
    strain = pxx * pxx + pyy * pyy + pzz * pzz + 2.0 * (pxy * pxy + pxz * pxz + pyz * pyz)
    size = jnp.sqrt(2.0 * strain)
    tau = 0.5 * (TAU + jnp.sqrt(TAU * TAU + SMAG * size * inverse))
    omega = 1.0 / tau
    keep = 1.0 - omega
    if sponge is not None:
        keep = jnp.where(sponge, 0.0, keep)
        omega = jnp.where(sponge, 1.0, omega)
        ux = jnp.where(sponge, aim, ux)
        uy = jnp.where(sponge, 0.0, uy)
        uz = jnp.where(sponge, 0.0, uz)
    square = 1.0 - 1.5 * (ux * ux + uy * uy + uz * uz)
    vx, vy, vz = 3.0 * ux, 3.0 * uy, 3.0 * uz
    share = rho * omega
    weighted = {w: share * w for w in sorted(set(WEIGHT))}
    post = [None] * 27
    for q in range(14):
        cx, cy, cz = VEL[q]
        along = None
        for c, v in ((cx, vx), (cy, vy), (cz, vz)):
            if c:
                along = (v if c > 0 else -v) if along is None else (along + v if c > 0 else along - v)
        scale = weighted[WEIGHT[q]]
        if along is None:
            post[q] = keep * f[q] + scale * square
            continue
        even = square + 0.5 * along * along
        post[q] = keep * f[q] + scale * (even + along)
        post[26 - q] = keep * f[26 - q] + scale * (even - along)
    return post


def lane_ids():
    return lax.broadcasted_iota(jnp.int32, (8, 128), 1)


def row_ids():
    return lax.broadcasted_iota(jnp.int32, (8, 128), 0)


def by_parity(axis, one, two, body):
    even = lax.rem(lax.axis_index(axis), 2) == 0
    pl.when(even)(lambda: body(one, two))
    pl.when(jnp.logical_not(even))(lambda: body(two, one))


def first_kernel(pops_at, solid_at, table_at, index_at, own, one, two, pops, solid, table, index, sems):
    copies = [
        pltpu.make_async_copy(source, target, sems.at[i])
        for i, (source, target) in enumerate(
            ((pops_at, pops), (solid_at, solid), (table_at, table), (index_at, index))
        )
    ]
    for copy in copies:
        copy.start()
    for copy in copies:
        copy.wait()
    lanes, rows = lane_ids(), row_ids()
    sponge = (lax.axis_index("gx") * NX + lanes) < SPONGE
    for z in range(NZ):
        aim = jnp.zeros((8, 128), F32)
        for y in range(NY):
            aim = jnp.where(rows == y, table[z, index[y]], aim)
        post = relaxed([pops[q, z] for q in range(27)], sponge, aim)
        for q in range(27):
            own[pl.ds((q * NZ + z) * 8, 8), :] = post[q]
        own[pl.ds((WALL * NZ + z) * 8, 8), :] = solid[z].astype(F32)
        own[pl.ds((AIM * NZ + z) * 8, 8), :] = aim

    def pack(yup, ydown):
        for out, edge, second, part in ((yup, 7, 6, 6), (ydown, 0, 1, 0)):
            out[pl.ds(0, CHANNELS * NZ), :] = own[pl.ds(edge, CHANNELS * NZ, stride=8), :]
            for a in range(3):
                out[pl.ds((CHANNELS + 3 * a) * NZ, 3 * NZ), :] = own[
                    pl.ds((9 * a + part) * NZ * 8 + second, 3 * NZ, stride=8), :
                ]

    by_parity("gy", one, two, pack)


def second_kernel(own, y_one, y_two, z_one, z_two):
    by_parity(
        "gy",
        y_one,
        y_two,
        lambda above, below: by_parity(
            "gz", z_one, z_two, lambda zup, zdown: pack_planes(own, below, above, zup, zdown)
        ),
    )


def pack_planes(own, below, above, zup, zdown):
    for out, first, second, part in ((zup, NZ - 1, NZ - 2, 2), (zdown, 0, 1, 0)):
        for k in range(Z_BLOCKS):
            channel, z = (k, first) if k < CHANNELS else (9 * part + k - CHANNELS, second)
            if k == Z_BLOCKS - 1:
                channel = WALL
            out[pl.ds(k * PITCH + 2, 8), :] = own[pl.ds((channel * NZ + z) * 8, 8), :]
        for halo, near, far, group in ((below, 1, 0, 6), (above, PITCH - 2, PITCH - 1, 0)):
            out[pl.ds(near, CHANNELS, stride=PITCH), :] = halo[pl.ds(first, CHANNELS, stride=NZ), :]
            out[pl.ds(CHANNELS * PITCH + near, 9, stride=PITCH), :] = halo[
                pl.ds(9 * part * NZ + second, 9, stride=NZ), :
            ]
            wall_first = halo[pl.ds(WALL * NZ + first, 1), :]
            wall_second = halo[pl.ds(WALL * NZ + second, 1), :]
            out[pl.ds((Z_BLOCKS - 1) * PITCH + near, 1), :] = wall_second
            for a in range(3):
                out[pl.ds((9 * a + group) * PITCH + far, 3, stride=PITCH), :] = halo[
                    pl.ds((CHANNELS + 3 * a) * NZ + first, 3, stride=NZ), :
                ]
            out[pl.ds((CHANNELS + group) * PITCH + far, 3, stride=PITCH), :] = halo[
                pl.ds((CHANNELS + 3 * part) * NZ + second, 3, stride=NZ), :
            ]
            out[pl.ds(WALL * PITCH + far, 1), :] = wall_first
            out[pl.ds((Z_BLOCKS - 1) * PITCH + far, 1), :] = wall_second


def plane_at(z):
    return PAD + (z + 2) * PITCH


def add_rows(full, above, below):
    for c in range(CHANNELS):
        for halo, near in ((below, 1), (above, PITCH - 2)):
            full[c, pl.ds(plane_at(0) + near, NZ, stride=PITCH), :] = halo[pl.ds(c * NZ, NZ), :]
    for halo, far, group in ((below, 0, 6), (above, PITCH - 1, 0)):
        for k in range(9):
            q = 9 * (k // 3) + group + k % 3
            full[q, pl.ds(plane_at(0) + far, NZ, stride=PITCH), :] = halo[
                pl.ds((CHANNELS + k) * NZ, NZ), :
            ]
        full[WALL, pl.ds(plane_at(0) + far, NZ, stride=PITCH), :] = halo[pl.ds(WALL * NZ, NZ), :]


def add_planes(full, ceiling, floor):
    for c in range(CHANNELS):
        full[c, pl.ds(plane_at(-1), PITCH), :] = floor[pl.ds(c * PITCH, PITCH), :]
        full[c, pl.ds(plane_at(NZ), PITCH), :] = ceiling[pl.ds(c * PITCH, PITCH), :]
    for halo, far, group in ((floor, -2, 18), (ceiling, NZ + 1, 0)):
        for k in range(10):
            q = group + k if k < 9 else WALL
            full[q, pl.ds(plane_at(far), PITCH), :] = halo[pl.ds((CHANNELS + k) * PITCH, PITCH), :]


def third_kernel(own, y_one, y_two, z_one, z_two, full, pack):
    last = lax.axis_size("gz") - 1
    here = lax.axis_index("gz")
    for c in range(CHANNELS):
        for z in range(NZ):
            full[c, pl.ds(plane_at(z) + 2, 8), :] = own[pl.ds((c * NZ + z) * 8, 8), :]
    by_parity("gy", y_one, y_two, functools.partial(add_rows, full))
    by_parity("gz", z_one, z_two, functools.partial(add_planes, full))

    @pl.when(here == 0)
    def _():
        full[WALL, pl.ds(plane_at(-1), PITCH), :] = jnp.ones((PITCH, 128), F32)

    @pl.when(here == last)
    def _():
        for q in range(9):
            full[q, pl.ds(plane_at(NZ), PITCH), :] = full[q + 18, pl.ds(plane_at(NZ - 1), PITCH), :]

    slot = lane_ids() // 4
    for t in range(FLAT // 8):
        packed = jnp.zeros((8, 128), F32)
        for c in range(CHANNELS):
            moved = pltpu.roll(full[c, pl.ds(PAD + 8 * t, 8), :], (4 * c + 2) % 128, 1)
            packed = jnp.where(slot == c, moved, packed)
        pack[pl.ds(8 * t, 8), :] = packed


def last_kernel(full, mine, x_one, x_two, out, post, west, east, turn, walls, back):
    here_x, size_x = lax.axis_index("gx"), lax.axis_size("gx")
    top = lax.axis_index("gz") == lax.axis_size("gz") - 1
    lanes, rows = lane_ids(), row_ids()

    def spread(right, left):
        west[pl.ds(PAD, FLAT), :] = left[...]
        east[pl.ds(PAD, FLAT), :] = right[...]

    by_parity("gx", x_one, x_two, spread)

    def edged(value, cx, channel, start):
        if cx == 0:
            return value
        if cx > 0:
            column = pltpu.roll(west[pl.ds(start, 8), :], (128 - 4 * channel - 1) % 128, 1)
            return jnp.where(lanes == 0, column, pltpu.roll(value, 1, 1))
        column = pltpu.roll(east[pl.ds(start, 8), :], (127 - 4 * channel - 2) % 128, 1)
        return jnp.where(lanes == 127, column, pltpu.roll(value, 127, 1))

    for cx in (-1, 0, 1):
        for t in range(FLAT // 8):
            start = PAD + 8 * t
            walls[cx + 1, pl.ds(start, 8), :] = edged(full[WALL, pl.ds(start, 8), :], cx, WALL, start)

    for i, source in enumerate((mine[...], west[pl.ds(PAD, FLAT), :], east[pl.ds(PAD, FLAT), :])):
        block = jnp.concatenate([source, jnp.zeros((128 - FLAT, 128), F32)], axis=0)
        turn[i, pl.ds(PAD, 128), :] = block.T
    strip = []
    for c in range(CHANNELS):
        a = turn[1, pl.ds(PAD + 4 * c, 8), :]
        b = turn[0, pl.ds(PAD + 4 * c, 8), :]
        d = turn[0, pl.ds(PAD + 4 * c - 4, 8), :]
        e = turn[2, pl.ds(PAD + 4 * c - 4, 8), :]
        strip.append(jnp.where(rows < 2, a, jnp.where(rows < 4, b, jnp.where(rows < 6, d, e))))

    def shifted(value, q):
        cx, cy, cz = VEL[q]
        if cx:
            value = pltpu.roll(value, cx % 8, 0)
        step = (PITCH * cz + cy) % 128
        return pltpu.roll(value, step, 1) if step else value

    moved = []
    for q in range(27):
        value = shifted(strip[q], q)
        if q != 13:
            value = jnp.where(shifted(strip[WALL], q) != 0.0, strip[26 - q], value)
        moved.append(jnp.where(strip[WALL] != 0.0, WEIGHT[q], value))
    column = here_x * NX + jnp.where(rows < 4, rows - 2, rows + (NX - 6))
    column = lax.rem(column + size_x * NX, size_x * NX)
    sides = relaxed(moved, column < SPONGE, strip[AIM])
    lid = top & (lanes >= (NZ + 2) * PITCH) & (lanes < (NZ + 3) * PITCH)
    for q in range(9):
        sides[q] = jnp.where(lid, pltpu.roll(sides[q + 18], PITCH, 1), sides[q])
    merged = []
    for k in range(9):
        merged.append(jnp.where(rows < 4, sides[3 * k + 2], sides[3 * k]))
    merged = jnp.concatenate(merged + [jnp.zeros((128 - 72, 128), F32)], axis=0)
    back[...] = merged.T

    sponge = (here_x * NX + lanes) < SPONGE
    for u in range(UNITS):
        cell = PAD + PITCH + 8 * u
        f = []
        solid = walls[1, pl.ds(cell, 8), :] != 0.0
        for q in range(27):
            cx, cy, cz = VEL[q]
            start = cell - PITCH * cz - cy
            value = edged(full[q, pl.ds(start, 8), :], cx, q, start)
            if q != 13:
                blocked = walls[cx + 1, pl.ds(start, 8), :] != 0.0
                value = jnp.where(blocked, full[26 - q, pl.ds(cell, 8), :], value)
            f.append(jnp.where(solid, WEIGHT[q], value))
        done = relaxed(f, sponge, full[AIM, pl.ds(cell, 8), :])
        for q in range(27):
            post[q, pl.ds(8 * u, 8), :] = done[q]

    @pl.when(top)
    def _():
        for q in range(9):
            post[q, pl.ds((NZ + 1) * PITCH, PITCH), :] = post[q + 18, pl.ds(NZ * PITCH, PITCH), :]

    for z in range(NZ):
        cell = (z + 1) * PITCH + 2
        solid = walls[1, pl.ds(PAD + PITCH + cell, 8), :] != 0.0
        for q in range(27):
            cx, cy, cz = VEL[q]
            start = cell - PITCH * cz - cy
            value = post[q, pl.ds(start, 8), :]
            if cx:
                lane = 8 * (q // 3) + (1 if cx > 0 else 6)
                edge = 0 if cx > 0 else 127
                side = pltpu.roll(back[pl.ds(PITCH + start, 8), :], (edge - lane) % 128, 1)
                value = jnp.where(lanes == edge, side, pltpu.roll(value, cx % 128, 1))
            if q != 13:
                blocked = walls[cx + 1, pl.ds(PAD + PITCH + start, 8), :] != 0.0
                value = jnp.where(blocked, post[26 - q, pl.ds(cell, 8), :], value)
            out[q, z] = jnp.where(solid, WEIGHT[q], value)


def swap(value, axis, turn, wrap):
    size = lax.axis_size(axis)
    pairs = [(i, (i + 1) % size) for i in range(turn, size if wrap else size - 1, 2)]
    return lax.ppermute(value, axis, pairs + [(j, i) for i, j in pairs])


def shape(*dims):
    return jax.ShapeDtypeStruct(dims, F32)


def shards(pops, solid, profile_table, profile_index):
    own, y_one, y_two = pl.pallas_call(
        first_kernel,
        out_shape=[shape(CHANNELS * NZ * 8, 128), shape(Y_ROWS, 128), shape(Y_ROWS, 128)],
        in_specs=[HBM] * 4,
        out_specs=[VMEM] * 3,
        scratch_shapes=[
            pltpu.VMEM(pops.shape, F32),
            pltpu.VMEM(solid.shape, jnp.int32),
            pltpu.SMEM(profile_table.shape[::-1], F32),
            pltpu.SMEM(profile_index.shape, jnp.int32),
            pltpu.SemaphoreType.DMA((4,)),
        ],
        compiler_params=PARAMS,
        name="collide",
    )(pops, solid, profile_table.T, profile_index)
    y_two = swap(y_two, "gy", 1, True)
    y_one = swap(y_one, "gy", 0, True)
    z_one, z_two = pl.pallas_call(
        second_kernel,
        out_shape=[shape(Z_ROWS, 128)] * 2,
        in_specs=[VMEM] * 3,
        out_specs=[VMEM] * 2,
        compiler_params=PARAMS,
        name="pack_z",
    )(own, y_one, y_two)
    z_two = swap(z_two, "gz", 1, False)
    z_one = swap(z_one, "gz", 0, False)
    full, mine = pl.pallas_call(
        third_kernel,
        out_shape=[shape(CHANNELS, ROWS, 128), shape(FLAT, 128)],
        in_specs=[VMEM] * 5,
        out_specs=[VMEM] * 2,
        compiler_params=PARAMS,
        name="pack_x",
    )(own, y_one, y_two, z_one, z_two)
    x_one = swap(mine, "gx", 0, True)
    x_two = x_one if lax.axis_size("gx") == 2 else swap(mine, "gx", 1, True)
    return pl.pallas_call(
        last_kernel,
        out_shape=shape(27, NZ, NY, NX),
        in_specs=[VMEM] * 4,
        out_specs=VMEM,
        scratch_shapes=[
            pltpu.VMEM((27, UNITS * 8, 128), F32),
            pltpu.VMEM((ROWS, 128), F32),
            pltpu.VMEM((ROWS, 128), F32),
            pltpu.VMEM((3, PAD + 128 + PAD, 128), F32),
            pltpu.VMEM((3, ROWS, 128), F32),
            pltpu.VMEM((128, 128), F32),
        ],
        compiler_params=PARAMS,
        name="finish",
    )(full, mine, x_one, x_two)


def solution(mesh):
    return jax.shard_map(
        shards,
        mesh=mesh,
        in_specs=(P(None, "gz", "gy", "gx"), P("gz", "gy", "gx"), P(None, "gz"), P("gy")),
        out_specs=P(None, "gz", "gy", "gx"),
        check_vma=False,
    )
```

```python
import functools

import jax
import jax.numpy as jnp
import numpy as np
from jax import lax
from jax.experimental import pallas as pl
from jax.experimental.pallas import tpu as pltpu
from jax.sharding import PartitionSpec as P

SPONGE = 32
TAU = 0.52
SMAG = 18.0 * 1.4142135623730951 * 0.17 * 0.17

VEL = [(cx, cy, cz) for cz in (-1, 0, 1) for cy in (-1, 0, 1) for cx in (-1, 0, 1)]
WEIGHT = [
    float(np.array([8.0 / 27.0, 2.0 / 27.0, 1.0 / 54.0, 1.0 / 216.0])[cx * cx + cy * cy + cz * cz])
    for cx, cy, cz in VEL
]
WALL, AIM, CHANNELS = 27, 28, 29
NZ, NY, NX = 4, 8, 128
PITCH = NY + 4
FLAT = (NZ + 4) * PITCH
PAD = 8
ROWS = PAD + FLAT + PAD
UNITS = (NZ + 2) * PITCH // 8

PARAMS = pltpu.CompilerParams(vmem_limit_bytes=12 * 2**20)
VMEM = pl.BlockSpec(memory_space=pltpu.VMEM)
HBM = pl.BlockSpec(memory_space=pltpu.HBM)
F32 = jnp.float32

Y_ROWS = (CHANNELS + 9) * NZ
Z_BLOCKS = CHANNELS + 10
Z_PITCH = NY + 2
Z_FAR = Z_BLOCKS * Z_PITCH
Z_ROWS = -(-(Z_FAR + 2 * 12) // 8) * 8


def relaxed(f, sponge, aim):
    quad = {}
    for cz in (-1, 0, 1):
        line = {}
        for cy in (-1, 0, 1):
            base = 9 * (cz + 1) + 3 * (cy + 1)
            both = f[base + 2] + f[base]
            line[cy] = (both + f[base + 1], f[base + 2] - f[base], both)
        s = line[1][0] + line[-1][0]
        sx = line[1][1] + line[-1][1]
        quad[cz] = dict(
            n=s + line[0][0],
            y=line[1][0] - line[-1][0],
            yy=s,
            x=sx + line[0][1],
            xy=line[1][1] - line[-1][1],
            xx=line[1][2] + line[-1][2] + line[0][2],
        )
    up, mid, down = quad[1], quad[0], quad[-1]
    zz = up["n"] + down["n"]
    rho = zz + mid["n"]
    jz = up["n"] - down["n"]
    jy = up["y"] + down["y"] + mid["y"]
    jx = up["x"] + down["x"] + mid["x"]
    inverse = 1.0 / rho
    ux, uy, uz = jx * inverse, jy * inverse, jz * inverse
    third = rho * (1.0 / 3.0)
    pxx = (up["xx"] + down["xx"] + mid["xx"]) - (third + jx * ux)
    pyy = (up["yy"] + down["yy"] + mid["yy"]) - (third + jy * uy)
    pzz = zz - (third + jz * uz)
    pxy = (up["xy"] + down["xy"] + mid["xy"]) - jx * uy
    pxz = (up["x"] - down["x"]) - jx * uz
    pyz = (up["y"] - down["y"]) - jy * uz
    strain = pxx * pxx + pyy * pyy + pzz * pzz + 2.0 * (pxy * pxy + pxz * pxz + pyz * pyz)
    size = jnp.sqrt(2.0 * strain)
    tau = 0.5 * (TAU + jnp.sqrt(TAU * TAU + SMAG * size * inverse))
    omega = 1.0 / tau
    keep = 1.0 - omega
    if sponge is not None:
        keep = jnp.where(sponge, 0.0, keep)
        omega = jnp.where(sponge, 1.0, omega)
        ux = jnp.where(sponge, aim, ux)
        uy = jnp.where(sponge, 0.0, uy)
        uz = jnp.where(sponge, 0.0, uz)
    square = 1.0 - 1.5 * (ux * ux + uy * uy + uz * uz)
    vx, vy, vz = 3.0 * ux, 3.0 * uy, 3.0 * uz
    share = rho * omega
    weighted = {w: share * w for w in sorted(set(WEIGHT))}
    post = [None] * 27
    for q in range(14):
        cx, cy, cz = VEL[q]
        along = None
        for c, v in ((cx, vx), (cy, vy), (cz, vz)):
            if c:
                along = (v if c > 0 else -v) if along is None else (along + v if c > 0 else along - v)
        scale = weighted[WEIGHT[q]]
        if along is None:
            post[q] = keep * f[q] + scale * square
            continue
        even = square + 0.5 * along * along
        post[q] = keep * f[q] + scale * (even + along)
        post[26 - q] = keep * f[26 - q] + scale * (even - along)
    return post


def lane_ids():
    return lax.broadcasted_iota(jnp.int32, (8, 128), 1)


def row_ids():
    return lax.broadcasted_iota(jnp.int32, (8, 128), 0)


def by_parity(axis, one, two, body):
    even = lax.rem(lax.axis_index(axis), 2) == 0
    pl.when(even)(lambda: body(one, two))
    pl.when(jnp.logical_not(even))(lambda: body(two, one))


def first_kernel(pops_at, solid_at, table_at, index_at, own, one, two, pops, solid, table, index, sems):
    copies = [
        pltpu.make_async_copy(source, target, sems.at[i])
        for i, (source, target) in enumerate(
            ((pops_at, pops), (solid_at, solid), (table_at, table), (index_at, index))
        )
    ]
    for copy in copies:
        copy.start()
    for copy in copies:
        copy.wait()
    lanes, rows = lane_ids(), row_ids()
    sponge = (lax.axis_index("gx") * NX + lanes) < SPONGE
    for z in range(NZ):
        aim = jnp.zeros((8, 128), F32)
        for y in range(NY):
            aim = jnp.where(rows == y, table[z, index[y]], aim)
        post = relaxed([pops[q, z] for q in range(27)], sponge, aim)
        for q in range(27):
            own[pl.ds((q * NZ + z) * 8, 8), :] = post[q]
        own[pl.ds((WALL * NZ + z) * 8, 8), :] = solid[z].astype(F32)
        own[pl.ds((AIM * NZ + z) * 8, 8), :] = aim

    def pack(yup, ydown):
        for out, edge, second, part in ((yup, 7, 6, 6), (ydown, 0, 1, 0)):
            out[pl.ds(0, CHANNELS * NZ), :] = own[pl.ds(edge, CHANNELS * NZ, stride=8), :]
            for a in range(3):
                out[pl.ds((CHANNELS + 3 * a) * NZ, 3 * NZ), :] = own[
                    pl.ds((9 * a + part) * NZ * 8 + second, 3 * NZ, stride=8), :
                ]

    by_parity("gy", one, two, pack)


def second_kernel(own, y_one, y_two, z_two, z_one):
    by_parity(
        "gy",
        y_one,
        y_two,
        lambda above, below: by_parity(
            "gz", z_one, z_two, lambda zup, zdown: pack_planes(own, below, above, zup, zdown)
        ),
    )


def pack_planes(own, below, above, zup, zdown):
    for out, first, second, part in ((zup, NZ - 1, NZ - 2, 2), (zdown, 0, 1, 0)):
        for k in range(Z_BLOCKS):
            channel, z = (k, first) if k < CHANNELS else (9 * part + k - CHANNELS, second)
            if k == Z_BLOCKS - 1:
                channel = WALL
            out[pl.ds(k * Z_PITCH + 1, 8), :] = own[pl.ds((channel * NZ + z) * 8, 8), :]
        for side, (halo, near, group) in enumerate(((below, 0, 2), (above, Z_PITCH - 1, 0))):
            out[pl.ds(near, CHANNELS, stride=Z_PITCH), :] = halo[
                pl.ds(first, CHANNELS, stride=NZ), :
            ]
            out[pl.ds(CHANNELS * Z_PITCH + near, 9, stride=Z_PITCH), :] = halo[
                pl.ds(9 * part * NZ + second, 9, stride=NZ), :
            ]
            out[pl.ds((Z_BLOCKS - 1) * Z_PITCH + near, 1), :] = halo[
                pl.ds(WALL * NZ + second, 1), :
            ]
            far = Z_FAR + 12 * side
            out[pl.ds(far, 9), :] = halo[pl.ds(CHANNELS * NZ + first, 9, stride=NZ), :]
            out[pl.ds(far + 9, 3), :] = halo[
                pl.ds((CHANNELS + 3 * part) * NZ + second, 3, stride=NZ), :
            ]


def plane_at(z):
    return PAD + (z + 2) * PITCH


def add_rows(full, above, below):
    for c in range(CHANNELS):
        for halo, near in ((below, 1), (above, PITCH - 2)):
            full[c, pl.ds(plane_at(0) + near, NZ, stride=PITCH), :] = halo[pl.ds(c * NZ, NZ), :]
    for halo, far, group in ((below, 0, 6), (above, PITCH - 1, 0)):
        for k in range(9):
            q = 9 * (k // 3) + group + k % 3
            full[q, pl.ds(plane_at(0) + far, NZ, stride=PITCH), :] = halo[
                pl.ds((CHANNELS + k) * NZ, NZ), :
            ]
        full[WALL, pl.ds(plane_at(0) + far, NZ, stride=PITCH), :] = halo[pl.ds(WALL * NZ, NZ), :]


def add_planes(full, ceiling, floor):
    for halo, near, far, part in ((floor, -1, -2, 2), (ceiling, NZ, NZ + 1, 0)):
        blocks = [(c, near) for c in range(CHANNELS)]
        blocks += [(9 * part + k, far) for k in range(9)] + [(WALL, far)]
        for k, (c, z) in enumerate(blocks):
            full[c, pl.ds(plane_at(z) + 1, Z_PITCH), :] = halo[pl.ds(k * Z_PITCH, Z_PITCH), :]
        for side, (row, group) in enumerate(((0, 2), (PITCH - 1, 0))):
            start = Z_FAR + 12 * side
            for k in range(9):
                q = 9 * (k // 3) + 3 * group + k % 3
                full[q, pl.ds(plane_at(near) + row, 1), :] = halo[pl.ds(start + k, 1), :]
            for k in range(3):
                q = 9 * part + 3 * group + k
                full[q, pl.ds(plane_at(far) + row, 1), :] = halo[pl.ds(start + 9 + k, 1), :]
            first = 0 if side == 0 else Z_PITCH - 1
            for k, z in ((WALL, near), (Z_BLOCKS - 1, far)):
                full[WALL, pl.ds(plane_at(z) + row, 1), :] = halo[pl.ds(k * Z_PITCH + first, 1), :]


def third_kernel(own, y_one, y_two, z_two, z_one, full, pack):
    last = lax.axis_size("gz") - 1
    here = lax.axis_index("gz")
    for c in range(CHANNELS):
        for z in range(NZ):
            full[c, pl.ds(plane_at(z) + 2, 8), :] = own[pl.ds((c * NZ + z) * 8, 8), :]
    by_parity("gy", y_one, y_two, functools.partial(add_rows, full))
    by_parity("gz", z_one, z_two, functools.partial(add_planes, full))

    @pl.when(here == 0)
    def _():
        full[WALL, pl.ds(plane_at(-1), PITCH), :] = jnp.ones((PITCH, 128), F32)

    @pl.when(here == last)
    def _():
        for q in range(9):
            full[q, pl.ds(plane_at(NZ), PITCH), :] = full[q + 18, pl.ds(plane_at(NZ - 1), PITCH), :]

    slot = lane_ids() // 4
    for t in range(FLAT // 8):
        packed = jnp.zeros((8, 128), F32)
        for c in range(CHANNELS):
            moved = pltpu.roll(full[c, pl.ds(PAD + 8 * t, 8), :], (4 * c + 2) % 128, 1)
            packed = jnp.where(slot == c, moved, packed)
        pack[pl.ds(8 * t, 8), :] = packed


def last_kernel(full, mine, x_one, x_two, out, post, west, east, turn, walls, back):
    here_x, size_x = lax.axis_index("gx"), lax.axis_size("gx")
    top = lax.axis_index("gz") == lax.axis_size("gz") - 1
    lanes, rows = lane_ids(), row_ids()

    def spread(right, left):
        west[pl.ds(PAD, FLAT), :] = left[...]
        east[pl.ds(PAD, FLAT), :] = right[...]

    by_parity("gx", x_one, x_two, spread)

    def edged(value, cx, channel, start):
        if cx == 0:
            return value
        if cx > 0:
            column = pltpu.roll(west[pl.ds(start, 8), :], (128 - 4 * channel - 1) % 128, 1)
            return jnp.where(lanes == 0, column, pltpu.roll(value, 1, 1))
        column = pltpu.roll(east[pl.ds(start, 8), :], (127 - 4 * channel - 2) % 128, 1)
        return jnp.where(lanes == 127, column, pltpu.roll(value, 127, 1))

    for cx in (-1, 0, 1):
        for t in range(FLAT // 8):
            start = PAD + 8 * t
            walls[cx + 1, pl.ds(start, 8), :] = edged(full[WALL, pl.ds(start, 8), :], cx, WALL, start)

    for i, source in enumerate((mine[...], west[pl.ds(PAD, FLAT), :], east[pl.ds(PAD, FLAT), :])):
        block = jnp.concatenate([source, jnp.zeros((128 - FLAT, 128), F32)], axis=0)
        turn[i, pl.ds(PAD, 128), :] = block.T
    strip = []
    for c in range(CHANNELS):
        a = turn[1, pl.ds(PAD + 4 * c, 8), :]
        b = turn[0, pl.ds(PAD + 4 * c, 8), :]
        d = turn[0, pl.ds(PAD + 4 * c - 4, 8), :]
        e = turn[2, pl.ds(PAD + 4 * c - 4, 8), :]
        strip.append(jnp.where(rows < 2, a, jnp.where(rows < 4, b, jnp.where(rows < 6, d, e))))

    def shifted(value, q):
        cx, cy, cz = VEL[q]
        if cx:
            value = pltpu.roll(value, cx % 8, 0)
        step = (PITCH * cz + cy) % 128
        return pltpu.roll(value, step, 1) if step else value

    moved = []
    for q in range(27):
        value = shifted(strip[q], q)
        if q != 13:
            value = jnp.where(shifted(strip[WALL], q) != 0.0, strip[26 - q], value)
        moved.append(jnp.where(strip[WALL] != 0.0, WEIGHT[q], value))
    column = here_x * NX + jnp.where(rows < 4, rows - 2, rows + (NX - 6))
    column = lax.rem(column + size_x * NX, size_x * NX)
    sides = relaxed(moved, column < SPONGE, strip[AIM])
    lid = top & (lanes >= (NZ + 2) * PITCH) & (lanes < (NZ + 3) * PITCH)
    for q in range(9):
        sides[q] = jnp.where(lid, pltpu.roll(sides[q + 18], PITCH, 1), sides[q])
    merged = []
    for k in range(9):
        merged.append(jnp.where(rows < 4, sides[3 * k + 2], sides[3 * k]))
    merged = jnp.concatenate(merged + [jnp.zeros((128 - 72, 128), F32)], axis=0)
    back[...] = merged.T

    sponge = (here_x * NX + lanes) < SPONGE
    for u in range(UNITS):
        cell = PAD + PITCH + 8 * u
        f = []
        solid = walls[1, pl.ds(cell, 8), :] != 0.0
        for q in range(27):
            cx, cy, cz = VEL[q]
            start = cell - PITCH * cz - cy
            value = edged(full[q, pl.ds(start, 8), :], cx, q, start)
            if q != 13:
                blocked = walls[cx + 1, pl.ds(start, 8), :] != 0.0
                value = jnp.where(blocked, full[26 - q, pl.ds(cell, 8), :], value)
            f.append(jnp.where(solid, WEIGHT[q], value))
        done = relaxed(f, sponge, full[AIM, pl.ds(cell, 8), :])
        for q in range(27):
            post[q, pl.ds(8 * u, 8), :] = done[q]

    @pl.when(top)
    def _():
        for q in range(9):
            post[q, pl.ds((NZ + 1) * PITCH, PITCH), :] = post[q + 18, pl.ds(NZ * PITCH, PITCH), :]

    for z in range(NZ):
        cell = (z + 1) * PITCH + 2
        solid = walls[1, pl.ds(PAD + PITCH + cell, 8), :] != 0.0
        for q in range(27):
            cx, cy, cz = VEL[q]
            start = cell - PITCH * cz - cy
            value = post[q, pl.ds(start, 8), :]
            if cx:
                lane = 8 * (q // 3) + (1 if cx > 0 else 6)
                edge = 0 if cx > 0 else 127
                side = pltpu.roll(back[pl.ds(PITCH + start, 8), :], (edge - lane) % 128, 1)
                value = jnp.where(lanes == edge, side, pltpu.roll(value, cx % 128, 1))
            if q != 13:
                blocked = walls[cx + 1, pl.ds(PAD + PITCH + start, 8), :] != 0.0
                value = jnp.where(blocked, post[26 - q, pl.ds(cell, 8), :], value)
            out[q, z] = jnp.where(solid, WEIGHT[q], value)


def swap(value, axis, turn, wrap):
    size = lax.axis_size(axis)
    pairs = [(i, (i + 1) % size) for i in range(turn, size if wrap else size - 1, 2)]
    return lax.ppermute(value, axis, pairs + [(j, i) for i, j in pairs])


def shape(*dims):
    return jax.ShapeDtypeStruct(dims, F32)


def shards(pops, solid, profile_table, profile_index):
    own, y_one, y_two = pl.pallas_call(
        first_kernel,
        out_shape=[shape(CHANNELS * NZ * 8, 128), shape(Y_ROWS, 128), shape(Y_ROWS, 128)],
        in_specs=[HBM] * 4,
        out_specs=[VMEM] * 3,
        scratch_shapes=[
            pltpu.VMEM(pops.shape, F32),
            pltpu.VMEM(solid.shape, jnp.int32),
            pltpu.SMEM(profile_table.shape[::-1], F32),
            pltpu.SMEM(profile_index.shape, jnp.int32),
            pltpu.SemaphoreType.DMA((4,)),
        ],
        compiler_params=PARAMS,
        name="collide",
    )(*(pltpu.with_memory_space_constraint(a, pltpu.HBM) for a in (pops, solid, profile_table.T, profile_index)))
    y_two = swap(y_two, "gy", 1, True)
    y_one = swap(y_one, "gy", 0, True)
    z_two, z_one = pl.pallas_call(
        second_kernel,
        out_shape=[shape(Z_ROWS, 128)] * 2,
        in_specs=[VMEM] * 3,
        out_specs=[VMEM] * 2,
        compiler_params=PARAMS,
        name="pack_z",
    )(own, y_one, y_two)
    z_two = swap(z_two, "gz", 1, False)
    z_one = swap(z_one, "gz", 0, False)
    full, mine = pl.pallas_call(
        third_kernel,
        out_shape=[shape(CHANNELS, ROWS, 128), shape(FLAT, 128)],
        in_specs=[VMEM] * 5,
        out_specs=[VMEM] * 2,
        compiler_params=PARAMS,
        name="pack_x",
    )(own, y_one, y_two, z_two, z_one)
    x_one = swap(mine, "gx", 0, True)
    x_two = x_one if lax.axis_size("gx") == 2 else swap(mine, "gx", 1, True)
    return pl.pallas_call(
        last_kernel,
        out_shape=shape(27, NZ, NY, NX),
        in_specs=[VMEM] * 4,
        out_specs=VMEM,
        scratch_shapes=[
            pltpu.VMEM((27, UNITS * 8, 128), F32),
            pltpu.VMEM((ROWS, 128), F32),
            pltpu.VMEM((ROWS, 128), F32),
            pltpu.VMEM((3, PAD + 128 + PAD, 128), F32),
            pltpu.VMEM((3, ROWS, 128), F32),
            pltpu.VMEM((128, 128), F32),
        ],
        compiler_params=PARAMS,
        name="finish",
    )(full, mine, x_one, x_two)


def solution(mesh):
    return jax.shard_map(
        shards,
        mesh=mesh,
        in_specs=(P(None, "gz", "gy", "gx"), P("gz", "gy", "gx"), P(None, "gz"), P("gy")),
        out_specs=P(None, "gz", "gy", "gx"),
        check_vma=False,
    )
```

```python
import functools

import jax
import jax.numpy as jnp
import numpy as np
from jax import lax
from jax.experimental import pallas as pl
from jax.experimental.pallas import tpu as pltpu
from jax.sharding import PartitionSpec as P

SPONGE = 32
TAU = 0.52
SMAG = 18.0 * 1.4142135623730951 * 0.17 * 0.17

VEL = [(cx, cy, cz) for cz in (-1, 0, 1) for cy in (-1, 0, 1) for cx in (-1, 0, 1)]
WEIGHT = [
    float(np.array([8.0 / 27.0, 2.0 / 27.0, 1.0 / 54.0, 1.0 / 216.0])[cx * cx + cy * cy + cz * cz])
    for cx, cy, cz in VEL
]
WALL, AIM, CHANNELS = 27, 28, 29
NZ, NY, NX = 4, 8, 128
PITCH = NY + 4
FLAT = (NZ + 4) * PITCH
PAD = 8
ROWS = PAD + FLAT + PAD
UNITS = (NZ + 2) * PITCH // 8

PARAMS = pltpu.CompilerParams(vmem_limit_bytes=12 * 2**20)
VMEM = pl.BlockSpec(memory_space=pltpu.VMEM)
HBM = pl.BlockSpec(memory_space=pltpu.HBM)
F32 = jnp.float32

Y_ROWS = (CHANNELS + 9) * NZ
Z_BLOCKS = CHANNELS + 10
Z_PITCH = NY + 2
Z_FAR = Z_BLOCKS * Z_PITCH
Z_ROWS = -(-(Z_FAR + 2 * 12) // 8) * 8

X_ROWS = 2 * (WALL + 1)


def relaxed(f, sponge, aim):
    quad = {}
    for cz in (-1, 0, 1):
        line = {}
        for cy in (-1, 0, 1):
            base = 9 * (cz + 1) + 3 * (cy + 1)
            both = f[base + 2] + f[base]
            line[cy] = (both + f[base + 1], f[base + 2] - f[base], both)
        s = line[1][0] + line[-1][0]
        sx = line[1][1] + line[-1][1]
        quad[cz] = dict(
            n=s + line[0][0],
            y=line[1][0] - line[-1][0],
            yy=s,
            x=sx + line[0][1],
            xy=line[1][1] - line[-1][1],
            xx=line[1][2] + line[-1][2] + line[0][2],
        )
    up, mid, down = quad[1], quad[0], quad[-1]
    zz = up["n"] + down["n"]
    rho = zz + mid["n"]
    jz = up["n"] - down["n"]
    jy = up["y"] + down["y"] + mid["y"]
    jx = up["x"] + down["x"] + mid["x"]
    inverse = 1.0 / rho
    ux, uy, uz = jx * inverse, jy * inverse, jz * inverse
    third = rho * (1.0 / 3.0)
    pxx = (up["xx"] + down["xx"] + mid["xx"]) - (third + jx * ux)
    pyy = (up["yy"] + down["yy"] + mid["yy"]) - (third + jy * uy)
    pzz = zz - (third + jz * uz)
    pxy = (up["xy"] + down["xy"] + mid["xy"]) - jx * uy
    pxz = (up["x"] - down["x"]) - jx * uz
    pyz = (up["y"] - down["y"]) - jy * uz
    strain = pxx * pxx + pyy * pyy + pzz * pzz + 2.0 * (pxy * pxy + pxz * pxz + pyz * pyz)
    size = jnp.sqrt(2.0 * strain)
    tau = 0.5 * (TAU + jnp.sqrt(TAU * TAU + SMAG * size * inverse))
    omega = 1.0 / tau
    keep = 1.0 - omega
    if sponge is not None:
        keep = jnp.where(sponge, 0.0, keep)
        omega = jnp.where(sponge, 1.0, omega)
        ux = jnp.where(sponge, aim, ux)
        uy = jnp.where(sponge, 0.0, uy)
        uz = jnp.where(sponge, 0.0, uz)
    square = 1.0 - 1.5 * (ux * ux + uy * uy + uz * uz)
    vx, vy, vz = 3.0 * ux, 3.0 * uy, 3.0 * uz
    share = rho * omega
    weighted = {w: share * w for w in sorted(set(WEIGHT))}
    post = [None] * 27
    for q in range(14):
        cx, cy, cz = VEL[q]
        along = None
        for c, v in ((cx, vx), (cy, vy), (cz, vz)):
            if c:
                along = (v if c > 0 else -v) if along is None else (along + v if c > 0 else along - v)
        scale = weighted[WEIGHT[q]]
        if along is None:
            post[q] = keep * f[q] + scale * square
            continue
        even = square + 0.5 * along * along
        post[q] = keep * f[q] + scale * (even + along)
        post[26 - q] = keep * f[26 - q] + scale * (even - along)
    return post


def lane_ids():
    return lax.broadcasted_iota(jnp.int32, (8, 128), 1)


def row_ids():
    return lax.broadcasted_iota(jnp.int32, (8, 128), 0)


def by_parity(axis, one, two, body):
    even = lax.rem(lax.axis_index(axis), 2) == 0
    pl.when(even)(lambda: body(one, two))
    pl.when(jnp.logical_not(even))(lambda: body(two, one))


def first_kernel(pops_at, solid_at, table_at, index_at, own, one, two, pops, solid, table, index, sems):
    copies = [
        pltpu.make_async_copy(source, target, sems.at[i])
        for i, (source, target) in enumerate(
            ((pops_at, pops), (solid_at, solid), (table_at, table), (index_at, index))
        )
    ]
    for copy in copies:
        copy.start()
    for copy in copies:
        copy.wait()
    lanes, rows = lane_ids(), row_ids()
    sponge = (lax.axis_index("gx") * NX + lanes) < SPONGE
    for z in range(NZ):
        aim = jnp.zeros((8, 128), F32)
        for y in range(NY):
            aim = jnp.where(rows == y, table[z, index[y]], aim)
        post = relaxed([pops[q, z] for q in range(27)], sponge, aim)
        for q in range(27):
            own[pl.ds((q * NZ + z) * 8, 8), :] = post[q]
        own[pl.ds((WALL * NZ + z) * 8, 8), :] = solid[z].astype(F32)
        own[pl.ds((AIM * NZ + z) * 8, 8), :] = aim

    def pack(yup, ydown):
        for out, edge, second, part in ((yup, 7, 6, 6), (ydown, 0, 1, 0)):
            out[pl.ds(0, CHANNELS * NZ), :] = own[pl.ds(edge, CHANNELS * NZ, stride=8), :]
            for a in range(3):
                out[pl.ds((CHANNELS + 3 * a) * NZ, 3 * NZ), :] = own[
                    pl.ds((9 * a + part) * NZ * 8 + second, 3 * NZ, stride=8), :
                ]

    by_parity("gy", one, two, pack)


def second_kernel(own, y_one, y_two, z_two, z_one):
    by_parity(
        "gy",
        y_one,
        y_two,
        lambda above, below: by_parity(
            "gz", z_one, z_two, lambda zup, zdown: pack_planes(own, below, above, zup, zdown)
        ),
    )


def pack_planes(own, below, above, zup, zdown):
    for out, first, second, part in ((zup, NZ - 1, NZ - 2, 2), (zdown, 0, 1, 0)):
        for k in range(Z_BLOCKS):
            channel, z = (k, first) if k < CHANNELS else (9 * part + k - CHANNELS, second)
            if k == Z_BLOCKS - 1:
                channel = WALL
            out[pl.ds(k * Z_PITCH + 1, 8), :] = own[pl.ds((channel * NZ + z) * 8, 8), :]
        for side, (halo, near, group) in enumerate(((below, 0, 2), (above, Z_PITCH - 1, 0))):
            out[pl.ds(near, CHANNELS, stride=Z_PITCH), :] = halo[
                pl.ds(first, CHANNELS, stride=NZ), :
            ]
            out[pl.ds(CHANNELS * Z_PITCH + near, 9, stride=Z_PITCH), :] = halo[
                pl.ds(9 * part * NZ + second, 9, stride=NZ), :
            ]
            out[pl.ds((Z_BLOCKS - 1) * Z_PITCH + near, 1), :] = halo[
                pl.ds(WALL * NZ + second, 1), :
            ]
            far = Z_FAR + 12 * side
            out[pl.ds(far, 9), :] = halo[pl.ds(CHANNELS * NZ + first, 9, stride=NZ), :]
            out[pl.ds(far + 9, 3), :] = halo[
                pl.ds((CHANNELS + 3 * part) * NZ + second, 3, stride=NZ), :
            ]


def plane_at(z):
    return PAD + (z + 2) * PITCH


def add_rows(full, above, below):
    for c in range(CHANNELS):
        for halo, near in ((below, 1), (above, PITCH - 2)):
            full[c, pl.ds(plane_at(0) + near, NZ, stride=PITCH), :] = halo[pl.ds(c * NZ, NZ), :]
    for halo, far, group in ((below, 0, 6), (above, PITCH - 1, 0)):
        for k in range(9):
            q = 9 * (k // 3) + group + k % 3
            full[q, pl.ds(plane_at(0) + far, NZ, stride=PITCH), :] = halo[
                pl.ds((CHANNELS + k) * NZ, NZ), :
            ]
        full[WALL, pl.ds(plane_at(0) + far, NZ, stride=PITCH), :] = halo[pl.ds(WALL * NZ, NZ), :]


def add_planes(full, ceiling, floor):
    for halo, near, far, part in ((floor, -1, -2, 2), (ceiling, NZ, NZ + 1, 0)):
        blocks = [(c, near) for c in range(CHANNELS)]
        blocks += [(9 * part + k, far) for k in range(9)] + [(WALL, far)]
        for k, (c, z) in enumerate(blocks):
            full[c, pl.ds(plane_at(z) + 1, Z_PITCH), :] = halo[pl.ds(k * Z_PITCH, Z_PITCH), :]
        for side, (row, group) in enumerate(((0, 2), (PITCH - 1, 0))):
            start = Z_FAR + 12 * side
            for k in range(9):
                q = 9 * (k // 3) + 3 * group + k % 3
                full[q, pl.ds(plane_at(near) + row, 1), :] = halo[pl.ds(start + k, 1), :]
            for k in range(3):
                q = 9 * part + 3 * group + k
                full[q, pl.ds(plane_at(far) + row, 1), :] = halo[pl.ds(start + 9 + k, 1), :]
            first = 0 if side == 0 else Z_PITCH - 1
            for k, z in ((WALL, near), (Z_BLOCKS - 1, far)):
                full[WALL, pl.ds(plane_at(z) + row, 1), :] = halo[pl.ds(k * Z_PITCH + first, 1), :]


def third_kernel(own, y_one, y_two, z_two, z_one, full, columns, message, pack):
    last = lax.axis_size("gz") - 1
    here = lax.axis_index("gz")
    for c in range(CHANNELS):
        for z in range(NZ):
            full[c, pl.ds(plane_at(z) + 2, 8), :] = own[pl.ds((c * NZ + z) * 8, 8), :]
    by_parity("gy", y_one, y_two, functools.partial(add_rows, full))
    by_parity("gz", z_one, z_two, functools.partial(add_planes, full))

    @pl.when(here == 0)
    def _():
        full[WALL, pl.ds(plane_at(-1), PITCH), :] = jnp.ones((PITCH, 128), F32)

    @pl.when(here == last)
    def _():
        for q in range(9):
            full[q, pl.ds(plane_at(NZ), PITCH), :] = full[q + 18, pl.ds(plane_at(NZ - 1), PITCH), :]

    slot = lane_ids() // 4
    pack[pl.ds(FLAT, 128 - FLAT), :] = jnp.zeros((128 - FLAT, 128), F32)
    for t in range(FLAT // 8):
        packed = jnp.zeros((8, 128), F32)
        for c in range(CHANNELS):
            moved = pltpu.roll(full[c, pl.ds(PAD + 8 * t, 8), :], (4 * c + 2) % 128, 1)
            packed = jnp.where(slot == c, moved, packed)
        pack[pl.ds(8 * t, 8), :] = packed
    columns[pl.ds(PAD, 128), :] = pack[...].T

    def row(c, i, count):
        return columns[pl.ds(PAD + 4 * c + i, count), :]

    def returned(q, near, far):
        cx, cy, cz = VEL[q]
        step = (-PITCH * cz - cy) % 128
        value = row(26 - q, near, 8)
        value = pltpu.roll(value, step, 1) if step else value
        return jnp.where(row(WALL, far, 8) != 0.0, value, row(q, far, 8))[:1]

    for c in range(WALL + 1):
        cx = VEL[c][0] if c < 27 else 0
        if cx == 0:
            message[pl.ds(2 * c, 2), :] = row(c, 1, 2)
        elif cx > 0:
            message[pl.ds(2 * c, 1), :] = returned(c, 1, 0)
            message[pl.ds(2 * c + 1, 1), :] = row(c, 1, 1)
        else:
            message[pl.ds(2 * c, 1), :] = row(c, 2, 1)
            message[pl.ds(2 * c + 1, 1), :] = returned(c, 2, 3)


def block_kernel(full, post, walls):
    top = lax.axis_index("gz") == lax.axis_size("gz") - 1
    sponge = (lax.axis_index("gx") * NX + lane_ids()) < SPONGE
    for t in range(ROWS // 8):
        rows = pl.ds(8 * t, 8)
        flags = full[WALL, rows, :]
        for cx in (-1, 0, 1):
            walls[cx + 1, rows, :] = pltpu.roll(flags, cx % 128, 1) if cx else flags
    for u in range(UNITS):
        cell = PAD + PITCH + 8 * u
        f = []
        solid = walls[1, pl.ds(cell, 8), :] != 0.0
        for q in range(27):
            cx, cy, cz = VEL[q]
            start = cell - PITCH * cz - cy
            value = full[q, pl.ds(start, 8), :]
            if cx:
                value = pltpu.roll(value, cx % 128, 1)
            if q != 13:
                blocked = walls[cx + 1, pl.ds(start, 8), :] != 0.0
                value = jnp.where(blocked, full[26 - q, pl.ds(cell, 8), :], value)
            f.append(jnp.where(solid, WEIGHT[q], value))
        done = relaxed(f, sponge, full[AIM, pl.ds(cell, 8), :])
        for q in range(27):
            post[q, pl.ds(8 * u, 8), :] = done[q]

    @pl.when(top)
    def _():
        for q in range(9):
            post[q, pl.ds((NZ + 1) * PITCH, PITCH), :] = post[q + 18, pl.ds(NZ * PITCH, PITCH), :]


def last_kernel(full, block, columns, x_one, x_two, out, west, east, post, walls, back, done, sems):
    here_x, size_x = lax.axis_index("gx"), lax.axis_size("gx")
    top = lax.axis_index("gz") == lax.axis_size("gz") - 1
    lanes, rows = lane_ids(), row_ids()

    def spread(right, left):
        west[pl.ds(PAD, X_ROWS), :] = left[...]
        east[pl.ds(PAD, X_ROWS), :] = right[...]

    by_parity("gx", x_one, x_two, spread)

    strip = []
    for c in range(CHANNELS):
        cx = VEL[c][0] if c < 27 else 0
        value = jnp.where(
            rows < 4, columns[pl.ds(PAD + 4 * c, 8), :], columns[pl.ds(PAD + 4 * c - 4, 8), :]
        )
        if c <= WALL and cx >= 0:
            value = jnp.where(rows < 2, west[pl.ds(PAD + 2 * c - (cx == 0), 8), :], value)
        if c <= WALL and cx <= 0:
            value = jnp.where(rows >= 6, east[pl.ds(PAD + 2 * c - 6 + (cx == 0), 8), :], value)
        strip.append(value)
    strip[WALL] = jnp.where((rows == 0) | (rows == 7), 0.0, strip[WALL])

    def shifted(value, q):
        cx, cy, cz = VEL[q]
        if cx:
            value = pltpu.roll(value, cx % 8, 0)
        step = (PITCH * cz + cy) % 128
        return pltpu.roll(value, step, 1) if step else value

    moved = []
    for q in range(27):
        value = shifted(strip[q], q)
        if q != 13:
            value = jnp.where(shifted(strip[WALL], q) != 0.0, strip[26 - q], value)
        moved.append(jnp.where(strip[WALL] != 0.0, WEIGHT[q], value))
    column = here_x * NX + jnp.where(rows < 4, rows - 2, rows + (NX - 6))
    column = lax.rem(column + size_x * NX, size_x * NX)
    sides = relaxed(moved, column < SPONGE, strip[AIM])
    lid = top & (lanes >= (NZ + 2) * PITCH) & (lanes < (NZ + 3) * PITCH)
    for q in range(9):
        sides[q] = jnp.where(lid, pltpu.roll(sides[q + 18], PITCH, 1), sides[q])
    sides.append(strip[WALL])
    sides = [
        jnp.where((rows == 1) | (rows == 5), pltpu.roll(side, 4, 0), side) for side in sides
    ]
    sides += [jnp.zeros((8, 128), F32)] * 4
    for i in range(2):
        back[i] = jnp.concatenate(sides[16 * i : 16 * i + 16], axis=0).T

    def column_at(c, place, lane, start):
        value = back[c // 16, pl.ds(start, 8), :]
        return pltpu.roll(value, (lane - 8 * (c % 16) - place) % 128, 1)

    rim = (lanes == 0) | (lanes == 127)
    for u in range(UNITS):
        for q in range(27):
            post[q, pl.ds(8 * u, 8), :] = jnp.where(
                rim, column_at(q, 2, 0, PITCH + 8 * u), block[q, pl.ds(8 * u, 8), :]
            )
        flags = full[WALL, pl.ds(PAD + PITCH + 8 * u, 8), :]
        walls[1, pl.ds(8 * u, 8), :] = flags
        for cx, edge, place in ((1, 0, 5), (-1, 127, 6)):
            walls[cx + 1, pl.ds(8 * u, 8), :] = jnp.where(
                lanes == edge, column_at(WALL, place, edge, PITCH + 8 * u), pltpu.roll(flags, cx % 128, 1)
            )

    copies = []
    for z in range(NZ):
        cell = (z + 1) * PITCH + 2
        solid = walls[1, pl.ds(cell, 8), :] != 0.0
        for q in range(27):
            cx, cy, cz = VEL[q]
            start = cell - PITCH * cz - cy
            value = post[q, pl.ds(start, 8), :]
            if cx:
                edge, place = (0, 5) if cx > 0 else (127, 6)
                side = column_at(q, place, edge, PITCH + start)
                value = jnp.where(lanes == edge, side, pltpu.roll(value, cx % 128, 1))
            if q != 13:
                blocked = walls[cx + 1, pl.ds(start, 8), :] != 0.0
                value = jnp.where(blocked, post[26 - q, pl.ds(cell, 8), :], value)
            done[q, z] = jnp.where(solid, WEIGHT[q], value)
        copies.append(pltpu.make_async_copy(done.at[:, z], out.at[:, z], sems.at[z]))
        copies[-1].start()
    for copy in copies:
        copy.wait()


def swap(value, axis, turn, wrap):
    size = lax.axis_size(axis)
    pairs = [(i, (i + 1) % size) for i in range(turn, size if wrap else size - 1, 2)]
    return lax.ppermute(value, axis, pairs + [(j, i) for i, j in pairs])


def shape(*dims):
    return jax.ShapeDtypeStruct(dims, F32)


def shards(pops, solid, profile_table, profile_index):
    own, y_one, y_two = pl.pallas_call(
        first_kernel,
        out_shape=[shape(CHANNELS * NZ * 8, 128), shape(Y_ROWS, 128), shape(Y_ROWS, 128)],
        in_specs=[HBM] * 4,
        out_specs=[VMEM] * 3,
        scratch_shapes=[
            pltpu.VMEM(pops.shape, F32),
            pltpu.VMEM(solid.shape, jnp.int32),
            pltpu.SMEM(profile_table.shape[::-1], F32),
            pltpu.SMEM(profile_index.shape, jnp.int32),
            pltpu.SemaphoreType.DMA((4,)),
        ],
        compiler_params=PARAMS,
        name="collide",
    )(*(pltpu.with_memory_space_constraint(a, pltpu.HBM) for a in (pops, solid, profile_table.T, profile_index)))
    y_two = swap(y_two, "gy", 1, True)
    y_one = swap(y_one, "gy", 0, True)
    z_two, z_one = pl.pallas_call(
        second_kernel,
        out_shape=[shape(Z_ROWS, 128)] * 2,
        in_specs=[VMEM] * 3,
        out_specs=[VMEM] * 2,
        compiler_params=PARAMS,
        name="pack_z",
    )(own, y_one, y_two)
    z_two = swap(z_two, "gz", 1, False)
    z_one = swap(z_one, "gz", 0, False)
    full, columns, message = pl.pallas_call(
        third_kernel,
        out_shape=[shape(CHANNELS, ROWS, 128), shape(PAD + 128 + PAD, 128), shape(X_ROWS, 128)],
        in_specs=[VMEM] * 5,
        out_specs=[VMEM] * 3,
        scratch_shapes=[pltpu.VMEM((128, 128), F32)],
        compiler_params=PARAMS,
        name="pack_x",
    )(own, y_one, y_two, z_two, z_one)
    x_one = swap(message, "gx", 0, True)
    x_two = x_one if lax.axis_size("gx") == 2 else swap(message, "gx", 1, True)
    block = pl.pallas_call(
        block_kernel,
        out_shape=shape(27, UNITS * 8, 128),
        in_specs=[VMEM],
        out_specs=VMEM,
        scratch_shapes=[pltpu.VMEM((3, ROWS, 128), F32)],
        compiler_params=PARAMS,
        cost_estimate=pl.CostEstimate(
            flops=27 * 20 * UNITS * 1024, bytes_accessed=2**22, transcendentals=0
        ),
        name="block",
    )(full)
    return pl.pallas_call(
        last_kernel,
        out_shape=shape(27, NZ, NY, NX),
        in_specs=[VMEM] * 5,
        out_specs=HBM,
        scratch_shapes=[
            pltpu.VMEM((PAD + X_ROWS + PAD, 128), F32),
            pltpu.VMEM((PAD + X_ROWS + PAD, 128), F32),
            pltpu.VMEM((27, UNITS * 8, 128), F32),
            pltpu.VMEM((3, UNITS * 8, 128), F32),
            pltpu.VMEM((2, 128, 128), F32),
            pltpu.VMEM((27, NZ, NY, NX), F32),
            pltpu.SemaphoreType.DMA((NZ,)),
        ],
        compiler_params=PARAMS,
        name="finish",
    )(full, block, columns, x_one, x_two)


def solution(mesh):
    return jax.shard_map(
        shards,
        mesh=mesh,
        in_specs=(P(None, "gz", "gy", "gx"), P("gz", "gy", "gx"), P(None, "gz"), P("gy")),
        out_specs=P(None, "gz", "gy", "gx"),
        check_vma=False,
    )
```

```python
import functools

import jax
import jax.numpy as jnp
import numpy as np
from jax import lax
from jax.experimental import pallas as pl
from jax.experimental.pallas import tpu as pltpu
from jax.sharding import PartitionSpec as P

SPONGE = 32
TAU = 0.52
SMAG = 18.0 * 1.4142135623730951 * 0.17 * 0.17

VEL = [(cx, cy, cz) for cz in (-1, 0, 1) for cy in (-1, 0, 1) for cx in (-1, 0, 1)]
WEIGHT = [
    float(np.array([8.0 / 27.0, 2.0 / 27.0, 1.0 / 54.0, 1.0 / 216.0])[cx * cx + cy * cy + cz * cz])
    for cx, cy, cz in VEL
]
WALL, AIM, CHANNELS = 27, 28, 29
NZ, NY, NX = 4, 8, 128
PITCH = NY + 4
FLAT = (NZ + 4) * PITCH
PAD = 8
ROWS = PAD + FLAT + PAD
UNITS = (NZ + 2) * PITCH // 8

PARAMS = pltpu.CompilerParams(vmem_limit_bytes=12 * 2**20)
VMEM = pl.BlockSpec(memory_space=pltpu.VMEM)
HBM = pl.BlockSpec(memory_space=pltpu.HBM)
F32 = jnp.float32

Y_ROWS = (CHANNELS + 9) * NZ
Z_BLOCKS = CHANNELS + 10
Z_PITCH = NY + 2
Z_FAR = Z_BLOCKS * Z_PITCH
Z_ROWS = -(-(Z_FAR + 2 * 12) // 8) * 8

OWN = NZ * PITCH
EDGE = 2 * PITCH


def relaxed(f, sponge, aim):
    quad = {}
    for cz in (-1, 0, 1):
        line = {}
        for cy in (-1, 0, 1):
            base = 9 * (cz + 1) + 3 * (cy + 1)
            both = f[base + 2] + f[base]
            line[cy] = (both + f[base + 1], f[base + 2] - f[base], both)
        s = line[1][0] + line[-1][0]
        sx = line[1][1] + line[-1][1]
        quad[cz] = dict(
            n=s + line[0][0],
            y=line[1][0] - line[-1][0],
            yy=s,
            x=sx + line[0][1],
            xy=line[1][1] - line[-1][1],
            xx=line[1][2] + line[-1][2] + line[0][2],
        )
    up, mid, down = quad[1], quad[0], quad[-1]
    zz = up["n"] + down["n"]
    rho = zz + mid["n"]
    jz = up["n"] - down["n"]
    jy = up["y"] + down["y"] + mid["y"]
    jx = up["x"] + down["x"] + mid["x"]
    inverse = 1.0 / rho
    ux, uy, uz = jx * inverse, jy * inverse, jz * inverse
    third = rho * (1.0 / 3.0)
    pxx = (up["xx"] + down["xx"] + mid["xx"]) - (third + jx * ux)
    pyy = (up["yy"] + down["yy"] + mid["yy"]) - (third + jy * uy)
    pzz = zz - (third + jz * uz)
    pxy = (up["xy"] + down["xy"] + mid["xy"]) - jx * uy
    pxz = (up["x"] - down["x"]) - jx * uz
    pyz = (up["y"] - down["y"]) - jy * uz
    strain = pxx * pxx + pyy * pyy + pzz * pzz + 2.0 * (pxy * pxy + pxz * pxz + pyz * pyz)
    size = jnp.sqrt(2.0 * strain)
    tau = 0.5 * (TAU + jnp.sqrt(TAU * TAU + SMAG * size * inverse))
    omega = 1.0 / tau
    keep = 1.0 - omega
    if sponge is not None:
        keep = jnp.where(sponge, 0.0, keep)
        omega = jnp.where(sponge, 1.0, omega)
        ux = jnp.where(sponge, aim, ux)
        uy = jnp.where(sponge, 0.0, uy)
        uz = jnp.where(sponge, 0.0, uz)
    square = 1.0 - 1.5 * (ux * ux + uy * uy + uz * uz)
    vx, vy, vz = 3.0 * ux, 3.0 * uy, 3.0 * uz
    share = rho * omega
    weighted = {w: share * w for w in sorted(set(WEIGHT))}
    post = [None] * 27
    for q in range(14):
        cx, cy, cz = VEL[q]
        along = None
        for c, v in ((cx, vx), (cy, vy), (cz, vz)):
            if c:
                along = (v if c > 0 else -v) if along is None else (along + v if c > 0 else along - v)
        scale = weighted[WEIGHT[q]]
        if along is None:
            post[q] = keep * f[q] + scale * square
            continue
        even = square + 0.5 * along * along
        post[q] = keep * f[q] + scale * (even + along)
        post[26 - q] = keep * f[26 - q] + scale * (even - along)
    return post


def lane_ids():
    return lax.broadcasted_iota(jnp.int32, (8, 128), 1)


def row_ids():
    return lax.broadcasted_iota(jnp.int32, (8, 128), 0)


def by_parity(axis, one, two, body):
    even = lax.rem(lax.axis_index(axis), 2) == 0
    pl.when(even)(lambda: body(one, two))
    pl.when(jnp.logical_not(even))(lambda: body(two, one))


def first_kernel(pops_at, solid_at, table_at, index_at, own, one, two, pops, solid, table, index, sems):
    copies = [
        pltpu.make_async_copy(source, target, sems.at[i])
        for i, (source, target) in enumerate(
            ((pops_at, pops), (solid_at, solid), (table_at, table), (index_at, index))
        )
    ]
    for copy in copies:
        copy.start()
    for copy in copies:
        copy.wait()
    lanes, rows = lane_ids(), row_ids()
    sponge = (lax.axis_index("gx") * NX + lanes) < SPONGE
    for z in range(NZ):
        aim = jnp.zeros((8, 128), F32)
        for y in range(NY):
            aim = jnp.where(rows == y, table[z, index[y]], aim)
        post = relaxed([pops[q, z] for q in range(27)], sponge, aim)
        for q in range(27):
            own[pl.ds((q * NZ + z) * 8, 8), :] = post[q]
        own[pl.ds((WALL * NZ + z) * 8, 8), :] = solid[z].astype(F32)
        own[pl.ds((AIM * NZ + z) * 8, 8), :] = aim

    def pack(yup, ydown):
        for out, edge, second, part in ((yup, 7, 6, 6), (ydown, 0, 1, 0)):
            out[pl.ds(0, CHANNELS * NZ), :] = own[pl.ds(edge, CHANNELS * NZ, stride=8), :]
            for a in range(3):
                out[pl.ds((CHANNELS + 3 * a) * NZ, 3 * NZ), :] = own[
                    pl.ds((9 * a + part) * NZ * 8 + second, 3 * NZ, stride=8), :
                ]

    by_parity("gy", one, two, pack)


def second_kernel(own, y_one, y_two, z_two, z_one):
    by_parity(
        "gy",
        y_one,
        y_two,
        lambda above, below: by_parity(
            "gz", z_one, z_two, lambda zup, zdown: pack_planes(own, below, above, zup, zdown)
        ),
    )


def pack_planes(own, below, above, zup, zdown):
    for out, first, second, part in ((zup, NZ - 1, NZ - 2, 2), (zdown, 0, 1, 0)):
        for k in range(Z_BLOCKS):
            channel, z = (k, first) if k < CHANNELS else (9 * part + k - CHANNELS, second)
            if k == Z_BLOCKS - 1:
                channel = WALL
            out[pl.ds(k * Z_PITCH + 1, 8), :] = own[pl.ds((channel * NZ + z) * 8, 8), :]
        for side, (halo, near, group) in enumerate(((below, 0, 2), (above, Z_PITCH - 1, 0))):
            out[pl.ds(near, CHANNELS, stride=Z_PITCH), :] = halo[
                pl.ds(first, CHANNELS, stride=NZ), :
            ]
            out[pl.ds(CHANNELS * Z_PITCH + near, 9, stride=Z_PITCH), :] = halo[
                pl.ds(9 * part * NZ + second, 9, stride=NZ), :
            ]
            out[pl.ds((Z_BLOCKS - 1) * Z_PITCH + near, 1), :] = halo[
                pl.ds(WALL * NZ + second, 1), :
            ]
            far = Z_FAR + 12 * side
            out[pl.ds(far, 9), :] = halo[pl.ds(CHANNELS * NZ + first, 9, stride=NZ), :]
            out[pl.ds(far + 9, 3), :] = halo[
                pl.ds((CHANNELS + 3 * part) * NZ + second, 3, stride=NZ), :
            ]


def plane_at(z):
    return PAD + (z + 2) * PITCH


def add_rows(full, above, below):
    for c in range(CHANNELS):
        for halo, near in ((below, 1), (above, PITCH - 2)):
            full[c, pl.ds(plane_at(0) + near, NZ, stride=PITCH), :] = halo[pl.ds(c * NZ, NZ), :]
    for halo, far, group in ((below, 0, 6), (above, PITCH - 1, 0)):
        for k in range(9):
            q = 9 * (k // 3) + group + k % 3
            full[q, pl.ds(plane_at(0) + far, NZ, stride=PITCH), :] = halo[
                pl.ds((CHANNELS + k) * NZ, NZ), :
            ]
        full[WALL, pl.ds(plane_at(0) + far, NZ, stride=PITCH), :] = halo[pl.ds(WALL * NZ, NZ), :]


def add_planes(full, ceiling, floor):
    for halo, near, far, part in ((floor, -1, -2, 2), (ceiling, NZ, NZ + 1, 0)):
        blocks = [(c, near) for c in range(CHANNELS)]
        blocks += [(9 * part + k, far) for k in range(9)] + [(WALL, far)]
        for k, (c, z) in enumerate(blocks):
            full[c, pl.ds(plane_at(z) + 1, Z_PITCH), :] = halo[pl.ds(k * Z_PITCH, Z_PITCH), :]
        for side, (row, group) in enumerate(((0, 2), (PITCH - 1, 0))):
            start = Z_FAR + 12 * side
            for k in range(9):
                q = 9 * (k // 3) + 3 * group + k % 3
                full[q, pl.ds(plane_at(near) + row, 1), :] = halo[pl.ds(start + k, 1), :]
            for k in range(3):
                q = 9 * part + 3 * group + k
                full[q, pl.ds(plane_at(far) + row, 1), :] = halo[pl.ds(start + 9 + k, 1), :]
            first = 0 if side == 0 else Z_PITCH - 1
            for k, z in ((WALL, near), (Z_BLOCKS - 1, far)):
                full[WALL, pl.ds(plane_at(z) + row, 1), :] = halo[pl.ds(k * Z_PITCH + first, 1), :]


def pack_columns(full, pack, tiles):
    slot = lane_ids() // 4
    for source, target in tiles:
        packed = jnp.zeros((8, 128), F32)
        for c in range(CHANNELS):
            moved = pltpu.roll(full[c, pl.ds(PAD + 8 * source, 8), :], (4 * c + 2) % 128, 1)
            packed = jnp.where(slot == c, moved, packed)
        pack[pl.ds(8 * target, 8), :] = packed


def third_kernel(own, y_one, y_two, full, pack):
    for c in range(CHANNELS):
        for z in range(NZ):
            full[c, pl.ds(plane_at(z) + 2, 8), :] = own[pl.ds((c * NZ + z) * 8, 8), :]
    by_parity("gy", y_one, y_two, functools.partial(add_rows, full))
    pack_columns(full, pack, [(EDGE // 8 + t, t) for t in range(OWN // 8)])


def block_kernel(part, pack, z_two, z_one, full, post, mine, walls):
    last = lax.axis_size("gz") - 1
    here = lax.axis_index("gz")
    by_parity("gz", z_one, z_two, functools.partial(add_planes, full))

    @pl.when(here == 0)
    def _():
        full[WALL, pl.ds(plane_at(-1), PITCH), :] = jnp.ones((PITCH, 128), F32)

    @pl.when(here == last)
    def _():
        for q in range(9):
            full[q, pl.ds(plane_at(NZ), PITCH), :] = full[q + 18, pl.ds(plane_at(NZ - 1), PITCH), :]
        full[WALL, pl.ds(plane_at(NZ), PITCH), :] = jnp.zeros((PITCH, 128), F32)

    mine[pl.ds(EDGE, OWN), :] = pack[...]
    rest = [t for t in range(FLAT // 8) if not EDGE <= 8 * t < EDGE + OWN]
    pack_columns(full, mine, [(t, t) for t in rest])

    sponge = (lax.axis_index("gx") * NX + lane_ids()) < SPONGE
    for t in range(ROWS // 8):
        rows = pl.ds(8 * t, 8)
        flags = full[WALL, rows, :]
        for cx in (-1, 0, 1):
            walls[cx + 1, rows, :] = pltpu.roll(flags, cx % 128, 1) if cx else flags
    for u in range(UNITS):
        cell = PAD + PITCH + 8 * u
        f = []
        solid = walls[1, pl.ds(cell, 8), :] != 0.0
        for q in range(27):
            cx, cy, cz = VEL[q]
            start = cell - PITCH * cz - cy
            value = full[q, pl.ds(start, 8), :]
            if cx:
                value = pltpu.roll(value, cx % 128, 1)
            if q != 13:
                blocked = walls[cx + 1, pl.ds(start, 8), :] != 0.0
                value = jnp.where(blocked, full[26 - q, pl.ds(cell, 8), :], value)
            f.append(jnp.where(solid, WEIGHT[q], value))
        done = relaxed(f, sponge, full[AIM, pl.ds(cell, 8), :])
        for q in range(27):
            post[q, pl.ds(8 * u, 8), :] = done[q]

    @pl.when(here == last)
    def _():
        for q in range(9):
            post[q, pl.ds((NZ + 1) * PITCH, PITCH), :] = post[q + 18, pl.ds(NZ * PITCH, PITCH), :]


def last_kernel(block, sheet, mine, *refs):
    turns = 1 if lax.axis_size("gx") == 2 else 2
    beside, refs = refs[: 3 * turns], refs[3 * turns :]
    out, west, east, turn, post, walls, back, done, sems = refs
    here_x, size_x = lax.axis_index("gx"), lax.axis_size("gx")
    top = lax.axis_index("gz") == lax.axis_size("gz") - 1
    bottom = lax.axis_index("gz") == 0
    lanes, rows = lane_ids(), row_ids()

    def gather(target, level, one, two):
        target[pl.ds(EDGE, OWN), :] = level[...]

        def ends(above, below):
            target[pl.ds(0, EDGE), :] = below[pl.ds(OWN - EDGE, EDGE), :]
            target[pl.ds(EDGE + OWN, EDGE), :] = above[pl.ds(0, EDGE), :]

        by_parity("gz", one, two, ends)

    if turns == 1:
        gather(west, *beside)
        sources = (mine, west)
    else:

        def spread(right, left):
            gather(west, *left)
            gather(east, *right)

        by_parity("gx", beside[:3], beside[3:], spread)
        sources = (mine, west, east)

    for i, source in enumerate(sources):
        square = jnp.concatenate([source[...], jnp.zeros((128 - FLAT, 128), F32)], axis=0)
        turn[i, pl.ds(PAD, 128), :] = square.T

    strip = []
    for c in range(CHANNELS):
        first, second = pl.ds(PAD + 4 * c, 8), pl.ds(PAD + 4 * c - 4, 8)
        inner = jnp.where(rows < 4, turn[0, first, :], turn[0, second, :])
        outer = jnp.where(rows < 4, turn[1, first, :], turn[turns, second, :])
        strip.append(jnp.where((rows >= 2) & (rows < 6), inner, outer))

    ceiling = top & (lanes >= (NZ + 2) * PITCH) & (lanes < (NZ + 3) * PITCH)
    ground = bottom & (lanes >= PITCH) & (lanes < 2 * PITCH)
    for q in range(9):
        strip[q] = jnp.where(ceiling, pltpu.roll(strip[q + 18], PITCH, 1), strip[q])
    strip[WALL] = jnp.where(ceiling, 0.0, jnp.where(ground, 1.0, strip[WALL]))

    def shifted(value, q):
        cx, cy, cz = VEL[q]
        if cx:
            value = pltpu.roll(value, cx % 8, 0)
        step = (PITCH * cz + cy) % 128
        return pltpu.roll(value, step, 1) if step else value

    moved = []
    for q in range(27):
        value = shifted(strip[q], q)
        if q != 13:
            value = jnp.where(shifted(strip[WALL], q) != 0.0, strip[26 - q], value)
        moved.append(jnp.where(strip[WALL] != 0.0, WEIGHT[q], value))
    column = here_x * NX + jnp.where(rows < 4, rows - 2, rows + (NX - 6))
    column = lax.rem(column + size_x * NX, size_x * NX)
    sides = relaxed(moved, column < SPONGE, strip[AIM])
    for q in range(9):
        sides[q] = jnp.where(ceiling, pltpu.roll(sides[q + 18], PITCH, 1), sides[q])
    sides.append(strip[WALL])
    sides = [
        jnp.where((rows == 1) | (rows == 5), pltpu.roll(side, 4, 0), side) for side in sides
    ]
    sides += [jnp.zeros((8, 128), F32)] * 4
    for i in range(2):
        back[i] = jnp.concatenate(sides[16 * i : 16 * i + 16], axis=0).T

    def column_at(c, place, lane, start):
        value = back[c // 16, pl.ds(start, 8), :]
        return pltpu.roll(value, (lane - 8 * (c % 16) - place) % 128, 1)

    rim = (lanes == 0) | (lanes == 127)
    for u in range(UNITS):
        for q in range(27):
            post[q, pl.ds(8 * u, 8), :] = jnp.where(
                rim, column_at(q, 2, 0, PITCH + 8 * u), block[q, pl.ds(8 * u, 8), :]
            )
        flags = sheet[1, pl.ds(PAD + PITCH + 8 * u, 8), :]
        walls[1, pl.ds(8 * u, 8), :] = flags
        for cx, edge, place in ((1, 0, 5), (-1, 127, 6)):
            walls[cx + 1, pl.ds(8 * u, 8), :] = jnp.where(
                lanes == edge,
                column_at(WALL, place, edge, PITCH + 8 * u),
                sheet[cx + 1, pl.ds(PAD + PITCH + 8 * u, 8), :],
            )

    copies = []
    for z in range(NZ):
        cell = (z + 1) * PITCH + 2
        solid = walls[1, pl.ds(cell, 8), :] != 0.0
        for q in range(27):
            cx, cy, cz = VEL[q]
            start = cell - PITCH * cz - cy
            value = post[q, pl.ds(start, 8), :]
            if cx:
                edge, place = (0, 5) if cx > 0 else (127, 6)
                side = column_at(q, place, edge, PITCH + start)
                value = jnp.where(lanes == edge, side, pltpu.roll(value, cx % 128, 1))
            if q != 13:
                blocked = walls[cx + 1, pl.ds(start, 8), :] != 0.0
                value = jnp.where(blocked, post[26 - q, pl.ds(cell, 8), :], value)
            done[q, z] = jnp.where(solid, WEIGHT[q], value)
        copies.append(pltpu.make_async_copy(done.at[:, z], out.at[:, z], sems.at[z]))
        copies[-1].start()
    for copy in copies:
        copy.wait()


def partners(size, turn, wrap):
    result = list(range(size))
    for i in range(turn, size if wrap else size - 1, 2):
        j = (i + 1) % size
        result[i], result[j] = j, i
    return result


def swap(value, axis, turn, wrap):
    return lax.ppermute(value, axis, list(enumerate(partners(lax.axis_size(axis), turn, wrap))))


def swap_across(value, x_turn, z_turn):
    size = lax.axis_size("gz")
    over_x = partners(lax.axis_size("gx"), x_turn, True)
    over_z = partners(size, z_turn, False)
    pairs = []
    for i, far_i in enumerate(over_x):
        for j, far_j in enumerate(over_z):
            pairs.append((i * size + j, far_i * size + far_j if far_j != j else i * size + j))
    return lax.ppermute(value, ("gx", "gz"), pairs)


def shape(*dims):
    return jax.ShapeDtypeStruct(dims, F32)


def shards(pops, solid, profile_table, profile_index):
    own, y_one, y_two = pl.pallas_call(
        first_kernel,
        out_shape=[shape(CHANNELS * NZ * 8, 128), shape(Y_ROWS, 128), shape(Y_ROWS, 128)],
        in_specs=[HBM] * 4,
        out_specs=[VMEM] * 3,
        scratch_shapes=[
            pltpu.VMEM(pops.shape, F32),
            pltpu.VMEM(solid.shape, jnp.int32),
            pltpu.SMEM(profile_table.shape[::-1], F32),
            pltpu.SMEM(profile_index.shape, jnp.int32),
            pltpu.SemaphoreType.DMA((4,)),
        ],
        compiler_params=PARAMS,
        name="collide",
    )(*(pltpu.with_memory_space_constraint(a, pltpu.HBM) for a in (pops, solid, profile_table.T, profile_index)))
    y_two = swap(y_two, "gy", 1, True)
    y_one = swap(y_one, "gy", 0, True)
    z_two, z_one = pl.pallas_call(
        second_kernel,
        out_shape=[shape(Z_ROWS, 128)] * 2,
        in_specs=[VMEM] * 3,
        out_specs=[VMEM] * 2,
        compiler_params=PARAMS,
        name="pack_z",
    )(own, y_one, y_two)
    z_two = swap(z_two, "gz", 1, False)
    z_one = swap(z_one, "gz", 0, False)
    part, pack = pl.pallas_call(
        third_kernel,
        out_shape=[shape(CHANNELS, ROWS, 128), shape(OWN, 128)],
        in_specs=[VMEM] * 3,
        out_specs=[VMEM] * 2,
        compiler_params=PARAMS,
        name="pack_x",
    )(own, y_one, y_two)
    beside = []
    for turn in range(1 if lax.axis_size("gx") == 2 else 2):
        beside += [swap(pack, "gx", turn, True)]
        beside += [swap_across(pack, turn, 0), swap_across(pack, turn, 1)]
    full, block, mine, sheet = pl.pallas_call(
        block_kernel,
        out_shape=[
            shape(CHANNELS, ROWS, 128),
            shape(27, UNITS * 8, 128),
            shape(FLAT, 128),
            shape(3, ROWS, 128),
        ],
        in_specs=[VMEM] * 4,
        out_specs=[VMEM] * 4,
        input_output_aliases={0: 0},
        compiler_params=PARAMS,
        cost_estimate=pl.CostEstimate(
            flops=27 * 20 * UNITS * 1024, bytes_accessed=2**22, transcendentals=0
        ),
        name="block",
    )(part, pack, z_two, z_one)
    return pl.pallas_call(
        last_kernel,
        out_shape=shape(27, NZ, NY, NX),
        in_specs=[VMEM] * (3 + len(beside)),
        out_specs=HBM,
        scratch_shapes=[
            pltpu.VMEM((FLAT, 128), F32),
            pltpu.VMEM((FLAT, 128), F32),
            pltpu.VMEM((3, PAD + 128 + PAD, 128), F32),
            pltpu.VMEM((27, UNITS * 8, 128), F32),
            pltpu.VMEM((3, UNITS * 8, 128), F32),
            pltpu.VMEM((2, 128, 128), F32),
            pltpu.VMEM((27, NZ, NY, NX), F32),
            pltpu.SemaphoreType.DMA((NZ,)),
        ],
        compiler_params=PARAMS,
        name="finish",
    )(block, sheet, mine, *beside)


def solution(mesh):
    return jax.shard_map(
        shards,
        mesh=mesh,
        in_specs=(P(None, "gz", "gy", "gx"), P("gz", "gy", "gx"), P(None, "gz"), P("gy")),
        out_specs=P(None, "gz", "gy", "gx"),
        check_vma=False,
    )
```

```python
import functools

import jax
import jax.numpy as jnp
import numpy as np
from jax import lax
from jax.experimental import pallas as pl
from jax.experimental.pallas import tpu as pltpu
from jax.sharding import PartitionSpec as P

SPONGE = 32
TAU = 0.52
SMAG = 18.0 * 1.4142135623730951 * 0.17 * 0.17

VEL = [(cx, cy, cz) for cz in (-1, 0, 1) for cy in (-1, 0, 1) for cx in (-1, 0, 1)]
WEIGHT = [
    float(np.array([8.0 / 27.0, 2.0 / 27.0, 1.0 / 54.0, 1.0 / 216.0])[cx * cx + cy * cy + cz * cz])
    for cx, cy, cz in VEL
]
WALL, AIM, CHANNELS = 27, 28, 29
NZ, NY, NX = 4, 8, 128
PITCH = NY + 4
FLAT = (NZ + 4) * PITCH
PAD = 8
ROWS = PAD + FLAT + PAD
UNITS = (NZ + 2) * PITCH // 8

PARAMS = pltpu.CompilerParams(vmem_limit_bytes=12 * 2**20)
VMEM = pl.BlockSpec(memory_space=pltpu.VMEM)
HBM = pl.BlockSpec(memory_space=pltpu.HBM)
F32 = jnp.float32

Y_ROWS = (CHANNELS + 9) * NZ
Z_BLOCKS = CHANNELS + 10
Z_PITCH = NY + 2
Z_FAR = Z_BLOCKS * Z_PITCH
Z_ROWS = -(-(Z_FAR + 2 * 12) // 8) * 8

X_ROWS = 2 * (WALL + 1)


def relaxed(f, sponge, aim):
    quad = {}
    for cz in (-1, 0, 1):
        line = {}
        for cy in (-1, 0, 1):
            base = 9 * (cz + 1) + 3 * (cy + 1)
            both = f[base + 2] + f[base]
            line[cy] = (both + f[base + 1], f[base + 2] - f[base], both)
        s = line[1][0] + line[-1][0]
        sx = line[1][1] + line[-1][1]
        quad[cz] = dict(
            n=s + line[0][0],
            y=line[1][0] - line[-1][0],
            yy=s,
            x=sx + line[0][1],
            xy=line[1][1] - line[-1][1],
            xx=line[1][2] + line[-1][2] + line[0][2],
        )
    up, mid, down = quad[1], quad[0], quad[-1]
    zz = up["n"] + down["n"]
    rho = zz + mid["n"]
    jz = up["n"] - down["n"]
    jy = up["y"] + down["y"] + mid["y"]
    jx = up["x"] + down["x"] + mid["x"]
    inverse = 1.0 / rho
    ux, uy, uz = jx * inverse, jy * inverse, jz * inverse
    third = rho * (1.0 / 3.0)
    pxx = (up["xx"] + down["xx"] + mid["xx"]) - (third + jx * ux)
    pyy = (up["yy"] + down["yy"] + mid["yy"]) - (third + jy * uy)
    pzz = zz - (third + jz * uz)
    pxy = (up["xy"] + down["xy"] + mid["xy"]) - jx * uy
    pxz = (up["x"] - down["x"]) - jx * uz
    pyz = (up["y"] - down["y"]) - jy * uz
    strain = pxx * pxx + pyy * pyy + pzz * pzz + 2.0 * (pxy * pxy + pxz * pxz + pyz * pyz)
    size = jnp.sqrt(2.0 * strain)
    tau = 0.5 * (TAU + jnp.sqrt(TAU * TAU + SMAG * size * inverse))
    omega = 1.0 / tau
    keep = 1.0 - omega
    if sponge is not None:
        keep = jnp.where(sponge, 0.0, keep)
        omega = jnp.where(sponge, 1.0, omega)
        ux = jnp.where(sponge, aim, ux)
        uy = jnp.where(sponge, 0.0, uy)
        uz = jnp.where(sponge, 0.0, uz)
    square = 1.0 - 1.5 * (ux * ux + uy * uy + uz * uz)
    vx, vy, vz = 3.0 * ux, 3.0 * uy, 3.0 * uz
    share = rho * omega
    weighted = {w: share * w for w in sorted(set(WEIGHT))}
    post = [None] * 27
    for q in range(14):
        cx, cy, cz = VEL[q]
        along = None
        for c, v in ((cx, vx), (cy, vy), (cz, vz)):
            if c:
                along = (v if c > 0 else -v) if along is None else (along + v if c > 0 else along - v)
        scale = weighted[WEIGHT[q]]
        if along is None:
            post[q] = keep * f[q] + scale * square
            continue
        even = square + 0.5 * along * along
        post[q] = keep * f[q] + scale * (even + along)
        post[26 - q] = keep * f[26 - q] + scale * (even - along)
    return post


def lane_ids():
    return lax.broadcasted_iota(jnp.int32, (8, 128), 1)


def row_ids():
    return lax.broadcasted_iota(jnp.int32, (8, 128), 0)


def by_parity(axis, one, two, body):
    even = lax.rem(lax.axis_index(axis), 2) == 0
    pl.when(even)(lambda: body(one, two))
    pl.when(jnp.logical_not(even))(lambda: body(two, one))


def first_kernel(pops_at, solid_at, table_at, index_at, own, one, two, pops, solid, table, index, sems):
    copies = [
        pltpu.make_async_copy(source, target, sems.at[i])
        for i, (source, target) in enumerate(
            ((pops_at, pops), (solid_at, solid), (table_at, table), (index_at, index))
        )
    ]
    for copy in copies:
        copy.start()
    for copy in copies:
        copy.wait()
    lanes, rows = lane_ids(), row_ids()
    sponge = (lax.axis_index("gx") * NX + lanes) < SPONGE
    for z in range(NZ):
        aim = jnp.zeros((8, 128), F32)
        for y in range(NY):
            aim = jnp.where(rows == y, table[z, index[y]], aim)
        post = relaxed([pops[q, z] for q in range(27)], sponge, aim)
        for q in range(27):
            own[pl.ds((q * NZ + z) * 8, 8), :] = post[q]
        own[pl.ds((WALL * NZ + z) * 8, 8), :] = solid[z].astype(F32)
        own[pl.ds((AIM * NZ + z) * 8, 8), :] = aim

    def pack(yup, ydown):
        for out, edge, second, part in ((yup, 7, 6, 6), (ydown, 0, 1, 0)):
            out[pl.ds(0, CHANNELS * NZ), :] = own[pl.ds(edge, CHANNELS * NZ, stride=8), :]
            for a in range(3):
                out[pl.ds((CHANNELS + 3 * a) * NZ, 3 * NZ), :] = own[
                    pl.ds((9 * a + part) * NZ * 8 + second, 3 * NZ, stride=8), :
                ]

    by_parity("gy", one, two, pack)


def second_kernel(own, y_one, y_two, z_two, z_one):
    by_parity(
        "gy",
        y_one,
        y_two,
        lambda above, below: by_parity(
            "gz", z_one, z_two, lambda zup, zdown: pack_planes(own, below, above, zup, zdown)
        ),
    )


def pack_planes(own, below, above, zup, zdown):
    for out, first, second, part in ((zup, NZ - 1, NZ - 2, 2), (zdown, 0, 1, 0)):
        for k in range(Z_BLOCKS):
            channel, z = (k, first) if k < CHANNELS else (9 * part + k - CHANNELS, second)
            if k == Z_BLOCKS - 1:
                channel = WALL
            out[pl.ds(k * Z_PITCH + 1, 8), :] = own[pl.ds((channel * NZ + z) * 8, 8), :]
        for side, (halo, near, group) in enumerate(((below, 0, 2), (above, Z_PITCH - 1, 0))):
            out[pl.ds(near, CHANNELS, stride=Z_PITCH), :] = halo[
                pl.ds(first, CHANNELS, stride=NZ), :
            ]
            out[pl.ds(CHANNELS * Z_PITCH + near, 9, stride=Z_PITCH), :] = halo[
                pl.ds(9 * part * NZ + second, 9, stride=NZ), :
            ]
            out[pl.ds((Z_BLOCKS - 1) * Z_PITCH + near, 1), :] = halo[
                pl.ds(WALL * NZ + second, 1), :
            ]
            far = Z_FAR + 12 * side
            out[pl.ds(far, 9), :] = halo[pl.ds(CHANNELS * NZ + first, 9, stride=NZ), :]
            out[pl.ds(far + 9, 3), :] = halo[
                pl.ds((CHANNELS + 3 * part) * NZ + second, 3, stride=NZ), :
            ]


def plane_at(z):
    return PAD + (z + 2) * PITCH


def add_rows(full, above, below):
    for c in range(CHANNELS):
        for halo, near in ((below, 1), (above, PITCH - 2)):
            full[c, pl.ds(plane_at(0) + near, NZ, stride=PITCH), :] = halo[pl.ds(c * NZ, NZ), :]
    for halo, far, group in ((below, 0, 6), (above, PITCH - 1, 0)):
        for k in range(9):
            q = 9 * (k // 3) + group + k % 3
            full[q, pl.ds(plane_at(0) + far, NZ, stride=PITCH), :] = halo[
                pl.ds((CHANNELS + k) * NZ, NZ), :
            ]
        full[WALL, pl.ds(plane_at(0) + far, NZ, stride=PITCH), :] = halo[pl.ds(WALL * NZ, NZ), :]


def add_planes(full, ceiling, floor):
    for halo, near, far, part in ((floor, -1, -2, 2), (ceiling, NZ, NZ + 1, 0)):
        blocks = [(c, near) for c in range(CHANNELS)]
        blocks += [(9 * part + k, far) for k in range(9)] + [(WALL, far)]
        for k, (c, z) in enumerate(blocks):
            full[c, pl.ds(plane_at(z) + 1, Z_PITCH), :] = halo[pl.ds(k * Z_PITCH, Z_PITCH), :]
        for side, (row, group) in enumerate(((0, 2), (PITCH - 1, 0))):
            start = Z_FAR + 12 * side
            for k in range(9):
                q = 9 * (k // 3) + 3 * group + k % 3
                full[q, pl.ds(plane_at(near) + row, 1), :] = halo[pl.ds(start + k, 1), :]
            for k in range(3):
                q = 9 * part + 3 * group + k
                full[q, pl.ds(plane_at(far) + row, 1), :] = halo[pl.ds(start + 9 + k, 1), :]
            first = 0 if side == 0 else Z_PITCH - 1
            for k, z in ((WALL, near), (Z_BLOCKS - 1, far)):
                full[WALL, pl.ds(plane_at(z) + row, 1), :] = halo[pl.ds(k * Z_PITCH + first, 1), :]


def third_kernel(own, y_one, y_two, z_two, z_one, full, columns, messages, pack):
    last = lax.axis_size("gz") - 1
    here = lax.axis_index("gz")
    for c in range(CHANNELS):
        for z in range(NZ):
            full[c, pl.ds(plane_at(z) + 2, 8), :] = own[pl.ds((c * NZ + z) * 8, 8), :]
    by_parity("gy", y_one, y_two, functools.partial(add_rows, full))
    by_parity("gz", z_one, z_two, functools.partial(add_planes, full))

    @pl.when(here == 0)
    def _():
        full[WALL, pl.ds(plane_at(-1), PITCH), :] = jnp.ones((PITCH, 128), F32)

    @pl.when(here == last)
    def _():
        for q in range(9):
            full[q, pl.ds(plane_at(NZ), PITCH), :] = full[q + 18, pl.ds(plane_at(NZ - 1), PITCH), :]

    slot = lane_ids() // 4
    pack[pl.ds(FLAT, 128 - FLAT), :] = jnp.zeros((128 - FLAT, 128), F32)
    for t in range(FLAT // 8):
        packed = jnp.zeros((8, 128), F32)
        for c in range(CHANNELS):
            moved = pltpu.roll(full[c, pl.ds(PAD + 8 * t, 8), :], (4 * c + 2) % 128, 1)
            packed = jnp.where(slot == c, moved, packed)
        pack[pl.ds(8 * t, 8), :] = packed
    columns[pl.ds(PAD, 128), :] = pack[...].T

    def row(c, i, count):
        return columns[pl.ds(PAD + 4 * c + i, count), :]

    def returned(q, near, far):
        cx, cy, cz = VEL[q]
        step = (-PITCH * cz - cy) % 128
        value = row(26 - q, near, 8)
        value = pltpu.roll(value, step, 1) if step else value
        return jnp.where(row(WALL, far, 8) != 0.0, value, row(q, far, 8))[:1]

    message = messages.at[0]
    for c in range(WALL + 1):
        cx = VEL[c][0] if c < 27 else 0
        if cx == 0:
            message[pl.ds(2 * c, 2), :] = row(c, 1, 2)
        elif cx > 0:
            message[pl.ds(2 * c, 1), :] = returned(c, 1, 0)
            message[pl.ds(2 * c + 1, 1), :] = row(c, 1, 1)
        else:
            message[pl.ds(2 * c, 1), :] = row(c, 2, 1)
            message[pl.ds(2 * c + 1, 1), :] = returned(c, 2, 3)
    messages[1] = messages[0]


def block_kernel(full, post, walls):
    top = lax.axis_index("gz") == lax.axis_size("gz") - 1
    sponge = (lax.axis_index("gx") * NX + lane_ids()) < SPONGE
    for t in range(ROWS // 8):
        rows = pl.ds(8 * t, 8)
        flags = full[WALL, rows, :]
        for cx in (-1, 0, 1):
            walls[cx + 1, rows, :] = pltpu.roll(flags, cx % 128, 1) if cx else flags
    for u in range(UNITS):
        cell = PAD + PITCH + 8 * u
        f = []
        solid = walls[1, pl.ds(cell, 8), :] != 0.0
        for q in range(27):
            cx, cy, cz = VEL[q]
            start = cell - PITCH * cz - cy
            value = full[q, pl.ds(start, 8), :]
            if cx:
                value = pltpu.roll(value, cx % 128, 1)
            if q != 13:
                blocked = walls[cx + 1, pl.ds(start, 8), :] != 0.0
                value = jnp.where(blocked, full[26 - q, pl.ds(cell, 8), :], value)
            f.append(jnp.where(solid, WEIGHT[q], value))
        done = relaxed(f, sponge, full[AIM, pl.ds(cell, 8), :])
        for q in range(27):
            post[q, pl.ds(8 * u, 8), :] = done[q]

    @pl.when(top)
    def _():
        for q in range(9):
            post[q, pl.ds((NZ + 1) * PITCH, PITCH), :] = post[q + 18, pl.ds(NZ * PITCH, PITCH), :]


def last_kernel(full, block, columns, x_one, x_two, out, west, east, post, walls, back, done, sems):
    here_x, size_x = lax.axis_index("gx"), lax.axis_size("gx")
    top = lax.axis_index("gz") == lax.axis_size("gz") - 1
    lanes, rows = lane_ids(), row_ids()

    def spread(right, left):
        other = 1 - here_x if size_x == 2 else 0
        west[pl.ds(PAD, X_ROWS), :] = left[other]
        east[pl.ds(PAD, X_ROWS), :] = right[other]

    by_parity("gx", x_one, x_two, spread)

    strip = []
    for c in range(CHANNELS):
        cx = VEL[c][0] if c < 27 else 0
        value = jnp.where(
            rows < 4, columns[pl.ds(PAD + 4 * c, 8), :], columns[pl.ds(PAD + 4 * c - 4, 8), :]
        )
        if c <= WALL and cx >= 0:
            value = jnp.where(rows < 2, west[pl.ds(PAD + 2 * c - (cx == 0), 8), :], value)
        if c <= WALL and cx <= 0:
            value = jnp.where(rows >= 6, east[pl.ds(PAD + 2 * c - 6 + (cx == 0), 8), :], value)
        strip.append(value)
    strip[WALL] = jnp.where((rows == 0) | (rows == 7), 0.0, strip[WALL])

    def shifted(value, q):
        cx, cy, cz = VEL[q]
        if cx:
            value = pltpu.roll(value, cx % 8, 0)
        step = (PITCH * cz + cy) % 128
        return pltpu.roll(value, step, 1) if step else value

    moved = []
    for q in range(27):
        value = shifted(strip[q], q)
        if q != 13:
            value = jnp.where(shifted(strip[WALL], q) != 0.0, strip[26 - q], value)
        moved.append(jnp.where(strip[WALL] != 0.0, WEIGHT[q], value))
    column = here_x * NX + jnp.where(rows < 4, rows - 2, rows + (NX - 6))
    column = lax.rem(column + size_x * NX, size_x * NX)
    sides = relaxed(moved, column < SPONGE, strip[AIM])
    lid = top & (lanes >= (NZ + 2) * PITCH) & (lanes < (NZ + 3) * PITCH)
    for q in range(9):
        sides[q] = jnp.where(lid, pltpu.roll(sides[q + 18], PITCH, 1), sides[q])
    sides.append(strip[WALL])
    sides = [
        jnp.where((rows == 1) | (rows == 5), pltpu.roll(side, 4, 0), side) for side in sides
    ]
    sides += [jnp.zeros((8, 128), F32)] * 4
    for i in range(2):
        back[i] = jnp.concatenate(sides[16 * i : 16 * i + 16], axis=0).T

    def column_at(c, place, lane, start):
        value = back[c // 16, pl.ds(start, 8), :]
        return pltpu.roll(value, (lane - 8 * (c % 16) - place) % 128, 1)

    rim = (lanes == 0) | (lanes == 127)
    for u in range(UNITS):
        for q in range(27):
            post[q, pl.ds(8 * u, 8), :] = jnp.where(
                rim, column_at(q, 2, 0, PITCH + 8 * u), block[q, pl.ds(8 * u, 8), :]
            )
        flags = full[WALL, pl.ds(PAD + PITCH + 8 * u, 8), :]
        walls[1, pl.ds(8 * u, 8), :] = flags
        for cx, edge, place in ((1, 0, 5), (-1, 127, 6)):
            walls[cx + 1, pl.ds(8 * u, 8), :] = jnp.where(
                lanes == edge, column_at(WALL, place, edge, PITCH + 8 * u), pltpu.roll(flags, cx % 128, 1)
            )

    copies = []
    for z in range(NZ):
        cell = (z + 1) * PITCH + 2
        solid = walls[1, pl.ds(cell, 8), :] != 0.0
        for q in range(27):
            cx, cy, cz = VEL[q]
            start = cell - PITCH * cz - cy
            value = post[q, pl.ds(start, 8), :]
            if cx:
                edge, place = (0, 5) if cx > 0 else (127, 6)
                side = column_at(q, place, edge, PITCH + start)
                value = jnp.where(lanes == edge, side, pltpu.roll(value, cx % 128, 1))
            if q != 13:
                blocked = walls[cx + 1, pl.ds(start, 8), :] != 0.0
                value = jnp.where(blocked, post[26 - q, pl.ds(cell, 8), :], value)
            done[q, z] = jnp.where(solid, WEIGHT[q], value)
        copies.append(pltpu.make_async_copy(done.at[:, z], out.at[:, z], sems.at[z]))
        copies[-1].start()
    for copy in copies:
        copy.wait()


def swap(value, axis, turn, wrap):
    size = lax.axis_size(axis)
    pairs = [(i, (i + 1) % size) for i in range(turn, size if wrap else size - 1, 2)]
    return lax.ppermute(value, axis, pairs + [(j, i) for i, j in pairs])


def shape(*dims):
    return jax.ShapeDtypeStruct(dims, F32)


def shards(pops, solid, profile_table, profile_index):
    own, y_one, y_two = pl.pallas_call(
        first_kernel,
        out_shape=[shape(CHANNELS * NZ * 8, 128), shape(Y_ROWS, 128), shape(Y_ROWS, 128)],
        in_specs=[HBM] * 4,
        out_specs=[VMEM] * 3,
        scratch_shapes=[
            pltpu.VMEM(pops.shape, F32),
            pltpu.VMEM(solid.shape, jnp.int32),
            pltpu.SMEM(profile_table.shape[::-1], F32),
            pltpu.SMEM(profile_index.shape, jnp.int32),
            pltpu.SemaphoreType.DMA((4,)),
        ],
        compiler_params=PARAMS,
        name="collide",
    )(*(pltpu.with_memory_space_constraint(a, pltpu.HBM) for a in (pops, solid, profile_table.T, profile_index)))
    y_two = swap(y_two, "gy", 1, True)
    y_one = swap(y_one, "gy", 0, True)
    z_two, z_one = pl.pallas_call(
        second_kernel,
        out_shape=[shape(Z_ROWS, 128)] * 2,
        in_specs=[VMEM] * 3,
        out_specs=[VMEM] * 2,
        compiler_params=PARAMS,
        name="pack_z",
    )(own, y_one, y_two)
    z_two = swap(z_two, "gz", 1, False)
    z_one = swap(z_one, "gz", 0, False)
    full, columns, message = pl.pallas_call(
        third_kernel,
        out_shape=[shape(CHANNELS, ROWS, 128), shape(PAD + 128 + PAD, 128), shape(2, X_ROWS, 128)],
        in_specs=[VMEM] * 5,
        out_specs=[VMEM] * 3,
        scratch_shapes=[pltpu.VMEM((128, 128), F32)],
        compiler_params=PARAMS,
        name="pack_x",
    )(own, y_one, y_two, z_two, z_one)
    if lax.axis_size("gx") == 2:
        x_one = x_two = lax.all_to_all(message, "gx", 0, 0)
    else:
        x_one, x_two = swap(message, "gx", 0, True), swap(message, "gx", 1, True)
    block = pl.pallas_call(
        block_kernel,
        out_shape=shape(27, UNITS * 8, 128),
        in_specs=[VMEM],
        out_specs=VMEM,
        scratch_shapes=[pltpu.VMEM((3, ROWS, 128), F32)],
        compiler_params=PARAMS,
        cost_estimate=pl.CostEstimate(
            flops=27 * 20 * UNITS * 1024, bytes_accessed=2**22, transcendentals=0
        ),
        name="block",
    )(full)
    return pl.pallas_call(
        last_kernel,
        out_shape=shape(27, NZ, NY, NX),
        in_specs=[VMEM] * 5,
        out_specs=HBM,
        scratch_shapes=[
            pltpu.VMEM((PAD + X_ROWS + PAD, 128), F32),
            pltpu.VMEM((PAD + X_ROWS + PAD, 128), F32),
            pltpu.VMEM((27, UNITS * 8, 128), F32),
            pltpu.VMEM((3, UNITS * 8, 128), F32),
            pltpu.VMEM((2, 128, 128), F32),
            pltpu.VMEM((27, NZ, NY, NX), F32),
            pltpu.SemaphoreType.DMA((NZ,)),
        ],
        compiler_params=PARAMS,
        name="finish",
    )(full, block, columns, x_one, x_two)


def solution(mesh):
    return jax.shard_map(
        shards,
        mesh=mesh,
        in_specs=(P(None, "gz", "gy", "gx"), P("gz", "gy", "gx"), P(None, "gz"), P("gy")),
        out_specs=P(None, "gz", "gy", "gx"),
        check_vma=False,
    )
```

```python
import functools

import jax
import jax.numpy as jnp
import numpy as np
from jax import lax
from jax.experimental import pallas as pl
from jax.experimental.pallas import tpu as pltpu
from jax.sharding import PartitionSpec as P

SPONGE = 32
TAU = 0.52
SMAG = 18.0 * 1.4142135623730951 * 0.17 * 0.17

VEL = [(cx, cy, cz) for cz in (-1, 0, 1) for cy in (-1, 0, 1) for cx in (-1, 0, 1)]
WEIGHT = [
    float(np.array([8.0 / 27.0, 2.0 / 27.0, 1.0 / 54.0, 1.0 / 216.0])[cx * cx + cy * cy + cz * cz])
    for cx, cy, cz in VEL
]
WALL, AIM, CHANNELS = 27, 28, 29
NZ, NY, NX = 4, 8, 128
PITCH = NY + 4
FLAT = (NZ + 4) * PITCH
PAD = 8
ROWS = PAD + FLAT + PAD
UNITS = (NZ + 2) * PITCH // 8

PARAMS = pltpu.CompilerParams(vmem_limit_bytes=12 * 2**20)
VMEM = pl.BlockSpec(memory_space=pltpu.VMEM)
HBM = pl.BlockSpec(memory_space=pltpu.HBM)
F32 = jnp.float32

Y_ROWS = (CHANNELS + 9) * NZ
Z_BLOCKS = CHANNELS + 10
Z_PITCH = NY + 2
Z_FAR = Z_BLOCKS * Z_PITCH
Z_ROWS = -(-(Z_FAR + 2 * 12) // 8) * 8

X_ROWS = 2 * (WALL + 1)


def relaxed(f, sponge, aim):
    quad = {}
    for cz in (-1, 0, 1):
        line = {}
        for cy in (-1, 0, 1):
            base = 9 * (cz + 1) + 3 * (cy + 1)
            both = f[base + 2] + f[base]
            line[cy] = (both + f[base + 1], f[base + 2] - f[base], both)
        s = line[1][0] + line[-1][0]
        sx = line[1][1] + line[-1][1]
        quad[cz] = dict(
            n=s + line[0][0],
            y=line[1][0] - line[-1][0],
            yy=s,
            x=sx + line[0][1],
            xy=line[1][1] - line[-1][1],
            xx=line[1][2] + line[-1][2] + line[0][2],
        )
    up, mid, down = quad[1], quad[0], quad[-1]
    zz = up["n"] + down["n"]
    rho = zz + mid["n"]
    jz = up["n"] - down["n"]
    jy = up["y"] + down["y"] + mid["y"]
    jx = up["x"] + down["x"] + mid["x"]
    inverse = 1.0 / rho
    ux, uy, uz = jx * inverse, jy * inverse, jz * inverse
    third = rho * (1.0 / 3.0)
    pxx = (up["xx"] + down["xx"] + mid["xx"]) - (third + jx * ux)
    pyy = (up["yy"] + down["yy"] + mid["yy"]) - (third + jy * uy)
    pzz = zz - (third + jz * uz)
    pxy = (up["xy"] + down["xy"] + mid["xy"]) - jx * uy
    pxz = (up["x"] - down["x"]) - jx * uz
    pyz = (up["y"] - down["y"]) - jy * uz
    strain = pxx * pxx + pyy * pyy + pzz * pzz + 2.0 * (pxy * pxy + pxz * pxz + pyz * pyz)
    size = jnp.sqrt(2.0 * strain)
    tau = 0.5 * (TAU + jnp.sqrt(TAU * TAU + SMAG * size * inverse))
    omega = 1.0 / tau
    keep = 1.0 - omega
    if sponge is not None:
        keep = jnp.where(sponge, 0.0, keep)
        omega = jnp.where(sponge, 1.0, omega)
        ux = jnp.where(sponge, aim, ux)
        uy = jnp.where(sponge, 0.0, uy)
        uz = jnp.where(sponge, 0.0, uz)
    square = 1.0 - 1.5 * (ux * ux + uy * uy + uz * uz)
    vx, vy, vz = 3.0 * ux, 3.0 * uy, 3.0 * uz
    share = rho * omega
    weighted = {w: share * w for w in sorted(set(WEIGHT))}
    post = [None] * 27
    for q in range(14):
        cx, cy, cz = VEL[q]
        along = None
        for c, v in ((cx, vx), (cy, vy), (cz, vz)):
            if c:
                along = (v if c > 0 else -v) if along is None else (along + v if c > 0 else along - v)
        scale = weighted[WEIGHT[q]]
        if along is None:
            post[q] = keep * f[q] + scale * square
            continue
        even = square + 0.5 * along * along
        post[q] = keep * f[q] + scale * (even + along)
        post[26 - q] = keep * f[26 - q] + scale * (even - along)
    return post


def lane_ids():
    return lax.broadcasted_iota(jnp.int32, (8, 128), 1)


def row_ids():
    return lax.broadcasted_iota(jnp.int32, (8, 128), 0)


def by_parity(axis, one, two, body):
    even = lax.rem(lax.axis_index(axis), 2) == 0
    pl.when(even)(lambda: body(one, two))
    pl.when(jnp.logical_not(even))(lambda: body(two, one))


def first_kernel(pops_at, solid_at, table_at, index_at, own, two, one, pops, solid, table, index, sems):
    small = ((table_at, table), (index_at, index), (solid_at, solid))
    planes = [(pops_at.at[:, z], pops.at[:, z]) for z in range(NZ)]
    copies = [
        pltpu.make_async_copy(source, target, sems.at[i])
        for i, (source, target) in enumerate((*small, *planes))
    ]
    for copy in copies:
        copy.start()
    for copy in copies[:3]:
        copy.wait()
    lanes, rows = lane_ids(), row_ids()
    sponge = (lax.axis_index("gx") * NX + lanes) < SPONGE
    for z in range(NZ):
        aim = jnp.zeros((8, 128), F32)
        for y in range(NY):
            aim = jnp.where(rows == y, table[z, index[y]], aim)
        copies[3 + z].wait()
        post = relaxed([pops[q, z] for q in range(27)], sponge, aim)
        for q in range(27):
            own[pl.ds((q * NZ + z) * 8, 8), :] = post[q]
        own[pl.ds((WALL * NZ + z) * 8, 8), :] = solid[z].astype(F32)
        own[pl.ds((AIM * NZ + z) * 8, 8), :] = aim

    def pack(yup, ydown):
        for out, edge, second, part in ((yup, 7, 6, 6), (ydown, 0, 1, 0)):
            out[pl.ds(0, CHANNELS * NZ), :] = own[pl.ds(edge, CHANNELS * NZ, stride=8), :]
            for a in range(3):
                out[pl.ds((CHANNELS + 3 * a) * NZ, 3 * NZ), :] = own[
                    pl.ds((9 * a + part) * NZ * 8 + second, 3 * NZ, stride=8), :
                ]

    by_parity("gy", one, two, pack)


def second_kernel(own, y_two, y_one, z_two, z_one):
    by_parity(
        "gy",
        y_one,
        y_two,
        lambda above, below: by_parity(
            "gz", z_one, z_two, lambda zup, zdown: pack_planes(own, below, above, zup, zdown)
        ),
    )


def pack_planes(own, below, above, zup, zdown):
    for out, first, second, part in ((zup, NZ - 1, NZ - 2, 2), (zdown, 0, 1, 0)):
        for k in range(Z_BLOCKS):
            channel, z = (k, first) if k < CHANNELS else (9 * part + k - CHANNELS, second)
            if k == Z_BLOCKS - 1:
                channel = WALL
            out[pl.ds(k * Z_PITCH + 1, 8), :] = own[pl.ds((channel * NZ + z) * 8, 8), :]
        for side, (halo, near, group) in enumerate(((below, 0, 2), (above, Z_PITCH - 1, 0))):
            out[pl.ds(near, CHANNELS, stride=Z_PITCH), :] = halo[
                pl.ds(first, CHANNELS, stride=NZ), :
            ]
            out[pl.ds(CHANNELS * Z_PITCH + near, 9, stride=Z_PITCH), :] = halo[
                pl.ds(9 * part * NZ + second, 9, stride=NZ), :
            ]
            out[pl.ds((Z_BLOCKS - 1) * Z_PITCH + near, 1), :] = halo[
                pl.ds(WALL * NZ + second, 1), :
            ]
            far = Z_FAR + 12 * side
            out[pl.ds(far, 9), :] = halo[pl.ds(CHANNELS * NZ + first, 9, stride=NZ), :]
            out[pl.ds(far + 9, 3), :] = halo[
                pl.ds((CHANNELS + 3 * part) * NZ + second, 3, stride=NZ), :
            ]


def plane_at(z):
    return PAD + (z + 2) * PITCH


def add_rows(full, above, below):
    for c in range(CHANNELS):
        for halo, near in ((below, 1), (above, PITCH - 2)):
            full[c, pl.ds(plane_at(0) + near, NZ, stride=PITCH), :] = halo[pl.ds(c * NZ, NZ), :]
    for halo, far, group in ((below, 0, 6), (above, PITCH - 1, 0)):
        for k in range(9):
            q = 9 * (k // 3) + group + k % 3
            full[q, pl.ds(plane_at(0) + far, NZ, stride=PITCH), :] = halo[
                pl.ds((CHANNELS + k) * NZ, NZ), :
            ]
        full[WALL, pl.ds(plane_at(0) + far, NZ, stride=PITCH), :] = halo[pl.ds(WALL * NZ, NZ), :]


def add_planes(full, ceiling, floor):
    for halo, near, far, part in ((floor, -1, -2, 2), (ceiling, NZ, NZ + 1, 0)):
        blocks = [(c, near) for c in range(CHANNELS)]
        blocks += [(9 * part + k, far) for k in range(9)] + [(WALL, far)]
        for k, (c, z) in enumerate(blocks):
            full[c, pl.ds(plane_at(z) + 1, Z_PITCH), :] = halo[pl.ds(k * Z_PITCH, Z_PITCH), :]
        for side, (row, group) in enumerate(((0, 2), (PITCH - 1, 0))):
            start = Z_FAR + 12 * side
            for k in range(9):
                q = 9 * (k // 3) + 3 * group + k % 3
                full[q, pl.ds(plane_at(near) + row, 1), :] = halo[pl.ds(start + k, 1), :]
            for k in range(3):
                q = 9 * part + 3 * group + k
                full[q, pl.ds(plane_at(far) + row, 1), :] = halo[pl.ds(start + 9 + k, 1), :]
            first = 0 if side == 0 else Z_PITCH - 1
            for k, z in ((WALL, near), (Z_BLOCKS - 1, far)):
                full[WALL, pl.ds(plane_at(z) + row, 1), :] = halo[pl.ds(k * Z_PITCH + first, 1), :]


def third_kernel(own, y_two, y_one, z_two, z_one, full, columns, message, pack):
    last = lax.axis_size("gz") - 1
    here = lax.axis_index("gz")
    for c in range(CHANNELS):
        for z in range(NZ):
            full[c, pl.ds(plane_at(z) + 2, 8), :] = own[pl.ds((c * NZ + z) * 8, 8), :]
    by_parity("gy", y_one, y_two, functools.partial(add_rows, full))
    by_parity("gz", z_one, z_two, functools.partial(add_planes, full))

    @pl.when(here == 0)
    def _():
        full[WALL, pl.ds(plane_at(-1), PITCH), :] = jnp.ones((PITCH, 128), F32)

    @pl.when(here == last)
    def _():
        for q in range(9):
            full[q, pl.ds(plane_at(NZ), PITCH), :] = full[q + 18, pl.ds(plane_at(NZ - 1), PITCH), :]

    slot = lane_ids() // 4
    pack[pl.ds(FLAT, 128 - FLAT), :] = jnp.zeros((128 - FLAT, 128), F32)
    for t in range(FLAT // 8):
        packed = jnp.zeros((8, 128), F32)
        for c in range(CHANNELS):
            moved = pltpu.roll(full[c, pl.ds(PAD + 8 * t, 8), :], (4 * c + 2) % 128, 1)
            packed = jnp.where(slot == c, moved, packed)
        pack[pl.ds(8 * t, 8), :] = packed
    columns[pl.ds(PAD, 128), :] = pack[...].T

    def row(c, i, count):
        return columns[pl.ds(PAD + 4 * c + i, count), :]

    def returned(q, near, far):
        cx, cy, cz = VEL[q]
        step = (-PITCH * cz - cy) % 128
        value = row(26 - q, near, 8)
        value = pltpu.roll(value, step, 1) if step else value
        return jnp.where(row(WALL, far, 8) != 0.0, value, row(q, far, 8))[:1]

    for c in range(WALL + 1):
        cx = VEL[c][0] if c < 27 else 0
        if cx == 0:
            message[pl.ds(2 * c, 2), :] = row(c, 1, 2)
        elif cx > 0:
            message[pl.ds(2 * c, 1), :] = returned(c, 1, 0)
            message[pl.ds(2 * c + 1, 1), :] = row(c, 1, 1)
        else:
            message[pl.ds(2 * c, 1), :] = row(c, 2, 1)
            message[pl.ds(2 * c + 1, 1), :] = returned(c, 2, 3)


def block_kernel(full, post, walls):
    top = lax.axis_index("gz") == lax.axis_size("gz") - 1
    sponge = (lax.axis_index("gx") * NX + lane_ids()) < SPONGE
    for t in range(ROWS // 8):
        rows = pl.ds(8 * t, 8)
        flags = full[WALL, rows, :]
        for cx in (-1, 0, 1):
            walls[cx + 1, rows, :] = pltpu.roll(flags, cx % 128, 1) if cx else flags
    for u in range(UNITS):
        cell = PAD + PITCH + 8 * u
        f = []
        solid = walls[1, pl.ds(cell, 8), :] != 0.0
        for q in range(27):
            cx, cy, cz = VEL[q]
            start = cell - PITCH * cz - cy
            value = full[q, pl.ds(start, 8), :]
            if cx:
                value = pltpu.roll(value, cx % 128, 1)
            if q != 13:
                blocked = walls[cx + 1, pl.ds(start, 8), :] != 0.0
                value = jnp.where(blocked, full[26 - q, pl.ds(cell, 8), :], value)
            f.append(jnp.where(solid, WEIGHT[q], value))
        done = relaxed(f, sponge, full[AIM, pl.ds(cell, 8), :])
        for q in range(27):
            post[q, pl.ds(8 * u, 8), :] = done[q]

    @pl.when(top)
    def _():
        for q in range(9):
            post[q, pl.ds((NZ + 1) * PITCH, PITCH), :] = post[q + 18, pl.ds(NZ * PITCH, PITCH), :]


def last_kernel(full, block, columns, x_one, x_two, out, west, east, post, walls, back, done, sems):
    here_x, size_x = lax.axis_index("gx"), lax.axis_size("gx")
    top = lax.axis_index("gz") == lax.axis_size("gz") - 1
    lanes, rows = lane_ids(), row_ids()

    def spread(right, left):
        west[pl.ds(PAD, X_ROWS), :] = left[...]
        east[pl.ds(PAD, X_ROWS), :] = right[...]

    by_parity("gx", x_one, x_two, spread)

    strip = []
    for c in range(CHANNELS):
        cx = VEL[c][0] if c < 27 else 0
        value = jnp.where(
            rows < 4, columns[pl.ds(PAD + 4 * c, 8), :], columns[pl.ds(PAD + 4 * c - 4, 8), :]
        )
        if c <= WALL and cx >= 0:
            value = jnp.where(rows < 2, west[pl.ds(PAD + 2 * c - (cx == 0), 8), :], value)
        if c <= WALL and cx <= 0:
            value = jnp.where(rows >= 6, east[pl.ds(PAD + 2 * c - 6 + (cx == 0), 8), :], value)
        strip.append(value)
    strip[WALL] = jnp.where((rows == 0) | (rows == 7), 0.0, strip[WALL])

    def shifted(value, q):
        cx, cy, cz = VEL[q]
        if cx:
            value = pltpu.roll(value, cx % 8, 0)
        step = (PITCH * cz + cy) % 128
        return pltpu.roll(value, step, 1) if step else value

    moved = []
    for q in range(27):
        value = shifted(strip[q], q)
        if q != 13:
            value = jnp.where(shifted(strip[WALL], q) != 0.0, strip[26 - q], value)
        moved.append(jnp.where(strip[WALL] != 0.0, WEIGHT[q], value))
    column = here_x * NX + jnp.where(rows < 4, rows - 2, rows + (NX - 6))
    column = lax.rem(column + size_x * NX, size_x * NX)
    sides = relaxed(moved, column < SPONGE, strip[AIM])
    lid = top & (lanes >= (NZ + 2) * PITCH) & (lanes < (NZ + 3) * PITCH)
    for q in range(9):
        sides[q] = jnp.where(lid, pltpu.roll(sides[q + 18], PITCH, 1), sides[q])
    sides.append(strip[WALL])
    sides = [
        jnp.where((rows == 1) | (rows == 5), pltpu.roll(side, 4, 0), side) for side in sides
    ]
    sides += [jnp.zeros((8, 128), F32)] * 4
    for i in range(2):
        back[i] = jnp.concatenate(sides[16 * i : 16 * i + 16], axis=0).T

    def column_at(c, place, lane, start):
        value = back[c // 16, pl.ds(start, 8), :]
        return pltpu.roll(value, (lane - 8 * (c % 16) - place) % 128, 1)

    rim = (lanes == 0) | (lanes == 127)
    for u in range(UNITS):
        for q in range(27):
            post[q, pl.ds(8 * u, 8), :] = jnp.where(
                rim, column_at(q, 2, 0, PITCH + 8 * u), block[q, pl.ds(8 * u, 8), :]
            )
        flags = full[WALL, pl.ds(PAD + PITCH + 8 * u, 8), :]
        walls[1, pl.ds(8 * u, 8), :] = flags
        for cx, edge, place in ((1, 0, 5), (-1, 127, 6)):
            walls[cx + 1, pl.ds(8 * u, 8), :] = jnp.where(
                lanes == edge, column_at(WALL, place, edge, PITCH + 8 * u), pltpu.roll(flags, cx % 128, 1)
            )

    copies = []
    for z in range(NZ):
        cell = (z + 1) * PITCH + 2
        solid = walls[1, pl.ds(cell, 8), :] != 0.0
        for q in range(27):
            cx, cy, cz = VEL[q]
            start = cell - PITCH * cz - cy
            value = post[q, pl.ds(start, 8), :]
            if cx:
                edge, place = (0, 5) if cx > 0 else (127, 6)
                side = column_at(q, place, edge, PITCH + start)
                value = jnp.where(lanes == edge, side, pltpu.roll(value, cx % 128, 1))
            if q != 13:
                blocked = walls[cx + 1, pl.ds(start, 8), :] != 0.0
                value = jnp.where(blocked, post[26 - q, pl.ds(cell, 8), :], value)
            done[q, z] = jnp.where(solid, WEIGHT[q], value)
        copies.append(pltpu.make_async_copy(done.at[:, z], out.at[:, z], sems.at[z]))
        copies[-1].start()
    for copy in copies:
        copy.wait()


def swap(value, axis, turn, wrap):
    size = lax.axis_size(axis)
    pairs = [(i, (i + 1) % size) for i in range(turn, size if wrap else size - 1, 2)]
    return lax.ppermute(value, axis, pairs + [(j, i) for i, j in pairs])


def shape(*dims):
    return jax.ShapeDtypeStruct(dims, F32)


def shards(pops, solid, profile_table, profile_index):
    own, y_two, y_one = pl.pallas_call(
        first_kernel,
        out_shape=[shape(CHANNELS * NZ * 8, 128), shape(Y_ROWS, 128), shape(Y_ROWS, 128)],
        in_specs=[HBM] * 4,
        out_specs=[VMEM] * 3,
        scratch_shapes=[
            pltpu.VMEM(pops.shape, F32),
            pltpu.VMEM(solid.shape, jnp.int32),
            pltpu.SMEM(profile_table.shape[::-1], F32),
            pltpu.SMEM(profile_index.shape, jnp.int32),
            pltpu.SemaphoreType.DMA((3 + NZ,)),
        ],
        compiler_params=PARAMS,
        name="collide",
    )(*(pltpu.with_memory_space_constraint(a, pltpu.HBM) for a in (pops, solid, profile_table.T, profile_index)))
    y_two = swap(y_two, "gy", 1, True)
    y_one = swap(y_one, "gy", 0, True)
    z_two, z_one = pl.pallas_call(
        second_kernel,
        out_shape=[shape(Z_ROWS, 128)] * 2,
        in_specs=[VMEM] * 3,
        out_specs=[VMEM] * 2,
        compiler_params=PARAMS,
        name="pack_z",
    )(own, y_two, y_one)
    z_two = swap(z_two, "gz", 1, False)
    z_one = swap(z_one, "gz", 0, False)
    full, columns, message = pl.pallas_call(
        third_kernel,
        out_shape=[shape(CHANNELS, ROWS, 128), shape(PAD + 128 + PAD, 128), shape(X_ROWS, 128)],
        in_specs=[VMEM] * 5,
        out_specs=[VMEM] * 3,
        scratch_shapes=[pltpu.VMEM((128, 128), F32)],
        compiler_params=PARAMS,
        name="pack_x",
    )(own, y_two, y_one, z_two, z_one)
    x_one = swap(message, "gx", 0, True)
    x_two = x_one if lax.axis_size("gx") == 2 else swap(message, "gx", 1, True)
    block = pl.pallas_call(
        block_kernel,
        out_shape=shape(27, UNITS * 8, 128),
        in_specs=[VMEM],
        out_specs=VMEM,
        scratch_shapes=[pltpu.VMEM((3, ROWS, 128), F32)],
        compiler_params=PARAMS,
        cost_estimate=pl.CostEstimate(
            flops=27 * 20 * UNITS * 1024, bytes_accessed=2**22, transcendentals=0
        ),
        name="block",
    )(full)
    return pl.pallas_call(
        last_kernel,
        out_shape=shape(27, NZ, NY, NX),
        in_specs=[VMEM] * 5,
        out_specs=HBM,
        scratch_shapes=[
            pltpu.VMEM((PAD + X_ROWS + PAD, 128), F32),
            pltpu.VMEM((PAD + X_ROWS + PAD, 128), F32),
            pltpu.VMEM((27, UNITS * 8, 128), F32),
            pltpu.VMEM((3, UNITS * 8, 128), F32),
            pltpu.VMEM((2, 128, 128), F32),
            pltpu.VMEM((27, NZ, NY, NX), F32),
            pltpu.SemaphoreType.DMA((NZ,)),
        ],
        compiler_params=PARAMS,
        name="finish",
    )(full, block, columns, x_one, x_two)


def solution(mesh):
    return jax.shard_map(
        shards,
        mesh=mesh,
        in_specs=(P(None, "gz", "gy", "gx"), P("gz", "gy", "gx"), P(None, "gz"), P("gy")),
        out_specs=P(None, "gz", "gy", "gx"),
        check_vma=False,
    )
```

```python
import functools

import jax
import jax.numpy as jnp
import numpy as np
from jax import lax
from jax.experimental import pallas as pl
from jax.experimental.pallas import tpu as pltpu
from jax.sharding import PartitionSpec as P

SPONGE = 32
TAU = 0.52
SMAG = 18.0 * 1.4142135623730951 * 0.17 * 0.17

VEL = [(cx, cy, cz) for cz in (-1, 0, 1) for cy in (-1, 0, 1) for cx in (-1, 0, 1)]
WEIGHT = [
    float(np.array([8.0 / 27.0, 2.0 / 27.0, 1.0 / 54.0, 1.0 / 216.0])[cx * cx + cy * cy + cz * cz])
    for cx, cy, cz in VEL
]
WALL, AIM, CHANNELS = 27, 28, 29
NZ, NY, NX = 4, 8, 128
PITCH = NY + 4
FLAT = (NZ + 4) * PITCH
PAD = 8
ROWS = PAD + FLAT + PAD
UNITS = (NZ + 2) * PITCH // 8

PARAMS = pltpu.CompilerParams(vmem_limit_bytes=12 * 2**20)
VMEM = pl.BlockSpec(memory_space=pltpu.VMEM)
HBM = pl.BlockSpec(memory_space=pltpu.HBM)
F32 = jnp.float32

Y_ROWS = (CHANNELS + 9) * NZ
Z_BLOCKS = CHANNELS + 10
Z_FAR = 2 * Z_BLOCKS
Z_ROWS = -(-(Z_FAR + 2 * 12) // 8) * 8

X_ROWS = 2 * (WALL + 1)


def relaxed(f, sponge, aim):
    quad = {}
    for cz in (-1, 0, 1):
        line = {}
        for cy in (-1, 0, 1):
            base = 9 * (cz + 1) + 3 * (cy + 1)
            both = f[base + 2] + f[base]
            line[cy] = (both + f[base + 1], f[base + 2] - f[base], both)
        s = line[1][0] + line[-1][0]
        sx = line[1][1] + line[-1][1]
        quad[cz] = dict(
            n=s + line[0][0],
            y=line[1][0] - line[-1][0],
            yy=s,
            x=sx + line[0][1],
            xy=line[1][1] - line[-1][1],
            xx=line[1][2] + line[-1][2] + line[0][2],
        )
    up, mid, down = quad[1], quad[0], quad[-1]
    zz = up["n"] + down["n"]
    rho = zz + mid["n"]
    jz = up["n"] - down["n"]
    jy = up["y"] + down["y"] + mid["y"]
    jx = up["x"] + down["x"] + mid["x"]
    inverse = 1.0 / rho
    ux, uy, uz = jx * inverse, jy * inverse, jz * inverse
    third = rho * (1.0 / 3.0)
    pxx = (up["xx"] + down["xx"] + mid["xx"]) - (third + jx * ux)
    pyy = (up["yy"] + down["yy"] + mid["yy"]) - (third + jy * uy)
    pzz = zz - (third + jz * uz)
    pxy = (up["xy"] + down["xy"] + mid["xy"]) - jx * uy
    pxz = (up["x"] - down["x"]) - jx * uz
    pyz = (up["y"] - down["y"]) - jy * uz
    strain = pxx * pxx + pyy * pyy + pzz * pzz + 2.0 * (pxy * pxy + pxz * pxz + pyz * pyz)
    size = jnp.sqrt(2.0 * strain)
    tau = 0.5 * (TAU + jnp.sqrt(TAU * TAU + SMAG * size * inverse))
    omega = 1.0 / tau
    keep = 1.0 - omega
    if sponge is not None:
        keep = jnp.where(sponge, 0.0, keep)
        omega = jnp.where(sponge, 1.0, omega)
        ux = jnp.where(sponge, aim, ux)
        uy = jnp.where(sponge, 0.0, uy)
        uz = jnp.where(sponge, 0.0, uz)
    square = 1.0 - 1.5 * (ux * ux + uy * uy + uz * uz)
    vx, vy, vz = 3.0 * ux, 3.0 * uy, 3.0 * uz
    share = rho * omega
    weighted = {w: share * w for w in sorted(set(WEIGHT))}
    post = [None] * 27
    for q in range(14):
        cx, cy, cz = VEL[q]
        along = None
        for c, v in ((cx, vx), (cy, vy), (cz, vz)):
            if c:
                along = (v if c > 0 else -v) if along is None else (along + v if c > 0 else along - v)
        scale = weighted[WEIGHT[q]]
        if along is None:
            post[q] = keep * f[q] + scale * square
            continue
        even = square + 0.5 * along * along
        post[q] = keep * f[q] + scale * (even + along)
        post[26 - q] = keep * f[26 - q] + scale * (even - along)
    return post


def lane_ids():
    return lax.broadcasted_iota(jnp.int32, (8, 128), 1)


def row_ids():
    return lax.broadcasted_iota(jnp.int32, (8, 128), 0)


def by_parity(axis, one, two, body):
    even = lax.rem(lax.axis_index(axis), 2) == 0
    pl.when(even)(lambda: body(one, two))
    pl.when(jnp.logical_not(even))(lambda: body(two, one))


def z_blocks(near, far, part):
    blocks = [(c, near) for c in range(CHANNELS)]
    return blocks + [(9 * part + k, far) for k in range(9)] + [(WALL, far)]


def first_kernel(pops_at, solid_at, table_at, index_at, own, two, one, *scratch):
    pops, solid, table, index, sems = scratch
    small = ((table_at, table), (index_at, index), (solid_at, solid))
    planes = [(pops_at.at[:, z], pops.at[:, z]) for z in range(NZ)]
    copies = [
        pltpu.make_async_copy(source, target, sems.at[i])
        for i, (source, target) in enumerate((*small, *planes))
    ]
    for copy in copies:
        copy.start()
    for copy in copies[:3]:
        copy.wait()
    lanes, rows = lane_ids(), row_ids()
    sponge = (lax.axis_index("gx") * NX + lanes) < SPONGE
    for z in range(NZ):
        aim = jnp.zeros((8, 128), F32)
        for y in range(NY):
            aim = jnp.where(rows == y, table[z, index[y]], aim)
        copies[3 + z].wait()
        post = relaxed([pops[q, z] for q in range(27)], sponge, aim)
        for q in range(27):
            own[pl.ds((q * NZ + z) * 8, 8), :] = post[q]
        own[pl.ds((WALL * NZ + z) * 8, 8), :] = solid[z].astype(F32)
        own[pl.ds((AIM * NZ + z) * 8, 8), :] = aim

    def pack(yup, ydown):
        for out, edge, second, part in ((yup, 7, 6, 6), (ydown, 0, 1, 0)):
            out[pl.ds(0, CHANNELS * NZ), :] = own[pl.ds(edge, CHANNELS * NZ, stride=8), :]
            for a in range(3):
                out[pl.ds((CHANNELS + 3 * a) * NZ, 3 * NZ), :] = own[
                    pl.ds((9 * a + part) * NZ * 8 + second, 3 * NZ, stride=8), :
                ]

    by_parity("gy", one, two, pack)


def ahead_kernel(own, two, one):
    def pack(zup, zdown):
        for out, first, second, part in ((zup, NZ - 1, NZ - 2, 2), (zdown, 0, 1, 0)):
            for k, (c, z) in enumerate(z_blocks(first, second, part)):
                out[pl.ds(8 * k, 8), :] = own[pl.ds((c * NZ + z) * 8, 8), :]

    by_parity("gz", one, two, pack)


def second_kernel(own, y_two, y_one, z_two, z_one):
    by_parity(
        "gy",
        y_one,
        y_two,
        lambda above, below: by_parity(
            "gz", z_one, z_two, lambda zup, zdown: pack_planes(own, below, above, zup, zdown)
        ),
    )


def pack_planes(own, below, above, zup, zdown):
    for out, first, second, part in ((zup, NZ - 1, NZ - 2, 2), (zdown, 0, 1, 0)):
        for side, halo in enumerate((below, above)):
            near = side * Z_BLOCKS
            out[pl.ds(near, CHANNELS), :] = halo[pl.ds(first, CHANNELS, stride=NZ), :]
            out[pl.ds(near + CHANNELS, 9), :] = halo[pl.ds(9 * part * NZ + second, 9, stride=NZ), :]
            out[pl.ds(near + Z_BLOCKS - 1, 1), :] = halo[pl.ds(WALL * NZ + second, 1), :]
            far = Z_FAR + 12 * side
            out[pl.ds(far, 9), :] = halo[pl.ds(CHANNELS * NZ + first, 9, stride=NZ), :]
            out[pl.ds(far + 9, 3), :] = halo[
                pl.ds((CHANNELS + 3 * part) * NZ + second, 3, stride=NZ), :
            ]


def plane_at(z):
    return PAD + (z + 2) * PITCH


def add_rows(full, above, below):
    for c in range(CHANNELS):
        for halo, near in ((below, 1), (above, PITCH - 2)):
            full[c, pl.ds(plane_at(0) + near, NZ, stride=PITCH), :] = halo[pl.ds(c * NZ, NZ), :]
    for halo, far, group in ((below, 0, 6), (above, PITCH - 1, 0)):
        for k in range(9):
            q = 9 * (k // 3) + group + k % 3
            full[q, pl.ds(plane_at(0) + far, NZ, stride=PITCH), :] = halo[
                pl.ds((CHANNELS + k) * NZ, NZ), :
            ]
        full[WALL, pl.ds(plane_at(0) + far, NZ, stride=PITCH), :] = halo[pl.ds(WALL * NZ, NZ), :]


def add_own_planes(full, ceiling, floor):
    for halo, near, far, part in ((floor, -1, -2, 2), (ceiling, NZ, NZ + 1, 0)):
        for k, (c, z) in enumerate(z_blocks(near, far, part)):
            full[c, pl.ds(plane_at(z) + 2, 8), :] = halo[pl.ds(8 * k, 8), :]


def add_planes(full, ceiling, floor):
    for halo, near, far, part in ((floor, -1, -2, 2), (ceiling, NZ, NZ + 1, 0)):
        for k, (c, z) in enumerate(z_blocks(near, far, part)):
            for side, row in enumerate((1, PITCH - 2)):
                start = side * Z_BLOCKS + k
                full[c, pl.ds(plane_at(z) + row, 1), :] = halo[pl.ds(start, 1), :]
        for side, (row, group) in enumerate(((0, 2), (PITCH - 1, 0))):
            start = Z_FAR + 12 * side
            for k in range(9):
                q = 9 * (k // 3) + 3 * group + k % 3
                full[q, pl.ds(plane_at(near) + row, 1), :] = halo[pl.ds(start + k, 1), :]
            for k in range(3):
                q = 9 * part + 3 * group + k
                full[q, pl.ds(plane_at(far) + row, 1), :] = halo[pl.ds(start + 9 + k, 1), :]
            for k, z in ((WALL, near), (Z_BLOCKS - 1, far)):
                flag = halo[pl.ds(side * Z_BLOCKS + k, 1), :]
                full[WALL, pl.ds(plane_at(z) + row, 1), :] = flag


def third_kernel(own, y_two, y_one, two, one, z_two, z_one, full, columns, message, pack):
    last = lax.axis_size("gz") - 1
    here = lax.axis_index("gz")
    for c in range(CHANNELS):
        for z in range(NZ):
            full[c, pl.ds(plane_at(z) + 2, 8), :] = own[pl.ds((c * NZ + z) * 8, 8), :]
    by_parity("gy", y_one, y_two, functools.partial(add_rows, full))
    by_parity("gz", one, two, functools.partial(add_own_planes, full))
    by_parity("gz", z_one, z_two, functools.partial(add_planes, full))

    @pl.when(here == 0)
    def _():
        full[WALL, pl.ds(plane_at(-1), PITCH), :] = jnp.ones((PITCH, 128), F32)

    @pl.when(here == last)
    def _():
        for q in range(9):
            full[q, pl.ds(plane_at(NZ), PITCH), :] = full[q + 18, pl.ds(plane_at(NZ - 1), PITCH), :]

    slot = lane_ids() // 4
    pack[pl.ds(FLAT, 128 - FLAT), :] = jnp.zeros((128 - FLAT, 128), F32)
    for t in range(FLAT // 8):
        packed = jnp.zeros((8, 128), F32)
        for c in range(CHANNELS):
            moved = pltpu.roll(full[c, pl.ds(PAD + 8 * t, 8), :], (4 * c + 2) % 128, 1)
            packed = jnp.where(slot == c, moved, packed)
        pack[pl.ds(8 * t, 8), :] = packed
    columns[pl.ds(PAD, 128), :] = pack[...].T

    def row(c, i, count):
        return columns[pl.ds(PAD + 4 * c + i, count), :]

    def returned(q, near, far):
        cx, cy, cz = VEL[q]
        step = (-PITCH * cz - cy) % 128
        value = row(26 - q, near, 8)
        value = pltpu.roll(value, step, 1) if step else value
        return jnp.where(row(WALL, far, 8) != 0.0, value, row(q, far, 8))[:1]

    for c in range(WALL + 1):
        cx = VEL[c][0] if c < 27 else 0
        if cx == 0:
            message[pl.ds(2 * c, 2), :] = row(c, 1, 2)
        elif cx > 0:
            message[pl.ds(2 * c, 1), :] = returned(c, 1, 0)
            message[pl.ds(2 * c + 1, 1), :] = row(c, 1, 1)
        else:
            message[pl.ds(2 * c, 1), :] = row(c, 2, 1)
            message[pl.ds(2 * c + 1, 1), :] = returned(c, 2, 3)


def block_kernel(full, post, walls):
    top = lax.axis_index("gz") == lax.axis_size("gz") - 1
    sponge = (lax.axis_index("gx") * NX + lane_ids()) < SPONGE
    for t in range(ROWS // 8):
        rows = pl.ds(8 * t, 8)
        flags = full[WALL, rows, :]
        for cx in (-1, 0, 1):
            walls[cx + 1, rows, :] = pltpu.roll(flags, cx % 128, 1) if cx else flags
    for u in range(UNITS):
        cell = PAD + PITCH + 8 * u
        f = []
        solid = walls[1, pl.ds(cell, 8), :] != 0.0
        for q in range(27):
            cx, cy, cz = VEL[q]
            start = cell - PITCH * cz - cy
            value = full[q, pl.ds(start, 8), :]
            if cx:
                value = pltpu.roll(value, cx % 128, 1)
            if q != 13:
                blocked = walls[cx + 1, pl.ds(start, 8), :] != 0.0
                value = jnp.where(blocked, full[26 - q, pl.ds(cell, 8), :], value)
            f.append(jnp.where(solid, WEIGHT[q], value))
        done = relaxed(f, sponge, full[AIM, pl.ds(cell, 8), :])
        for q in range(27):
            post[q, pl.ds(8 * u, 8), :] = done[q]

    @pl.when(top)
    def _():
        for q in range(9):
            post[q, pl.ds((NZ + 1) * PITCH, PITCH), :] = post[q + 18, pl.ds(NZ * PITCH, PITCH), :]


def last_kernel(full, block, columns, x_one, x_two, out, west, east, post, walls, back, done, sems):
    here_x, size_x = lax.axis_index("gx"), lax.axis_size("gx")
    top = lax.axis_index("gz") == lax.axis_size("gz") - 1
    lanes, rows = lane_ids(), row_ids()

    def spread(right, left):
        west[pl.ds(PAD, X_ROWS), :] = left[...]
        east[pl.ds(PAD, X_ROWS), :] = right[...]

    by_parity("gx", x_one, x_two, spread)

    strip = []
    for c in range(CHANNELS):
        cx = VEL[c][0] if c < 27 else 0
        value = jnp.where(
            rows < 4, columns[pl.ds(PAD + 4 * c, 8), :], columns[pl.ds(PAD + 4 * c - 4, 8), :]
        )
        if c <= WALL and cx >= 0:
            value = jnp.where(rows < 2, west[pl.ds(PAD + 2 * c - (cx == 0), 8), :], value)
        if c <= WALL and cx <= 0:
            value = jnp.where(rows >= 6, east[pl.ds(PAD + 2 * c - 6 + (cx == 0), 8), :], value)
        strip.append(value)
    strip[WALL] = jnp.where((rows == 0) | (rows == 7), 0.0, strip[WALL])

    def shifted(value, q):
        cx, cy, cz = VEL[q]
        if cx:
            value = pltpu.roll(value, cx % 8, 0)
        step = (PITCH * cz + cy) % 128
        return pltpu.roll(value, step, 1) if step else value

    moved = []
    for q in range(27):
        value = shifted(strip[q], q)
        if q != 13:
            value = jnp.where(shifted(strip[WALL], q) != 0.0, strip[26 - q], value)
        moved.append(jnp.where(strip[WALL] != 0.0, WEIGHT[q], value))
    column = here_x * NX + jnp.where(rows < 4, rows - 2, rows + (NX - 6))
    column = lax.rem(column + size_x * NX, size_x * NX)
    sides = relaxed(moved, column < SPONGE, strip[AIM])
    lid = top & (lanes >= (NZ + 2) * PITCH) & (lanes < (NZ + 3) * PITCH)
    for q in range(9):
        sides[q] = jnp.where(lid, pltpu.roll(sides[q + 18], PITCH, 1), sides[q])
    sides.append(strip[WALL])
    sides = [
        jnp.where((rows == 1) | (rows == 5), pltpu.roll(side, 4, 0), side) for side in sides
    ]
    sides += [jnp.zeros((8, 128), F32)] * 4
    for i in range(2):
        back[i] = jnp.concatenate(sides[16 * i : 16 * i + 16], axis=0).T

    def column_at(c, place, lane, start):
        value = back[c // 16, pl.ds(start, 8), :]
        return pltpu.roll(value, (lane - 8 * (c % 16) - place) % 128, 1)

    rim = (lanes == 0) | (lanes == 127)
    for u in range(UNITS):
        for q in range(27):
            post[q, pl.ds(8 * u, 8), :] = jnp.where(
                rim, column_at(q, 2, 0, PITCH + 8 * u), block[q, pl.ds(8 * u, 8), :]
            )
        flags = full[WALL, pl.ds(PAD + PITCH + 8 * u, 8), :]
        walls[1, pl.ds(8 * u, 8), :] = flags
        for cx, edge, place in ((1, 0, 5), (-1, 127, 6)):
            walls[cx + 1, pl.ds(8 * u, 8), :] = jnp.where(
                lanes == edge, column_at(WALL, place, edge, PITCH + 8 * u), pltpu.roll(flags, cx % 128, 1)
            )

    copies = []
    for z in range(NZ):
        cell = (z + 1) * PITCH + 2
        solid = walls[1, pl.ds(cell, 8), :] != 0.0
        for q in range(27):
            cx, cy, cz = VEL[q]
            start = cell - PITCH * cz - cy
            value = post[q, pl.ds(start, 8), :]
            if cx:
                edge, place = (0, 5) if cx > 0 else (127, 6)
                side = column_at(q, place, edge, PITCH + start)
                value = jnp.where(lanes == edge, side, pltpu.roll(value, cx % 128, 1))
            if q != 13:
                blocked = walls[cx + 1, pl.ds(start, 8), :] != 0.0
                value = jnp.where(blocked, post[26 - q, pl.ds(cell, 8), :], value)
            done[q, z] = jnp.where(solid, WEIGHT[q], value)
        copies.append(pltpu.make_async_copy(done.at[:, z], out.at[:, z], sems.at[z]))
        copies[-1].start()
    for copy in copies:
        copy.wait()


def swap(value, axis, turn, wrap):
    size = lax.axis_size(axis)
    pairs = [(i, (i + 1) % size) for i in range(turn, size if wrap else size - 1, 2)]
    return lax.ppermute(value, axis, pairs + [(j, i) for i, j in pairs])


def shape(*dims):
    return jax.ShapeDtypeStruct(dims, F32)


def shards(pops, solid, profile_table, profile_index):
    own, y_two, y_one = pl.pallas_call(
        first_kernel,
        out_shape=[shape(CHANNELS * NZ * 8, 128), shape(Y_ROWS, 128), shape(Y_ROWS, 128)],
        in_specs=[HBM] * 4,
        out_specs=[VMEM] * 3,
        scratch_shapes=[
            pltpu.VMEM(pops.shape, F32),
            pltpu.VMEM(solid.shape, jnp.int32),
            pltpu.SMEM(profile_table.shape[::-1], F32),
            pltpu.SMEM(profile_index.shape, jnp.int32),
            pltpu.SemaphoreType.DMA((3 + NZ,)),
        ],
        compiler_params=PARAMS,
        name="collide",
    )(*(pltpu.with_memory_space_constraint(a, pltpu.HBM) for a in (pops, solid, profile_table.T, profile_index)))
    y_two = swap(y_two, "gy", 1, True)
    y_one = swap(y_one, "gy", 0, True)
    own_two, own_one = pl.pallas_call(
        ahead_kernel,
        out_shape=[shape(Z_BLOCKS * 8, 128)] * 2,
        in_specs=[VMEM],
        out_specs=[VMEM] * 2,
        compiler_params=PARAMS,
        name="pack_own",
    )(own)
    own_two = swap(own_two, "gz", 1, False)
    own_one = swap(own_one, "gz", 0, False)
    z_two, z_one = pl.pallas_call(
        second_kernel,
        out_shape=[shape(Z_ROWS, 128)] * 2,
        in_specs=[VMEM] * 3,
        out_specs=[VMEM] * 2,
        compiler_params=PARAMS,
        cost_estimate=pl.CostEstimate(flops=10**9, bytes_accessed=2**20, transcendentals=0),
        name="pack_z",
    )(own, y_two, y_one)
    z_two = swap(z_two, "gz", 1, False)
    z_one = swap(z_one, "gz", 0, False)
    full, columns, message = pl.pallas_call(
        third_kernel,
        out_shape=[shape(CHANNELS, ROWS, 128), shape(PAD + 128 + PAD, 128), shape(X_ROWS, 128)],
        in_specs=[VMEM] * 7,
        out_specs=[VMEM] * 3,
        scratch_shapes=[pltpu.VMEM((128, 128), F32)],
        compiler_params=PARAMS,
        name="pack_x",
    )(own, y_two, y_one, own_two, own_one, z_two, z_one)
    x_one = swap(message, "gx", 0, True)
    x_two = x_one if lax.axis_size("gx") == 2 else swap(message, "gx", 1, True)
    block = pl.pallas_call(
        block_kernel,
        out_shape=shape(27, UNITS * 8, 128),
        in_specs=[VMEM],
        out_specs=VMEM,
        scratch_shapes=[pltpu.VMEM((3, ROWS, 128), F32)],
        compiler_params=PARAMS,
        cost_estimate=pl.CostEstimate(
            flops=27 * 20 * UNITS * 1024, bytes_accessed=2**22, transcendentals=0
        ),
        name="block",
    )(full)
    return pl.pallas_call(
        last_kernel,
        out_shape=shape(27, NZ, NY, NX),
        in_specs=[VMEM] * 5,
        out_specs=HBM,
        scratch_shapes=[
            pltpu.VMEM((PAD + X_ROWS + PAD, 128), F32),
            pltpu.VMEM((PAD + X_ROWS + PAD, 128), F32),
            pltpu.VMEM((27, UNITS * 8, 128), F32),
            pltpu.VMEM((3, UNITS * 8, 128), F32),
            pltpu.VMEM((2, 128, 128), F32),
            pltpu.VMEM((27, NZ, NY, NX), F32),
            pltpu.SemaphoreType.DMA((NZ,)),
        ],
        compiler_params=PARAMS,
        name="finish",
    )(full, block, columns, x_one, x_two)


def solution(mesh):
    return jax.shard_map(
        shards,
        mesh=mesh,
        in_specs=(P(None, "gz", "gy", "gx"), P("gz", "gy", "gx"), P(None, "gz"), P("gy")),
        out_specs=P(None, "gz", "gy", "gx"),
        check_vma=False,
    )
```

```python
import functools

import jax
import jax.numpy as jnp
import numpy as np
from jax import lax
from jax.experimental import pallas as pl
from jax.experimental.pallas import tpu as pltpu
from jax.sharding import PartitionSpec as P

SPONGE = 32
TAU = 0.52
SMAG = 18.0 * 1.4142135623730951 * 0.17 * 0.17

VEL = [(cx, cy, cz) for cz in (-1, 0, 1) for cy in (-1, 0, 1) for cx in (-1, 0, 1)]
WEIGHT = [
    float(np.array([8.0 / 27.0, 2.0 / 27.0, 1.0 / 54.0, 1.0 / 216.0])[cx * cx + cy * cy + cz * cz])
    for cx, cy, cz in VEL
]
WALL, AIM, CHANNELS = 27, 28, 29
NZ, NY, NX = 4, 8, 128
PITCH = NY + 4
FLAT = (NZ + 4) * PITCH
PAD = 8
ROWS = PAD + FLAT + PAD
UNITS = (NZ + 2) * PITCH // 8

PARAMS = pltpu.CompilerParams(vmem_limit_bytes=12 * 2**20)
VMEM = pl.BlockSpec(memory_space=pltpu.VMEM)
HBM = pl.BlockSpec(memory_space=pltpu.HBM)
F32 = jnp.float32

Y_ROWS = (CHANNELS + 9) * NZ
Z_BLOCKS = CHANNELS + 10
Z_FAR = 2 * Z_BLOCKS
Z_ROWS = -(-(Z_FAR + 2 * 12) // 8) * 8

X_ROWS = 2 * (WALL + 1)


def relaxed(f, sponge, aim):
    quad = {}
    for cz in (-1, 0, 1):
        line = {}
        for cy in (-1, 0, 1):
            base = 9 * (cz + 1) + 3 * (cy + 1)
            both = f[base + 2] + f[base]
            line[cy] = (both + f[base + 1], f[base + 2] - f[base], both)
        s = line[1][0] + line[-1][0]
        sx = line[1][1] + line[-1][1]
        quad[cz] = dict(
            n=s + line[0][0],
            y=line[1][0] - line[-1][0],
            yy=s,
            x=sx + line[0][1],
            xy=line[1][1] - line[-1][1],
            xx=line[1][2] + line[-1][2] + line[0][2],
        )
    up, mid, down = quad[1], quad[0], quad[-1]
    zz = up["n"] + down["n"]
    rho = zz + mid["n"]
    jz = up["n"] - down["n"]
    jy = up["y"] + down["y"] + mid["y"]
    jx = up["x"] + down["x"] + mid["x"]
    inverse = 1.0 / rho
    ux, uy, uz = jx * inverse, jy * inverse, jz * inverse
    third = rho * (1.0 / 3.0)
    pxx = (up["xx"] + down["xx"] + mid["xx"]) - (third + jx * ux)
    pyy = (up["yy"] + down["yy"] + mid["yy"]) - (third + jy * uy)
    pzz = zz - (third + jz * uz)
    pxy = (up["xy"] + down["xy"] + mid["xy"]) - jx * uy
    pxz = (up["x"] - down["x"]) - jx * uz
    pyz = (up["y"] - down["y"]) - jy * uz
    strain = pxx * pxx + pyy * pyy + pzz * pzz + 2.0 * (pxy * pxy + pxz * pxz + pyz * pyz)
    size = jnp.sqrt(2.0 * strain)
    tau = 0.5 * (TAU + jnp.sqrt(TAU * TAU + SMAG * size * inverse))
    omega = 1.0 / tau
    keep = 1.0 - omega
    if sponge is not None:
        keep = jnp.where(sponge, 0.0, keep)
        omega = jnp.where(sponge, 1.0, omega)
        ux = jnp.where(sponge, aim, ux)
        uy = jnp.where(sponge, 0.0, uy)
        uz = jnp.where(sponge, 0.0, uz)
    square = 1.0 - 1.5 * (ux * ux + uy * uy + uz * uz)
    vx, vy, vz = 3.0 * ux, 3.0 * uy, 3.0 * uz
    share = rho * omega
    weighted = {w: share * w for w in sorted(set(WEIGHT))}
    post = [None] * 27
    for q in range(14):
        cx, cy, cz = VEL[q]
        along = None
        for c, v in ((cx, vx), (cy, vy), (cz, vz)):
            if c:
                along = (v if c > 0 else -v) if along is None else (along + v if c > 0 else along - v)
        scale = weighted[WEIGHT[q]]
        if along is None:
            post[q] = keep * f[q] + scale * square
            continue
        even = square + 0.5 * along * along
        post[q] = keep * f[q] + scale * (even + along)
        post[26 - q] = keep * f[26 - q] + scale * (even - along)
    return post


def lane_ids():
    return lax.broadcasted_iota(jnp.int32, (8, 128), 1)


def row_ids():
    return lax.broadcasted_iota(jnp.int32, (8, 128), 0)


def by_parity(axis, one, two, body):
    even = lax.rem(lax.axis_index(axis), 2) == 0
    pl.when(even)(lambda: body(one, two))
    pl.when(jnp.logical_not(even))(lambda: body(two, one))


def z_blocks(near, far, part):
    blocks = [(c, near) for c in range(CHANNELS)]
    return blocks + [(9 * part + k, far) for k in range(9)] + [(WALL, far)]


def first_kernel(pops_at, solid_at, table_at, index_at, own, two, one, *scratch):
    pops, solid, table, index, sems = scratch
    small = ((table_at, table), (index_at, index), (solid_at, solid))
    planes = [(pops_at.at[:, z], pops.at[:, z]) for z in range(NZ)]
    copies = [
        pltpu.make_async_copy(source, target, sems.at[i])
        for i, (source, target) in enumerate((*small, *planes))
    ]
    for copy in copies:
        copy.start()
    for copy in copies[:3]:
        copy.wait()
    lanes, rows = lane_ids(), row_ids()
    sponge = (lax.axis_index("gx") * NX + lanes) < SPONGE
    for z in range(NZ):
        aim = jnp.zeros((8, 128), F32)
        for y in range(NY):
            aim = jnp.where(rows == y, table[z, index[y]], aim)
        copies[3 + z].wait()
        post = relaxed([pops[q, z] for q in range(27)], sponge, aim)
        for q in range(27):
            own[pl.ds((q * NZ + z) * 8, 8), :] = post[q]
        own[pl.ds((WALL * NZ + z) * 8, 8), :] = solid[z].astype(F32)
        own[pl.ds((AIM * NZ + z) * 8, 8), :] = aim

    def pack(yup, ydown):
        for out, edge, second, part in ((yup, 7, 6, 6), (ydown, 0, 1, 0)):
            out[pl.ds(0, CHANNELS * NZ), :] = own[pl.ds(edge, CHANNELS * NZ, stride=8), :]
            for a in range(3):
                out[pl.ds((CHANNELS + 3 * a) * NZ, 3 * NZ), :] = own[
                    pl.ds((9 * a + part) * NZ * 8 + second, 3 * NZ, stride=8), :
                ]

    by_parity("gy", one, two, pack)


def ahead_kernel(own, two, one):
    def pack(zup, zdown):
        for out, first, second, part in ((zup, NZ - 1, NZ - 2, 2), (zdown, 0, 1, 0)):
            for k, (c, z) in enumerate(z_blocks(first, second, part)):
                out[pl.ds(8 * k, 8), :] = own[pl.ds((c * NZ + z) * 8, 8), :]

    by_parity("gz", one, two, pack)


def second_kernel(own, y_two, y_one, z_two, z_one):
    by_parity(
        "gy",
        y_one,
        y_two,
        lambda above, below: by_parity(
            "gz", z_one, z_two, lambda zup, zdown: pack_planes(own, below, above, zup, zdown)
        ),
    )


def pack_planes(own, below, above, zup, zdown):
    for out, first, second, part in ((zup, NZ - 1, NZ - 2, 2), (zdown, 0, 1, 0)):
        for side, halo in enumerate((below, above)):
            near = side * Z_BLOCKS
            out[pl.ds(near, CHANNELS), :] = halo[pl.ds(first, CHANNELS, stride=NZ), :]
            out[pl.ds(near + CHANNELS, 9), :] = halo[pl.ds(9 * part * NZ + second, 9, stride=NZ), :]
            out[pl.ds(near + Z_BLOCKS - 1, 1), :] = halo[pl.ds(WALL * NZ + second, 1), :]
            far = Z_FAR + 12 * side
            out[pl.ds(far, 9), :] = halo[pl.ds(CHANNELS * NZ + first, 9, stride=NZ), :]
            out[pl.ds(far + 9, 3), :] = halo[
                pl.ds((CHANNELS + 3 * part) * NZ + second, 3, stride=NZ), :
            ]


def plane_at(z):
    return PAD + (z + 2) * PITCH


def add_rows(full, above, below):
    for c in range(CHANNELS):
        for halo, near in ((below, 1), (above, PITCH - 2)):
            full[c, pl.ds(plane_at(0) + near, NZ, stride=PITCH), :] = halo[pl.ds(c * NZ, NZ), :]
    for halo, far, group in ((below, 0, 6), (above, PITCH - 1, 0)):
        for k in range(9):
            q = 9 * (k // 3) + group + k % 3
            full[q, pl.ds(plane_at(0) + far, NZ, stride=PITCH), :] = halo[
                pl.ds((CHANNELS + k) * NZ, NZ), :
            ]
        full[WALL, pl.ds(plane_at(0) + far, NZ, stride=PITCH), :] = halo[pl.ds(WALL * NZ, NZ), :]


def add_own_planes(full, ceiling, floor):
    for halo, near, far, part in ((floor, -1, -2, 2), (ceiling, NZ, NZ + 1, 0)):
        for k, (c, z) in enumerate(z_blocks(near, far, part)):
            full[c, pl.ds(plane_at(z) + 2, 8), :] = halo[pl.ds(8 * k, 8), :]


def add_planes(full, ceiling, floor):
    for halo, near, far, part in ((floor, -1, -2, 2), (ceiling, NZ, NZ + 1, 0)):
        for k, (c, z) in enumerate(z_blocks(near, far, part)):
            for side, row in enumerate((1, PITCH - 2)):
                start = side * Z_BLOCKS + k
                full[c, pl.ds(plane_at(z) + row, 1), :] = halo[pl.ds(start, 1), :]
        for side, (row, group) in enumerate(((0, 2), (PITCH - 1, 0))):
            start = Z_FAR + 12 * side
            for k in range(9):
                q = 9 * (k // 3) + 3 * group + k % 3
                full[q, pl.ds(plane_at(near) + row, 1), :] = halo[pl.ds(start + k, 1), :]
            for k in range(3):
                q = 9 * part + 3 * group + k
                full[q, pl.ds(plane_at(far) + row, 1), :] = halo[pl.ds(start + 9 + k, 1), :]
            for k, z in ((WALL, near), (Z_BLOCKS - 1, far)):
                flag = halo[pl.ds(side * Z_BLOCKS + k, 1), :]
                full[WALL, pl.ds(plane_at(z) + row, 1), :] = flag


def pack_columns(full, pack, tiles):
    slot = lane_ids() // 4
    for t in tiles:
        packed = jnp.zeros((8, 128), F32)
        for c in range(CHANNELS):
            moved = pltpu.roll(full[c, pl.ds(PAD + 8 * t, 8), :], (4 * c + 2) % 128, 1)
            packed = jnp.where(slot == c, moved, packed)
        pack[pl.ds(8 * t, 8), :] = packed


OWN_TILES = range(2 * PITCH // 8, (NZ + 2) * PITCH // 8)


def fill_kernel(own, y_two, y_one, two, one, full, pack):
    for c in range(CHANNELS):
        for z in range(NZ):
            full[c, pl.ds(plane_at(z) + 2, 8), :] = own[pl.ds((c * NZ + z) * 8, 8), :]
    by_parity("gy", y_one, y_two, functools.partial(add_rows, full))
    by_parity("gz", one, two, functools.partial(add_own_planes, full))
    pack_columns(full, pack, OWN_TILES)
    pack[pl.ds(FLAT, 128 - FLAT), :] = jnp.zeros((128 - FLAT, 128), F32)


def third_kernel(part, packed, z_two, z_one, full, pack, columns, message):
    last = lax.axis_size("gz") - 1
    here = lax.axis_index("gz")
    by_parity("gz", z_one, z_two, functools.partial(add_planes, full))

    @pl.when(here == 0)
    def _():
        full[WALL, pl.ds(plane_at(-1), PITCH), :] = jnp.ones((PITCH, 128), F32)

    @pl.when(here == last)
    def _():
        for q in range(9):
            full[q, pl.ds(plane_at(NZ), PITCH), :] = full[q + 18, pl.ds(plane_at(NZ - 1), PITCH), :]

    pack_columns(full, pack, [t for t in range(FLAT // 8) if t not in OWN_TILES])
    columns[pl.ds(PAD, 128), :] = pack[...].T

    def row(c, i, count):
        return columns[pl.ds(PAD + 4 * c + i, count), :]

    def returned(q, near, far):
        cx, cy, cz = VEL[q]
        step = (-PITCH * cz - cy) % 128
        value = row(26 - q, near, 8)
        value = pltpu.roll(value, step, 1) if step else value
        return jnp.where(row(WALL, far, 8) != 0.0, value, row(q, far, 8))[:1]

    for c in range(WALL + 1):
        cx = VEL[c][0] if c < 27 else 0
        if cx == 0:
            message[pl.ds(2 * c, 2), :] = row(c, 1, 2)
        elif cx > 0:
            message[pl.ds(2 * c, 1), :] = returned(c, 1, 0)
            message[pl.ds(2 * c + 1, 1), :] = row(c, 1, 1)
        else:
            message[pl.ds(2 * c, 1), :] = row(c, 2, 1)
            message[pl.ds(2 * c + 1, 1), :] = returned(c, 2, 3)


def block_kernel(full, post, walls):
    top = lax.axis_index("gz") == lax.axis_size("gz") - 1
    sponge = (lax.axis_index("gx") * NX + lane_ids()) < SPONGE
    for t in range(ROWS // 8):
        rows = pl.ds(8 * t, 8)
        flags = full[WALL, rows, :]
        for cx in (-1, 0, 1):
            walls[cx + 1, rows, :] = pltpu.roll(flags, cx % 128, 1) if cx else flags
    for u in range(UNITS):
        cell = PAD + PITCH + 8 * u
        f = []
        solid = walls[1, pl.ds(cell, 8), :] != 0.0
        for q in range(27):
            cx, cy, cz = VEL[q]
            start = cell - PITCH * cz - cy
            value = full[q, pl.ds(start, 8), :]
            if cx:
                value = pltpu.roll(value, cx % 128, 1)
            if q != 13:
                blocked = walls[cx + 1, pl.ds(start, 8), :] != 0.0
                value = jnp.where(blocked, full[26 - q, pl.ds(cell, 8), :], value)
            f.append(jnp.where(solid, WEIGHT[q], value))
        done = relaxed(f, sponge, full[AIM, pl.ds(cell, 8), :])
        for q in range(27):
            post[q, pl.ds(8 * u, 8), :] = done[q]

    @pl.when(top)
    def _():
        for q in range(9):
            post[q, pl.ds((NZ + 1) * PITCH, PITCH), :] = post[q + 18, pl.ds(NZ * PITCH, PITCH), :]


def last_kernel(full, block, columns, x_one, x_two, out, west, east, walls, back, done, sems):
    here_x, size_x = lax.axis_index("gx"), lax.axis_size("gx")
    top = lax.axis_index("gz") == lax.axis_size("gz") - 1
    lanes, rows = lane_ids(), row_ids()

    def spread(right, left):
        west[pl.ds(PAD, X_ROWS), :] = left[...]
        east[pl.ds(PAD, X_ROWS), :] = right[...]

    by_parity("gx", x_one, x_two, spread)

    strip = []
    for c in range(CHANNELS):
        cx = VEL[c][0] if c < 27 else 0
        value = jnp.where(
            rows < 4, columns[pl.ds(PAD + 4 * c, 8), :], columns[pl.ds(PAD + 4 * c - 4, 8), :]
        )
        if c <= WALL and cx >= 0:
            value = jnp.where(rows < 2, west[pl.ds(PAD + 2 * c - (cx == 0), 8), :], value)
        if c <= WALL and cx <= 0:
            value = jnp.where(rows >= 6, east[pl.ds(PAD + 2 * c - 6 + (cx == 0), 8), :], value)
        strip.append(value)
    strip[WALL] = jnp.where((rows == 0) | (rows == 7), 0.0, strip[WALL])

    def shifted(value, q):
        cx, cy, cz = VEL[q]
        if cx:
            value = pltpu.roll(value, cx % 8, 0)
        step = (PITCH * cz + cy) % 128
        return pltpu.roll(value, step, 1) if step else value

    moved = []
    for q in range(27):
        value = shifted(strip[q], q)
        if q != 13:
            value = jnp.where(shifted(strip[WALL], q) != 0.0, strip[26 - q], value)
        moved.append(jnp.where(strip[WALL] != 0.0, WEIGHT[q], value))
    column = here_x * NX + jnp.where(rows < 4, rows - 2, rows + (NX - 6))
    column = lax.rem(column + size_x * NX, size_x * NX)
    sides = relaxed(moved, column < SPONGE, strip[AIM])
    lid = top & (lanes >= (NZ + 2) * PITCH) & (lanes < (NZ + 3) * PITCH)
    for q in range(9):
        sides[q] = jnp.where(lid, pltpu.roll(sides[q + 18], PITCH, 1), sides[q])
    ends = [jnp.where(rows == 1, pltpu.roll(side, 4, 0), side) for side in sides]
    ends += [jnp.zeros((8, 128), F32)] * 5
    for i in range(2):
        back[i] = jnp.concatenate(ends[16 * i : 16 * i + 16], axis=0).T
    pairs = [jnp.where(rows < 4, sides[3 * k + 2], sides[3 * k]) for k in range(9)]
    pairs += [strip[WALL]] + [jnp.zeros((8, 128), F32)] * 6
    back[2] = jnp.concatenate(pairs, axis=0).T

    def column_at(i, place, lane, start):
        return pltpu.roll(back[i, pl.ds(start, 8), :], (lane - place) % 128, 1)

    rim = (lanes == 0) | (lanes == 127)

    def rimmed(q, start):
        ends = column_at(q // 16, 8 * (q % 16) + 2, 0, PITCH + start)
        return jnp.where(rim, ends, block[q, pl.ds(start, 8), :])

    for u in range(UNITS):
        flags = full[WALL, pl.ds(PAD + PITCH + 8 * u, 8), :]
        walls[1, pl.ds(8 * u, 8), :] = flags
        for cx, edge, place in ((1, 0, 73), (-1, 127, 78)):
            walls[cx + 1, pl.ds(8 * u, 8), :] = jnp.where(
                lanes == edge, column_at(2, place, edge, PITCH + 8 * u), pltpu.roll(flags, cx % 128, 1)
            )

    copies = []
    for z in range(NZ):
        cell = (z + 1) * PITCH + 2
        solid = walls[1, pl.ds(cell, 8), :] != 0.0
        for q in range(27):
            cx, cy, cz = VEL[q]
            start = cell - PITCH * cz - cy
            if cx > 0:
                side = column_at(2, 8 * (q // 3) + 1, 0, PITCH + start)
                value = jnp.where(lanes < 2, side, pltpu.roll(block[q, pl.ds(start, 8), :], 1, 1))
            elif cx < 0:
                side = column_at(2, 8 * (q // 3) + 5, 126, PITCH + start)
                value = jnp.where(lanes > 125, side, pltpu.roll(block[q, pl.ds(start, 8), :], 127, 1))
            else:
                value = rimmed(q, start)
            if q != 13:
                blocked = walls[cx + 1, pl.ds(start, 8), :] != 0.0
                value = jnp.where(blocked, rimmed(26 - q, cell), value)
            done[q, z] = jnp.where(solid, WEIGHT[q], value)
        copies.append(pltpu.make_async_copy(done.at[:, z], out.at[:, z], sems.at[z]))
        copies[-1].start()
    for copy in copies:
        copy.wait()


def swap(value, axis, turn, wrap):
    size = lax.axis_size(axis)
    pairs = [(i, (i + 1) % size) for i in range(turn, size if wrap else size - 1, 2)]
    return lax.ppermute(value, axis, pairs + [(j, i) for i, j in pairs])


def shape(*dims):
    return jax.ShapeDtypeStruct(dims, F32)


def shards(pops, solid, profile_table, profile_index):
    own, y_two, y_one = pl.pallas_call(
        first_kernel,
        out_shape=[shape(CHANNELS * NZ * 8, 128), shape(Y_ROWS, 128), shape(Y_ROWS, 128)],
        in_specs=[HBM] * 4,
        out_specs=[VMEM] * 3,
        scratch_shapes=[
            pltpu.VMEM(pops.shape, F32),
            pltpu.VMEM(solid.shape, jnp.int32),
            pltpu.SMEM(profile_table.shape[::-1], F32),
            pltpu.SMEM(profile_index.shape, jnp.int32),
            pltpu.SemaphoreType.DMA((3 + NZ,)),
        ],
        compiler_params=PARAMS,
        name="collide",
    )(*(pltpu.with_memory_space_constraint(a, pltpu.HBM) for a in (pops, solid, profile_table.T, profile_index)))
    y_two = swap(y_two, "gy", 1, True)
    y_one = swap(y_one, "gy", 0, True)
    own_two, own_one = pl.pallas_call(
        ahead_kernel,
        out_shape=[shape(Z_BLOCKS * 8, 128)] * 2,
        in_specs=[VMEM],
        out_specs=[VMEM] * 2,
        compiler_params=PARAMS,
        name="pack_own",
    )(own)
    own_two = swap(own_two, "gz", 1, False)
    own_one = swap(own_one, "gz", 0, False)
    z_two, z_one = pl.pallas_call(
        second_kernel,
        out_shape=[shape(Z_ROWS, 128)] * 2,
        in_specs=[VMEM] * 3,
        out_specs=[VMEM] * 2,
        compiler_params=PARAMS,
        cost_estimate=pl.CostEstimate(flops=10**9, bytes_accessed=2**20, transcendentals=0),
        name="pack_z",
    )(own, y_two, y_one)
    z_two = swap(z_two, "gz", 1, False)
    z_one = swap(z_one, "gz", 0, False)
    part, packed = pl.pallas_call(
        fill_kernel,
        out_shape=[shape(CHANNELS, ROWS, 128), shape(128, 128)],
        in_specs=[VMEM] * 5,
        out_specs=[VMEM] * 2,
        compiler_params=PARAMS,
        cost_estimate=pl.CostEstimate(flops=10**6, bytes_accessed=2**22, transcendentals=0),
        name="fill",
    )(own, y_two, y_one, own_two, own_one)
    full, packed, columns, message = pl.pallas_call(
        third_kernel,
        out_shape=[
            shape(CHANNELS, ROWS, 128),
            shape(128, 128),
            shape(PAD + 128 + PAD, 128),
            shape(X_ROWS, 128),
        ],
        in_specs=[VMEM] * 4,
        out_specs=[VMEM] * 4,
        input_output_aliases={0: 0, 1: 1},
        compiler_params=PARAMS,
        name="pack_x",
    )(part, packed, z_two, z_one)
    x_one = swap(message, "gx", 0, True)
    x_two = x_one if lax.axis_size("gx") == 2 else swap(message, "gx", 1, True)
    block = pl.pallas_call(
        block_kernel,
        out_shape=shape(27, UNITS * 8, 128),
        in_specs=[VMEM],
        out_specs=VMEM,
        scratch_shapes=[pltpu.VMEM((3, ROWS, 128), F32)],
        compiler_params=PARAMS,
        cost_estimate=pl.CostEstimate(
            flops=27 * 20 * UNITS * 1024, bytes_accessed=2**22, transcendentals=0
        ),
        name="block",
    )(full)
    return pl.pallas_call(
        last_kernel,
        out_shape=shape(27, NZ, NY, NX),
        in_specs=[VMEM] * 5,
        out_specs=HBM,
        scratch_shapes=[
            pltpu.VMEM((PAD + X_ROWS + PAD, 128), F32),
            pltpu.VMEM((PAD + X_ROWS + PAD, 128), F32),
            pltpu.VMEM((3, UNITS * 8, 128), F32),
            pltpu.VMEM((3, 128, 128), F32),
            pltpu.VMEM((27, NZ, NY, NX), F32),
            pltpu.SemaphoreType.DMA((NZ,)),
        ],
        compiler_params=PARAMS,
        name="finish",
    )(full, block, columns, x_one, x_two)


def solution(mesh):
    return jax.shard_map(
        shards,
        mesh=mesh,
        in_specs=(P(None, "gz", "gy", "gx"), P("gz", "gy", "gx"), P(None, "gz"), P("gy")),
        out_specs=P(None, "gz", "gy", "gx"),
        check_vma=False,
    )
```

```python
import functools

import jax
import jax.numpy as jnp
import numpy as np
from jax import lax
from jax.experimental import pallas as pl
from jax.experimental.pallas import tpu as pltpu
from jax.sharding import PartitionSpec as P

SPONGE = 32
TAU = 0.52
SMAG = 18.0 * 1.4142135623730951 * 0.17 * 0.17

VEL = [(cx, cy, cz) for cz in (-1, 0, 1) for cy in (-1, 0, 1) for cx in (-1, 0, 1)]
WEIGHT = [
    float(np.array([8.0 / 27.0, 2.0 / 27.0, 1.0 / 54.0, 1.0 / 216.0])[cx * cx + cy * cy + cz * cz])
    for cx, cy, cz in VEL
]
WALL, AIM, CHANNELS = 27, 28, 29
NZ, NY, NX = 4, 8, 128
PITCH = NY + 4
FLAT = (NZ + 4) * PITCH
PAD = 8
ROWS = PAD + FLAT + PAD
UNITS = (NZ + 2) * PITCH // 8

PARAMS = pltpu.CompilerParams(vmem_limit_bytes=12 * 2**20)
VMEM = pl.BlockSpec(memory_space=pltpu.VMEM)
HBM = pl.BlockSpec(memory_space=pltpu.HBM)
F32 = jnp.float32

Y_ROWS = (CHANNELS + 9) * NZ
Z_BLOCKS = CHANNELS + 10
Z_FAR = 2 * Z_BLOCKS
Z_ROWS = -(-(Z_FAR + 2 * 12) // 8) * 8 + 2 * PITCH

OWN = NZ * PITCH
EDGE = 2 * PITCH


def relaxed(f, sponge, aim):
    quad = {}
    for cz in (-1, 0, 1):
        line = {}
        for cy in (-1, 0, 1):
            base = 9 * (cz + 1) + 3 * (cy + 1)
            both = f[base + 2] + f[base]
            line[cy] = (both + f[base + 1], f[base + 2] - f[base], both)
        s = line[1][0] + line[-1][0]
        sx = line[1][1] + line[-1][1]
        quad[cz] = dict(
            n=s + line[0][0],
            y=line[1][0] - line[-1][0],
            yy=s,
            x=sx + line[0][1],
            xy=line[1][1] - line[-1][1],
            xx=line[1][2] + line[-1][2] + line[0][2],
        )
    up, mid, down = quad[1], quad[0], quad[-1]
    zz = up["n"] + down["n"]
    rho = zz + mid["n"]
    jz = up["n"] - down["n"]
    jy = up["y"] + down["y"] + mid["y"]
    jx = up["x"] + down["x"] + mid["x"]
    inverse = 1.0 / rho
    ux, uy, uz = jx * inverse, jy * inverse, jz * inverse
    third = rho * (1.0 / 3.0)
    pxx = (up["xx"] + down["xx"] + mid["xx"]) - (third + jx * ux)
    pyy = (up["yy"] + down["yy"] + mid["yy"]) - (third + jy * uy)
    pzz = zz - (third + jz * uz)
    pxy = (up["xy"] + down["xy"] + mid["xy"]) - jx * uy
    pxz = (up["x"] - down["x"]) - jx * uz
    pyz = (up["y"] - down["y"]) - jy * uz
    strain = pxx * pxx + pyy * pyy + pzz * pzz + 2.0 * (pxy * pxy + pxz * pxz + pyz * pyz)
    size = jnp.sqrt(2.0 * strain)
    tau = 0.5 * (TAU + jnp.sqrt(TAU * TAU + SMAG * size * inverse))
    omega = 1.0 / tau
    keep = 1.0 - omega
    if sponge is not None:
        keep = jnp.where(sponge, 0.0, keep)
        omega = jnp.where(sponge, 1.0, omega)
        ux = jnp.where(sponge, aim, ux)
        uy = jnp.where(sponge, 0.0, uy)
        uz = jnp.where(sponge, 0.0, uz)
    square = 1.0 - 1.5 * (ux * ux + uy * uy + uz * uz)
    vx, vy, vz = 3.0 * ux, 3.0 * uy, 3.0 * uz
    share = rho * omega
    weighted = {w: share * w for w in sorted(set(WEIGHT))}
    post = [None] * 27
    for q in range(14):
        cx, cy, cz = VEL[q]
        along = None
        for c, v in ((cx, vx), (cy, vy), (cz, vz)):
            if c:
                along = (v if c > 0 else -v) if along is None else (along + v if c > 0 else along - v)
        scale = weighted[WEIGHT[q]]
        if along is None:
            post[q] = keep * f[q] + scale * square
            continue
        even = square + 0.5 * along * along
        post[q] = keep * f[q] + scale * (even + along)
        post[26 - q] = keep * f[26 - q] + scale * (even - along)
    return post


def lane_ids():
    return lax.broadcasted_iota(jnp.int32, (8, 128), 1)


def row_ids():
    return lax.broadcasted_iota(jnp.int32, (8, 128), 0)


def by_parity(axis, one, two, body):
    even = lax.rem(lax.axis_index(axis), 2) == 0
    pl.when(even)(lambda: body(one, two))
    pl.when(jnp.logical_not(even))(lambda: body(two, one))


def z_blocks(near, far, part):
    blocks = [(c, near) for c in range(CHANNELS)]
    return blocks + [(9 * part + k, far) for k in range(9)] + [(WALL, far)]


def first_kernel(pops_at, solid_at, table_at, index_at, own, two, one, *scratch):
    pops, solid, table, index, sems = scratch
    small = ((table_at, table), (index_at, index), (solid_at, solid))
    planes = [(pops_at.at[:, z], pops.at[:, z]) for z in range(NZ)]
    copies = [
        pltpu.make_async_copy(source, target, sems.at[i])
        for i, (source, target) in enumerate((*small, *planes))
    ]
    for copy in copies:
        copy.start()
    for copy in copies[:3]:
        copy.wait()
    lanes, rows = lane_ids(), row_ids()
    sponge = (lax.axis_index("gx") * NX + lanes) < SPONGE
    for z in range(NZ):
        aim = jnp.zeros((8, 128), F32)
        for y in range(NY):
            aim = jnp.where(rows == y, table[z, index[y]], aim)
        copies[3 + z].wait()
        post = relaxed([pops[q, z] for q in range(27)], sponge, aim)
        for q in range(27):
            own[pl.ds((q * NZ + z) * 8, 8), :] = post[q]
        own[pl.ds((WALL * NZ + z) * 8, 8), :] = solid[z].astype(F32)
        own[pl.ds((AIM * NZ + z) * 8, 8), :] = aim

    def pack(yup, ydown):
        for out, edge, second, part in ((yup, 7, 6, 6), (ydown, 0, 1, 0)):
            out[pl.ds(0, CHANNELS * NZ), :] = own[pl.ds(edge, CHANNELS * NZ, stride=8), :]
            for a in range(3):
                out[pl.ds((CHANNELS + 3 * a) * NZ, 3 * NZ), :] = own[
                    pl.ds((9 * a + part) * NZ * 8 + second, 3 * NZ, stride=8), :
                ]

    by_parity("gy", one, two, pack)


def ahead_kernel(own, columns, two, one):
    slot = lane_ids() // 4
    for z in range(NZ):
        packed = jnp.zeros((8, 128), F32)
        for c in range(CHANNELS):
            moved = pltpu.roll(own[pl.ds((c * NZ + z) * 8, 8), :], (4 * c + 2) % 128, 1)
            packed = jnp.where(slot == c, moved, packed)
        columns[pl.ds(8 * z, 8), :] = packed

    def pack(zup, zdown):
        for out, first, second, part in ((zup, NZ - 1, NZ - 2, 2), (zdown, 0, 1, 0)):
            for k, (c, z) in enumerate(z_blocks(first, second, part)):
                out[pl.ds(8 * k, 8), :] = own[pl.ds((c * NZ + z) * 8, 8), :]

    by_parity("gz", one, two, pack)


def second_kernel(y_two, y_one, *refs):
    turns = 1 if lax.axis_size("gx") == 2 else 2
    level, refs = refs[: 3 * turns], refs[3 * turns :]
    z_two, z_one, beside = refs

    def gather(straight, two, one, lanes):
        def put(target, count, source, start):
            value = source[pl.ds(start, count), :]
            if lanes is not None:
                value = jnp.where(lanes[:count], value, beside[pl.ds(target, count), :])
            beside[pl.ds(target, count), :] = value

        def rows(above, below):
            for z in range(NZ):
                put(z * PITCH, 2, below, z * NY + NY - 2)
                put(z * PITCH + 2, NY, straight, z * NY)
                put(z * PITCH + 2 + NY, 2, above, z * NY)

        by_parity("gy", one, two, rows)

    if turns == 1:
        gather(*level, None)
    else:
        right_lanes = lax.rem(lane_ids(), 4) >= 2

        def sides(right, left):
            gather(*left, None)
            gather(*right, right_lanes)

        by_parity("gx", level[:3], level[3:], sides)

    by_parity(
        "gy",
        y_one,
        y_two,
        lambda above, below: by_parity(
            "gz",
            z_one,
            z_two,
            lambda zup, zdown: pack_planes(below, above, beside, zup, zdown),
        ),
    )


def pack_planes(below, above, beside, zup, zdown):
    for out, first, second, part in ((zup, NZ - 1, NZ - 2, 2), (zdown, 0, 1, 0)):
        start = min(first, second) * PITCH
        out[pl.ds(Z_ROWS - EDGE, EDGE), :] = beside[pl.ds(start, EDGE), :]
        for side, halo in enumerate((below, above)):
            near = side * Z_BLOCKS
            out[pl.ds(near, CHANNELS), :] = halo[pl.ds(first, CHANNELS, stride=NZ), :]
            out[pl.ds(near + CHANNELS, 9), :] = halo[pl.ds(9 * part * NZ + second, 9, stride=NZ), :]
            out[pl.ds(near + Z_BLOCKS - 1, 1), :] = halo[pl.ds(WALL * NZ + second, 1), :]
            far = Z_FAR + 12 * side
            out[pl.ds(far, 9), :] = halo[pl.ds(CHANNELS * NZ + first, 9, stride=NZ), :]
            out[pl.ds(far + 9, 3), :] = halo[
                pl.ds((CHANNELS + 3 * part) * NZ + second, 3, stride=NZ), :
            ]


def plane_at(z):
    return PAD + (z + 2) * PITCH


def add_rows(full, above, below):
    for c in range(CHANNELS):
        for halo, near in ((below, 1), (above, PITCH - 2)):
            full[c, pl.ds(plane_at(0) + near, NZ, stride=PITCH), :] = halo[pl.ds(c * NZ, NZ), :]
    for halo, far, group in ((below, 0, 6), (above, PITCH - 1, 0)):
        for k in range(9):
            q = 9 * (k // 3) + group + k % 3
            full[q, pl.ds(plane_at(0) + far, NZ, stride=PITCH), :] = halo[
                pl.ds((CHANNELS + k) * NZ, NZ), :
            ]
        full[WALL, pl.ds(plane_at(0) + far, NZ, stride=PITCH), :] = halo[pl.ds(WALL * NZ, NZ), :]


def add_own_planes(full, ceiling, floor):
    for halo, near, far, part in ((floor, -1, -2, 2), (ceiling, NZ, NZ + 1, 0)):
        for k, (c, z) in enumerate(z_blocks(near, far, part)):
            full[c, pl.ds(plane_at(z) + 2, 8), :] = halo[pl.ds(8 * k, 8), :]


def add_planes(full, ceiling, floor):
    for halo, near, far, part in ((floor, -1, -2, 2), (ceiling, NZ, NZ + 1, 0)):
        for k, (c, z) in enumerate(z_blocks(near, far, part)):
            for side, row in enumerate((1, PITCH - 2)):
                start = side * Z_BLOCKS + k
                full[c, pl.ds(plane_at(z) + row, 1), :] = halo[pl.ds(start, 1), :]
        for side, (row, group) in enumerate(((0, 2), (PITCH - 1, 0))):
            start = Z_FAR + 12 * side
            for k in range(9):
                q = 9 * (k // 3) + 3 * group + k % 3
                full[q, pl.ds(plane_at(near) + row, 1), :] = halo[pl.ds(start + k, 1), :]
            for k in range(3):
                q = 9 * part + 3 * group + k
                full[q, pl.ds(plane_at(far) + row, 1), :] = halo[pl.ds(start + 9 + k, 1), :]
            for k, z in ((WALL, near), (Z_BLOCKS - 1, far)):
                flag = halo[pl.ds(side * Z_BLOCKS + k, 1), :]
                full[WALL, pl.ds(plane_at(z) + row, 1), :] = flag


def pack_columns(full, pack, tiles):
    slot = lane_ids() // 4
    for t in tiles:
        packed = jnp.zeros((8, 128), F32)
        for c in range(CHANNELS):
            moved = pltpu.roll(full[c, pl.ds(PAD + 8 * t, 8), :], (4 * c + 2) % 128, 1)
            packed = jnp.where(slot == c, moved, packed)
        pack[pl.ds(8 * t, 8), :] = packed


OWN_TILES = range(EDGE // 8, (EDGE + OWN) // 8)
INNER = range(2 * PITCH // 8, NZ * PITCH // 8)


def roll_walls(full, walls, tiles):
    for t in tiles:
        rows = pl.ds(8 * t, 8)
        flags = full[WALL, rows, :]
        for cx in (-1, 0, 1):
            walls[cx + 1, rows, :] = pltpu.roll(flags, cx % 128, 1) if cx else flags


def step_rows(full, walls, post, sponge, units):
    for u in units:
        cell = PAD + PITCH + 8 * u
        f = []
        solid = walls[1, pl.ds(cell, 8), :] != 0.0
        for q in range(27):
            cx, cy, cz = VEL[q]
            start = cell - PITCH * cz - cy
            value = full[q, pl.ds(start, 8), :]
            if cx:
                value = pltpu.roll(value, cx % 128, 1)
            if q != 13:
                blocked = walls[cx + 1, pl.ds(start, 8), :] != 0.0
                value = jnp.where(blocked, full[26 - q, pl.ds(cell, 8), :], value)
            f.append(jnp.where(solid, WEIGHT[q], value))
        done = relaxed(f, sponge, full[AIM, pl.ds(cell, 8), :])
        for q in range(27):
            post[q, pl.ds(8 * u, 8), :] = done[q]


def fill_kernel(own, y_two, y_one, two, one, full, mine, post, walls):
    for c in range(CHANNELS):
        for z in range(NZ):
            full[c, pl.ds(plane_at(z) + 2, 8), :] = own[pl.ds((c * NZ + z) * 8, 8), :]
    by_parity("gy", y_one, y_two, functools.partial(add_rows, full))
    by_parity("gz", one, two, functools.partial(add_own_planes, full))
    pack_columns(full, mine, OWN_TILES)
    sponge = (lax.axis_index("gx") * NX + lane_ids()) < SPONGE
    roll_walls(full, walls, range(ROWS // 8))
    step_rows(full, walls, post, sponge, INNER)


def last_kernel(
    part, packed, inner, beside, z_two, z_one, out, full, mine, post, walls, near, turn, sheet, back,
    done, sems
):
    here_x, size_x = lax.axis_index("gx"), lax.axis_size("gx")
    here, last = lax.axis_index("gz"), lax.axis_size("gz") - 1
    top, bottom = here == last, here == 0
    lanes, rows = lane_ids(), row_ids()

    def add_halo(ceiling, floor):
        add_planes(full, ceiling, floor)
        near[pl.ds(0, EDGE), :] = floor[pl.ds(Z_ROWS - EDGE, EDGE), :]
        near[pl.ds(EDGE + OWN, EDGE), :] = ceiling[pl.ds(Z_ROWS - EDGE, EDGE), :]

    by_parity("gz", z_one, z_two, add_halo)

    @pl.when(bottom)
    def _():
        full[WALL, pl.ds(plane_at(-1), PITCH), :] = jnp.ones((PITCH, 128), F32)

    @pl.when(top)
    def _():
        for q in range(9):
            full[q, pl.ds(plane_at(NZ), PITCH), :] = full[q + 18, pl.ds(plane_at(NZ - 1), PITCH), :]

    near[pl.ds(EDGE, OWN), :] = beside[...]
    pack_columns(full, mine, [t for t in range(FLAT // 8) if t not in OWN_TILES])

    for i, source in enumerate((mine, near)):
        square = jnp.concatenate([source[...], jnp.zeros((128 - FLAT, 128), F32)], axis=0)
        turn[i, pl.ds(PAD, 128), :] = square.T

    strip = []
    for c in range(CHANNELS):
        first, second = pl.ds(PAD + 4 * c, 8), pl.ds(PAD + 4 * c - 4, 8)
        own = jnp.where(rows < 4, turn[0, first, :], turn[0, second, :])
        other = jnp.where(rows < 4, turn[1, first, :], turn[1, second, :])
        strip.append(jnp.where((rows >= 2) & (rows < 6), own, other))

    ceiling = top & (lanes >= (NZ + 2) * PITCH) & (lanes < (NZ + 3) * PITCH)
    ground = bottom & (lanes >= PITCH) & (lanes < 2 * PITCH)
    for q in range(9):
        strip[q] = jnp.where(ceiling, pltpu.roll(strip[q + 18], PITCH, 1), strip[q])
    strip[WALL] = jnp.where(ceiling, 0.0, jnp.where(ground, 1.0, strip[WALL]))

    def shifted(value, q):
        cx, cy, cz = VEL[q]
        if cx:
            value = pltpu.roll(value, cx % 8, 0)
        step = (PITCH * cz + cy) % 128
        return pltpu.roll(value, step, 1) if step else value

    moved = []
    for q in range(27):
        value = shifted(strip[q], q)
        if q != 13:
            value = jnp.where(shifted(strip[WALL], q) != 0.0, strip[26 - q], value)
        moved.append(jnp.where(strip[WALL] != 0.0, WEIGHT[q], value))
    column = here_x * NX + jnp.where(rows < 4, rows - 2, rows + (NX - 6))
    column = lax.rem(column + size_x * NX, size_x * NX)
    sides = relaxed(moved, column < SPONGE, strip[AIM])
    for q in range(9):
        sides[q] = jnp.where(ceiling, pltpu.roll(sides[q + 18], PITCH, 1), sides[q])
    ends = [jnp.where(rows == 1, pltpu.roll(side, 4, 0), side) for side in sides]
    ends += [jnp.zeros((8, 128), F32)] * 5
    for i in range(2):
        back[i] = jnp.concatenate(ends[16 * i : 16 * i + 16], axis=0).T
    pairs = [jnp.where(rows < 4, sides[3 * k + 2], sides[3 * k]) for k in range(9)]
    pairs += [strip[WALL]] + [jnp.zeros((8, 128), F32)] * 6
    back[2] = jnp.concatenate(pairs, axis=0).T

    sponge = (here_x * NX + lanes) < SPONGE
    roll_walls(full, walls, [t for t in range(ROWS // 8)])
    step_rows(full, walls, post, sponge, [u for u in range(UNITS) if u not in INNER])

    def column_at(i, place, lane, start):
        return pltpu.roll(back[i, pl.ds(start, 8), :], (lane - place) % 128, 1)

    for u in range(UNITS):
        cell = pl.ds(PAD + PITCH + 8 * u, 8)
        sheet[1, pl.ds(8 * u, 8), :] = walls[1, cell, :]
        for cx, edge, place in ((1, 0, 73), (-1, 127, 78)):
            side = column_at(2, place, edge, PITCH + 8 * u)
            sheet[cx + 1, pl.ds(8 * u, 8), :] = jnp.where(lanes == edge, side, walls[cx + 1, cell, :])

    rim = (lanes == 0) | (lanes == 127)

    def block(q, z, start):
        value = post[q, pl.ds(start, 8), :]
        if z == NZ - 1 and VEL[q][2] < 0:
            value = jnp.where(top, post[q + 18, pl.ds(start - PITCH, 8), :], value)
        return value

    def rimmed(value, q, start):
        return jnp.where(rim, column_at(q // 16, 8 * (q % 16) + 2, 0, PITCH + start), value)

    copies = []
    for z in range(NZ):
        cell = (z + 1) * PITCH + 2
        solid = sheet[1, pl.ds(cell, 8), :] != 0.0
        for q in range(27):
            cx, cy, cz = VEL[q]
            start = cell - PITCH * cz - cy
            value = block(q, z, start)
            if cx > 0:
                side = column_at(2, 8 * (q // 3) + 1, 0, PITCH + start)
                value = jnp.where(lanes < 2, side, pltpu.roll(value, 1, 1))
            elif cx < 0:
                side = column_at(2, 8 * (q // 3) + 5, 126, PITCH + start)
                value = jnp.where(lanes > 125, side, pltpu.roll(value, 127, 1))
            else:
                value = rimmed(value, q, start)
            if q != 13:
                blocked = sheet[cx + 1, pl.ds(start, 8), :] != 0.0
                value = jnp.where(blocked, rimmed(post[26 - q, pl.ds(cell, 8), :], 26 - q, cell), value)
            done[q, z] = jnp.where(solid, WEIGHT[q], value)
        copies.append(pltpu.make_async_copy(done.at[:, z], out.at[:, z], sems.at[z]))
        copies[-1].start()
    for copy in copies:
        copy.wait()


def pairs(size, turn, wrap):
    ahead = [(i, (i + 1) % size) for i in range(turn, size if wrap else size - 1, 2)]
    return ahead + [(j, i) for i, j in ahead]


def swap(value, axis, turn, wrap):
    return lax.ppermute(value, axis, pairs(lax.axis_size(axis), turn, wrap))


def swap_across(value, x_turn, y_turn):
    size = lax.axis_size("gy")
    over_x = pairs(lax.axis_size("gx"), x_turn, True)
    over_y = pairs(size, y_turn, True)
    both = [(i * size + j, far_i * size + far_j) for i, far_i in over_x for j, far_j in over_y]
    return lax.ppermute(value, ("gx", "gy"), both)


def shape(*dims):
    return jax.ShapeDtypeStruct(dims, F32)


def shards(pops, solid, profile_table, profile_index):
    own, y_two, y_one = pl.pallas_call(
        first_kernel,
        out_shape=[shape(CHANNELS * NZ * 8, 128), shape(Y_ROWS, 128), shape(Y_ROWS, 128)],
        in_specs=[HBM] * 4,
        out_specs=[VMEM] * 3,
        scratch_shapes=[
            pltpu.VMEM(pops.shape, F32),
            pltpu.VMEM(solid.shape, jnp.int32),
            pltpu.SMEM(profile_table.shape[::-1], F32),
            pltpu.SMEM(profile_index.shape, jnp.int32),
            pltpu.SemaphoreType.DMA((3 + NZ,)),
        ],
        compiler_params=PARAMS,
        name="collide",
    )(*(pltpu.with_memory_space_constraint(a, pltpu.HBM) for a in (pops, solid, profile_table.T, profile_index)))
    y_two = swap(y_two, "gy", 1, True)
    y_one = swap(y_one, "gy", 0, True)
    columns, own_two, own_one = pl.pallas_call(
        ahead_kernel,
        out_shape=[shape(NZ * NY, 128), *[shape(Z_BLOCKS * 8, 128)] * 2],
        in_specs=[VMEM],
        out_specs=[VMEM] * 3,
        compiler_params=PARAMS,
        name="pack_own",
    )(own)
    level = []
    for turn in range(1 if lax.axis_size("gx") == 2 else 2):
        level += [swap(columns, "gx", turn, True)]
        level += [swap_across(columns, turn, 1), swap_across(columns, turn, 0)]
    own_two = swap(own_two, "gz", 1, False)
    own_one = swap(own_one, "gz", 0, False)
    z_two, z_one, beside = pl.pallas_call(
        second_kernel,
        out_shape=[*[shape(Z_ROWS, 128)] * 2, shape(OWN, 128)],
        in_specs=[VMEM] * (2 + len(level)),
        out_specs=[VMEM] * 3,
        compiler_params=PARAMS,
        cost_estimate=pl.CostEstimate(flops=10**9, bytes_accessed=2**20, transcendentals=0),
        name="pack_z",
    )(y_two, y_one, *level)
    z_two = swap(z_two, "gz", 1, False)
    z_one = swap(z_one, "gz", 0, False)
    part, packed, inner = pl.pallas_call(
        fill_kernel,
        out_shape=[shape(CHANNELS, ROWS, 128), shape(FLAT, 128), shape(27, UNITS * 8, 128)],
        in_specs=[VMEM] * 5,
        out_specs=[VMEM] * 3,
        scratch_shapes=[pltpu.VMEM((3, ROWS, 128), F32)],
        compiler_params=PARAMS,
        cost_estimate=pl.CostEstimate(flops=10**6, bytes_accessed=2**22, transcendentals=0),
        name="fill",
    )(own, y_two, y_one, own_two, own_one)
    return pl.pallas_call(
        last_kernel,
        out_shape=[
            shape(27, NZ, NY, NX),
            shape(CHANNELS, ROWS, 128),
            shape(FLAT, 128),
            shape(27, UNITS * 8, 128),
        ],
        in_specs=[VMEM] * 6,
        out_specs=[HBM] + [VMEM] * 3,
        input_output_aliases={0: 1, 1: 2, 2: 3},
        scratch_shapes=[
            pltpu.VMEM((3, ROWS, 128), F32),
            pltpu.VMEM((FLAT, 128), F32),
            pltpu.VMEM((2, PAD + 128 + PAD, 128), F32),
            pltpu.VMEM((3, UNITS * 8, 128), F32),
            pltpu.VMEM((3, 128, 128), F32),
            pltpu.VMEM((27, NZ, NY, NX), F32),
            pltpu.SemaphoreType.DMA((NZ,)),
        ],
        compiler_params=PARAMS,
        name="finish",
    )(part, packed, inner, beside, z_two, z_one)[0]


def solution(mesh):
    return jax.shard_map(
        shards,
        mesh=mesh,
        in_specs=(P(None, "gz", "gy", "gx"), P("gz", "gy", "gx"), P(None, "gz"), P("gy")),
        out_specs=P(None, "gz", "gy", "gx"),
        check_vma=False,
    )
```

```python
import functools

import jax
import jax.numpy as jnp
import numpy as np
from jax import lax
from jax.experimental import pallas as pl
from jax.experimental.pallas import tpu as pltpu
from jax.sharding import PartitionSpec as P

SPONGE = 32
TAU = 0.52
SMAG = 18.0 * 1.4142135623730951 * 0.17 * 0.17

VEL = [(cx, cy, cz) for cz in (-1, 0, 1) for cy in (-1, 0, 1) for cx in (-1, 0, 1)]
WEIGHT = [
    float(np.array([8.0 / 27.0, 2.0 / 27.0, 1.0 / 54.0, 1.0 / 216.0])[cx * cx + cy * cy + cz * cz])
    for cx, cy, cz in VEL
]
WALL, AIM, CHANNELS = 27, 28, 29
NZ, NY, NX = 4, 8, 128
PITCH = NY + 4
FLAT = (NZ + 4) * PITCH
PAD = 8
ROWS = PAD + FLAT + PAD
UNITS = (NZ + 2) * PITCH // 8

PARAMS = pltpu.CompilerParams(vmem_limit_bytes=12 * 2**20)
VMEM = pl.BlockSpec(memory_space=pltpu.VMEM)
HBM = pl.BlockSpec(memory_space=pltpu.HBM)
F32 = jnp.float32

Y_ROWS = (CHANNELS + 9) * NZ
Z_BLOCKS = CHANNELS + 10
Z_FAR = 2 * Z_BLOCKS
Z_ROWS = -(-(Z_FAR + 2 * 12) // 8) * 8

X_ROWS = 2 * (WALL + 1)


def relaxed(f, sponge, aim):
    quad = {}
    for cz in (-1, 0, 1):
        line = {}
        for cy in (-1, 0, 1):
            base = 9 * (cz + 1) + 3 * (cy + 1)
            both = f[base + 2] + f[base]
            line[cy] = (both + f[base + 1], f[base + 2] - f[base], both)
        s = line[1][0] + line[-1][0]
        sx = line[1][1] + line[-1][1]
        quad[cz] = dict(
            n=s + line[0][0],
            y=line[1][0] - line[-1][0],
            yy=s,
            x=sx + line[0][1],
            xy=line[1][1] - line[-1][1],
            xx=line[1][2] + line[-1][2] + line[0][2],
        )
    up, mid, down = quad[1], quad[0], quad[-1]
    zz = up["n"] + down["n"]
    rho = zz + mid["n"]
    jz = up["n"] - down["n"]
    jy = up["y"] + down["y"] + mid["y"]
    jx = up["x"] + down["x"] + mid["x"]
    inverse = 1.0 / rho
    ux, uy, uz = jx * inverse, jy * inverse, jz * inverse
    third = rho * (1.0 / 3.0)
    pxx = (up["xx"] + down["xx"] + mid["xx"]) - (third + jx * ux)
    pyy = (up["yy"] + down["yy"] + mid["yy"]) - (third + jy * uy)
    pzz = zz - (third + jz * uz)
    pxy = (up["xy"] + down["xy"] + mid["xy"]) - jx * uy
    pxz = (up["x"] - down["x"]) - jx * uz
    pyz = (up["y"] - down["y"]) - jy * uz
    strain = pxx * pxx + pyy * pyy + pzz * pzz + 2.0 * (pxy * pxy + pxz * pxz + pyz * pyz)
    size = jnp.sqrt(2.0 * strain)
    tau = 0.5 * (TAU + jnp.sqrt(TAU * TAU + SMAG * size * inverse))
    omega = 1.0 / tau
    keep = 1.0 - omega
    if sponge is not None:
        keep = jnp.where(sponge, 0.0, keep)
        omega = jnp.where(sponge, 1.0, omega)
        ux = jnp.where(sponge, aim, ux)
        uy = jnp.where(sponge, 0.0, uy)
        uz = jnp.where(sponge, 0.0, uz)
    square = 1.0 - 1.5 * (ux * ux + uy * uy + uz * uz)
    vx, vy, vz = 3.0 * ux, 3.0 * uy, 3.0 * uz
    share = rho * omega
    weighted = {w: share * w for w in sorted(set(WEIGHT))}
    post = [None] * 27
    for q in range(14):
        cx, cy, cz = VEL[q]
        along = None
        for c, v in ((cx, vx), (cy, vy), (cz, vz)):
            if c:
                along = (v if c > 0 else -v) if along is None else (along + v if c > 0 else along - v)
        scale = weighted[WEIGHT[q]]
        if along is None:
            post[q] = keep * f[q] + scale * square
            continue
        even = square + 0.5 * along * along
        post[q] = keep * f[q] + scale * (even + along)
        post[26 - q] = keep * f[26 - q] + scale * (even - along)
    return post


def lane_ids():
    return lax.broadcasted_iota(jnp.int32, (8, 128), 1)


def row_ids():
    return lax.broadcasted_iota(jnp.int32, (8, 128), 0)


def by_parity(axis, one, two, body):
    even = lax.rem(lax.axis_index(axis), 2) == 0
    pl.when(even)(lambda: body(one, two))
    pl.when(jnp.logical_not(even))(lambda: body(two, one))


def z_blocks(near, far, part):
    blocks = [(c, near) for c in range(CHANNELS)]
    return blocks + [(9 * part + k, far) for k in range(9)] + [(WALL, far)]


def first_kernel(pops_at, solid_at, table_at, index_at, own, two, one, *scratch):
    pops, solid, table, index, sems = scratch
    small = ((table_at, table), (index_at, index), (solid_at, solid))
    parts = [(pl.ds(q, 9), z) for z in range(NZ) for q in (0, 9, 18)]
    planes = [(pops_at.at[part], pops.at[part]) for part in parts]
    copies = [
        pltpu.make_async_copy(source, target, sems.at[i])
        for i, (source, target) in enumerate((*small, *planes))
    ]
    for copy in copies:
        copy.start()
    for copy in copies[:3]:
        copy.wait()
    lanes, rows = lane_ids(), row_ids()
    sponge = (lax.axis_index("gx") * NX + lanes) < SPONGE
    for z in range(NZ):
        aim = jnp.zeros((8, 128), F32)
        for y in range(NY):
            aim = jnp.where(rows == y, table[z, index[y]], aim)
        for copy in copies[3 * z + 3 : 3 * z + 6]:
            copy.wait()
        post = relaxed([pops[q, z] for q in range(27)], sponge, aim)
        for q in range(27):
            own[pl.ds((q * NZ + z) * 8, 8), :] = post[q]
        own[pl.ds((WALL * NZ + z) * 8, 8), :] = solid[z].astype(F32)
        own[pl.ds((AIM * NZ + z) * 8, 8), :] = aim

    def pack(yup, ydown):
        for out, edge, second, part in ((yup, 7, 6, 6), (ydown, 0, 1, 0)):
            out[pl.ds(0, CHANNELS * NZ), :] = own[pl.ds(edge, CHANNELS * NZ, stride=8), :]
            for a in range(3):
                out[pl.ds((CHANNELS + 3 * a) * NZ, 3 * NZ), :] = own[
                    pl.ds((9 * a + part) * NZ * 8 + second, 3 * NZ, stride=8), :
                ]

    by_parity("gy", one, two, pack)


def ahead_kernel(own, two, one):
    def pack(zup, zdown):
        for out, first, second, part in ((zup, NZ - 1, NZ - 2, 2), (zdown, 0, 1, 0)):
            for k, (c, z) in enumerate(z_blocks(first, second, part)):
                out[pl.ds(8 * k, 8), :] = own[pl.ds((c * NZ + z) * 8, 8), :]

    by_parity("gz", one, two, pack)


def second_kernel(own, y_two, y_one, z_two, z_one):
    by_parity(
        "gy",
        y_one,
        y_two,
        lambda above, below: by_parity(
            "gz", z_one, z_two, lambda zup, zdown: pack_planes(own, below, above, zup, zdown)
        ),
    )


def pack_planes(own, below, above, zup, zdown):
    for out, first, second, part in ((zup, NZ - 1, NZ - 2, 2), (zdown, 0, 1, 0)):
        for side, halo in enumerate((below, above)):
            near = side * Z_BLOCKS
            out[pl.ds(near, CHANNELS), :] = halo[pl.ds(first, CHANNELS, stride=NZ), :]
            out[pl.ds(near + CHANNELS, 9), :] = halo[pl.ds(9 * part * NZ + second, 9, stride=NZ), :]
            out[pl.ds(near + Z_BLOCKS - 1, 1), :] = halo[pl.ds(WALL * NZ + second, 1), :]
            far = Z_FAR + 12 * side
            out[pl.ds(far, 9), :] = halo[pl.ds(CHANNELS * NZ + first, 9, stride=NZ), :]
            out[pl.ds(far + 9, 3), :] = halo[
                pl.ds((CHANNELS + 3 * part) * NZ + second, 3, stride=NZ), :
            ]


def plane_at(z):
    return PAD + (z + 2) * PITCH


def add_rows(full, above, below):
    for c in range(CHANNELS):
        for halo, near in ((below, 1), (above, PITCH - 2)):
            full[pl.ds(c * ROWS + plane_at(0) + near, NZ, stride=PITCH), :] = halo[pl.ds(c * NZ, NZ), :]
    for halo, far, group in ((below, 0, 6), (above, PITCH - 1, 0)):
        for k in range(9):
            q = 9 * (k // 3) + group + k % 3
            full[pl.ds(q * ROWS + plane_at(0) + far, NZ, stride=PITCH), :] = halo[
                pl.ds((CHANNELS + k) * NZ, NZ), :
            ]
        full[pl.ds(WALL * ROWS + plane_at(0) + far, NZ, stride=PITCH), :] = halo[pl.ds(WALL * NZ, NZ), :]


def add_own_planes(full, ceiling, floor):
    for halo, near, far, part in ((floor, -1, -2, 2), (ceiling, NZ, NZ + 1, 0)):
        for k, (c, z) in enumerate(z_blocks(near, far, part)):
            full[pl.ds(c * ROWS + plane_at(z) + 2, 8), :] = halo[pl.ds(8 * k, 8), :]


def add_planes(full, ceiling, floor):
    def put(count, channel, z, row, source):
        start = channel * ROWS + plane_at(z) + row
        full[pl.ds(start, count, stride=ROWS), :] = source

    for halo, near, far, part in ((floor, -1, -2, 2), (ceiling, NZ, NZ + 1, 0)):
        for side, (row, beyond, group) in enumerate(((1, 0, 2), (PITCH - 2, PITCH - 1, 0))):
            start = side * Z_BLOCKS
            put(CHANNELS, 0, near, row, halo[pl.ds(start, CHANNELS), :])
            put(9, 9 * part, far, row, halo[pl.ds(start + CHANNELS, 9), :])
            first, second = (halo[pl.ds(start + k, 1), :] for k in (WALL, Z_BLOCKS - 1))
            put(1, WALL, far, row, second)
            start = Z_FAR + 12 * side
            for k in range(3):
                put(3, 9 * k + 3 * group, near, beyond, halo[pl.ds(start + 3 * k, 3), :])
            put(3, 9 * part + 3 * group, far, beyond, halo[pl.ds(start + 9, 3), :])
            put(1, WALL, near, beyond, first)
            put(1, WALL, far, beyond, second)


def pack_columns(full, pack, tiles):
    slot = lane_ids() // 4
    for t in tiles:
        packed = jnp.zeros((8, 128), F32)
        for c in range(CHANNELS):
            moved = pltpu.roll(full[pl.ds(c * ROWS + PAD + 8 * t, 8), :], (4 * c + 2) % 128, 1)
            packed = jnp.where(slot == c, moved, packed)
        pack[pl.ds(8 * t, 8), :] = packed


OWN_TILES = range(2 * PITCH // 8, (NZ + 2) * PITCH // 8)


def fill_kernel(own, y_two, y_one, two, one, full, pack):
    for c in range(CHANNELS):
        for z in range(NZ):
            full[pl.ds(c * ROWS + plane_at(z) + 2, 8), :] = own[pl.ds((c * NZ + z) * 8, 8), :]
    by_parity("gy", y_one, y_two, functools.partial(add_rows, full))
    by_parity("gz", one, two, functools.partial(add_own_planes, full))
    pack_columns(full, pack, OWN_TILES)
    pack[pl.ds(FLAT, 128 - FLAT), :] = jnp.zeros((128 - FLAT, 128), F32)


def third_kernel(part, packed, z_two, z_one, full, pack, columns, message):
    last = lax.axis_size("gz") - 1
    here = lax.axis_index("gz")
    by_parity("gz", z_one, z_two, functools.partial(add_planes, full))

    @pl.when(here == 0)
    def _():
        full[pl.ds(WALL * ROWS + plane_at(-1), PITCH), :] = jnp.ones((PITCH, 128), F32)

    @pl.when(here == last)
    def _():
        for q in range(9):
            full[pl.ds(q * ROWS + plane_at(NZ), PITCH), :] = full[pl.ds((q + 18) * ROWS + plane_at(NZ - 1), PITCH), :]

    pack_columns(full, pack, [t for t in range(FLAT // 8) if t not in OWN_TILES])
    columns[pl.ds(PAD, 128), :] = pack[...].T

    def row(c, i, count):
        return columns[pl.ds(PAD + 4 * c + i, count), :]

    def returned(q, near, far):
        cx, cy, cz = VEL[q]
        step = (-PITCH * cz - cy) % 128
        value = row(26 - q, near, 8)
        value = pltpu.roll(value, step, 1) if step else value
        return jnp.where(row(WALL, far, 8) != 0.0, value, row(q, far, 8))[:1]

    for c in range(WALL + 1):
        cx = VEL[c][0] if c < 27 else 0
        if cx == 0:
            message[pl.ds(2 * c, 2), :] = row(c, 1, 2)
        elif cx > 0:
            message[pl.ds(2 * c, 1), :] = returned(c, 1, 0)
            message[pl.ds(2 * c + 1, 1), :] = row(c, 1, 1)
        else:
            message[pl.ds(2 * c, 1), :] = row(c, 2, 1)
            message[pl.ds(2 * c + 1, 1), :] = returned(c, 2, 3)


def block_kernel(full, post, walls):
    top = lax.axis_index("gz") == lax.axis_size("gz") - 1
    sponge = (lax.axis_index("gx") * NX + lane_ids()) < SPONGE
    for t in range(ROWS // 8):
        rows = pl.ds(8 * t, 8)
        flags = full[pl.ds(WALL * ROWS + 8 * t, 8), :]
        for cx in (-1, 0, 1):
            walls[cx + 1, rows, :] = pltpu.roll(flags, cx % 128, 1) if cx else flags
    for u in range(UNITS):
        cell = PAD + PITCH + 8 * u
        f = []
        solid = walls[1, pl.ds(cell, 8), :] != 0.0
        for q in range(27):
            cx, cy, cz = VEL[q]
            start = cell - PITCH * cz - cy
            value = full[pl.ds(q * ROWS + start, 8), :]
            if cx:
                value = pltpu.roll(value, cx % 128, 1)
            if q != 13:
                blocked = walls[cx + 1, pl.ds(start, 8), :] != 0.0
                value = jnp.where(blocked, full[pl.ds((26 - q) * ROWS + cell, 8), :], value)
            f.append(jnp.where(solid, WEIGHT[q], value))
        done = relaxed(f, sponge, full[pl.ds(AIM * ROWS + cell, 8), :])
        for q in range(27):
            post[q, pl.ds(8 * u, 8), :] = done[q]

    @pl.when(top)
    def _():
        for q in range(9):
            post[q, pl.ds((NZ + 1) * PITCH, PITCH), :] = post[q + 18, pl.ds(NZ * PITCH, PITCH), :]


def last_kernel(full, block, columns, x_one, x_two, out, west, east, column, walls, back, done, sems):
    here_x, size_x = lax.axis_index("gx"), lax.axis_size("gx")
    top = lax.axis_index("gz") == lax.axis_size("gz") - 1
    lanes, rows = lane_ids(), row_ids()

    def spread(right, left):
        west[pl.ds(PAD, X_ROWS), :] = left[...]
        east[pl.ds(PAD, X_ROWS), :] = right[...]

    by_parity("gx", x_one, x_two, spread)

    strip = []
    for c in range(CHANNELS):
        cx = VEL[c][0] if c < 27 else 0
        value = jnp.where(
            rows < 4, columns[pl.ds(PAD + 4 * c, 8), :], columns[pl.ds(PAD + 4 * c - 4, 8), :]
        )
        if c <= WALL and cx >= 0:
            value = jnp.where(rows < 2, west[pl.ds(PAD + 2 * c - (cx == 0), 8), :], value)
        if c <= WALL and cx <= 0:
            value = jnp.where(rows >= 6, east[pl.ds(PAD + 2 * c - 6 + (cx == 0), 8), :], value)
        strip.append(value)
    strip[WALL] = jnp.where((rows == 0) | (rows == 7), 0.0, strip[WALL])

    def shifted(value, q):
        cx, cy, cz = VEL[q]
        if cx:
            value = pltpu.roll(value, cx % 8, 0)
        step = (PITCH * cz + cy) % 128
        return pltpu.roll(value, step, 1) if step else value

    moved = []
    for q in range(27):
        value = shifted(strip[q], q)
        if q != 13:
            value = jnp.where(shifted(strip[WALL], q) != 0.0, strip[26 - q], value)
        moved.append(jnp.where(strip[WALL] != 0.0, WEIGHT[q], value))
    place = here_x * NX + jnp.where(rows < 4, rows - 2, rows + (NX - 6))
    place = lax.rem(place + size_x * NX, size_x * NX)
    sides = relaxed(moved, place < SPONGE, strip[AIM])
    lid = top & (lanes >= (NZ + 2) * PITCH) & (lanes < (NZ + 3) * PITCH)
    for q in range(9):
        sides[q] = jnp.where(lid, pltpu.roll(sides[q + 18], PITCH, 1), sides[q])
    for q, side in enumerate(sides + [strip[WALL]]):
        column[pl.ds(PAD + 8 * q, 8), :] = side

    def picked(wanted):
        value = None
        for sublane, (q, row) in enumerate(wanted):
            moved = column[pl.ds(PAD + 8 * q + row - sublane, 8), :]
            value = moved if value is None else jnp.where(rows == sublane, moved, value)
        return value

    packed = []
    for k in range(9):
        a, b = 3 * k + 2, 3 * k
        packed.append(
            picked([(a, 5), (a, 2), (a, 1), (a, 2), (b, 5), (b, 2), (b, 5), (b, 6)])
        )
    rest = [(3 * k + 1, row) for k in range(9) for row in (5, 2)] + [(27, 1), (27, 6)]
    packed += [picked(rest[i : i + 8]) for i in range(0, len(rest), 8)]
    packed += [jnp.zeros((8, 128), F32)] * (16 - len(packed))
    back[...] = jnp.concatenate(packed, axis=0).T

    def column_at(place, lane, start):
        return pltpu.roll(back[pl.ds(start, 8), :], (lane - place) % 128, 1)

    rim = (lanes == 0) | (lanes == 127)

    def rimmed(q, start):
        k = q // 3
        ends = column_at((8 * k + 5, 73 + 2 * k, 8 * k + 1)[q % 3], 0, PITCH + start)
        return jnp.where(rim, ends, block[q, pl.ds(start, 8), :])

    for u in range(UNITS):
        flags = full[pl.ds(WALL * ROWS + PAD + PITCH + 8 * u, 8), :]
        walls[1, pl.ds(8 * u, 8), :] = flags
        for cx, edge, place in ((1, 0, 90), (-1, 127, 91)):
            walls[cx + 1, pl.ds(8 * u, 8), :] = jnp.where(
                lanes == edge, column_at(place, edge, PITCH + 8 * u), pltpu.roll(flags, cx % 128, 1)
            )

    copies = []
    for z in range(NZ):
        cell = (z + 1) * PITCH + 2
        solid = walls[1, pl.ds(cell, 8), :] != 0.0
        for q in range(27):
            cx, cy, cz = VEL[q]
            start = cell - PITCH * cz - cy
            if cx > 0:
                side = column_at(8 * (q // 3) + 2, 0, PITCH + start)
                value = jnp.where(lanes < 2, side, pltpu.roll(block[q, pl.ds(start, 8), :], 1, 1))
            elif cx < 0:
                side = column_at(8 * (q // 3) + 6, 126, PITCH + start)
                value = jnp.where(lanes > 125, side, pltpu.roll(block[q, pl.ds(start, 8), :], 127, 1))
            else:
                value = rimmed(q, start)
            if q != 13:
                blocked = walls[cx + 1, pl.ds(start, 8), :] != 0.0
                value = jnp.where(blocked, rimmed(26 - q, cell), value)
            done[q, z] = jnp.where(solid, WEIGHT[q], value)
        copies.append(pltpu.make_async_copy(done.at[:, z], out.at[:, z], sems.at[z]))
        copies[-1].start()
    for copy in copies:
        copy.wait()


def swap(value, axis, turn, wrap):
    size = lax.axis_size(axis)
    pairs = [(i, (i + 1) % size) for i in range(turn, size if wrap else size - 1, 2)]
    return lax.ppermute(value, axis, pairs + [(j, i) for i, j in pairs])


def shape(*dims):
    return jax.ShapeDtypeStruct(dims, F32)


def shards(pops, solid, profile_table, profile_index):
    own, y_two, y_one = pl.pallas_call(
        first_kernel,
        out_shape=[shape(CHANNELS * NZ * 8, 128), shape(Y_ROWS, 128), shape(Y_ROWS, 128)],
        in_specs=[HBM] * 4,
        out_specs=[VMEM] * 3,
        scratch_shapes=[
            pltpu.VMEM(pops.shape, F32),
            pltpu.VMEM(solid.shape, jnp.int32),
            pltpu.SMEM(profile_table.shape[::-1], F32),
            pltpu.SMEM(profile_index.shape, jnp.int32),
            pltpu.SemaphoreType.DMA((3 + 3 * NZ,)),
        ],
        compiler_params=PARAMS,
        name="collide",
    )(*(pltpu.with_memory_space_constraint(a, pltpu.HBM) for a in (pops, solid, profile_table.T, profile_index)))
    y_two = swap(y_two, "gy", 1, True)
    y_one = swap(y_one, "gy", 0, True)
    own_two, own_one = pl.pallas_call(
        ahead_kernel,
        out_shape=[shape(Z_BLOCKS * 8, 128)] * 2,
        in_specs=[VMEM],
        out_specs=[VMEM] * 2,
        compiler_params=PARAMS,
        name="pack_own",
    )(own)
    own_two = swap(own_two, "gz", 1, False)
    own_one = swap(own_one, "gz", 0, False)
    z_two, z_one = pl.pallas_call(
        second_kernel,
        out_shape=[shape(Z_ROWS, 128)] * 2,
        in_specs=[VMEM] * 3,
        out_specs=[VMEM] * 2,
        compiler_params=PARAMS,
        cost_estimate=pl.CostEstimate(flops=10**9, bytes_accessed=2**20, transcendentals=0),
        name="pack_z",
    )(own, y_two, y_one)
    z_two = swap(z_two, "gz", 1, False)
    z_one = swap(z_one, "gz", 0, False)
    part, packed = pl.pallas_call(
        fill_kernel,
        out_shape=[shape(CHANNELS * ROWS, 128), shape(128, 128)],
        in_specs=[VMEM] * 5,
        out_specs=[VMEM] * 2,
        compiler_params=PARAMS,
        cost_estimate=pl.CostEstimate(flops=10**6, bytes_accessed=2**22, transcendentals=0),
        name="fill",
    )(own, y_two, y_one, own_two, own_one)
    full, packed, columns, message = pl.pallas_call(
        third_kernel,
        out_shape=[
            shape(CHANNELS * ROWS, 128),
            shape(128, 128),
            shape(PAD + 128 + PAD, 128),
            shape(X_ROWS, 128),
        ],
        in_specs=[VMEM] * 4,
        out_specs=[VMEM] * 4,
        input_output_aliases={0: 0, 1: 1},
        compiler_params=PARAMS,
        name="pack_x",
    )(part, packed, z_two, z_one)
    x_one = swap(message, "gx", 0, True)
    x_two = x_one if lax.axis_size("gx") == 2 else swap(message, "gx", 1, True)
    block = pl.pallas_call(
        block_kernel,
        out_shape=shape(27, UNITS * 8, 128),
        in_specs=[VMEM],
        out_specs=VMEM,
        scratch_shapes=[pltpu.VMEM((3, ROWS, 128), F32)],
        compiler_params=PARAMS,
        cost_estimate=pl.CostEstimate(
            flops=27 * 20 * UNITS * 1024, bytes_accessed=2**22, transcendentals=0
        ),
        name="block",
    )(full)
    return pl.pallas_call(
        last_kernel,
        out_shape=shape(27, NZ, NY, NX),
        in_specs=[VMEM] * 5,
        out_specs=HBM,
        scratch_shapes=[
            pltpu.VMEM((PAD + X_ROWS + PAD, 128), F32),
            pltpu.VMEM((PAD + X_ROWS + PAD, 128), F32),
            pltpu.VMEM((PAD + 28 * 8 + PAD, 128), F32),
            pltpu.VMEM((3, UNITS * 8, 128), F32),
            pltpu.VMEM((128, 128), F32),
            pltpu.VMEM((27, NZ, NY, NX), F32),
            pltpu.SemaphoreType.DMA((NZ,)),
        ],
        compiler_params=PARAMS,
        name="finish",
    )(full, block, columns, x_one, x_two)


def solution(mesh):
    return jax.shard_map(
        shards,
        mesh=mesh,
        in_specs=(P(None, "gz", "gy", "gx"), P("gz", "gy", "gx"), P(None, "gz"), P("gy")),
        out_specs=P(None, "gz", "gy", "gx"),
        check_vma=False,
    )
```

```python
import functools

import jax
import jax.numpy as jnp
import numpy as np
from jax import lax
from jax.experimental import pallas as pl
from jax.experimental.pallas import tpu as pltpu
from jax.sharding import PartitionSpec as P

SPONGE = 32
TAU = 0.52
SMAG = 18.0 * 1.4142135623730951 * 0.17 * 0.17

VEL = [(cx, cy, cz) for cz in (-1, 0, 1) for cy in (-1, 0, 1) for cx in (-1, 0, 1)]
WEIGHT = [
    float(np.array([8.0 / 27.0, 2.0 / 27.0, 1.0 / 54.0, 1.0 / 216.0])[cx * cx + cy * cy + cz * cz])
    for cx, cy, cz in VEL
]
WALL, AIM, CHANNELS = 27, 28, 29
NZ, NY, NX = 4, 8, 128
PITCH = NY + 4
FLAT = (NZ + 4) * PITCH
PAD = 8
ROWS = PAD + FLAT + PAD
UNITS = (NZ + 2) * PITCH // 8

PARAMS = pltpu.CompilerParams(vmem_limit_bytes=12 * 2**20)
VMEM = pl.BlockSpec(memory_space=pltpu.VMEM)
HBM = pl.BlockSpec(memory_space=pltpu.HBM)
F32 = jnp.float32

MIXED = 24
Y_ROWS = (MIXED + 1 + 9) * NZ
Z_BLOCKS = CHANNELS + 10
Z_FAR = 2 * Z_BLOCKS
Z_ROWS = -(-(Z_FAR + 2 * 12) // 8) * 8

X_ROWS = 2 * (WALL + 1)


def relaxed(f, sponge, aim):
    quad = {}
    for cz in (-1, 0, 1):
        line = {}
        for cy in (-1, 0, 1):
            base = 9 * (cz + 1) + 3 * (cy + 1)
            both = f[base + 2] + f[base]
            line[cy] = (both + f[base + 1], f[base + 2] - f[base], both)
        s = line[1][0] + line[-1][0]
        sx = line[1][1] + line[-1][1]
        quad[cz] = dict(
            n=s + line[0][0],
            y=line[1][0] - line[-1][0],
            yy=s,
            x=sx + line[0][1],
            xy=line[1][1] - line[-1][1],
            xx=line[1][2] + line[-1][2] + line[0][2],
        )
    up, mid, down = quad[1], quad[0], quad[-1]
    zz = up["n"] + down["n"]
    rho = zz + mid["n"]
    jz = up["n"] - down["n"]
    jy = up["y"] + down["y"] + mid["y"]
    jx = up["x"] + down["x"] + mid["x"]
    inverse = 1.0 / rho
    ux, uy, uz = jx * inverse, jy * inverse, jz * inverse
    third = rho * (1.0 / 3.0)
    pxx = (up["xx"] + down["xx"] + mid["xx"]) - (third + jx * ux)
    pyy = (up["yy"] + down["yy"] + mid["yy"]) - (third + jy * uy)
    pzz = zz - (third + jz * uz)
    pxy = (up["xy"] + down["xy"] + mid["xy"]) - jx * uy
    pxz = (up["x"] - down["x"]) - jx * uz
    pyz = (up["y"] - down["y"]) - jy * uz
    strain = pxx * pxx + pyy * pyy + pzz * pzz + 2.0 * (pxy * pxy + pxz * pxz + pyz * pyz)
    size = jnp.sqrt(2.0 * strain)
    tau = 0.5 * (TAU + jnp.sqrt(TAU * TAU + SMAG * size * inverse))
    omega = 1.0 / tau
    keep = 1.0 - omega
    if sponge is not None:
        keep = jnp.where(sponge, 0.0, keep)
        omega = jnp.where(sponge, 1.0, omega)
        ux = jnp.where(sponge, aim, ux)
        uy = jnp.where(sponge, 0.0, uy)
        uz = jnp.where(sponge, 0.0, uz)
    square = 1.0 - 1.5 * (ux * ux + uy * uy + uz * uz)
    vx, vy, vz = 3.0 * ux, 3.0 * uy, 3.0 * uz
    share = rho * omega
    weighted = {w: share * w for w in sorted(set(WEIGHT))}
    post = [None] * 27
    for q in range(14):
        cx, cy, cz = VEL[q]
        along = None
        for c, v in ((cx, vx), (cy, vy), (cz, vz)):
            if c:
                along = (v if c > 0 else -v) if along is None else (along + v if c > 0 else along - v)
        scale = weighted[WEIGHT[q]]
        if along is None:
            post[q] = keep * f[q] + scale * square
            continue
        even = square + 0.5 * along * along
        post[q] = keep * f[q] + scale * (even + along)
        post[26 - q] = keep * f[26 - q] + scale * (even - along)
    return post


def lane_ids():
    return lax.broadcasted_iota(jnp.int32, (8, 128), 1)


def row_ids():
    return lax.broadcasted_iota(jnp.int32, (8, 128), 0)


def by_parity(axis, one, two, body):
    even = lax.rem(lax.axis_index(axis), 2) == 0
    pl.when(even)(lambda: body(one, two))
    pl.when(jnp.logical_not(even))(lambda: body(two, one))


def z_blocks(near, far, part):
    blocks = [(c, near) for c in range(CHANNELS)]
    return blocks + [(9 * part + k, far) for k in range(9)] + [(WALL, far)]


def first_kernel(pops_at, solid_at, table_at, index_at, own, two, one, *scratch):
    pops, solid, table, index, sems = scratch
    small = ((table_at, table), (index_at, index), (solid_at, solid))
    parts = [(pl.ds(q, 9), z) for z in range(NZ) for q in (0, 9, 18)]
    planes = [(pops_at.at[part], pops.at[part]) for part in parts]
    copies = [
        pltpu.make_async_copy(source, target, sems.at[i])
        for i, (source, target) in enumerate((*small, *planes))
    ]
    for copy in copies:
        copy.start()
    for copy in copies[:3]:
        copy.wait()
    lanes, rows = lane_ids(), row_ids()
    sponge = (lax.axis_index("gx") * NX + lanes) < SPONGE
    for z in range(NZ):
        aim = jnp.zeros((8, 128), F32)
        for y in range(NY):
            aim = jnp.where(rows == y, table[z, index[y]], aim)
        for copy in copies[3 * z + 3 : 3 * z + 6]:
            copy.wait()
        post = relaxed([pops[q, z] for q in range(27)], sponge, aim)
        for q in range(27):
            own[pl.ds((q * NZ + z) * 8, 8), :] = post[q]
        own[pl.ds((WALL * NZ + z) * 8, 8), :] = solid[z].astype(F32)
        own[pl.ds((AIM * NZ + z) * 8, 8), :] = aim

    def pack(yup, ydown):
        inside = lax.rem(lanes, 4)
        for out, edge, second, part in ((yup, 7, 6, 6), (ydown, 0, 1, 0)):
            back = 15 - part
            for first, count, place in ((0, back, 0), (back + 3, 24 - back, back)):
                out[pl.ds(place * NZ, count * NZ), :] = own[
                    pl.ds(first * NZ * 8 + edge, count * NZ, stride=8), :
                ]
            for z in range(NZ):
                west, east, aim, flag = (
                    own[pl.ds((c * NZ + z) * 8, 8), :] for c in (back, back + 2, AIM, WALL)
                )
                mixed = jnp.where(inside < 2, jnp.where(inside == 0, west, aim), flag)
                mixed = jnp.where(inside == 3, east, mixed)
                out[pl.ds(MIXED * NZ + z, 1), :] = mixed[edge : edge + 1]
            for a in range(3):
                out[pl.ds((MIXED + 1 + 3 * a) * NZ, 3 * NZ), :] = own[
                    pl.ds((9 * a + part) * NZ * 8 + second, 3 * NZ, stride=8), :
                ]

    by_parity("gy", one, two, pack)


def ahead_kernel(own, two, one):
    def pack(zup, zdown):
        for out, first, second, part in ((zup, NZ - 1, NZ - 2, 2), (zdown, 0, 1, 0)):
            for k, (c, z) in enumerate(z_blocks(first, second, part)):
                out[pl.ds(8 * k, 8), :] = own[pl.ds((c * NZ + z) * 8, 8), :]

    by_parity("gz", one, two, pack)


def y_runs(part):
    back = 15 - part
    return (0, back, 0), (back, 3, None), (back + 3, 24 - back, back)


def spread_mixed(below, above, flags, aims):
    flags[pl.ds(0, NZ), :] = below[pl.ds(MIXED * NZ, NZ), :]
    flags[pl.ds(NZ, NZ), :] = above[pl.ds(MIXED * NZ, NZ), :]
    mixed = flags[...]
    inside = lax.rem(lane_ids(), 4)
    moved = {k: pltpu.roll(mixed, k % 128, 1) if k else mixed for k in (-2, -1, 0, 1, 2)}

    def from_lane(source):
        value = moved[0]
        for lane in range(4):
            if lane != source:
                value = jnp.where(inside == lane, moved[lane - source], value)
        return value

    aims[...] = from_lane(1)
    flags[...] = from_lane(2)


def second_kernel(y_two, y_one, z_two, z_one, flags, aims):
    def pack(above, below):
        spread_mixed(below, above, flags, aims)
        by_parity(
            "gz",
            z_one,
            z_two,
            lambda zup, zdown: pack_planes(below, above, flags, aims, zup, zdown),
        )

    by_parity("gy", y_one, y_two, pack)


def pack_planes(below, above, flags, aims, zup, zdown):
    for out, first, second, part in ((zup, NZ - 1, NZ - 2, 2), (zdown, 0, 1, 0)):
        for side, (halo, inward) in enumerate(((below, 6), (above, 0))):
            near = side * Z_BLOCKS
            for channel, count, place in y_runs(inward):
                if place is None:
                    row = halo[pl.ds(MIXED * NZ + first, 1), :]
                    out[pl.ds(near + channel, 3), :] = jnp.broadcast_to(row, (3, 128))
                else:
                    out[pl.ds(near + channel, count), :] = halo[
                        pl.ds(place * NZ + first, count, stride=NZ), :
                    ]
            out[pl.ds(near + WALL, 1), :] = flags[pl.ds(side * NZ + first, 1), :]
            out[pl.ds(near + AIM, 1), :] = aims[pl.ds(side * NZ + first, 1), :]
            place = 15 if part else 0
            out[pl.ds(near + CHANNELS, 9), :] = halo[pl.ds(place * NZ + second, 9, stride=NZ), :]
            out[pl.ds(near + Z_BLOCKS - 1, 1), :] = flags[pl.ds(side * NZ + second, 1), :]
            far = Z_FAR + 12 * side
            start = (MIXED + 1) * NZ
            out[pl.ds(far, 9), :] = halo[pl.ds(start + first, 9, stride=NZ), :]
            out[pl.ds(far + 9, 3), :] = halo[pl.ds(start + 3 * part * NZ + second, 3, stride=NZ), :]


def plane_at(z):
    return PAD + (z + 2) * PITCH


def add_rows(full, flags, aims, above, below):
    spread_mixed(below, above, flags, aims)

    def put(channel, row, source):
        full[pl.ds(channel * ROWS + plane_at(0) + row, NZ, stride=PITCH), :] = source

    sides = ((below, 1, 0, 6), (above, PITCH - 2, PITCH - 1, 0))
    for side, (halo, near, far, inward) in enumerate(sides):
        for first, count, place in y_runs(inward):
            for k in range(count):
                row = MIXED if place is None else place + k
                put(first + k, near, halo[pl.ds(row * NZ, NZ), :])
        flag = flags[pl.ds(side * NZ, NZ), :]
        put(WALL, near, flag)
        put(WALL, far, flag)
        put(AIM, near, aims[pl.ds(side * NZ, NZ), :])
        for k in range(9):
            q = 9 * (k // 3) + inward + k % 3
            put(q, far, halo[pl.ds((MIXED + 1 + k) * NZ, NZ), :])


def add_own_planes(full, ceiling, floor):
    for halo, near, far, part in ((floor, -1, -2, 2), (ceiling, NZ, NZ + 1, 0)):
        for k, (c, z) in enumerate(z_blocks(near, far, part)):
            full[pl.ds(c * ROWS + plane_at(z) + 2, 8), :] = halo[pl.ds(8 * k, 8), :]


def add_planes(full, ceiling, floor):
    def put(count, channel, z, row, source):
        start = channel * ROWS + plane_at(z) + row
        full[pl.ds(start, count, stride=ROWS), :] = source

    for halo, near, far, part in ((floor, -1, -2, 2), (ceiling, NZ, NZ + 1, 0)):
        for side, (row, beyond, group) in enumerate(((1, 0, 2), (PITCH - 2, PITCH - 1, 0))):
            start = side * Z_BLOCKS
            put(CHANNELS, 0, near, row, halo[pl.ds(start, CHANNELS), :])
            put(9, 9 * part, far, row, halo[pl.ds(start + CHANNELS, 9), :])
            first, second = (halo[pl.ds(start + k, 1), :] for k in (WALL, Z_BLOCKS - 1))
            put(1, WALL, far, row, second)
            start = Z_FAR + 12 * side
            for k in range(3):
                put(3, 9 * k + 3 * group, near, beyond, halo[pl.ds(start + 3 * k, 3), :])
            put(3, 9 * part + 3 * group, far, beyond, halo[pl.ds(start + 9, 3), :])
            put(1, WALL, near, beyond, first)
            put(1, WALL, far, beyond, second)


def pack_columns(full, pack, tiles):
    slot = lane_ids() // 4
    for t in tiles:
        packed = jnp.zeros((8, 128), F32)
        for c in range(CHANNELS):
            moved = pltpu.roll(full[pl.ds(c * ROWS + PAD + 8 * t, 8), :], (4 * c + 2) % 128, 1)
            packed = jnp.where(slot == c, moved, packed)
        pack[pl.ds(8 * t, 8), :] = packed


OWN_TILES = range(2 * PITCH // 8, (NZ + 2) * PITCH // 8)


def fill_kernel(own, y_two, y_one, two, one, full, pack, flags, aims):
    for c in range(CHANNELS):
        for z in range(NZ):
            full[pl.ds(c * ROWS + plane_at(z) + 2, 8), :] = own[pl.ds((c * NZ + z) * 8, 8), :]
    by_parity("gy", y_one, y_two, functools.partial(add_rows, full, flags, aims))
    by_parity("gz", one, two, functools.partial(add_own_planes, full))
    pack_columns(full, pack, OWN_TILES)
    pack[pl.ds(FLAT, 128 - FLAT), :] = jnp.zeros((128 - FLAT, 128), F32)


def third_kernel(part, packed, z_two, z_one, full, pack, columns, message):
    last = lax.axis_size("gz") - 1
    here = lax.axis_index("gz")
    by_parity("gz", z_one, z_two, functools.partial(add_planes, full))

    @pl.when(here == 0)
    def _():
        full[pl.ds(WALL * ROWS + plane_at(-1), PITCH), :] = jnp.ones((PITCH, 128), F32)

    @pl.when(here == last)
    def _():
        for q in range(9):
            full[pl.ds(q * ROWS + plane_at(NZ), PITCH), :] = full[pl.ds((q + 18) * ROWS + plane_at(NZ - 1), PITCH), :]

    pack_columns(full, pack, [t for t in range(FLAT // 8) if t not in OWN_TILES])
    columns[pl.ds(PAD, 128), :] = pack[...].T

    def row(c, i, count):
        return columns[pl.ds(PAD + 4 * c + i, count), :]

    def returned(q, near, far):
        cx, cy, cz = VEL[q]
        step = (-PITCH * cz - cy) % 128
        value = row(26 - q, near, 8)
        value = pltpu.roll(value, step, 1) if step else value
        return jnp.where(row(WALL, far, 8) != 0.0, value, row(q, far, 8))[:1]

    for c in range(WALL + 1):
        cx = VEL[c][0] if c < 27 else 0
        if cx == 0:
            message[pl.ds(2 * c, 2), :] = row(c, 1, 2)
        elif cx > 0:
            message[pl.ds(2 * c, 1), :] = returned(c, 1, 0)
            message[pl.ds(2 * c + 1, 1), :] = row(c, 1, 1)
        else:
            message[pl.ds(2 * c, 1), :] = row(c, 2, 1)
            message[pl.ds(2 * c + 1, 1), :] = returned(c, 2, 3)


def block_kernel(full, post, walls):
    top = lax.axis_index("gz") == lax.axis_size("gz") - 1
    sponge = (lax.axis_index("gx") * NX + lane_ids()) < SPONGE
    for t in range(ROWS // 8):
        rows = pl.ds(8 * t, 8)
        flags = full[pl.ds(WALL * ROWS + 8 * t, 8), :]
        for cx in (-1, 0, 1):
            walls[cx + 1, rows, :] = pltpu.roll(flags, cx % 128, 1) if cx else flags
    for u in range(UNITS):
        cell = PAD + PITCH + 8 * u
        f = []
        solid = walls[1, pl.ds(cell, 8), :] != 0.0
        for q in range(27):
            cx, cy, cz = VEL[q]
            start = cell - PITCH * cz - cy
            value = full[pl.ds(q * ROWS + start, 8), :]
            if cx:
                value = pltpu.roll(value, cx % 128, 1)
            if q != 13:
                blocked = walls[cx + 1, pl.ds(start, 8), :] != 0.0
                value = jnp.where(blocked, full[pl.ds((26 - q) * ROWS + cell, 8), :], value)
            f.append(jnp.where(solid, WEIGHT[q], value))
        done = relaxed(f, sponge, full[pl.ds(AIM * ROWS + cell, 8), :])
        for q in range(27):
            post[q, pl.ds(8 * u, 8), :] = done[q]

    @pl.when(top)
    def _():
        for q in range(9):
            post[q, pl.ds((NZ + 1) * PITCH, PITCH), :] = post[q + 18, pl.ds(NZ * PITCH, PITCH), :]


def last_kernel(full, block, columns, x_one, x_two, out, west, east, column, walls, back, done, sems):
    here_x, size_x = lax.axis_index("gx"), lax.axis_size("gx")
    top = lax.axis_index("gz") == lax.axis_size("gz") - 1
    lanes, rows = lane_ids(), row_ids()

    def spread(right, left):
        west[pl.ds(PAD, X_ROWS), :] = left[...]
        east[pl.ds(PAD, X_ROWS), :] = right[...]

    by_parity("gx", x_one, x_two, spread)

    strip = []
    for c in range(CHANNELS):
        cx = VEL[c][0] if c < 27 else 0
        value = jnp.where(
            rows < 4, columns[pl.ds(PAD + 4 * c, 8), :], columns[pl.ds(PAD + 4 * c - 4, 8), :]
        )
        if c <= WALL and cx >= 0:
            value = jnp.where(rows < 2, west[pl.ds(PAD + 2 * c - (cx == 0), 8), :], value)
        if c <= WALL and cx <= 0:
            value = jnp.where(rows >= 6, east[pl.ds(PAD + 2 * c - 6 + (cx == 0), 8), :], value)
        strip.append(value)
    strip[WALL] = jnp.where((rows == 0) | (rows == 7), 0.0, strip[WALL])

    def shifted(value, q):
        cx, cy, cz = VEL[q]
        if cx:
            value = pltpu.roll(value, cx % 8, 0)
        step = (PITCH * cz + cy) % 128
        return pltpu.roll(value, step, 1) if step else value

    moved = []
    for q in range(27):
        value = shifted(strip[q], q)
        if q != 13:
            value = jnp.where(shifted(strip[WALL], q) != 0.0, strip[26 - q], value)
        moved.append(jnp.where(strip[WALL] != 0.0, WEIGHT[q], value))
    place = here_x * NX + jnp.where(rows < 4, rows - 2, rows + (NX - 6))
    place = lax.rem(place + size_x * NX, size_x * NX)
    sides = relaxed(moved, place < SPONGE, strip[AIM])
    lid = top & (lanes >= (NZ + 2) * PITCH) & (lanes < (NZ + 3) * PITCH)
    for q in range(9):
        sides[q] = jnp.where(lid, pltpu.roll(sides[q + 18], PITCH, 1), sides[q])
    for q, side in enumerate(sides + [strip[WALL]]):
        column[pl.ds(PAD + 8 * q, 8), :] = side

    def picked(wanted):
        value = None
        for sublane, (q, row) in enumerate(wanted):
            moved = column[pl.ds(PAD + 8 * q + row - sublane, 8), :]
            value = moved if value is None else jnp.where(rows == sublane, moved, value)
        return value

    packed = []
    for k in range(9):
        a, b = 3 * k + 2, 3 * k
        packed.append(
            picked([(a, 5), (a, 2), (a, 1), (a, 2), (b, 5), (b, 2), (b, 5), (b, 6)])
        )
    rest = [(3 * k + 1, row) for k in range(9) for row in (5, 2)] + [(27, 1), (27, 6)]
    packed += [picked(rest[i : i + 8]) for i in range(0, len(rest), 8)]
    packed += [jnp.zeros((8, 128), F32)] * (16 - len(packed))
    back[...] = jnp.concatenate(packed, axis=0).T

    def column_at(place, lane, start):
        return pltpu.roll(back[pl.ds(start, 8), :], (lane - place) % 128, 1)

    rim = (lanes == 0) | (lanes == 127)

    def rimmed(q, start):
        k = q // 3
        ends = column_at((8 * k + 5, 73 + 2 * k, 8 * k + 1)[q % 3], 0, PITCH + start)
        return jnp.where(rim, ends, block[q, pl.ds(start, 8), :])

    for u in range(UNITS):
        flags = full[pl.ds(WALL * ROWS + PAD + PITCH + 8 * u, 8), :]
        walls[1, pl.ds(8 * u, 8), :] = flags
        for cx, edge, place in ((1, 0, 90), (-1, 127, 91)):
            walls[cx + 1, pl.ds(8 * u, 8), :] = jnp.where(
                lanes == edge, column_at(place, edge, PITCH + 8 * u), pltpu.roll(flags, cx % 128, 1)
            )

    copies = []
    for z in range(NZ):
        cell = (z + 1) * PITCH + 2
        solid = walls[1, pl.ds(cell, 8), :] != 0.0
        for q in range(27):
            cx, cy, cz = VEL[q]
            start = cell - PITCH * cz - cy
            if cx > 0:
                side = column_at(8 * (q // 3) + 2, 0, PITCH + start)
                value = jnp.where(lanes < 2, side, pltpu.roll(block[q, pl.ds(start, 8), :], 1, 1))
            elif cx < 0:
                side = column_at(8 * (q // 3) + 6, 126, PITCH + start)
                value = jnp.where(lanes > 125, side, pltpu.roll(block[q, pl.ds(start, 8), :], 127, 1))
            else:
                value = rimmed(q, start)
            if q != 13:
                blocked = walls[cx + 1, pl.ds(start, 8), :] != 0.0
                value = jnp.where(blocked, rimmed(26 - q, cell), value)
            done[q, z] = jnp.where(solid, WEIGHT[q], value)
        copies.append(pltpu.make_async_copy(done.at[:, z], out.at[:, z], sems.at[z]))
        copies[-1].start()
    for copy in copies:
        copy.wait()


def swap(value, axis, turn, wrap):
    size = lax.axis_size(axis)
    pairs = [(i, (i + 1) % size) for i in range(turn, size if wrap else size - 1, 2)]
    return lax.ppermute(value, axis, pairs + [(j, i) for i, j in pairs])


def shape(*dims):
    return jax.ShapeDtypeStruct(dims, F32)


def shards(pops, solid, profile_table, profile_index):
    own, y_two, y_one = pl.pallas_call(
        first_kernel,
        out_shape=[shape(CHANNELS * NZ * 8, 128), shape(Y_ROWS, 128), shape(Y_ROWS, 128)],
        in_specs=[HBM] * 4,
        out_specs=[VMEM] * 3,
        scratch_shapes=[
            pltpu.VMEM(pops.shape, F32),
            pltpu.VMEM(solid.shape, jnp.int32),
            pltpu.SMEM(profile_table.shape[::-1], F32),
            pltpu.SMEM(profile_index.shape, jnp.int32),
            pltpu.SemaphoreType.DMA((3 + 3 * NZ,)),
        ],
        compiler_params=PARAMS,
        name="collide",
    )(*(pltpu.with_memory_space_constraint(a, pltpu.HBM) for a in (pops, solid, profile_table.T, profile_index)))
    y_two = swap(y_two, "gy", 1, True)
    y_one = swap(y_one, "gy", 0, True)
    own_two, own_one = pl.pallas_call(
        ahead_kernel,
        out_shape=[shape(Z_BLOCKS * 8, 128)] * 2,
        in_specs=[VMEM],
        out_specs=[VMEM] * 2,
        compiler_params=PARAMS,
        name="pack_own",
    )(own)
    own_two = swap(own_two, "gz", 1, False)
    own_one = swap(own_one, "gz", 0, False)
    z_two, z_one = pl.pallas_call(
        second_kernel,
        out_shape=[shape(Z_ROWS, 128)] * 2,
        in_specs=[VMEM] * 2,
        out_specs=[VMEM] * 2,
        scratch_shapes=[pltpu.VMEM((2 * NZ, 128), F32)] * 2,
        compiler_params=PARAMS,
        cost_estimate=pl.CostEstimate(flops=10**9, bytes_accessed=2**20, transcendentals=0),
        name="pack_z",
    )(y_two, y_one)
    z_two = swap(z_two, "gz", 1, False)
    z_one = swap(z_one, "gz", 0, False)
    part, packed = pl.pallas_call(
        fill_kernel,
        out_shape=[shape(CHANNELS * ROWS, 128), shape(128, 128)],
        in_specs=[VMEM] * 5,
        out_specs=[VMEM] * 2,
        scratch_shapes=[pltpu.VMEM((2 * NZ, 128), F32)] * 2,
        compiler_params=PARAMS,
        cost_estimate=pl.CostEstimate(flops=10**6, bytes_accessed=2**22, transcendentals=0),
        name="fill",
    )(own, y_two, y_one, own_two, own_one)
    full, packed, columns, message = pl.pallas_call(
        third_kernel,
        out_shape=[
            shape(CHANNELS * ROWS, 128),
            shape(128, 128),
            shape(PAD + 128 + PAD, 128),
            shape(X_ROWS, 128),
        ],
        in_specs=[VMEM] * 4,
        out_specs=[VMEM] * 4,
        input_output_aliases={0: 0, 1: 1},
        compiler_params=PARAMS,
        name="pack_x",
    )(part, packed, z_two, z_one)
    x_one = swap(message, "gx", 0, True)
    x_two = x_one if lax.axis_size("gx") == 2 else swap(message, "gx", 1, True)
    block = pl.pallas_call(
        block_kernel,
        out_shape=shape(27, UNITS * 8, 128),
        in_specs=[VMEM],
        out_specs=VMEM,
        scratch_shapes=[pltpu.VMEM((3, ROWS, 128), F32)],
        compiler_params=PARAMS,
        cost_estimate=pl.CostEstimate(
            flops=27 * 20 * UNITS * 1024, bytes_accessed=2**22, transcendentals=0
        ),
        name="block",
    )(full)
    return pl.pallas_call(
        last_kernel,
        out_shape=shape(27, NZ, NY, NX),
        in_specs=[VMEM] * 5,
        out_specs=HBM,
        scratch_shapes=[
            pltpu.VMEM((PAD + X_ROWS + PAD, 128), F32),
            pltpu.VMEM((PAD + X_ROWS + PAD, 128), F32),
            pltpu.VMEM((PAD + 28 * 8 + PAD, 128), F32),
            pltpu.VMEM((3, UNITS * 8, 128), F32),
            pltpu.VMEM((128, 128), F32),
            pltpu.VMEM((27, NZ, NY, NX), F32),
            pltpu.SemaphoreType.DMA((NZ,)),
        ],
        compiler_params=PARAMS,
        name="finish",
    )(full, block, columns, x_one, x_two)


def solution(mesh):
    return jax.shard_map(
        shards,
        mesh=mesh,
        in_specs=(P(None, "gz", "gy", "gx"), P("gz", "gy", "gx"), P(None, "gz"), P("gy")),
        out_specs=P(None, "gz", "gy", "gx"),
        check_vma=False,
    )
```

```python
import functools

import jax
import jax.numpy as jnp
import numpy as np
from jax import lax
from jax.experimental import pallas as pl
from jax.experimental.pallas import tpu as pltpu
from jax.sharding import PartitionSpec as P

SPONGE = 32
TAU = 0.52
SMAG = 18.0 * 1.4142135623730951 * 0.17 * 0.17

VEL = [(cx, cy, cz) for cz in (-1, 0, 1) for cy in (-1, 0, 1) for cx in (-1, 0, 1)]
WEIGHT = [
    float(np.array([8.0 / 27.0, 2.0 / 27.0, 1.0 / 54.0, 1.0 / 216.0])[cx * cx + cy * cy + cz * cz])
    for cx, cy, cz in VEL
]
WALL, AIM, CHANNELS = 27, 28, 29
NZ, NY, NX = 4, 8, 128
PITCH = NY + 4
FLAT = (NZ + 4) * PITCH
PAD = 8
ROWS = PAD + FLAT + PAD
UNITS = (NZ + 2) * PITCH // 8

PARAMS = pltpu.CompilerParams(vmem_limit_bytes=12 * 2**20)
VMEM = pl.BlockSpec(memory_space=pltpu.VMEM)
HBM = pl.BlockSpec(memory_space=pltpu.HBM)
F32 = jnp.float32

MIXED = 24
Y_ROWS = (MIXED + 1 + 9) * NZ
Z_BLOCKS = CHANNELS + 10
Z_FAR = 2 * Z_BLOCKS
Z_ROWS = -(-(Z_FAR + 2 * 12) // 8) * 8

X_ROWS = 2 * (WALL + 1)


def relaxed(f, sponge, aim):
    quad = {}
    for cz in (-1, 0, 1):
        line = {}
        for cy in (-1, 0, 1):
            base = 9 * (cz + 1) + 3 * (cy + 1)
            both = f[base + 2] + f[base]
            line[cy] = (both + f[base + 1], f[base + 2] - f[base], both)
        s = line[1][0] + line[-1][0]
        sx = line[1][1] + line[-1][1]
        quad[cz] = dict(
            n=s + line[0][0],
            y=line[1][0] - line[-1][0],
            yy=s,
            x=sx + line[0][1],
            xy=line[1][1] - line[-1][1],
            xx=line[1][2] + line[-1][2] + line[0][2],
        )
    up, mid, down = quad[1], quad[0], quad[-1]
    zz = up["n"] + down["n"]
    rho = zz + mid["n"]
    jz = up["n"] - down["n"]
    jy = up["y"] + down["y"] + mid["y"]
    jx = up["x"] + down["x"] + mid["x"]
    inverse = 1.0 / rho
    ux, uy, uz = jx * inverse, jy * inverse, jz * inverse
    third = rho * (1.0 / 3.0)
    pxx = (up["xx"] + down["xx"] + mid["xx"]) - (third + jx * ux)
    pyy = (up["yy"] + down["yy"] + mid["yy"]) - (third + jy * uy)
    pzz = zz - (third + jz * uz)
    pxy = (up["xy"] + down["xy"] + mid["xy"]) - jx * uy
    pxz = (up["x"] - down["x"]) - jx * uz
    pyz = (up["y"] - down["y"]) - jy * uz
    strain = pxx * pxx + pyy * pyy + pzz * pzz + 2.0 * (pxy * pxy + pxz * pxz + pyz * pyz)
    size = jnp.sqrt(2.0 * strain)
    tau = 0.5 * (TAU + jnp.sqrt(TAU * TAU + SMAG * size * inverse))
    omega = 1.0 / tau
    keep = 1.0 - omega
    if sponge is not None:
        keep = jnp.where(sponge, 0.0, keep)
        omega = jnp.where(sponge, 1.0, omega)
        ux = jnp.where(sponge, aim, ux)
        uy = jnp.where(sponge, 0.0, uy)
        uz = jnp.where(sponge, 0.0, uz)
    square = 1.0 - 1.5 * (ux * ux + uy * uy + uz * uz)
    vx, vy, vz = 3.0 * ux, 3.0 * uy, 3.0 * uz
    share = rho * omega
    weighted = {w: share * w for w in sorted(set(WEIGHT))}
    post = [None] * 27
    for q in range(14):
        cx, cy, cz = VEL[q]
        along = None
        for c, v in ((cx, vx), (cy, vy), (cz, vz)):
            if c:
                along = (v if c > 0 else -v) if along is None else (along + v if c > 0 else along - v)
        scale = weighted[WEIGHT[q]]
        if along is None:
            post[q] = keep * f[q] + scale * square
            continue
        even = square + 0.5 * along * along
        post[q] = keep * f[q] + scale * (even + along)
        post[26 - q] = keep * f[26 - q] + scale * (even - along)
    return post


def lane_ids():
    return lax.broadcasted_iota(jnp.int32, (8, 128), 1)


def row_ids():
    return lax.broadcasted_iota(jnp.int32, (8, 128), 0)


def by_parity(axis, one, two, body):
    even = lax.rem(lax.axis_index(axis), 2) == 0
    pl.when(even)(lambda: body(one, two))
    pl.when(jnp.logical_not(even))(lambda: body(two, one))


def z_blocks(near, far, part):
    blocks = [(c, near) for c in range(CHANNELS)]
    return blocks + [(9 * part + k, far) for k in range(9)] + [(WALL, far)]


def first_kernel(pops_at, solid_at, table_at, index_at, own, two, one, *scratch):
    pops, solid, table, index, sems = scratch
    parts = [(pl.ds(q, 9), z) for z in range(NZ) for q in (0, 9, 18)]
    planes = [(pops_at.at[part], pops.at[part]) for part in parts]
    small = [(table_at, table), (index_at, index)]
    copies = [
        pltpu.make_async_copy(source, target, sems.at[i])
        for i, (source, target) in enumerate([*small, *planes, (solid_at, solid)])
    ]
    for copy in copies:
        copy.start()
    for copy in copies[:2]:
        copy.wait()
    lanes, rows = lane_ids(), row_ids()
    sponge = (lax.axis_index("gx") * NX + lanes) < SPONGE
    profiles = [index[y] for y in range(NY)]
    aims = []
    for z in range(NZ):
        aim = jnp.zeros((8, 128), F32)
        for y, profile in enumerate(profiles):
            aim = jnp.where(rows == y, table[z, profile], aim)
        aims.append(aim)
    for z, aim in enumerate(aims):
        for copy in copies[3 * z + 2 : 3 * z + 5]:
            copy.wait()
        post = relaxed([pops[q, z] for q in range(27)], sponge, aim)
        for q in range(27):
            own[pl.ds((q * NZ + z) * 8, 8), :] = post[q]
        own[pl.ds((AIM * NZ + z) * 8, 8), :] = aim
    copies[-1].wait()
    for z in range(NZ):
        own[pl.ds((WALL * NZ + z) * 8, 8), :] = solid[z].astype(F32)

    def pack(yup, ydown):
        inside = lax.rem(lanes, 4)
        for out, edge, second, part in ((yup, 7, 6, 6), (ydown, 0, 1, 0)):
            back = 15 - part
            for first, count, place in ((0, back, 0), (back + 3, 24 - back, back)):
                out[pl.ds(place * NZ, count * NZ), :] = own[
                    pl.ds(first * NZ * 8 + edge, count * NZ, stride=8), :
                ]
            for z in range(NZ):
                west, east, aim, flag = (
                    own[pl.ds((c * NZ + z) * 8, 8), :] for c in (back, back + 2, AIM, WALL)
                )
                mixed = jnp.where(inside < 2, jnp.where(inside == 0, west, aim), flag)
                mixed = jnp.where(inside == 3, east, mixed)
                out[pl.ds(MIXED * NZ + z, 1), :] = mixed[edge : edge + 1]
            for a in range(3):
                out[pl.ds((MIXED + 1 + 3 * a) * NZ, 3 * NZ), :] = own[
                    pl.ds((9 * a + part) * NZ * 8 + second, 3 * NZ, stride=8), :
                ]

    by_parity("gy", one, two, pack)


def ahead_kernel(own, two, one):
    def pack(zup, zdown):
        for out, first, second, part in ((zup, NZ - 1, NZ - 2, 2), (zdown, 0, 1, 0)):
            for k, (c, z) in enumerate(z_blocks(first, second, part)):
                out[pl.ds(8 * k, 8), :] = own[pl.ds((c * NZ + z) * 8, 8), :]

    by_parity("gz", one, two, pack)


def y_runs(part):
    back = 15 - part
    return (0, back, 0), (back, 3, None), (back + 3, 24 - back, back)


def spread_mixed(below, above, flags, aims):
    flags[pl.ds(0, NZ), :] = below[pl.ds(MIXED * NZ, NZ), :]
    flags[pl.ds(NZ, NZ), :] = above[pl.ds(MIXED * NZ, NZ), :]
    mixed = flags[...]
    inside = lax.rem(lane_ids(), 4)
    moved = {k: pltpu.roll(mixed, k % 128, 1) if k else mixed for k in (-2, -1, 0, 1, 2)}

    def from_lane(source):
        value = moved[0]
        for lane in range(4):
            if lane != source:
                value = jnp.where(inside == lane, moved[lane - source], value)
        return value

    aims[...] = from_lane(1)
    flags[...] = from_lane(2)


def second_kernel(y_two, y_one, z_two, z_one, flags, aims):
    def pack(above, below):
        spread_mixed(below, above, flags, aims)
        by_parity(
            "gz",
            z_one,
            z_two,
            lambda zup, zdown: pack_planes(below, above, flags, aims, zup, zdown),
        )

    by_parity("gy", y_one, y_two, pack)


def pack_planes(below, above, flags, aims, zup, zdown):
    for out, first, second, part in ((zup, NZ - 1, NZ - 2, 2), (zdown, 0, 1, 0)):
        for side, (halo, inward) in enumerate(((below, 6), (above, 0))):
            near = side * Z_BLOCKS
            for channel, count, place in y_runs(inward):
                if place is None:
                    row = halo[pl.ds(MIXED * NZ + first, 1), :]
                    out[pl.ds(near + channel, 3), :] = jnp.broadcast_to(row, (3, 128))
                else:
                    out[pl.ds(near + channel, count), :] = halo[
                        pl.ds(place * NZ + first, count, stride=NZ), :
                    ]
            out[pl.ds(near + WALL, 1), :] = flags[pl.ds(side * NZ + first, 1), :]
            out[pl.ds(near + AIM, 1), :] = aims[pl.ds(side * NZ + first, 1), :]
            place = 15 if part else 0
            out[pl.ds(near + CHANNELS, 9), :] = halo[pl.ds(place * NZ + second, 9, stride=NZ), :]
            out[pl.ds(near + Z_BLOCKS - 1, 1), :] = flags[pl.ds(side * NZ + second, 1), :]
            far = Z_FAR + 12 * side
            start = (MIXED + 1) * NZ
            out[pl.ds(far, 9), :] = halo[pl.ds(start + first, 9, stride=NZ), :]
            out[pl.ds(far + 9, 3), :] = halo[pl.ds(start + 3 * part * NZ + second, 3, stride=NZ), :]


def plane_at(z):
    return PAD + (z + 2) * PITCH


def add_rows(full, flags, aims, above, below):
    spread_mixed(below, above, flags, aims)

    def put(channel, row, source):
        full[pl.ds(channel * ROWS + plane_at(0) + row, NZ, stride=PITCH), :] = source

    sides = ((below, 1, 0, 6), (above, PITCH - 2, PITCH - 1, 0))
    for side, (halo, near, far, inward) in enumerate(sides):
        for first, count, place in y_runs(inward):
            for k in range(count):
                row = MIXED if place is None else place + k
                put(first + k, near, halo[pl.ds(row * NZ, NZ), :])
        flag = flags[pl.ds(side * NZ, NZ), :]
        put(WALL, near, flag)
        put(WALL, far, flag)
        put(AIM, near, aims[pl.ds(side * NZ, NZ), :])
        for k in range(9):
            q = 9 * (k // 3) + inward + k % 3
            put(q, far, halo[pl.ds((MIXED + 1 + k) * NZ, NZ), :])


def add_own_planes(full, ceiling, floor):
    for halo, near, far, part in ((floor, -1, -2, 2), (ceiling, NZ, NZ + 1, 0)):
        for k, (c, z) in enumerate(z_blocks(near, far, part)):
            full[pl.ds(c * ROWS + plane_at(z) + 2, 8), :] = halo[pl.ds(8 * k, 8), :]


def add_planes(full, ceiling, floor):
    def put(count, channel, z, row, source):
        start = channel * ROWS + plane_at(z) + row
        full[pl.ds(start, count, stride=ROWS), :] = source

    for halo, near, far, part in ((floor, -1, -2, 2), (ceiling, NZ, NZ + 1, 0)):
        for side, (row, beyond, group) in enumerate(((1, 0, 2), (PITCH - 2, PITCH - 1, 0))):
            start = side * Z_BLOCKS
            put(CHANNELS, 0, near, row, halo[pl.ds(start, CHANNELS), :])
            put(9, 9 * part, far, row, halo[pl.ds(start + CHANNELS, 9), :])
            first, second = (halo[pl.ds(start + k, 1), :] for k in (WALL, Z_BLOCKS - 1))
            put(1, WALL, far, row, second)
            start = Z_FAR + 12 * side
            for k in range(3):
                put(3, 9 * k + 3 * group, near, beyond, halo[pl.ds(start + 3 * k, 3), :])
            put(3, 9 * part + 3 * group, far, beyond, halo[pl.ds(start + 9, 3), :])
            put(1, WALL, near, beyond, first)
            put(1, WALL, far, beyond, second)


def pack_columns(full, pack, tiles):
    slot = lane_ids() // 4
    for t in tiles:
        packed = jnp.zeros((8, 128), F32)
        for c in range(CHANNELS):
            moved = pltpu.roll(full[pl.ds(c * ROWS + PAD + 8 * t, 8), :], (4 * c + 2) % 128, 1)
            packed = jnp.where(slot == c, moved, packed)
        pack[pl.ds(8 * t, 8), :] = packed


OWN_TILES = range(2 * PITCH // 8, (NZ + 2) * PITCH // 8)


def fill_kernel(own, y_two, y_one, two, one, full, pack, flags, aims):
    for c in range(CHANNELS):
        for z in range(NZ):
            full[pl.ds(c * ROWS + plane_at(z) + 2, 8), :] = own[pl.ds((c * NZ + z) * 8, 8), :]
    by_parity("gy", y_one, y_two, functools.partial(add_rows, full, flags, aims))
    by_parity("gz", one, two, functools.partial(add_own_planes, full))
    pack_columns(full, pack, OWN_TILES)
    pack[pl.ds(FLAT, 128 - FLAT), :] = jnp.zeros((128 - FLAT, 128), F32)


def third_kernel(part, packed, z_two, z_one, full, pack, columns, message):
    last = lax.axis_size("gz") - 1
    here = lax.axis_index("gz")
    by_parity("gz", z_one, z_two, functools.partial(add_planes, full))

    @pl.when(here == 0)
    def _():
        full[pl.ds(WALL * ROWS + plane_at(-1), PITCH), :] = jnp.ones((PITCH, 128), F32)

    @pl.when(here == last)
    def _():
        for q in range(9):
            full[pl.ds(q * ROWS + plane_at(NZ), PITCH), :] = full[pl.ds((q + 18) * ROWS + plane_at(NZ - 1), PITCH), :]

    pack_columns(full, pack, [t for t in range(FLAT // 8) if t not in OWN_TILES])
    columns[pl.ds(PAD, 128), :] = pack[...].T

    def row(c, i, count):
        return columns[pl.ds(PAD + 4 * c + i, count), :]

    def returned(q, near, far):
        cx, cy, cz = VEL[q]
        step = (-PITCH * cz - cy) % 128
        value = row(26 - q, near, 8)
        value = pltpu.roll(value, step, 1) if step else value
        return jnp.where(row(WALL, far, 8) != 0.0, value, row(q, far, 8))[:1]

    for c in range(WALL + 1):
        cx = VEL[c][0] if c < 27 else 0
        if cx == 0:
            message[pl.ds(2 * c, 2), :] = row(c, 1, 2)
        elif cx > 0:
            message[pl.ds(2 * c, 1), :] = returned(c, 1, 0)
            message[pl.ds(2 * c + 1, 1), :] = row(c, 1, 1)
        else:
            message[pl.ds(2 * c, 1), :] = row(c, 2, 1)
            message[pl.ds(2 * c + 1, 1), :] = returned(c, 2, 3)


def block_kernel(full, post, walls):
    top = lax.axis_index("gz") == lax.axis_size("gz") - 1
    sponge = (lax.axis_index("gx") * NX + lane_ids()) < SPONGE
    for t in range(ROWS // 8):
        rows = pl.ds(8 * t, 8)
        flags = full[pl.ds(WALL * ROWS + 8 * t, 8), :]
        for cx in (-1, 0, 1):
            walls[cx + 1, rows, :] = pltpu.roll(flags, cx % 128, 1) if cx else flags
    for u in range(UNITS):
        cell = PAD + PITCH + 8 * u
        f = []
        solid = walls[1, pl.ds(cell, 8), :] != 0.0
        for q in range(27):
            cx, cy, cz = VEL[q]
            start = cell - PITCH * cz - cy
            value = full[pl.ds(q * ROWS + start, 8), :]
            if cx:
                value = pltpu.roll(value, cx % 128, 1)
            if q != 13:
                blocked = walls[cx + 1, pl.ds(start, 8), :] != 0.0
                value = jnp.where(blocked, full[pl.ds((26 - q) * ROWS + cell, 8), :], value)
            f.append(jnp.where(solid, WEIGHT[q], value))
        done = relaxed(f, sponge, full[pl.ds(AIM * ROWS + cell, 8), :])
        for q in range(27):
            post[q, pl.ds(8 * u, 8), :] = done[q]

    @pl.when(top)
    def _():
        for q in range(9):
            post[q, pl.ds((NZ + 1) * PITCH, PITCH), :] = post[q + 18, pl.ds(NZ * PITCH, PITCH), :]


def last_kernel(full, block, columns, x_one, x_two, out, west, east, column, walls, back, done, sems):
    here_x, size_x = lax.axis_index("gx"), lax.axis_size("gx")
    top = lax.axis_index("gz") == lax.axis_size("gz") - 1
    lanes, rows = lane_ids(), row_ids()

    if size_x == 2:

        def beside(side, start):
            first = min(max(start, 0), X_ROWS - 8)
            value = x_one[pl.ds(first, 8), :]
            return pltpu.roll(value, (first - start) % 8, 0) if first != start else value

    else:

        def spread(right, left):
            west[pl.ds(PAD, X_ROWS), :] = left[...]
            east[pl.ds(PAD, X_ROWS), :] = right[...]

        by_parity("gx", x_one, x_two, spread)

        def beside(side, start):
            return (west if side < 0 else east)[pl.ds(PAD + start, 8), :]

    strip = []
    for c in range(CHANNELS):
        cx = VEL[c][0] if c < 27 else 0
        value = jnp.where(
            rows < 4, columns[pl.ds(PAD + 4 * c, 8), :], columns[pl.ds(PAD + 4 * c - 4, 8), :]
        )
        if c <= WALL and cx >= 0:
            value = jnp.where(rows < 2, beside(-1, 2 * c - (cx == 0)), value)
        if c <= WALL and cx <= 0:
            value = jnp.where(rows >= 6, beside(1, 2 * c - 6 + (cx == 0)), value)
        strip.append(value)
    strip[WALL] = jnp.where((rows == 0) | (rows == 7), 0.0, strip[WALL])

    def shifted(value, q):
        cx, cy, cz = VEL[q]
        if cx:
            value = pltpu.roll(value, cx % 8, 0)
        step = (PITCH * cz + cy) % 128
        return pltpu.roll(value, step, 1) if step else value

    moved = []
    for q in range(27):
        value = shifted(strip[q], q)
        if q != 13:
            value = jnp.where(shifted(strip[WALL], q) != 0.0, strip[26 - q], value)
        moved.append(jnp.where(strip[WALL] != 0.0, WEIGHT[q], value))
    place = here_x * NX + jnp.where(rows < 4, rows - 2, rows + (NX - 6))
    place = lax.rem(place + size_x * NX, size_x * NX)
    sides = relaxed(moved, place < SPONGE, strip[AIM])
    lid = top & (lanes >= (NZ + 2) * PITCH) & (lanes < (NZ + 3) * PITCH)
    for q in range(9):
        sides[q] = jnp.where(lid, pltpu.roll(sides[q + 18], PITCH, 1), sides[q])
    for q, side in enumerate(sides + [strip[WALL]]):
        column[pl.ds(PAD + 8 * q, 8), :] = side

    def picked(wanted):
        value = None
        for sublane, (q, row) in enumerate(wanted):
            moved = column[pl.ds(PAD + 8 * q + row - sublane, 8), :]
            value = moved if value is None else jnp.where(rows == sublane, moved, value)
        return value

    packed = []
    for k in range(9):
        a, b = 3 * k + 2, 3 * k
        packed.append(
            picked([(a, 5), (a, 2), (a, 1), (a, 2), (b, 5), (b, 2), (b, 5), (b, 6)])
        )
    rest = [(3 * k + 1, row) for k in range(9) for row in (5, 2)] + [(27, 1), (27, 6)]
    packed += [picked(rest[i : i + 8]) for i in range(0, len(rest), 8)]
    packed += [jnp.zeros((8, 128), F32)] * (16 - len(packed))
    back[...] = jnp.concatenate(packed, axis=0).T

    def column_at(place, lane, start):
        return pltpu.roll(back[pl.ds(start, 8), :], (lane - place) % 128, 1)

    rim = (lanes == 0) | (lanes == 127)

    def rimmed(q, start):
        k = q // 3
        ends = column_at((8 * k + 5, 73 + 2 * k, 8 * k + 1)[q % 3], 0, PITCH + start)
        return jnp.where(rim, ends, block[q, pl.ds(start, 8), :])

    for u in range(UNITS):
        flags = full[pl.ds(WALL * ROWS + PAD + PITCH + 8 * u, 8), :]
        walls[1, pl.ds(8 * u, 8), :] = flags
        for cx, edge, place in ((1, 0, 90), (-1, 127, 91)):
            walls[cx + 1, pl.ds(8 * u, 8), :] = jnp.where(
                lanes == edge, column_at(place, edge, PITCH + 8 * u), pltpu.roll(flags, cx % 128, 1)
            )

    copies = []
    for z in range(NZ):
        cell = (z + 1) * PITCH + 2
        solid = walls[1, pl.ds(cell, 8), :] != 0.0
        for q in range(27):
            cx, cy, cz = VEL[q]
            start = cell - PITCH * cz - cy
            if cx > 0:
                side = column_at(8 * (q // 3) + 2, 0, PITCH + start)
                value = jnp.where(lanes < 2, side, pltpu.roll(block[q, pl.ds(start, 8), :], 1, 1))
            elif cx < 0:
                side = column_at(8 * (q // 3) + 6, 126, PITCH + start)
                value = jnp.where(lanes > 125, side, pltpu.roll(block[q, pl.ds(start, 8), :], 127, 1))
            else:
                value = rimmed(q, start)
            if q != 13:
                blocked = walls[cx + 1, pl.ds(start, 8), :] != 0.0
                value = jnp.where(blocked, rimmed(26 - q, cell), value)
            done[q, z] = jnp.where(solid, WEIGHT[q], value)
        copies.append(pltpu.make_async_copy(done.at[:, z], out.at[:, z], sems.at[z]))
        copies[-1].start()
    for copy in copies:
        copy.wait()


def swap(value, axis, turn, wrap):
    size = lax.axis_size(axis)
    pairs = [(i, (i + 1) % size) for i in range(turn, size if wrap else size - 1, 2)]
    return lax.ppermute(value, axis, pairs + [(j, i) for i, j in pairs])


def shape(*dims):
    return jax.ShapeDtypeStruct(dims, F32)


def shards(pops, solid, profile_table, profile_index):
    own, y_two, y_one = pl.pallas_call(
        first_kernel,
        out_shape=[shape(CHANNELS * NZ * 8, 128), shape(Y_ROWS, 128), shape(Y_ROWS, 128)],
        in_specs=[HBM] * 4,
        out_specs=[VMEM] * 3,
        scratch_shapes=[
            pltpu.VMEM(pops.shape, F32),
            pltpu.VMEM(solid.shape, jnp.int32),
            pltpu.SMEM(profile_table.shape[::-1], F32),
            pltpu.SMEM(profile_index.shape, jnp.int32),
            pltpu.SemaphoreType.DMA((3 + 3 * NZ,)),
        ],
        compiler_params=PARAMS,
        name="collide",
    )(*(pltpu.with_memory_space_constraint(a, pltpu.HBM) for a in (pops, solid, profile_table.T, profile_index)))
    y_two = swap(y_two, "gy", 1, True)
    y_one = swap(y_one, "gy", 0, True)
    own_two, own_one = pl.pallas_call(
        ahead_kernel,
        out_shape=[shape(Z_BLOCKS * 8, 128)] * 2,
        in_specs=[VMEM],
        out_specs=[VMEM] * 2,
        compiler_params=PARAMS,
        name="pack_own",
    )(own)
    own_two = swap(own_two, "gz", 1, False)
    own_one = swap(own_one, "gz", 0, False)
    z_two, z_one = pl.pallas_call(
        second_kernel,
        out_shape=[shape(Z_ROWS, 128)] * 2,
        in_specs=[VMEM] * 2,
        out_specs=[VMEM] * 2,
        scratch_shapes=[pltpu.VMEM((2 * NZ, 128), F32)] * 2,
        compiler_params=PARAMS,
        cost_estimate=pl.CostEstimate(flops=10**9, bytes_accessed=2**20, transcendentals=0),
        name="pack_z",
    )(y_two, y_one)
    z_two = swap(z_two, "gz", 1, False)
    z_one = swap(z_one, "gz", 0, False)
    part, packed = pl.pallas_call(
        fill_kernel,
        out_shape=[shape(CHANNELS * ROWS, 128), shape(128, 128)],
        in_specs=[VMEM] * 5,
        out_specs=[VMEM] * 2,
        scratch_shapes=[pltpu.VMEM((2 * NZ, 128), F32)] * 2,
        compiler_params=PARAMS,
        cost_estimate=pl.CostEstimate(flops=10**6, bytes_accessed=2**22, transcendentals=0),
        name="fill",
    )(own, y_two, y_one, own_two, own_one)
    full, packed, columns, message = pl.pallas_call(
        third_kernel,
        out_shape=[
            shape(CHANNELS * ROWS, 128),
            shape(128, 128),
            shape(PAD + 128 + PAD, 128),
            shape(X_ROWS, 128),
        ],
        in_specs=[VMEM] * 4,
        out_specs=[VMEM] * 4,
        input_output_aliases={0: 0, 1: 1},
        compiler_params=PARAMS,
        name="pack_x",
    )(part, packed, z_two, z_one)
    x_one = swap(message, "gx", 0, True)
    x_two = x_one if lax.axis_size("gx") == 2 else swap(message, "gx", 1, True)
    block = pl.pallas_call(
        block_kernel,
        out_shape=shape(27, UNITS * 8, 128),
        in_specs=[VMEM],
        out_specs=VMEM,
        scratch_shapes=[pltpu.VMEM((3, ROWS, 128), F32)],
        compiler_params=PARAMS,
        cost_estimate=pl.CostEstimate(
            flops=27 * 20 * UNITS * 1024, bytes_accessed=2**22, transcendentals=0
        ),
        name="block",
    )(full)
    return pl.pallas_call(
        last_kernel,
        out_shape=shape(27, NZ, NY, NX),
        in_specs=[VMEM] * 5,
        out_specs=HBM,
        scratch_shapes=[
            pltpu.VMEM((PAD + X_ROWS + PAD, 128), F32),
            pltpu.VMEM((PAD + X_ROWS + PAD, 128), F32),
            pltpu.VMEM((PAD + 28 * 8 + PAD, 128), F32),
            pltpu.VMEM((3, UNITS * 8, 128), F32),
            pltpu.VMEM((128, 128), F32),
            pltpu.VMEM((27, NZ, NY, NX), F32),
            pltpu.SemaphoreType.DMA((NZ,)),
        ],
        compiler_params=PARAMS,
        name="finish",
    )(full, block, columns, x_one, x_two)


def solution(mesh):
    return jax.shard_map(
        shards,
        mesh=mesh,
        in_specs=(P(None, "gz", "gy", "gx"), P("gz", "gy", "gx"), P(None, "gz"), P("gy")),
        out_specs=P(None, "gz", "gy", "gx"),
        check_vma=False,
    )
```

```python
import functools

import jax
import jax.numpy as jnp
import numpy as np
from jax import lax
from jax.experimental import pallas as pl
from jax.experimental.pallas import tpu as pltpu
from jax.sharding import PartitionSpec as P

SPONGE = 32
TAU = 0.52
SMAG = 18.0 * 1.4142135623730951 * 0.17 * 0.17

VEL = [(cx, cy, cz) for cz in (-1, 0, 1) for cy in (-1, 0, 1) for cx in (-1, 0, 1)]
WEIGHT = [
    float(np.array([8.0 / 27.0, 2.0 / 27.0, 1.0 / 54.0, 1.0 / 216.0])[cx * cx + cy * cy + cz * cz])
    for cx, cy, cz in VEL
]
WALL, AIM, CHANNELS = 27, 28, 29
NZ, NY, NX = 4, 8, 128
PITCH = NY + 4
FLAT = (NZ + 4) * PITCH
PAD = 8
ROWS = PAD + FLAT + PAD
SLABS = CHANNELS + 6
UNITS = (NZ + 2) * PITCH // 8

PARAMS = pltpu.CompilerParams(vmem_limit_bytes=12 * 2**20)
VMEM = pl.BlockSpec(memory_space=pltpu.VMEM)
HBM = pl.BlockSpec(memory_space=pltpu.HBM)
F32 = jnp.float32

MIXED = 24
Y_ROWS = (MIXED + 1 + 9) * NZ
Z_BLOCKS = CHANNELS + 10
Z_FAR = 2 * Z_BLOCKS
Z_ROWS = -(-(Z_FAR + 2 * 12) // 8) * 8

X_ROWS = 2 * (WALL + 1)


def relaxed(f, sponge, aim):
    quad = {}
    for cz in (-1, 0, 1):
        line = {}
        for cy in (-1, 0, 1):
            base = 9 * (cz + 1) + 3 * (cy + 1)
            both = f[base + 2] + f[base]
            line[cy] = (both + f[base + 1], f[base + 2] - f[base], both)
        s = line[1][0] + line[-1][0]
        sx = line[1][1] + line[-1][1]
        quad[cz] = dict(
            n=s + line[0][0],
            y=line[1][0] - line[-1][0],
            yy=s,
            x=sx + line[0][1],
            xy=line[1][1] - line[-1][1],
            xx=line[1][2] + line[-1][2] + line[0][2],
        )
    up, mid, down = quad[1], quad[0], quad[-1]
    zz = up["n"] + down["n"]
    rho = zz + mid["n"]
    jz = up["n"] - down["n"]
    jy = up["y"] + down["y"] + mid["y"]
    jx = up["x"] + down["x"] + mid["x"]
    inverse = 1.0 / rho
    ux, uy, uz = jx * inverse, jy * inverse, jz * inverse
    third = rho * (1.0 / 3.0)
    pxx = (up["xx"] + down["xx"] + mid["xx"]) - (third + jx * ux)
    pyy = (up["yy"] + down["yy"] + mid["yy"]) - (third + jy * uy)
    pzz = zz - (third + jz * uz)
    pxy = (up["xy"] + down["xy"] + mid["xy"]) - jx * uy
    pxz = (up["x"] - down["x"]) - jx * uz
    pyz = (up["y"] - down["y"]) - jy * uz
    strain = pxx * pxx + pyy * pyy + pzz * pzz + 2.0 * (pxy * pxy + pxz * pxz + pyz * pyz)
    size = jnp.sqrt(2.0 * strain)
    tau = 0.5 * (TAU + jnp.sqrt(TAU * TAU + SMAG * size * inverse))
    omega = 1.0 / tau
    keep = 1.0 - omega
    if sponge is not None:
        keep = jnp.where(sponge, 0.0, keep)
        omega = jnp.where(sponge, 1.0, omega)
        ux = jnp.where(sponge, aim, ux)
        uy = jnp.where(sponge, 0.0, uy)
        uz = jnp.where(sponge, 0.0, uz)
    square = 1.0 - 1.5 * (ux * ux + uy * uy + uz * uz)
    vx, vy, vz = 3.0 * ux, 3.0 * uy, 3.0 * uz
    share = rho * omega
    weighted = {w: share * w for w in sorted(set(WEIGHT))}
    post = [None] * 27
    for q in range(14):
        cx, cy, cz = VEL[q]
        along = None
        for c, v in ((cx, vx), (cy, vy), (cz, vz)):
            if c:
                along = (v if c > 0 else -v) if along is None else (along + v if c > 0 else along - v)
        scale = weighted[WEIGHT[q]]
        if along is None:
            post[q] = keep * f[q] + scale * square
            continue
        even = square + 0.5 * along * along
        post[q] = keep * f[q] + scale * (even + along)
        post[26 - q] = keep * f[26 - q] + scale * (even - along)
    return post


def lane_ids():
    return lax.broadcasted_iota(jnp.int32, (8, 128), 1)


def row_ids():
    return lax.broadcasted_iota(jnp.int32, (8, 128), 0)


def by_parity(axis, one, two, body):
    even = lax.rem(lax.axis_index(axis), 2) == 0
    pl.when(even)(lambda: body(one, two))
    pl.when(jnp.logical_not(even))(lambda: body(two, one))


def z_blocks(near, far, part):
    blocks = [(c, near) for c in range(CHANNELS)]
    return blocks + [(9 * part + k, far) for k in range(9)] + [(WALL, far)]


def first_kernel(pops_at, solid_at, table_at, index_at, own, two, one, *scratch):
    pops, solid, table, index, sems = scratch
    parts = [(pl.ds(q, 9), z) for z in range(NZ) for q in (0, 9, 18)]
    planes = [(pops_at.at[part], pops.at[part]) for part in parts]
    small = [(table_at, table), (index_at, index)]
    copies = [
        pltpu.make_async_copy(source, target, sems.at[i])
        for i, (source, target) in enumerate([*small, *planes, (solid_at, solid)])
    ]
    for copy in copies:
        copy.start()
    for copy in copies[:2]:
        copy.wait()
    lanes, rows = lane_ids(), row_ids()
    sponge = (lax.axis_index("gx") * NX + lanes) < SPONGE
    profiles = [index[y] for y in range(NY)]
    aims = []
    for z in range(NZ):
        aim = jnp.zeros((8, 128), F32)
        for y, profile in enumerate(profiles):
            aim = jnp.where(rows == y, table[z, profile], aim)
        aims.append(aim)
    for z, aim in enumerate(aims):
        for copy in copies[3 * z + 2 : 3 * z + 5]:
            copy.wait()
        post = relaxed([pops[q, z] for q in range(27)], sponge, aim)
        for q in range(27):
            own[pl.ds((q * NZ + z) * 8, 8), :] = post[q]
        own[pl.ds((AIM * NZ + z) * 8, 8), :] = aim
    copies[-1].wait()
    for z in range(NZ):
        own[pl.ds((WALL * NZ + z) * 8, 8), :] = solid[z].astype(F32)

    def pack(yup, ydown):
        inside = lax.rem(lanes, 4)
        for out, edge, second, part in ((yup, 7, 6, 6), (ydown, 0, 1, 0)):
            back = 15 - part
            for first, count, place in ((0, back, 0), (back + 3, 24 - back, back)):
                out[pl.ds(place * NZ, count * NZ), :] = own[
                    pl.ds(first * NZ * 8 + edge, count * NZ, stride=8), :
                ]
            for z in range(NZ):
                west, east, aim, flag = (
                    own[pl.ds((c * NZ + z) * 8, 8), :] for c in (back, back + 2, AIM, WALL)
                )
                mixed = jnp.where(inside < 2, jnp.where(inside == 0, west, aim), flag)
                mixed = jnp.where(inside == 3, east, mixed)
                out[pl.ds(MIXED * NZ + z, 1), :] = mixed[edge : edge + 1]
            for a in range(3):
                out[pl.ds((MIXED + 1 + 3 * a) * NZ, 3 * NZ), :] = own[
                    pl.ds((9 * a + part) * NZ * 8 + second, 3 * NZ, stride=8), :
                ]

    by_parity("gy", one, two, pack)


def ahead_kernel(own, two, one):
    def pack(zup, zdown):
        for out, first, second, part in ((zup, NZ - 1, NZ - 2, 2), (zdown, 0, 1, 0)):
            for k, (c, z) in enumerate(z_blocks(first, second, part)):
                out[pl.ds(8 * k, 8), :] = own[pl.ds((c * NZ + z) * 8, 8), :]

    by_parity("gz", one, two, pack)


def y_runs(part):
    back = 15 - part
    return (0, back, 0), (back, 3, None), (back + 3, 24 - back, back)


def spread_mixed(below, above, flags, aims):
    flags[pl.ds(0, NZ), :] = below[pl.ds(MIXED * NZ, NZ), :]
    flags[pl.ds(NZ, NZ), :] = above[pl.ds(MIXED * NZ, NZ), :]
    mixed = flags[pl.ds(0, 2 * NZ), :]
    inside = lax.rem(lane_ids(), 4)
    moved = {k: pltpu.roll(mixed, k % 128, 1) if k else mixed for k in (-2, -1, 0, 1, 2)}

    def from_lane(source):
        value = moved[0]
        for lane in range(4):
            if lane != source:
                value = jnp.where(inside == lane, moved[lane - source], value)
        return value

    aims[pl.ds(0, 2 * NZ), :] = from_lane(1)
    flags[pl.ds(0, 2 * NZ), :] = from_lane(2)


def second_kernel(y_two, y_one, z_two, z_one, flags, aims):
    def pack(above, below):
        spread_mixed(below, above, flags, aims)
        by_parity(
            "gz",
            z_one,
            z_two,
            lambda zup, zdown: pack_planes(below, above, flags, aims, zup, zdown),
        )

    by_parity("gy", y_one, y_two, pack)


def pack_planes(below, above, flags, aims, zup, zdown):
    for out, first, second, part in ((zup, NZ - 1, NZ - 2, 2), (zdown, 0, 1, 0)):
        for side, (halo, inward) in enumerate(((below, 6), (above, 0))):
            near = side * Z_BLOCKS
            for channel, count, place in y_runs(inward):
                if place is None:
                    row = halo[pl.ds(MIXED * NZ + first, 1), :]
                    out[pl.ds(near + channel, 3), :] = jnp.broadcast_to(row, (3, 128))
                else:
                    out[pl.ds(near + channel, count), :] = halo[
                        pl.ds(place * NZ + first, count, stride=NZ), :
                    ]
            out[pl.ds(near + WALL, 1), :] = flags[pl.ds(side * NZ + first, 1), :]
            out[pl.ds(near + AIM, 1), :] = aims[pl.ds(side * NZ + first, 1), :]
            place = 15 if part else 0
            for k, count in ((0, 8), (8, 1)):
                out[pl.ds(near + CHANNELS + k, count), :] = halo[
                    pl.ds((place + k) * NZ + second, count, stride=NZ if count > 1 else 1), :
                ]
            out[pl.ds(near + Z_BLOCKS - 1, 1), :] = flags[pl.ds(side * NZ + second, 1), :]
            far = Z_FAR + 12 * side
            start = (MIXED + 1) * NZ
            out[pl.ds(far, 8), :] = halo[pl.ds(start + first, 8, stride=NZ), :]
            out[pl.ds(far + 8, 1), :] = halo[pl.ds(start + 8 * NZ + first, 1), :]
            for k in range(3):
                row = halo[pl.ds(start + (3 * part + k) * NZ + second, 1), :]
                out[pl.ds(far + 9 + k, 1), :] = row


def plane_at(z):
    return PAD + (z + 2) * PITCH


def add_rows(full, flags, aims, above, below):
    spread_mixed(below, above, flags, aims)

    def put(channel, row, source):
        full[pl.ds(channel * ROWS + plane_at(0) + row, NZ, stride=PITCH), :] = source

    sides = ((below, 1, 0, 6), (above, PITCH - 2, PITCH - 1, 0))
    for side, (halo, near, far, inward) in enumerate(sides):
        for first, count, place in y_runs(inward):
            for k in range(count):
                row = MIXED if place is None else place + k
                put(first + k, near, halo[pl.ds(row * NZ, NZ), :])
        flag = flags[pl.ds(side * NZ, NZ), :]
        put(WALL, near, flag)
        put(WALL, far, flag)
        put(AIM, near, aims[pl.ds(side * NZ, NZ), :])
        for k in range(9):
            q = 9 * (k // 3) + inward + k % 3
            put(q, far, halo[pl.ds((MIXED + 1 + k) * NZ, NZ), :])


def add_own_planes(full, ceiling, floor):
    for halo, near, far, part in ((floor, -1, -2, 2), (ceiling, NZ, NZ + 1, 0)):
        for k, (c, z) in enumerate(z_blocks(near, far, part)):
            full[pl.ds(c * ROWS + plane_at(z) + 2, 8), :] = halo[pl.ds(8 * k, 8), :]


def add_planes(full, ceiling, floor):
    def put(count, channel, z, row, source):
        start = channel * ROWS + plane_at(z) + row
        full[pl.ds(start, count, stride=ROWS), :] = source

    for halo, near, far, part in ((floor, -1, -2, 2), (ceiling, NZ, NZ + 1, 0)):
        for side, (row, beyond, group) in enumerate(((1, 0, 2), (PITCH - 2, PITCH - 1, 0))):
            start = side * Z_BLOCKS
            put(CHANNELS, 0, near, row, halo[pl.ds(start, CHANNELS), :])
            put(9, 9 * part, far, row, halo[pl.ds(start + CHANNELS, 9), :])
            first, second = (halo[pl.ds(start + k, 1), :] for k in (WALL, Z_BLOCKS - 1))
            put(1, WALL, far, row, second)
            start = Z_FAR + 12 * side
            for k in range(3):
                put(3, 9 * k + 3 * group, near, beyond, halo[pl.ds(start + 3 * k, 3), :])
            put(3, 9 * part + 3 * group, far, beyond, halo[pl.ds(start + 9, 3), :])
            put(1, WALL, near, beyond, first)
            put(1, WALL, far, beyond, second)


def pack_columns(full, pack, tiles):
    slot = lane_ids() // 4
    for t in tiles:
        packed = jnp.zeros((8, 128), F32)
        for c in range(CHANNELS):
            moved = pltpu.roll(full[pl.ds(c * ROWS + PAD + 8 * t, 8), :], (4 * c + 2) % 128, 1)
            packed = jnp.where(slot == c, moved, packed)
        pack[pl.ds(8 * t, 8), :] = packed


OWN_TILES = range(2 * PITCH // 8, (NZ + 2) * PITCH // 8)


def fill_kernel(own, y_two, y_one, two, one, full, pack, flags, aims):
    for c in range(CHANNELS):
        for z in range(NZ):
            full[pl.ds(c * ROWS + plane_at(z) + 2, 8), :] = own[pl.ds((c * NZ + z) * 8, 8), :]
    by_parity("gy", y_one, y_two, functools.partial(add_rows, full, flags, aims))
    by_parity("gz", one, two, functools.partial(add_own_planes, full))
    pack_columns(full, pack, OWN_TILES)
    pack[pl.ds(FLAT, 128 - FLAT), :] = jnp.zeros((128 - FLAT, 128), F32)


def third_kernel(part, packed, z_two, z_one, full, pack, columns, message):
    last = lax.axis_size("gz") - 1
    here = lax.axis_index("gz")
    by_parity("gz", z_one, z_two, functools.partial(add_planes, full))

    @pl.when(here == 0)
    def _():
        full[pl.ds(WALL * ROWS + plane_at(-1), PITCH), :] = jnp.ones((PITCH, 128), F32)

    @pl.when(here == last)
    def _():
        for q in range(9):
            full[pl.ds(q * ROWS + plane_at(NZ), PITCH), :] = full[pl.ds((q + 18) * ROWS + plane_at(NZ - 1), PITCH), :]

    pack_columns(full, pack, [t for t in range(FLAT // 8) if t not in OWN_TILES])
    columns[pl.ds(PAD, 128), :] = pack[...].T

    def row(c, i, count):
        return columns[pl.ds(PAD + 4 * c + i, count), :]

    def returned(q, near, far):
        cx, cy, cz = VEL[q]
        step = (-PITCH * cz - cy) % 128
        value = row(26 - q, near, 8)
        value = pltpu.roll(value, step, 1) if step else value
        return jnp.where(row(WALL, far, 8) != 0.0, value, row(q, far, 8))[:1]

    for c in range(WALL + 1):
        cx = VEL[c][0] if c < 27 else 0
        if cx == 0:
            message[pl.ds(2 * c, 2), :] = row(c, 1, 2)
        elif cx > 0:
            message[pl.ds(2 * c, 1), :] = returned(c, 1, 0)
            message[pl.ds(2 * c + 1, 1), :] = row(c, 1, 1)
        else:
            message[pl.ds(2 * c, 1), :] = row(c, 2, 1)
            message[pl.ds(2 * c + 1, 1), :] = returned(c, 2, 3)


def block_kernel(full, post, walls):
    top = lax.axis_index("gz") == lax.axis_size("gz") - 1
    sponge = (lax.axis_index("gx") * NX + lane_ids()) < SPONGE
    for t in range(ROWS // 8):
        rows = pl.ds(8 * t, 8)
        flags = full[pl.ds(WALL * ROWS + 8 * t, 8), :]
        for cx in (-1, 0, 1):
            walls[cx + 1, rows, :] = pltpu.roll(flags, cx % 128, 1) if cx else flags
    for u in range(UNITS):
        cell = PAD + PITCH + 8 * u
        f = []
        solid = walls[1, pl.ds(cell, 8), :] != 0.0
        for q in range(27):
            cx, cy, cz = VEL[q]
            start = cell - PITCH * cz - cy
            value = full[pl.ds(q * ROWS + start, 8), :]
            if cx:
                value = pltpu.roll(value, cx % 128, 1)
            if q != 13:
                blocked = walls[cx + 1, pl.ds(start, 8), :] != 0.0
                value = jnp.where(blocked, full[pl.ds((26 - q) * ROWS + cell, 8), :], value)
            f.append(jnp.where(solid, WEIGHT[q], value))
        done = relaxed(f, sponge, full[pl.ds(AIM * ROWS + cell, 8), :])
        for q in range(27):
            post[q, pl.ds(8 * u, 8), :] = done[q]

    @pl.when(top)
    def _():
        for q in range(9):
            post[q, pl.ds((NZ + 1) * PITCH, PITCH), :] = post[q + 18, pl.ds(NZ * PITCH, PITCH), :]


def last_kernel(full, block, columns, x_one, x_two, out, west, east, column, walls, back, done, sems):
    here_x, size_x = lax.axis_index("gx"), lax.axis_size("gx")
    top = lax.axis_index("gz") == lax.axis_size("gz") - 1
    lanes, rows = lane_ids(), row_ids()

    if size_x == 2:

        def beside(side, start):
            first = min(max(start, 0), X_ROWS - 8)
            value = x_one[pl.ds(first, 8), :]
            return pltpu.roll(value, (first - start) % 8, 0) if first != start else value

    else:

        def spread(right, left):
            west[pl.ds(PAD, X_ROWS), :] = left[...]
            east[pl.ds(PAD, X_ROWS), :] = right[...]

        by_parity("gx", x_one, x_two, spread)

        def beside(side, start):
            return (west if side < 0 else east)[pl.ds(PAD + start, 8), :]

    def strip_at(c, shift):
        cx = VEL[c][0] if c < 27 else 0
        at = rows - shift
        first = PAD + 4 * c - shift
        value = jnp.where(at < 4, columns[pl.ds(first, 8), :], columns[pl.ds(first - 4, 8), :])
        if c <= WALL and cx >= 0:
            value = jnp.where(at < 2, beside(-1, 2 * c - (cx == 0) - shift), value)
        if c <= WALL and cx <= 0:
            value = jnp.where(at >= 6, beside(1, 2 * c - 6 + (cx == 0) - shift), value)
        if c == WALL:
            value = jnp.where((at == 0) | (at == 7), 0.0, value)
        return value

    strip = [strip_at(c, 0) for c in range(CHANNELS)]
    flags_at = {cx: strip_at(WALL, cx) if cx else strip[WALL] for cx in (-1, 0, 1)}

    def moved_along(value, q):
        cx, cy, cz = VEL[q]
        step = (PITCH * cz + cy) % 128
        return pltpu.roll(value, step, 1) if step else value

    moved = []
    for q in range(27):
        cx = VEL[q][0]
        value = moved_along(strip_at(q, cx) if cx else strip[q], q)
        if q != 13:
            value = jnp.where(moved_along(flags_at[cx], q) != 0.0, strip[26 - q], value)
        moved.append(jnp.where(strip[WALL] != 0.0, WEIGHT[q], value))
    place = here_x * NX + jnp.where(rows < 4, rows - 2, rows + (NX - 6))
    place = lax.rem(place + size_x * NX, size_x * NX)
    sides = relaxed(moved, place < SPONGE, strip[AIM])
    lid = top & (lanes >= (NZ + 2) * PITCH) & (lanes < (NZ + 3) * PITCH)
    for q in range(9):
        sides[q] = jnp.where(lid, pltpu.roll(sides[q + 18], PITCH, 1), sides[q])
    for q, side in enumerate(sides + [strip[WALL]]):
        column[pl.ds(PAD + 8 * q, 8), :] = side

    def picked(wanted):
        value = None
        for sublane, (q, row) in enumerate(wanted):
            moved = column[pl.ds(PAD + 8 * q + row - sublane, 8), :]
            value = moved if value is None else jnp.where(rows == sublane, moved, value)
        return value

    packed = []
    for k in range(9):
        a, b = 3 * k + 2, 3 * k
        packed.append(
            picked([(a, 5), (a, 2), (a, 1), (a, 2), (b, 5), (b, 2), (b, 5), (b, 6)])
        )
    rest = [(3 * k + 1, row) for k in range(9) for row in (5, 2)] + [(27, 1), (27, 6)]
    packed += [picked(rest[i : i + 8]) for i in range(0, len(rest), 8)]
    packed += [jnp.zeros((8, 128), F32)] * (16 - len(packed))
    back[...] = jnp.concatenate(packed, axis=0).T

    def column_at(place, lane, start):
        return pltpu.roll(back[pl.ds(start, 8), :], (lane - place) % 128, 1)

    rim = (lanes == 0) | (lanes == 127)

    def rimmed(q, start):
        k = q // 3
        ends = column_at((8 * k + 5, 73 + 2 * k, 8 * k + 1)[q % 3], 0, PITCH + start)
        return jnp.where(rim, ends, block[q, pl.ds(start, 8), :])

    for u in range(UNITS):
        flags = full[pl.ds(WALL * ROWS + PAD + PITCH + 8 * u, 8), :]
        walls[1, pl.ds(8 * u, 8), :] = flags
        for cx, edge, place in ((1, 0, 90), (-1, 127, 91)):
            walls[cx + 1, pl.ds(8 * u, 8), :] = jnp.where(
                lanes == edge, column_at(place, edge, PITCH + 8 * u), pltpu.roll(flags, cx % 128, 1)
            )

    copies = []
    for z in range(NZ):
        cell = (z + 1) * PITCH + 2
        solid = walls[1, pl.ds(cell, 8), :] != 0.0
        for q in range(27):
            cx, cy, cz = VEL[q]
            start = cell - PITCH * cz - cy
            if cx > 0:
                side = column_at(8 * (q // 3) + 2, 0, PITCH + start)
                value = jnp.where(lanes < 2, side, pltpu.roll(block[q, pl.ds(start, 8), :], 1, 1))
            elif cx < 0:
                side = column_at(8 * (q // 3) + 6, 126, PITCH + start)
                value = jnp.where(lanes > 125, side, pltpu.roll(block[q, pl.ds(start, 8), :], 127, 1))
            else:
                value = rimmed(q, start)
            if q != 13:
                blocked = walls[cx + 1, pl.ds(start, 8), :] != 0.0
                value = jnp.where(blocked, rimmed(26 - q, cell), value)
            done[q, z] = jnp.where(solid, WEIGHT[q], value)
        copies.append(pltpu.make_async_copy(done.at[:, z], out.at[:, z], sems.at[z]))
        copies[-1].start()
    for copy in copies:
        copy.wait()


def swap(value, axis, turn, wrap):
    size = lax.axis_size(axis)
    pairs = [(i, (i + 1) % size) for i in range(turn, size if wrap else size - 1, 2)]
    return lax.ppermute(value, axis, pairs + [(j, i) for i, j in pairs])


def shape(*dims):
    return jax.ShapeDtypeStruct(dims, F32)


def shards(pops, solid, profile_table, profile_index):
    own, y_two, y_one = pl.pallas_call(
        first_kernel,
        out_shape=[shape(CHANNELS * NZ * 8, 128), shape(Y_ROWS, 128), shape(Y_ROWS, 128)],
        in_specs=[HBM] * 4,
        out_specs=[VMEM] * 3,
        scratch_shapes=[
            pltpu.VMEM(pops.shape, F32),
            pltpu.VMEM(solid.shape, jnp.int32),
            pltpu.SMEM(profile_table.shape[::-1], F32),
            pltpu.SMEM(profile_index.shape, jnp.int32),
            pltpu.SemaphoreType.DMA((3 + 3 * NZ,)),
        ],
        compiler_params=PARAMS,
        name="collide",
    )(*(pltpu.with_memory_space_constraint(a, pltpu.HBM) for a in (pops, solid, profile_table.T, profile_index)))
    y_two = swap(y_two, "gy", 1, True)
    y_one = swap(y_one, "gy", 0, True)
    own_two, own_one = pl.pallas_call(
        ahead_kernel,
        out_shape=[shape(Z_BLOCKS * 8, 128)] * 2,
        in_specs=[VMEM],
        out_specs=[VMEM] * 2,
        compiler_params=PARAMS,
        name="pack_own",
    )(own)
    own_two = swap(own_two, "gz", 1, False)
    own_one = swap(own_one, "gz", 0, False)
    z_two, z_one = pl.pallas_call(
        second_kernel,
        out_shape=[shape(Z_ROWS, 128)] * 2,
        in_specs=[VMEM] * 2,
        out_specs=[VMEM] * 2,
        scratch_shapes=[pltpu.VMEM((4 * NZ, 128), F32)] * 2,
        compiler_params=PARAMS,
        cost_estimate=pl.CostEstimate(flops=10**9, bytes_accessed=2**20, transcendentals=0),
        name="pack_z",
    )(y_two, y_one)
    z_two = swap(z_two, "gz", 1, False)
    z_one = swap(z_one, "gz", 0, False)
    part, packed = pl.pallas_call(
        fill_kernel,
        out_shape=[shape(SLABS * ROWS, 128), shape(128, 128)],
        in_specs=[VMEM] * 5,
        out_specs=[VMEM] * 2,
        scratch_shapes=[pltpu.VMEM((4 * NZ, 128), F32)] * 2,
        compiler_params=PARAMS,
        cost_estimate=pl.CostEstimate(flops=10**6, bytes_accessed=2**22, transcendentals=0),
        name="fill",
    )(own, y_two, y_one, own_two, own_one)
    full, packed, columns, message = pl.pallas_call(
        third_kernel,
        out_shape=[
            shape(SLABS * ROWS, 128),
            shape(128, 128),
            shape(PAD + 128 + PAD, 128),
            shape(X_ROWS, 128),
        ],
        in_specs=[VMEM] * 4,
        out_specs=[VMEM] * 4,
        input_output_aliases={0: 0, 1: 1},
        compiler_params=PARAMS,
        name="pack_x",
    )(part, packed, z_two, z_one)
    x_one = swap(message, "gx", 0, True)
    x_two = x_one if lax.axis_size("gx") == 2 else swap(message, "gx", 1, True)
    block = pl.pallas_call(
        block_kernel,
        out_shape=shape(27, UNITS * 8, 128),
        in_specs=[VMEM],
        out_specs=VMEM,
        scratch_shapes=[pltpu.VMEM((3, ROWS, 128), F32)],
        compiler_params=PARAMS,
        cost_estimate=pl.CostEstimate(
            flops=27 * 20 * UNITS * 1024, bytes_accessed=2**22, transcendentals=0
        ),
        name="block",
    )(full)
    return pl.pallas_call(
        last_kernel,
        out_shape=shape(27, NZ, NY, NX),
        in_specs=[VMEM] * 5,
        out_specs=HBM,
        scratch_shapes=[
            pltpu.VMEM((PAD + X_ROWS + PAD, 128), F32),
            pltpu.VMEM((PAD + X_ROWS + PAD, 128), F32),
            pltpu.VMEM((PAD + 28 * 8 + PAD, 128), F32),
            pltpu.VMEM((3, UNITS * 8, 128), F32),
            pltpu.VMEM((128, 128), F32),
            pltpu.VMEM((27, NZ, NY, NX), F32),
            pltpu.SemaphoreType.DMA((NZ,)),
        ],
        compiler_params=PARAMS,
        name="finish",
    )(full, block, columns, x_one, x_two)


def solution(mesh):
    return jax.shard_map(
        shards,
        mesh=mesh,
        in_specs=(P(None, "gz", "gy", "gx"), P("gz", "gy", "gx"), P(None, "gz"), P("gy")),
        out_specs=P(None, "gz", "gy", "gx"),
        check_vma=False,
    )
```

```python
import functools

import jax
import jax.numpy as jnp
import numpy as np
from jax import lax
from jax.experimental import pallas as pl
from jax.experimental.pallas import tpu as pltpu
from jax.sharding import PartitionSpec as P

SPONGE = 32
TAU = 0.52
SMAG = 18.0 * 1.4142135623730951 * 0.17 * 0.17

VEL = [(cx, cy, cz) for cz in (-1, 0, 1) for cy in (-1, 0, 1) for cx in (-1, 0, 1)]
WEIGHT = [
    float(np.array([8.0 / 27.0, 2.0 / 27.0, 1.0 / 54.0, 1.0 / 216.0])[cx * cx + cy * cy + cz * cz])
    for cx, cy, cz in VEL
]
WALL, AIM, CHANNELS = 27, 28, 29
NZ, NY, NX = 4, 8, 128
PITCH = NY + 4
FLAT = (NZ + 4) * PITCH
PAD = 8
ROWS = PAD + FLAT + PAD
SLABS = CHANNELS + 6
UNITS = (NZ + 2) * PITCH // 8

PARAMS = pltpu.CompilerParams(vmem_limit_bytes=12 * 2**20)
VMEM = pl.BlockSpec(memory_space=pltpu.VMEM)
HBM = pl.BlockSpec(memory_space=pltpu.HBM)
F32 = jnp.float32

MIXED = 24
Y_ROWS = (MIXED + 1 + 9) * NZ
Z_BLOCKS = CHANNELS + 10
Z_FAR = 2 * Z_BLOCKS
Z_ROWS = -(-(Z_FAR + 2 * 12) // 8) * 8

X_ROWS = 2 * (WALL + 1)


def relaxed(f, sponge, aim):
    quad = {}
    for cz in (-1, 0, 1):
        line = {}
        for cy in (-1, 0, 1):
            base = 9 * (cz + 1) + 3 * (cy + 1)
            both = f[base + 2] + f[base]
            line[cy] = (both + f[base + 1], f[base + 2] - f[base], both)
        s = line[1][0] + line[-1][0]
        sx = line[1][1] + line[-1][1]
        quad[cz] = dict(
            n=s + line[0][0],
            y=line[1][0] - line[-1][0],
            yy=s,
            x=sx + line[0][1],
            xy=line[1][1] - line[-1][1],
            xx=line[1][2] + line[-1][2] + line[0][2],
        )
    up, mid, down = quad[1], quad[0], quad[-1]
    zz = up["n"] + down["n"]
    rho = zz + mid["n"]
    jz = up["n"] - down["n"]
    jy = up["y"] + down["y"] + mid["y"]
    jx = up["x"] + down["x"] + mid["x"]
    inverse = 1.0 / rho
    ux, uy, uz = jx * inverse, jy * inverse, jz * inverse
    third = rho * (1.0 / 3.0)
    pxx = (up["xx"] + down["xx"] + mid["xx"]) - (third + jx * ux)
    pyy = (up["yy"] + down["yy"] + mid["yy"]) - (third + jy * uy)
    pzz = zz - (third + jz * uz)
    pxy = (up["xy"] + down["xy"] + mid["xy"]) - jx * uy
    pxz = (up["x"] - down["x"]) - jx * uz
    pyz = (up["y"] - down["y"]) - jy * uz
    strain = pxx * pxx + pyy * pyy + pzz * pzz + 2.0 * (pxy * pxy + pxz * pxz + pyz * pyz)
    size = jnp.sqrt(2.0 * strain)
    tau = 0.5 * (TAU + jnp.sqrt(TAU * TAU + SMAG * size * inverse))
    omega = 1.0 / tau
    keep = 1.0 - omega
    if sponge is not None:
        keep = jnp.where(sponge, 0.0, keep)
        omega = jnp.where(sponge, 1.0, omega)
        ux = jnp.where(sponge, aim, ux)
        uy = jnp.where(sponge, 0.0, uy)
        uz = jnp.where(sponge, 0.0, uz)
    square = 1.0 - 1.5 * (ux * ux + uy * uy + uz * uz)
    vx, vy, vz = 3.0 * ux, 3.0 * uy, 3.0 * uz
    share = rho * omega
    weighted = {w: share * w for w in sorted(set(WEIGHT))}
    post = [None] * 27
    for q in range(14):
        cx, cy, cz = VEL[q]
        along = None
        for c, v in ((cx, vx), (cy, vy), (cz, vz)):
            if c:
                along = (v if c > 0 else -v) if along is None else (along + v if c > 0 else along - v)
        scale = weighted[WEIGHT[q]]
        if along is None:
            post[q] = keep * f[q] + scale * square
            continue
        even = square + 0.5 * along * along
        post[q] = keep * f[q] + scale * (even + along)
        post[26 - q] = keep * f[26 - q] + scale * (even - along)
    return post


def lane_ids():
    return lax.broadcasted_iota(jnp.int32, (8, 128), 1)


def row_ids():
    return lax.broadcasted_iota(jnp.int32, (8, 128), 0)


def by_parity(axis, one, two, body):
    even = lax.rem(lax.axis_index(axis), 2) == 0
    pl.when(even)(lambda: body(one, two))
    pl.when(jnp.logical_not(even))(lambda: body(two, one))


def z_blocks(near, far, part):
    blocks = [(c, near) for c in range(CHANNELS)]
    return blocks + [(9 * part + k, far) for k in range(9)] + [(WALL, far)]


def first_kernel(pops_at, solid_at, table_at, index_at, own, two, one, *scratch):
    pops, solid, table, index, sems = scratch
    groups = [(pops_at.at[pl.ds(q, 9)], pops.at[pl.ds(q, 9)]) for q in (0, 9, 18)]
    small = [(table_at, table), (index_at, index)]
    copies = [
        pltpu.make_async_copy(source, target, sems.at[i])
        for i, (source, target) in enumerate([*small, *groups, (solid_at, solid)])
    ]
    for copy in copies:
        copy.start()
    for copy in copies[:2]:
        copy.wait()
    lanes, rows = lane_ids(), row_ids()
    sponge = (lax.axis_index("gx") * NX + lanes) < SPONGE
    profiles = [index[y] for y in range(NY)]
    aims = []
    for z in range(NZ):
        aim = jnp.zeros((8, 128), F32)
        for y, profile in enumerate(profiles):
            aim = jnp.where(rows == y, table[z, profile], aim)
        aims.append(aim)
    for copy in copies[2:-1]:
        copy.wait()
    for z, aim in enumerate(aims):
        post = relaxed([pops[q, z] for q in range(27)], sponge, aim)
        for q in range(27):
            own[pl.ds((q * NZ + z) * 8, 8), :] = post[q]
        own[pl.ds((AIM * NZ + z) * 8, 8), :] = aim
    copies[-1].wait()
    for z in range(NZ):
        own[pl.ds((WALL * NZ + z) * 8, 8), :] = solid[z].astype(F32)

    def pack(yup, ydown):
        inside = lax.rem(lanes, 4)
        for out, edge, second, part in ((yup, 7, 6, 6), (ydown, 0, 1, 0)):
            back = 15 - part
            for first, count, place in ((0, back, 0), (back + 3, 24 - back, back)):
                out[pl.ds(place * NZ, count * NZ), :] = own[
                    pl.ds(first * NZ * 8 + edge, count * NZ, stride=8), :
                ]
            for z in range(NZ):
                west, east, aim, flag = (
                    own[pl.ds((c * NZ + z) * 8, 8), :] for c in (back, back + 2, AIM, WALL)
                )
                mixed = jnp.where(inside < 2, jnp.where(inside == 0, west, aim), flag)
                mixed = jnp.where(inside == 3, east, mixed)
                out[pl.ds(MIXED * NZ + z, 1), :] = mixed[edge : edge + 1]
            for a in range(3):
                out[pl.ds((MIXED + 1 + 3 * a) * NZ, 3 * NZ), :] = own[
                    pl.ds((9 * a + part) * NZ * 8 + second, 3 * NZ, stride=8), :
                ]

    by_parity("gy", one, two, pack)


def ahead_kernel(own, two, one):
    def pack(zup, zdown):
        for out, first, second, part in ((zup, NZ - 1, NZ - 2, 2), (zdown, 0, 1, 0)):
            for k, (c, z) in enumerate(z_blocks(first, second, part)):
                out[pl.ds(8 * k, 8), :] = own[pl.ds((c * NZ + z) * 8, 8), :]

    by_parity("gz", one, two, pack)


def y_runs(part):
    back = 15 - part
    return (0, back, 0), (back, 3, None), (back + 3, 24 - back, back)


def spread_mixed(below, above, flags, aims):
    flags[pl.ds(0, NZ), :] = below[pl.ds(MIXED * NZ, NZ), :]
    flags[pl.ds(NZ, NZ), :] = above[pl.ds(MIXED * NZ, NZ), :]
    mixed = flags[pl.ds(0, 2 * NZ), :]
    inside = lax.rem(lane_ids(), 4)
    moved = {k: pltpu.roll(mixed, k % 128, 1) if k else mixed for k in (-2, -1, 0, 1, 2)}

    def from_lane(source):
        value = moved[0]
        for lane in range(4):
            if lane != source:
                value = jnp.where(inside == lane, moved[lane - source], value)
        return value

    aims[pl.ds(0, 2 * NZ), :] = from_lane(1)
    flags[pl.ds(0, 2 * NZ), :] = from_lane(2)


def second_kernel(y_two, y_one, z_two, z_one, flags, aims):
    def pack(above, below):
        spread_mixed(below, above, flags, aims)
        by_parity(
            "gz",
            z_one,
            z_two,
            lambda zup, zdown: pack_planes(below, above, flags, aims, zup, zdown),
        )

    by_parity("gy", y_one, y_two, pack)


def pack_planes(below, above, flags, aims, zup, zdown):
    for out, first, second, part in ((zup, NZ - 1, NZ - 2, 2), (zdown, 0, 1, 0)):
        for side, (halo, inward) in enumerate(((below, 6), (above, 0))):
            near = side * Z_BLOCKS
            for channel, count, place in y_runs(inward):
                if place is None:
                    row = halo[pl.ds(MIXED * NZ + first, 1), :]
                    out[pl.ds(near + channel, 3), :] = jnp.broadcast_to(row, (3, 128))
                else:
                    out[pl.ds(near + channel, count), :] = halo[
                        pl.ds(place * NZ + first, count, stride=NZ), :
                    ]
            out[pl.ds(near + WALL, 1), :] = flags[pl.ds(side * NZ + first, 1), :]
            out[pl.ds(near + AIM, 1), :] = aims[pl.ds(side * NZ + first, 1), :]
            place = 15 if part else 0
            for k, count in ((0, 8), (8, 1)):
                out[pl.ds(near + CHANNELS + k, count), :] = halo[
                    pl.ds((place + k) * NZ + second, count, stride=NZ if count > 1 else 1), :
                ]
            out[pl.ds(near + Z_BLOCKS - 1, 1), :] = flags[pl.ds(side * NZ + second, 1), :]
            far = Z_FAR + 12 * side
            start = (MIXED + 1) * NZ
            out[pl.ds(far, 8), :] = halo[pl.ds(start + first, 8, stride=NZ), :]
            out[pl.ds(far + 8, 1), :] = halo[pl.ds(start + 8 * NZ + first, 1), :]
            for k in range(3):
                row = halo[pl.ds(start + (3 * part + k) * NZ + second, 1), :]
                out[pl.ds(far + 9 + k, 1), :] = row


def plane_at(z):
    return PAD + (z + 2) * PITCH


def add_rows(full, flags, aims, above, below):
    spread_mixed(below, above, flags, aims)

    def put(channel, row, source):
        full[pl.ds(channel * ROWS + plane_at(0) + row, NZ, stride=PITCH), :] = source

    sides = ((below, 1, 0, 6), (above, PITCH - 2, PITCH - 1, 0))
    for side, (halo, near, far, inward) in enumerate(sides):
        for first, count, place in y_runs(inward):
            for k in range(count):
                row = MIXED if place is None else place + k
                put(first + k, near, halo[pl.ds(row * NZ, NZ), :])
        flag = flags[pl.ds(side * NZ, NZ), :]
        put(WALL, near, flag)
        put(WALL, far, flag)
        put(AIM, near, aims[pl.ds(side * NZ, NZ), :])
        for k in range(9):
            q = 9 * (k // 3) + inward + k % 3
            put(q, far, halo[pl.ds((MIXED + 1 + k) * NZ, NZ), :])


def add_own_planes(full, ceiling, floor):
    for halo, near, far, part in ((floor, -1, -2, 2), (ceiling, NZ, NZ + 1, 0)):
        for k, (c, z) in enumerate(z_blocks(near, far, part)):
            full[pl.ds(c * ROWS + plane_at(z) + 2, 8), :] = halo[pl.ds(8 * k, 8), :]


def add_planes(full, ceiling, floor):
    def put(count, channel, z, row, source):
        start = channel * ROWS + plane_at(z) + row
        full[pl.ds(start, count, stride=ROWS), :] = source

    for halo, near, far, part in ((floor, -1, -2, 2), (ceiling, NZ, NZ + 1, 0)):
        for side, (row, beyond, group) in enumerate(((1, 0, 2), (PITCH - 2, PITCH - 1, 0))):
            start = side * Z_BLOCKS
            put(CHANNELS, 0, near, row, halo[pl.ds(start, CHANNELS), :])
            put(9, 9 * part, far, row, halo[pl.ds(start + CHANNELS, 9), :])
            first, second = (halo[pl.ds(start + k, 1), :] for k in (WALL, Z_BLOCKS - 1))
            put(1, WALL, far, row, second)
            start = Z_FAR + 12 * side
            for k in range(3):
                put(3, 9 * k + 3 * group, near, beyond, halo[pl.ds(start + 3 * k, 3), :])
            put(3, 9 * part + 3 * group, far, beyond, halo[pl.ds(start + 9, 3), :])
            put(1, WALL, near, beyond, first)
            put(1, WALL, far, beyond, second)


def pack_columns(full, pack, tiles):
    slot = lane_ids() // 4
    for t in tiles:
        packed = jnp.zeros((8, 128), F32)
        for c in range(CHANNELS):
            moved = pltpu.roll(full[pl.ds(c * ROWS + PAD + 8 * t, 8), :], (4 * c + 2) % 128, 1)
            packed = jnp.where(slot == c, moved, packed)
        pack[pl.ds(8 * t, 8), :] = packed


OWN_TILES = range(2 * PITCH // 8, (NZ + 2) * PITCH // 8)


def fill_kernel(own, y_two, y_one, two, one, full, pack, flags, aims):
    for c in range(CHANNELS):
        for z in range(NZ):
            full[pl.ds(c * ROWS + plane_at(z) + 2, 8), :] = own[pl.ds((c * NZ + z) * 8, 8), :]
    by_parity("gy", y_one, y_two, functools.partial(add_rows, full, flags, aims))
    by_parity("gz", one, two, functools.partial(add_own_planes, full))
    pack_columns(full, pack, OWN_TILES)
    pack[pl.ds(FLAT, 128 - FLAT), :] = jnp.zeros((128 - FLAT, 128), F32)


def third_kernel(part, packed, z_two, z_one, full, pack, columns, message):
    last = lax.axis_size("gz") - 1
    here = lax.axis_index("gz")
    by_parity("gz", z_one, z_two, functools.partial(add_planes, full))

    @pl.when(here == 0)
    def _():
        full[pl.ds(WALL * ROWS + plane_at(-1), PITCH), :] = jnp.ones((PITCH, 128), F32)

    @pl.when(here == last)
    def _():
        for q in range(9):
            full[pl.ds(q * ROWS + plane_at(NZ), PITCH), :] = full[pl.ds((q + 18) * ROWS + plane_at(NZ - 1), PITCH), :]

    pack_columns(full, pack, [t for t in range(FLAT // 8) if t not in OWN_TILES])
    columns[pl.ds(PAD, 128), :] = pack[...].T

    def row(c, i, count):
        return columns[pl.ds(PAD + 4 * c + i, count), :]

    def returned(q, near, far):
        cx, cy, cz = VEL[q]
        step = (-PITCH * cz - cy) % 128
        value = row(26 - q, near, 8)
        value = pltpu.roll(value, step, 1) if step else value
        return jnp.where(row(WALL, far, 8) != 0.0, value, row(q, far, 8))[:1]

    for c in range(WALL + 1):
        cx = VEL[c][0] if c < 27 else 0
        if cx == 0:
            message[pl.ds(2 * c, 2), :] = row(c, 1, 2)
        elif cx > 0:
            message[pl.ds(2 * c, 1), :] = returned(c, 1, 0)
            message[pl.ds(2 * c + 1, 1), :] = row(c, 1, 1)
        else:
            message[pl.ds(2 * c, 1), :] = row(c, 2, 1)
            message[pl.ds(2 * c + 1, 1), :] = returned(c, 2, 3)


def block_kernel(full, post, walls):
    top = lax.axis_index("gz") == lax.axis_size("gz") - 1
    sponge = (lax.axis_index("gx") * NX + lane_ids()) < SPONGE
    for t in range(ROWS // 8):
        rows = pl.ds(8 * t, 8)
        flags = full[pl.ds(WALL * ROWS + 8 * t, 8), :]
        for cx in (-1, 0, 1):
            walls[cx + 1, rows, :] = pltpu.roll(flags, cx % 128, 1) if cx else flags
    for u in range(UNITS):
        cell = PAD + PITCH + 8 * u
        f = []
        solid = walls[1, pl.ds(cell, 8), :] != 0.0
        for q in range(27):
            cx, cy, cz = VEL[q]
            start = cell - PITCH * cz - cy
            value = full[pl.ds(q * ROWS + start, 8), :]
            if cx:
                value = pltpu.roll(value, cx % 128, 1)
            if q != 13:
                blocked = walls[cx + 1, pl.ds(start, 8), :] != 0.0
                value = jnp.where(blocked, full[pl.ds((26 - q) * ROWS + cell, 8), :], value)
            f.append(jnp.where(solid, WEIGHT[q], value))
        done = relaxed(f, sponge, full[pl.ds(AIM * ROWS + cell, 8), :])
        for q in range(27):
            post[q, pl.ds(8 * u, 8), :] = done[q]

    @pl.when(top)
    def _():
        for q in range(9):
            post[q, pl.ds((NZ + 1) * PITCH, PITCH), :] = post[q + 18, pl.ds(NZ * PITCH, PITCH), :]


def last_kernel(full, block, columns, x_one, x_two, out, west, east, column, walls, back, done, sems):
    here_x, size_x = lax.axis_index("gx"), lax.axis_size("gx")
    top = lax.axis_index("gz") == lax.axis_size("gz") - 1
    lanes, rows = lane_ids(), row_ids()

    if size_x == 2:

        def beside(side, start):
            first = min(max(start, 0), X_ROWS - 8)
            value = x_one[pl.ds(first, 8), :]
            return pltpu.roll(value, (first - start) % 8, 0) if first != start else value

    else:

        def spread(right, left):
            west[pl.ds(PAD, X_ROWS), :] = left[...]
            east[pl.ds(PAD, X_ROWS), :] = right[...]

        by_parity("gx", x_one, x_two, spread)

        def beside(side, start):
            return (west if side < 0 else east)[pl.ds(PAD + start, 8), :]

    def strip_at(c, shift):
        cx = VEL[c][0] if c < 27 else 0
        at = rows - shift
        first = PAD + 4 * c - shift
        value = jnp.where(at < 4, columns[pl.ds(first, 8), :], columns[pl.ds(first - 4, 8), :])
        if c <= WALL and cx >= 0:
            value = jnp.where(at < 2, beside(-1, 2 * c - (cx == 0) - shift), value)
        if c <= WALL and cx <= 0:
            value = jnp.where(at >= 6, beside(1, 2 * c - 6 + (cx == 0) - shift), value)
        if c == WALL:
            value = jnp.where((at == 0) | (at == 7), 0.0, value)
        return value

    strip = [strip_at(c, 0) for c in range(CHANNELS)]
    flags_at = {cx: strip_at(WALL, cx) if cx else strip[WALL] for cx in (-1, 0, 1)}

    def moved_along(value, q):
        cx, cy, cz = VEL[q]
        step = (PITCH * cz + cy) % 128
        return pltpu.roll(value, step, 1) if step else value

    moved = []
    for q in range(27):
        cx = VEL[q][0]
        value = moved_along(strip_at(q, cx) if cx else strip[q], q)
        if q != 13:
            value = jnp.where(moved_along(flags_at[cx], q) != 0.0, strip[26 - q], value)
        moved.append(jnp.where(strip[WALL] != 0.0, WEIGHT[q], value))
    place = here_x * NX + jnp.where(rows < 4, rows - 2, rows + (NX - 6))
    place = lax.rem(place + size_x * NX, size_x * NX)
    sides = relaxed(moved, place < SPONGE, strip[AIM])
    lid = top & (lanes >= (NZ + 2) * PITCH) & (lanes < (NZ + 3) * PITCH)
    for q in range(9):
        sides[q] = jnp.where(lid, pltpu.roll(sides[q + 18], PITCH, 1), sides[q])
    for q, side in enumerate(sides + [strip[WALL]]):
        column[pl.ds(PAD + 8 * q, 8), :] = side

    def picked(wanted):
        value = None
        for sublane, (q, row) in enumerate(wanted):
            moved = column[pl.ds(PAD + 8 * q + row - sublane, 8), :]
            value = moved if value is None else jnp.where(rows == sublane, moved, value)
        return value

    packed = []
    for k in range(9):
        a, b = 3 * k + 2, 3 * k
        packed.append(
            picked([(a, 5), (a, 2), (a, 1), (a, 2), (b, 5), (b, 2), (b, 5), (b, 6)])
        )
    rest = [(3 * k + 1, row) for k in range(9) for row in (5, 2)] + [(27, 1), (27, 6)]
    packed += [picked(rest[i : i + 8]) for i in range(0, len(rest), 8)]
    packed += [jnp.zeros((8, 128), F32)] * (16 - len(packed))
    back[...] = jnp.concatenate(packed, axis=0).T

    def column_at(place, lane, start):
        return pltpu.roll(back[pl.ds(start, 8), :], (lane - place) % 128, 1)

    rim = (lanes == 0) | (lanes == 127)

    def rimmed(q, start):
        k = q // 3
        ends = column_at((8 * k + 5, 73 + 2 * k, 8 * k + 1)[q % 3], 0, PITCH + start)
        return jnp.where(rim, ends, block[q, pl.ds(start, 8), :])

    for u in range(UNITS):
        flags = full[pl.ds(WALL * ROWS + PAD + PITCH + 8 * u, 8), :]
        walls[1, pl.ds(8 * u, 8), :] = flags
        for cx, edge, place in ((1, 0, 90), (-1, 127, 91)):
            walls[cx + 1, pl.ds(8 * u, 8), :] = jnp.where(
                lanes == edge, column_at(place, edge, PITCH + 8 * u), pltpu.roll(flags, cx % 128, 1)
            )

    cells = [(z + 1) * PITCH + 2 for z in range(NZ)]
    solids = [walls[1, pl.ds(cell, 8), :] != 0.0 for cell in cells]

    def streamed(q, z):
        cx, cy, cz = VEL[q]
        cell = cells[z]
        start = cell - PITCH * cz - cy
        if cx > 0:
            side = column_at(8 * (q // 3) + 2, 0, PITCH + start)
            value = jnp.where(lanes < 2, side, pltpu.roll(block[q, pl.ds(start, 8), :], 1, 1))
        elif cx < 0:
            side = column_at(8 * (q // 3) + 6, 126, PITCH + start)
            value = jnp.where(lanes > 125, side, pltpu.roll(block[q, pl.ds(start, 8), :], 127, 1))
        else:
            value = rimmed(q, start)
        if q != 13:
            blocked = walls[cx + 1, pl.ds(start, 8), :] != 0.0
            value = jnp.where(blocked, rimmed(26 - q, cell), value)
        return jnp.where(solids[z], WEIGHT[q], value)

    copies = []
    for first, count in ((0, 9), (9, 8), (17, 6), (23, 4)):
        for q in range(first, first + count):
            for z in range(NZ):
                done[q, z] = streamed(q, z)
        part = pl.ds(first, count)
        copies.append(pltpu.make_async_copy(done.at[part], out.at[part], sems.at[len(copies)]))
        copies[-1].start()
    for copy in copies:
        copy.wait()


def swap(value, axis, turn, wrap):
    size = lax.axis_size(axis)
    pairs = [(i, (i + 1) % size) for i in range(turn, size if wrap else size - 1, 2)]
    return lax.ppermute(value, axis, pairs + [(j, i) for i, j in pairs])


def shape(*dims):
    return jax.ShapeDtypeStruct(dims, F32)


def shards(pops, solid, profile_table, profile_index):
    own, y_two, y_one = pl.pallas_call(
        first_kernel,
        out_shape=[shape(CHANNELS * NZ * 8, 128), shape(Y_ROWS, 128), shape(Y_ROWS, 128)],
        in_specs=[HBM] * 4,
        out_specs=[VMEM] * 3,
        scratch_shapes=[
            pltpu.VMEM(pops.shape, F32),
            pltpu.VMEM(solid.shape, jnp.int32),
            pltpu.SMEM(profile_table.shape[::-1], F32),
            pltpu.SMEM(profile_index.shape, jnp.int32),
            pltpu.SemaphoreType.DMA((6,)),
        ],
        compiler_params=PARAMS,
        name="collide",
    )(*(pltpu.with_memory_space_constraint(a, pltpu.HBM) for a in (pops, solid, profile_table.T, profile_index)))
    y_two = swap(y_two, "gy", 1, True)
    y_one = swap(y_one, "gy", 0, True)
    own_two, own_one = pl.pallas_call(
        ahead_kernel,
        out_shape=[shape(Z_BLOCKS * 8, 128)] * 2,
        in_specs=[VMEM],
        out_specs=[VMEM] * 2,
        compiler_params=PARAMS,
        name="pack_own",
    )(own)
    own_two = swap(own_two, "gz", 1, False)
    own_one = swap(own_one, "gz", 0, False)
    z_two, z_one = pl.pallas_call(
        second_kernel,
        out_shape=[shape(Z_ROWS, 128)] * 2,
        in_specs=[VMEM] * 2,
        out_specs=[VMEM] * 2,
        scratch_shapes=[pltpu.VMEM((4 * NZ, 128), F32)] * 2,
        compiler_params=PARAMS,
        cost_estimate=pl.CostEstimate(flops=10**9, bytes_accessed=2**20, transcendentals=0),
        name="pack_z",
    )(y_two, y_one)
    z_two = swap(z_two, "gz", 1, False)
    z_one = swap(z_one, "gz", 0, False)
    part, packed = pl.pallas_call(
        fill_kernel,
        out_shape=[shape(SLABS * ROWS, 128), shape(128, 128)],
        in_specs=[VMEM] * 5,
        out_specs=[VMEM] * 2,
        scratch_shapes=[pltpu.VMEM((4 * NZ, 128), F32)] * 2,
        compiler_params=PARAMS,
        cost_estimate=pl.CostEstimate(flops=10**6, bytes_accessed=2**22, transcendentals=0),
        name="fill",
    )(own, y_two, y_one, own_two, own_one)
    full, packed, columns, message = pl.pallas_call(
        third_kernel,
        out_shape=[
            shape(SLABS * ROWS, 128),
            shape(128, 128),
            shape(PAD + 128 + PAD, 128),
            shape(X_ROWS, 128),
        ],
        in_specs=[VMEM] * 4,
        out_specs=[VMEM] * 4,
        input_output_aliases={0: 0, 1: 1},
        compiler_params=PARAMS,
        name="pack_x",
    )(part, packed, z_two, z_one)
    x_one = swap(message, "gx", 0, True)
    x_two = x_one if lax.axis_size("gx") == 2 else swap(message, "gx", 1, True)
    block = pl.pallas_call(
        block_kernel,
        out_shape=shape(27, UNITS * 8, 128),
        in_specs=[VMEM],
        out_specs=VMEM,
        scratch_shapes=[pltpu.VMEM((3, ROWS, 128), F32)],
        compiler_params=PARAMS,
        cost_estimate=pl.CostEstimate(
            flops=27 * 20 * UNITS * 1024, bytes_accessed=2**22, transcendentals=0
        ),
        name="block",
    )(full)
    return pl.pallas_call(
        last_kernel,
        out_shape=shape(27, NZ, NY, NX),
        in_specs=[VMEM] * 5,
        out_specs=HBM,
        scratch_shapes=[
            pltpu.VMEM((PAD + X_ROWS + PAD, 128), F32),
            pltpu.VMEM((PAD + X_ROWS + PAD, 128), F32),
            pltpu.VMEM((PAD + 28 * 8 + PAD, 128), F32),
            pltpu.VMEM((3, UNITS * 8, 128), F32),
            pltpu.VMEM((128, 128), F32),
            pltpu.VMEM((27, NZ, NY, NX), F32),
            pltpu.SemaphoreType.DMA((NZ,)),
        ],
        compiler_params=PARAMS,
        name="finish",
    )(full, block, columns, x_one, x_two)


def solution(mesh):
    return jax.shard_map(
        shards,
        mesh=mesh,
        in_specs=(P(None, "gz", "gy", "gx"), P("gz", "gy", "gx"), P(None, "gz"), P("gy")),
        out_specs=P(None, "gz", "gy", "gx"),
        check_vma=False,
    )
```

```python
import functools

import jax
import jax.numpy as jnp
import numpy as np
from jax import lax
from jax.experimental import pallas as pl
from jax.experimental.pallas import tpu as pltpu
from jax.sharding import PartitionSpec as P

SPONGE = 32
TAU = 0.52
SMAG = 18.0 * 1.4142135623730951 * 0.17 * 0.17

VEL = [(cx, cy, cz) for cz in (-1, 0, 1) for cy in (-1, 0, 1) for cx in (-1, 0, 1)]
WEIGHT = [
    float(np.array([8.0 / 27.0, 2.0 / 27.0, 1.0 / 54.0, 1.0 / 216.0])[cx * cx + cy * cy + cz * cz])
    for cx, cy, cz in VEL
]
WALL, AIM, CHANNELS = 27, 28, 29
NZ, NY, NX = 4, 8, 128
PITCH = NY + 4
FLAT = (NZ + 4) * PITCH
PAD = 8
ROWS = PAD + FLAT + PAD
SLABS = CHANNELS + 6
UNITS = (NZ + 2) * PITCH // 8

PARAMS = pltpu.CompilerParams(vmem_limit_bytes=12 * 2**20)
VMEM = pl.BlockSpec(memory_space=pltpu.VMEM)
HBM = pl.BlockSpec(memory_space=pltpu.HBM)
F32 = jnp.float32

MIXED = 24
Y_ROWS = (MIXED + 1 + 9) * NZ
Z_BLOCKS = CHANNELS + 10
Z_FAR = 2 * Z_BLOCKS
Z_ROWS = -(-(Z_FAR + 2 * 12) // 8) * 8

X_ROWS = 2 * (WALL + 1)


def relaxed(f, sponge, aim):
    quad = {}
    for cz in (-1, 0, 1):
        line = {}
        for cy in (-1, 0, 1):
            base = 9 * (cz + 1) + 3 * (cy + 1)
            both = f[base + 2] + f[base]
            line[cy] = (both + f[base + 1], f[base + 2] - f[base], both)
        s = line[1][0] + line[-1][0]
        sx = line[1][1] + line[-1][1]
        quad[cz] = dict(
            n=s + line[0][0],
            y=line[1][0] - line[-1][0],
            yy=s,
            x=sx + line[0][1],
            xy=line[1][1] - line[-1][1],
            xx=line[1][2] + line[-1][2] + line[0][2],
        )
    up, mid, down = quad[1], quad[0], quad[-1]
    zz = up["n"] + down["n"]
    rho = zz + mid["n"]
    jz = up["n"] - down["n"]
    jy = up["y"] + down["y"] + mid["y"]
    jx = up["x"] + down["x"] + mid["x"]
    inverse = 1.0 / rho
    ux, uy, uz = jx * inverse, jy * inverse, jz * inverse
    third = rho * (1.0 / 3.0)
    pxx = (up["xx"] + down["xx"] + mid["xx"]) - (third + jx * ux)
    pyy = (up["yy"] + down["yy"] + mid["yy"]) - (third + jy * uy)
    pzz = zz - (third + jz * uz)
    pxy = (up["xy"] + down["xy"] + mid["xy"]) - jx * uy
    pxz = (up["x"] - down["x"]) - jx * uz
    pyz = (up["y"] - down["y"]) - jy * uz
    strain = pxx * pxx + pyy * pyy + pzz * pzz + 2.0 * (pxy * pxy + pxz * pxz + pyz * pyz)
    size = jnp.sqrt(2.0 * strain)
    tau = 0.5 * (TAU + jnp.sqrt(TAU * TAU + SMAG * size * inverse))
    omega = 1.0 / tau
    keep = 1.0 - omega
    if sponge is not None:
        keep = jnp.where(sponge, 0.0, keep)
        omega = jnp.where(sponge, 1.0, omega)
        ux = jnp.where(sponge, aim, ux)
        uy = jnp.where(sponge, 0.0, uy)
        uz = jnp.where(sponge, 0.0, uz)
    square = 1.0 - 1.5 * (ux * ux + uy * uy + uz * uz)
    vx, vy, vz = 3.0 * ux, 3.0 * uy, 3.0 * uz
    share = rho * omega
    weighted = {w: share * w for w in sorted(set(WEIGHT))}
    post = [None] * 27
    for q in range(14):
        cx, cy, cz = VEL[q]
        along = None
        for c, v in ((cx, vx), (cy, vy), (cz, vz)):
            if c:
                along = (v if c > 0 else -v) if along is None else (along + v if c > 0 else along - v)
        scale = weighted[WEIGHT[q]]
        if along is None:
            post[q] = keep * f[q] + scale * square
            continue
        even = square + 0.5 * along * along
        post[q] = keep * f[q] + scale * (even + along)
        post[26 - q] = keep * f[26 - q] + scale * (even - along)
    return post


def lane_ids():
    return lax.broadcasted_iota(jnp.int32, (8, 128), 1)


def row_ids():
    return lax.broadcasted_iota(jnp.int32, (8, 128), 0)


def by_parity(axis, one, two, body):
    even = lax.rem(lax.axis_index(axis), 2) == 0
    pl.when(even)(lambda: body(one, two))
    pl.when(jnp.logical_not(even))(lambda: body(two, one))


def z_blocks(near, far, part):
    blocks = [(c, near) for c in range(CHANNELS)]
    return blocks + [(9 * part + k, far) for k in range(9)] + [(WALL, far)]


def first_kernel(pops_at, solid_at, table_at, index_at, own, two, one, *scratch):
    pops, solid, table, index, sems = scratch
    groups = [(pops_at.at[pl.ds(q, 9)], pops.at[pl.ds(q, 9)]) for q in (0, 9, 18)]
    small = [(table_at, table), (index_at, index)]
    copies = [
        pltpu.make_async_copy(source, target, sems.at[i])
        for i, (source, target) in enumerate([*small, *groups, (solid_at, solid)])
    ]
    for copy in copies:
        copy.start()
    for copy in copies[:2]:
        copy.wait()
    lanes, rows = lane_ids(), row_ids()
    sponge = (lax.axis_index("gx") * NX + lanes) < SPONGE
    profiles = [index[y] for y in range(NY)]
    for z in range(NZ):
        aim = jnp.zeros((8, 128), F32)
        for y, profile in enumerate(profiles):
            aim = jnp.where(rows == y, table[z, profile], aim)
        own[pl.ds((AIM * NZ + z) * 8, 8), :] = aim
    for copy in copies[2:-1]:
        copy.wait()

    def plane(z, carry):
        def at(c):
            return pl.ds(pl.multiple_of((c * NZ + z) * 8, 8), 8)

        post = relaxed([pops[q, z] for q in range(27)], sponge, own[at(AIM), :])
        for q in range(27):
            own[at(q), :] = post[q]
        return carry

    lax.fori_loop(0, NZ, plane, 0)
    copies[-1].wait()
    for z in range(NZ):
        own[pl.ds((WALL * NZ + z) * 8, 8), :] = solid[z].astype(F32)

    def pack(yup, ydown):
        inside = lax.rem(lanes, 4)
        for out, edge, second, part in ((yup, 7, 6, 6), (ydown, 0, 1, 0)):
            back = 15 - part
            for first, count, place in ((0, back, 0), (back + 3, 24 - back, back)):
                out[pl.ds(place * NZ, count * NZ), :] = own[
                    pl.ds(first * NZ * 8 + edge, count * NZ, stride=8), :
                ]
            for z in range(NZ):
                west, east, aim, flag = (
                    own[pl.ds((c * NZ + z) * 8, 8), :] for c in (back, back + 2, AIM, WALL)
                )
                mixed = jnp.where(inside < 2, jnp.where(inside == 0, west, aim), flag)
                mixed = jnp.where(inside == 3, east, mixed)
                out[pl.ds(MIXED * NZ + z, 1), :] = mixed[edge : edge + 1]
            for a in range(3):
                out[pl.ds((MIXED + 1 + 3 * a) * NZ, 3 * NZ), :] = own[
                    pl.ds((9 * a + part) * NZ * 8 + second, 3 * NZ, stride=8), :
                ]

    by_parity("gy", one, two, pack)


def ahead_kernel(own, two, one):
    def pack(zup, zdown):
        for out, first, second, part in ((zup, NZ - 1, NZ - 2, 2), (zdown, 0, 1, 0)):
            for k, (c, z) in enumerate(z_blocks(first, second, part)):
                out[pl.ds(8 * k, 8), :] = own[pl.ds((c * NZ + z) * 8, 8), :]

    by_parity("gz", one, two, pack)


def y_runs(part):
    back = 15 - part
    return (0, back, 0), (back, 3, None), (back + 3, 24 - back, back)


def spread_mixed(below, above, flags, aims):
    flags[pl.ds(0, NZ), :] = below[pl.ds(MIXED * NZ, NZ), :]
    flags[pl.ds(NZ, NZ), :] = above[pl.ds(MIXED * NZ, NZ), :]
    mixed = flags[pl.ds(0, 2 * NZ), :]
    inside = lax.rem(lane_ids(), 4)
    moved = {k: pltpu.roll(mixed, k % 128, 1) if k else mixed for k in (-2, -1, 0, 1, 2)}

    def from_lane(source):
        value = moved[0]
        for lane in range(4):
            if lane != source:
                value = jnp.where(inside == lane, moved[lane - source], value)
        return value

    aims[pl.ds(0, 2 * NZ), :] = from_lane(1)
    flags[pl.ds(0, 2 * NZ), :] = from_lane(2)


def second_kernel(y_two, y_one, z_two, z_one, flags, aims):
    def pack(above, below):
        spread_mixed(below, above, flags, aims)
        by_parity(
            "gz",
            z_one,
            z_two,
            lambda zup, zdown: pack_planes(below, above, flags, aims, zup, zdown),
        )

    by_parity("gy", y_one, y_two, pack)


def pack_planes(below, above, flags, aims, zup, zdown):
    for out, first, second, part in ((zup, NZ - 1, NZ - 2, 2), (zdown, 0, 1, 0)):
        for side, (halo, inward) in enumerate(((below, 6), (above, 0))):
            near = side * Z_BLOCKS
            for channel, count, place in y_runs(inward):
                if place is None:
                    row = halo[pl.ds(MIXED * NZ + first, 1), :]
                    out[pl.ds(near + channel, 3), :] = jnp.broadcast_to(row, (3, 128))
                else:
                    out[pl.ds(near + channel, count), :] = halo[
                        pl.ds(place * NZ + first, count, stride=NZ), :
                    ]
            out[pl.ds(near + WALL, 1), :] = flags[pl.ds(side * NZ + first, 1), :]
            out[pl.ds(near + AIM, 1), :] = aims[pl.ds(side * NZ + first, 1), :]
            place = 15 if part else 0
            for k, count in ((0, 8), (8, 1)):
                out[pl.ds(near + CHANNELS + k, count), :] = halo[
                    pl.ds((place + k) * NZ + second, count, stride=NZ if count > 1 else 1), :
                ]
            out[pl.ds(near + Z_BLOCKS - 1, 1), :] = flags[pl.ds(side * NZ + second, 1), :]
            far = Z_FAR + 12 * side
            start = (MIXED + 1) * NZ
            out[pl.ds(far, 8), :] = halo[pl.ds(start + first, 8, stride=NZ), :]
            out[pl.ds(far + 8, 1), :] = halo[pl.ds(start + 8 * NZ + first, 1), :]
            for k in range(3):
                row = halo[pl.ds(start + (3 * part + k) * NZ + second, 1), :]
                out[pl.ds(far + 9 + k, 1), :] = row


def plane_at(z):
    return PAD + (z + 2) * PITCH


def add_rows(full, flags, aims, above, below):
    spread_mixed(below, above, flags, aims)

    def put(channel, row, source):
        full[pl.ds(channel * ROWS + plane_at(0) + row, NZ, stride=PITCH), :] = source

    sides = ((below, 1, 0, 6), (above, PITCH - 2, PITCH - 1, 0))
    for side, (halo, near, far, inward) in enumerate(sides):
        for first, count, place in y_runs(inward):
            for k in range(count):
                row = MIXED if place is None else place + k
                put(first + k, near, halo[pl.ds(row * NZ, NZ), :])
        flag = flags[pl.ds(side * NZ, NZ), :]
        put(WALL, near, flag)
        put(WALL, far, flag)
        put(AIM, near, aims[pl.ds(side * NZ, NZ), :])
        for k in range(9):
            q = 9 * (k // 3) + inward + k % 3
            put(q, far, halo[pl.ds((MIXED + 1 + k) * NZ, NZ), :])


def add_own_planes(full, ceiling, floor):
    for halo, near, far, part in ((floor, -1, -2, 2), (ceiling, NZ, NZ + 1, 0)):
        for k, (c, z) in enumerate(z_blocks(near, far, part)):
            full[pl.ds(c * ROWS + plane_at(z) + 2, 8), :] = halo[pl.ds(8 * k, 8), :]


def add_planes(full, ceiling, floor):
    def put(count, channel, z, row, source):
        start = channel * ROWS + plane_at(z) + row
        full[pl.ds(start, count, stride=ROWS), :] = source

    for halo, near, far, part in ((floor, -1, -2, 2), (ceiling, NZ, NZ + 1, 0)):
        for side, (row, beyond, group) in enumerate(((1, 0, 2), (PITCH - 2, PITCH - 1, 0))):
            start = side * Z_BLOCKS
            put(CHANNELS, 0, near, row, halo[pl.ds(start, CHANNELS), :])
            put(9, 9 * part, far, row, halo[pl.ds(start + CHANNELS, 9), :])
            first, second = (halo[pl.ds(start + k, 1), :] for k in (WALL, Z_BLOCKS - 1))
            put(1, WALL, far, row, second)
            start = Z_FAR + 12 * side
            for k in range(3):
                put(3, 9 * k + 3 * group, near, beyond, halo[pl.ds(start + 3 * k, 3), :])
            put(3, 9 * part + 3 * group, far, beyond, halo[pl.ds(start + 9, 3), :])
            put(1, WALL, near, beyond, first)
            put(1, WALL, far, beyond, second)


def pack_columns(full, pack, tiles):
    slot = lane_ids() // 4
    for t in tiles:
        packed = jnp.zeros((8, 128), F32)
        for c in range(CHANNELS):
            moved = pltpu.roll(full[pl.ds(c * ROWS + PAD + 8 * t, 8), :], (4 * c + 2) % 128, 1)
            packed = jnp.where(slot == c, moved, packed)
        pack[pl.ds(8 * t, 8), :] = packed


OWN_TILES = range(2 * PITCH // 8, (NZ + 2) * PITCH // 8)


def fill_kernel(own, y_two, y_one, two, one, full, pack, flags, aims):
    for c in range(CHANNELS):
        for z in range(NZ):
            full[pl.ds(c * ROWS + plane_at(z) + 2, 8), :] = own[pl.ds((c * NZ + z) * 8, 8), :]
    by_parity("gy", y_one, y_two, functools.partial(add_rows, full, flags, aims))
    by_parity("gz", one, two, functools.partial(add_own_planes, full))
    pack_columns(full, pack, OWN_TILES)
    pack[pl.ds(FLAT, 128 - FLAT), :] = jnp.zeros((128 - FLAT, 128), F32)


def third_kernel(part, packed, z_two, z_one, full, pack, columns, message):
    last = lax.axis_size("gz") - 1
    here = lax.axis_index("gz")
    by_parity("gz", z_one, z_two, functools.partial(add_planes, full))

    @pl.when(here == 0)
    def _():
        full[pl.ds(WALL * ROWS + plane_at(-1), PITCH), :] = jnp.ones((PITCH, 128), F32)

    @pl.when(here == last)
    def _():
        for q in range(9):
            full[pl.ds(q * ROWS + plane_at(NZ), PITCH), :] = full[pl.ds((q + 18) * ROWS + plane_at(NZ - 1), PITCH), :]

    pack_columns(full, pack, [t for t in range(FLAT // 8) if t not in OWN_TILES])
    columns[pl.ds(PAD, 128), :] = pack[...].T

    def row(c, i, count):
        return columns[pl.ds(PAD + 4 * c + i, count), :]

    def returned(q, near, far):
        cx, cy, cz = VEL[q]
        step = (-PITCH * cz - cy) % 128
        value = row(26 - q, near, 8)
        value = pltpu.roll(value, step, 1) if step else value
        return jnp.where(row(WALL, far, 8) != 0.0, value, row(q, far, 8))[:1]

    for c in range(WALL + 1):
        cx = VEL[c][0] if c < 27 else 0
        if cx == 0:
            message[pl.ds(2 * c, 2), :] = row(c, 1, 2)
        elif cx > 0:
            message[pl.ds(2 * c, 1), :] = returned(c, 1, 0)
            message[pl.ds(2 * c + 1, 1), :] = row(c, 1, 1)
        else:
            message[pl.ds(2 * c, 1), :] = row(c, 2, 1)
            message[pl.ds(2 * c + 1, 1), :] = returned(c, 2, 3)


def block_kernel(full, post, walls):
    top = lax.axis_index("gz") == lax.axis_size("gz") - 1
    sponge = (lax.axis_index("gx") * NX + lane_ids()) < SPONGE
    for t in range(ROWS // 8):
        rows = pl.ds(8 * t, 8)
        flags = full[pl.ds(WALL * ROWS + 8 * t, 8), :]
        for cx in (-1, 0, 1):
            walls[cx + 1, rows, :] = pltpu.roll(flags, cx % 128, 1) if cx else flags
    for u in range(UNITS):
        cell = PAD + PITCH + 8 * u
        f = []
        solid = walls[1, pl.ds(cell, 8), :] != 0.0
        for q in range(27):
            cx, cy, cz = VEL[q]
            start = cell - PITCH * cz - cy
            value = full[pl.ds(q * ROWS + start, 8), :]
            if cx:
                value = pltpu.roll(value, cx % 128, 1)
            if q != 13:
                blocked = walls[cx + 1, pl.ds(start, 8), :] != 0.0
                value = jnp.where(blocked, full[pl.ds((26 - q) * ROWS + cell, 8), :], value)
            f.append(jnp.where(solid, WEIGHT[q], value))
        done = relaxed(f, sponge, full[pl.ds(AIM * ROWS + cell, 8), :])
        for q in range(27):
            post[q, pl.ds(8 * u, 8), :] = done[q]

    @pl.when(top)
    def _():
        for q in range(9):
            post[q, pl.ds((NZ + 1) * PITCH, PITCH), :] = post[q + 18, pl.ds(NZ * PITCH, PITCH), :]


def last_kernel(full, block, columns, x_one, x_two, out, west, east, column, walls, back, done, sems):
    here_x, size_x = lax.axis_index("gx"), lax.axis_size("gx")
    top = lax.axis_index("gz") == lax.axis_size("gz") - 1
    lanes, rows = lane_ids(), row_ids()

    if size_x == 2:

        def beside(side, start):
            first = min(max(start, 0), X_ROWS - 8)
            value = x_one[pl.ds(first, 8), :]
            return pltpu.roll(value, (first - start) % 8, 0) if first != start else value

    else:

        def spread(right, left):
            west[pl.ds(PAD, X_ROWS), :] = left[...]
            east[pl.ds(PAD, X_ROWS), :] = right[...]

        by_parity("gx", x_one, x_two, spread)

        def beside(side, start):
            return (west if side < 0 else east)[pl.ds(PAD + start, 8), :]

    def strip_at(c, shift):
        cx = VEL[c][0] if c < 27 else 0
        at = rows - shift
        first = PAD + 4 * c - shift
        value = jnp.where(at < 4, columns[pl.ds(first, 8), :], columns[pl.ds(first - 4, 8), :])
        if c <= WALL and cx >= 0:
            value = jnp.where(at < 2, beside(-1, 2 * c - (cx == 0) - shift), value)
        if c <= WALL and cx <= 0:
            value = jnp.where(at >= 6, beside(1, 2 * c - 6 + (cx == 0) - shift), value)
        if c == WALL:
            value = jnp.where((at == 0) | (at == 7), 0.0, value)
        return value

    strip = [strip_at(c, 0) for c in range(CHANNELS)]
    flags_at = {cx: strip_at(WALL, cx) if cx else strip[WALL] for cx in (-1, 0, 1)}

    def moved_along(value, q):
        cx, cy, cz = VEL[q]
        step = (PITCH * cz + cy) % 128
        return pltpu.roll(value, step, 1) if step else value

    moved = []
    for q in range(27):
        cx = VEL[q][0]
        value = moved_along(strip_at(q, cx) if cx else strip[q], q)
        if q != 13:
            value = jnp.where(moved_along(flags_at[cx], q) != 0.0, strip[26 - q], value)
        moved.append(jnp.where(strip[WALL] != 0.0, WEIGHT[q], value))
    place = here_x * NX + jnp.where(rows < 4, rows - 2, rows + (NX - 6))
    place = lax.rem(place + size_x * NX, size_x * NX)
    sides = relaxed(moved, place < SPONGE, strip[AIM])
    lid = top & (lanes >= (NZ + 2) * PITCH) & (lanes < (NZ + 3) * PITCH)
    for q in range(9):
        sides[q] = jnp.where(lid, pltpu.roll(sides[q + 18], PITCH, 1), sides[q])
    for q, side in enumerate(sides + [strip[WALL]]):
        column[pl.ds(PAD + 8 * q, 8), :] = side

    def picked(wanted):
        value = None
        for sublane, (q, row) in enumerate(wanted):
            moved = column[pl.ds(PAD + 8 * q + row - sublane, 8), :]
            value = moved if value is None else jnp.where(rows == sublane, moved, value)
        return value

    packed = []
    for k in range(9):
        a, b = 3 * k + 2, 3 * k
        packed.append(
            picked([(a, 5), (a, 2), (a, 1), (a, 2), (b, 5), (b, 2), (b, 5), (b, 6)])
        )
    rest = [(3 * k + 1, row) for k in range(9) for row in (5, 2)] + [(27, 1), (27, 6)]
    packed += [picked(rest[i : i + 8]) for i in range(0, len(rest), 8)]
    packed += [jnp.zeros((8, 128), F32)] * (16 - len(packed))
    back[...] = jnp.concatenate(packed, axis=0).T

    def column_at(place, lane, start):
        return pltpu.roll(back[pl.ds(start, 8), :], (lane - place) % 128, 1)

    rim = (lanes == 0) | (lanes == 127)

    def rimmed(q, start):
        k = q // 3
        ends = column_at((8 * k + 5, 73 + 2 * k, 8 * k + 1)[q % 3], 0, PITCH + start)
        return jnp.where(rim, ends, block[q, pl.ds(start, 8), :])

    for u in range(UNITS):
        flags = full[pl.ds(WALL * ROWS + PAD + PITCH + 8 * u, 8), :]
        walls[1, pl.ds(8 * u, 8), :] = flags
        for cx, edge, place in ((1, 0, 90), (-1, 127, 91)):
            walls[cx + 1, pl.ds(8 * u, 8), :] = jnp.where(
                lanes == edge, column_at(place, edge, PITCH + 8 * u), pltpu.roll(flags, cx % 128, 1)
            )

    cells = [(z + 1) * PITCH + 2 for z in range(NZ)]
    solids = [walls[1, pl.ds(cell, 8), :] != 0.0 for cell in cells]

    def streamed(q, z):
        cx, cy, cz = VEL[q]
        cell = cells[z]
        start = cell - PITCH * cz - cy
        if cx > 0:
            side = column_at(8 * (q // 3) + 2, 0, PITCH + start)
            value = jnp.where(lanes < 2, side, pltpu.roll(block[q, pl.ds(start, 8), :], 1, 1))
        elif cx < 0:
            side = column_at(8 * (q // 3) + 6, 126, PITCH + start)
            value = jnp.where(lanes > 125, side, pltpu.roll(block[q, pl.ds(start, 8), :], 127, 1))
        else:
            value = rimmed(q, start)
        if q != 13:
            blocked = walls[cx + 1, pl.ds(start, 8), :] != 0.0
            value = jnp.where(blocked, rimmed(26 - q, cell), value)
        return jnp.where(solids[z], WEIGHT[q], value)

    copies = []
    for first, count in ((0, 9), (9, 8), (17, 6), (23, 4)):
        for q in range(first, first + count):
            for z in range(NZ):
                done[q, z] = streamed(q, z)
        part = pl.ds(first, count)
        copies.append(pltpu.make_async_copy(done.at[part], out.at[part], sems.at[len(copies)]))
        copies[-1].start()
    for copy in copies:
        copy.wait()


def swap(value, axis, turn, wrap):
    size = lax.axis_size(axis)
    pairs = [(i, (i + 1) % size) for i in range(turn, size if wrap else size - 1, 2)]
    return lax.ppermute(value, axis, pairs + [(j, i) for i, j in pairs])


def shape(*dims):
    return jax.ShapeDtypeStruct(dims, F32)


def shards(pops, solid, profile_table, profile_index):
    own, y_two, y_one = pl.pallas_call(
        first_kernel,
        out_shape=[shape(CHANNELS * NZ * 8, 128), shape(Y_ROWS, 128), shape(Y_ROWS, 128)],
        in_specs=[HBM] * 4,
        out_specs=[VMEM] * 3,
        scratch_shapes=[
            pltpu.VMEM(pops.shape, F32),
            pltpu.VMEM(solid.shape, jnp.int32),
            pltpu.SMEM(profile_table.shape[::-1], F32),
            pltpu.SMEM(profile_index.shape, jnp.int32),
            pltpu.SemaphoreType.DMA((6,)),
        ],
        compiler_params=PARAMS,
        name="collide",
    )(*(pltpu.with_memory_space_constraint(a, pltpu.HBM) for a in (pops, solid, profile_table.T, profile_index)))
    y_two = swap(y_two, "gy", 1, True)
    y_one = swap(y_one, "gy", 0, True)
    own_two, own_one = pl.pallas_call(
        ahead_kernel,
        out_shape=[shape(Z_BLOCKS * 8, 128)] * 2,
        in_specs=[VMEM],
        out_specs=[VMEM] * 2,
        compiler_params=PARAMS,
        name="pack_own",
    )(own)
    own_two = swap(own_two, "gz", 1, False)
    own_one = swap(own_one, "gz", 0, False)
    z_two, z_one = pl.pallas_call(
        second_kernel,
        out_shape=[shape(Z_ROWS, 128)] * 2,
        in_specs=[VMEM] * 2,
        out_specs=[VMEM] * 2,
        scratch_shapes=[pltpu.VMEM((4 * NZ, 128), F32)] * 2,
        compiler_params=PARAMS,
        cost_estimate=pl.CostEstimate(flops=10**9, bytes_accessed=2**20, transcendentals=0),
        name="pack_z",
    )(y_two, y_one)
    z_two = swap(z_two, "gz", 1, False)
    z_one = swap(z_one, "gz", 0, False)
    part, packed = pl.pallas_call(
        fill_kernel,
        out_shape=[shape(SLABS * ROWS, 128), shape(128, 128)],
        in_specs=[VMEM] * 5,
        out_specs=[VMEM] * 2,
        scratch_shapes=[pltpu.VMEM((4 * NZ, 128), F32)] * 2,
        compiler_params=PARAMS,
        cost_estimate=pl.CostEstimate(flops=10**6, bytes_accessed=2**22, transcendentals=0),
        name="fill",
    )(own, y_two, y_one, own_two, own_one)
    full, packed, columns, message = pl.pallas_call(
        third_kernel,
        out_shape=[
            shape(SLABS * ROWS, 128),
            shape(128, 128),
            shape(PAD + 128 + PAD, 128),
            shape(X_ROWS, 128),
        ],
        in_specs=[VMEM] * 4,
        out_specs=[VMEM] * 4,
        input_output_aliases={0: 0, 1: 1},
        compiler_params=PARAMS,
        name="pack_x",
    )(part, packed, z_two, z_one)
    x_one = swap(message, "gx", 0, True)
    x_two = x_one if lax.axis_size("gx") == 2 else swap(message, "gx", 1, True)
    block = pl.pallas_call(
        block_kernel,
        out_shape=shape(27, UNITS * 8, 128),
        in_specs=[VMEM],
        out_specs=VMEM,
        scratch_shapes=[pltpu.VMEM((3, ROWS, 128), F32)],
        compiler_params=PARAMS,
        cost_estimate=pl.CostEstimate(
            flops=27 * 20 * UNITS * 1024, bytes_accessed=2**22, transcendentals=0
        ),
        name="block",
    )(full)
    return pl.pallas_call(
        last_kernel,
        out_shape=shape(27, NZ, NY, NX),
        in_specs=[VMEM] * 5,
        out_specs=HBM,
        scratch_shapes=[
            pltpu.VMEM((PAD + X_ROWS + PAD, 128), F32),
            pltpu.VMEM((PAD + X_ROWS + PAD, 128), F32),
            pltpu.VMEM((PAD + 28 * 8 + PAD, 128), F32),
            pltpu.VMEM((3, UNITS * 8, 128), F32),
            pltpu.VMEM((128, 128), F32),
            pltpu.VMEM((27, NZ, NY, NX), F32),
            pltpu.SemaphoreType.DMA((NZ,)),
        ],
        compiler_params=PARAMS,
        name="finish",
    )(full, block, columns, x_one, x_two)


def solution(mesh):
    return jax.shard_map(
        shards,
        mesh=mesh,
        in_specs=(P(None, "gz", "gy", "gx"), P("gz", "gy", "gx"), P(None, "gz"), P("gy")),
        out_specs=P(None, "gz", "gy", "gx"),
        check_vma=False,
    )
```

```python
import functools

import jax
import jax.numpy as jnp
import numpy as np
from jax import lax
from jax.experimental import pallas as pl
from jax.experimental.pallas import tpu as pltpu
from jax.sharding import PartitionSpec as P

SPONGE = 32
TAU = 0.52
SMAG = 18.0 * 1.4142135623730951 * 0.17 * 0.17

VEL = [(cx, cy, cz) for cz in (-1, 0, 1) for cy in (-1, 0, 1) for cx in (-1, 0, 1)]
WEIGHT = [
    float(np.array([8.0 / 27.0, 2.0 / 27.0, 1.0 / 54.0, 1.0 / 216.0])[cx * cx + cy * cy + cz * cz])
    for cx, cy, cz in VEL
]
WALL, AIM, CHANNELS = 27, 28, 29
NZ, NY, NX = 4, 8, 128
PITCH = NY + 4
FLAT = (NZ + 4) * PITCH
PAD = 8
ROWS = PAD + FLAT + PAD
SLABS = CHANNELS + 6
UNITS = (NZ + 2) * PITCH // 8

PARAMS = pltpu.CompilerParams(vmem_limit_bytes=12 * 2**20)
VMEM = pl.BlockSpec(memory_space=pltpu.VMEM)
HBM = pl.BlockSpec(memory_space=pltpu.HBM)
F32 = jnp.float32

MIXED = 24
Y_ROWS = (MIXED + 1 + 9) * NZ
Z_BLOCKS = CHANNELS + 10
Z_FAR = 2 * Z_BLOCKS
Z_ROWS = -(-(Z_FAR + 2 * 12) // 8) * 8

X_ROWS = 2 * (WALL + 1)


def relaxed(f, sponge, aim):
    quad = {}
    for cz in (-1, 0, 1):
        line = {}
        for cy in (-1, 0, 1):
            base = 9 * (cz + 1) + 3 * (cy + 1)
            both = f[base + 2] + f[base]
            line[cy] = (both + f[base + 1], f[base + 2] - f[base], both)
        s = line[1][0] + line[-1][0]
        sx = line[1][1] + line[-1][1]
        quad[cz] = dict(
            n=s + line[0][0],
            y=line[1][0] - line[-1][0],
            yy=s,
            x=sx + line[0][1],
            xy=line[1][1] - line[-1][1],
            xx=line[1][2] + line[-1][2] + line[0][2],
        )
    up, mid, down = quad[1], quad[0], quad[-1]
    zz = up["n"] + down["n"]
    rho = zz + mid["n"]
    jz = up["n"] - down["n"]
    jy = up["y"] + down["y"] + mid["y"]
    jx = up["x"] + down["x"] + mid["x"]
    inverse = 1.0 / rho
    ux, uy, uz = jx * inverse, jy * inverse, jz * inverse
    third = rho * (1.0 / 3.0)
    pxx = (up["xx"] + down["xx"] + mid["xx"]) - (third + jx * ux)
    pyy = (up["yy"] + down["yy"] + mid["yy"]) - (third + jy * uy)
    pzz = zz - (third + jz * uz)
    pxy = (up["xy"] + down["xy"] + mid["xy"]) - jx * uy
    pxz = (up["x"] - down["x"]) - jx * uz
    pyz = (up["y"] - down["y"]) - jy * uz
    strain = pxx * pxx + pyy * pyy + pzz * pzz + 2.0 * (pxy * pxy + pxz * pxz + pyz * pyz)
    size = jnp.sqrt(2.0 * strain)
    tau = 0.5 * (TAU + jnp.sqrt(TAU * TAU + SMAG * size * inverse))
    omega = 1.0 / tau
    keep = 1.0 - omega
    if sponge is not None:
        keep = jnp.where(sponge, 0.0, keep)
        omega = jnp.where(sponge, 1.0, omega)
        ux = jnp.where(sponge, aim, ux)
        uy = jnp.where(sponge, 0.0, uy)
        uz = jnp.where(sponge, 0.0, uz)
    square = 1.0 - 1.5 * (ux * ux + uy * uy + uz * uz)
    vx, vy, vz = 3.0 * ux, 3.0 * uy, 3.0 * uz
    share = rho * omega
    weighted = {w: share * w for w in sorted(set(WEIGHT))}
    post = [None] * 27
    for q in range(14):
        cx, cy, cz = VEL[q]
        along = None
        for c, v in ((cx, vx), (cy, vy), (cz, vz)):
            if c:
                along = (v if c > 0 else -v) if along is None else (along + v if c > 0 else along - v)
        scale = weighted[WEIGHT[q]]
        if along is None:
            post[q] = keep * f[q] + scale * square
            continue
        even = square + 0.5 * along * along
        post[q] = keep * f[q] + scale * (even + along)
        post[26 - q] = keep * f[26 - q] + scale * (even - along)
    return post


def lane_ids():
    return lax.broadcasted_iota(jnp.int32, (8, 128), 1)


def row_ids():
    return lax.broadcasted_iota(jnp.int32, (8, 128), 0)


def by_parity(axis, one, two, body):
    even = lax.rem(lax.axis_index(axis), 2) == 0
    pl.when(even)(lambda: body(one, two))
    pl.when(jnp.logical_not(even))(lambda: body(two, one))


def z_blocks(near, far, part):
    blocks = [(c, near) for c in range(CHANNELS)]
    return blocks + [(9 * part + k, far) for k in range(9)] + [(WALL, far)]


def first_kernel(pops_at, solid_at, table_at, index_at, own, two, one, *scratch):
    pops, solid, table, index, sems = scratch
    groups = [(pops_at.at[pl.ds(q, 9)], pops.at[pl.ds(q, 9)]) for q in (0, 9, 18)]
    small = [(table_at, table), (index_at, index)]
    copies = [
        pltpu.make_async_copy(source, target, sems.at[i])
        for i, (source, target) in enumerate([*small, *groups, (solid_at, solid)])
    ]
    for copy in copies:
        copy.start()
    for copy in copies[:2]:
        copy.wait()
    lanes, rows = lane_ids(), row_ids()
    sponge = (lax.axis_index("gx") * NX + lanes) < SPONGE
    profiles = [index[y] for y in range(NY)]
    aims = []
    for z in range(NZ):
        aim = jnp.zeros((8, 128), F32)
        for y, profile in enumerate(profiles):
            aim = jnp.where(rows == y, table[z, profile], aim)
        aims.append(aim)
    for copy in copies[2:-1]:
        copy.wait()
    for z, aim in enumerate(aims):
        post = relaxed([pops[q, z] for q in range(27)], sponge, aim)
        for q in range(27):
            own[pl.ds((q * NZ + z) * 8, 8), :] = post[q]
        own[pl.ds((AIM * NZ + z) * 8, 8), :] = aim
    copies[-1].wait()
    for z in range(NZ):
        own[pl.ds((WALL * NZ + z) * 8, 8), :] = solid[z].astype(F32)

    def pack(yup, ydown):
        inside = lax.rem(lanes, 4)
        for out, edge, second, part in ((yup, 7, 6, 6), (ydown, 0, 1, 0)):
            back = 15 - part
            for first, count, place in ((0, back, 0), (back + 3, 24 - back, back)):
                out[pl.ds(place * NZ, count * NZ), :] = own[
                    pl.ds(first * NZ * 8 + edge, count * NZ, stride=8), :
                ]
            for z in range(NZ):
                west, east, aim, flag = (
                    own[pl.ds((c * NZ + z) * 8, 8), :] for c in (back, back + 2, AIM, WALL)
                )
                mixed = jnp.where(inside < 2, jnp.where(inside == 0, west, aim), flag)
                mixed = jnp.where(inside == 3, east, mixed)
                out[pl.ds(MIXED * NZ + z, 1), :] = mixed[edge : edge + 1]
            for a in range(3):
                out[pl.ds((MIXED + 1 + 3 * a) * NZ, 3 * NZ), :] = own[
                    pl.ds((9 * a + part) * NZ * 8 + second, 3 * NZ, stride=8), :
                ]

    by_parity("gy", one, two, pack)


def ahead_kernel(own, two, one):
    def pack(zup, zdown):
        for out, first, second, part in ((zup, NZ - 1, NZ - 2, 2), (zdown, 0, 1, 0)):
            for k, (c, z) in enumerate(z_blocks(first, second, part)):
                out[pl.ds(8 * k, 8), :] = own[pl.ds((c * NZ + z) * 8, 8), :]

    by_parity("gz", one, two, pack)


def y_runs(part):
    back = 15 - part
    return (0, back, 0), (back, 3, None), (back + 3, 24 - back, back)


def spread_mixed(below, above, flags, aims):
    flags[pl.ds(0, NZ), :] = below[pl.ds(MIXED * NZ, NZ), :]
    flags[pl.ds(NZ, NZ), :] = above[pl.ds(MIXED * NZ, NZ), :]
    mixed = flags[pl.ds(0, 2 * NZ), :]
    inside = lax.rem(lane_ids(), 4)
    moved = {k: pltpu.roll(mixed, k % 128, 1) if k else mixed for k in (-2, -1, 0, 1, 2)}

    def from_lane(source):
        value = moved[0]
        for lane in range(4):
            if lane != source:
                value = jnp.where(inside == lane, moved[lane - source], value)
        return value

    aims[pl.ds(0, 2 * NZ), :] = from_lane(1)
    flags[pl.ds(0, 2 * NZ), :] = from_lane(2)


def second_kernel(y_two, y_one, z_one, z_two, flags, aims):
    def pack(above, below):
        spread_mixed(below, above, flags, aims)
        by_parity(
            "gz",
            z_one,
            z_two,
            lambda zup, zdown: pack_planes(below, above, flags, aims, zup, zdown),
        )

    by_parity("gy", y_one, y_two, pack)


def pack_planes(below, above, flags, aims, zup, zdown):
    for out, first, second, part in ((zup, NZ - 1, NZ - 2, 2), (zdown, 0, 1, 0)):
        for side, (halo, inward) in enumerate(((below, 6), (above, 0))):
            near = side * Z_BLOCKS
            for channel, count, place in y_runs(inward):
                if place is None:
                    row = halo[pl.ds(MIXED * NZ + first, 1), :]
                    out[pl.ds(near + channel, 3), :] = jnp.broadcast_to(row, (3, 128))
                else:
                    out[pl.ds(near + channel, count), :] = halo[
                        pl.ds(place * NZ + first, count, stride=NZ), :
                    ]
            out[pl.ds(near + WALL, 1), :] = flags[pl.ds(side * NZ + first, 1), :]
            out[pl.ds(near + AIM, 1), :] = aims[pl.ds(side * NZ + first, 1), :]
            place = 15 if part else 0
            for k, count in ((0, 8), (8, 1)):
                out[pl.ds(near + CHANNELS + k, count), :] = halo[
                    pl.ds((place + k) * NZ + second, count, stride=NZ if count > 1 else 1), :
                ]
            out[pl.ds(near + Z_BLOCKS - 1, 1), :] = flags[pl.ds(side * NZ + second, 1), :]
            far = Z_FAR + 12 * side
            start = (MIXED + 1) * NZ
            out[pl.ds(far, 8), :] = halo[pl.ds(start + first, 8, stride=NZ), :]
            out[pl.ds(far + 8, 1), :] = halo[pl.ds(start + 8 * NZ + first, 1), :]
            for k in range(3):
                row = halo[pl.ds(start + (3 * part + k) * NZ + second, 1), :]
                out[pl.ds(far + 9 + k, 1), :] = row


def plane_at(z):
    return PAD + (z + 2) * PITCH


def add_rows(full, flags, aims, above, below):
    spread_mixed(below, above, flags, aims)

    def put(channel, row, source):
        full[pl.ds(channel * ROWS + plane_at(0) + row, NZ, stride=PITCH), :] = source

    sides = ((below, 1, 0, 6), (above, PITCH - 2, PITCH - 1, 0))
    for side, (halo, near, far, inward) in enumerate(sides):
        for first, count, place in y_runs(inward):
            for k in range(count):
                row = MIXED if place is None else place + k
                put(first + k, near, halo[pl.ds(row * NZ, NZ), :])
        flag = flags[pl.ds(side * NZ, NZ), :]
        put(WALL, near, flag)
        put(WALL, far, flag)
        put(AIM, near, aims[pl.ds(side * NZ, NZ), :])
        for k in range(9):
            q = 9 * (k // 3) + inward + k % 3
            put(q, far, halo[pl.ds((MIXED + 1 + k) * NZ, NZ), :])


def add_own_planes(full, ceiling, floor):
    for halo, near, far, part in ((floor, -1, -2, 2), (ceiling, NZ, NZ + 1, 0)):
        for k, (c, z) in enumerate(z_blocks(near, far, part)):
            full[pl.ds(c * ROWS + plane_at(z) + 2, 8), :] = halo[pl.ds(8 * k, 8), :]


def add_planes(full, ceiling, floor):
    def put(count, channel, z, row, source):
        start = channel * ROWS + plane_at(z) + row
        full[pl.ds(start, count, stride=ROWS), :] = source

    for halo, near, far, part in ((floor, -1, -2, 2), (ceiling, NZ, NZ + 1, 0)):
        for side, (row, beyond, group) in enumerate(((1, 0, 2), (PITCH - 2, PITCH - 1, 0))):
            start = side * Z_BLOCKS
            put(CHANNELS, 0, near, row, halo[pl.ds(start, CHANNELS), :])
            put(9, 9 * part, far, row, halo[pl.ds(start + CHANNELS, 9), :])
            first, second = (halo[pl.ds(start + k, 1), :] for k in (WALL, Z_BLOCKS - 1))
            put(1, WALL, far, row, second)
            start = Z_FAR + 12 * side
            for k in range(3):
                put(3, 9 * k + 3 * group, near, beyond, halo[pl.ds(start + 3 * k, 3), :])
            put(3, 9 * part + 3 * group, far, beyond, halo[pl.ds(start + 9, 3), :])
            put(1, WALL, near, beyond, first)
            put(1, WALL, far, beyond, second)


def pack_columns(full, pack, tiles):
    slot = lane_ids() // 4
    for t in tiles:
        packed = jnp.zeros((8, 128), F32)
        for c in range(CHANNELS):
            moved = pltpu.roll(full[pl.ds(c * ROWS + PAD + 8 * t, 8), :], (4 * c + 2) % 128, 1)
            packed = jnp.where(slot == c, moved, packed)
        pack[pl.ds(8 * t, 8), :] = packed


OWN_TILES = range(2 * PITCH // 8, (NZ + 2) * PITCH // 8)


def fill_kernel(own, y_two, y_one, two, one, full, pack, flags, aims):
    for c in range(CHANNELS):
        for z in range(NZ):
            full[pl.ds(c * ROWS + plane_at(z) + 2, 8), :] = own[pl.ds((c * NZ + z) * 8, 8), :]
    by_parity("gy", y_one, y_two, functools.partial(add_rows, full, flags, aims))
    by_parity("gz", one, two, functools.partial(add_own_planes, full))
    pack_columns(full, pack, OWN_TILES)
    pack[pl.ds(FLAT, 128 - FLAT), :] = jnp.zeros((128 - FLAT, 128), F32)


def third_kernel(part, packed, z_one, z_two, full, pack, columns, message):
    last = lax.axis_size("gz") - 1
    here = lax.axis_index("gz")
    by_parity("gz", z_one, z_two, functools.partial(add_planes, full))

    @pl.when(here == 0)
    def _():
        full[pl.ds(WALL * ROWS + plane_at(-1), PITCH), :] = jnp.ones((PITCH, 128), F32)

    @pl.when(here == last)
    def _():
        for q in range(9):
            full[pl.ds(q * ROWS + plane_at(NZ), PITCH), :] = full[pl.ds((q + 18) * ROWS + plane_at(NZ - 1), PITCH), :]

    pack_columns(full, pack, [t for t in range(FLAT // 8) if t not in OWN_TILES])
    columns[pl.ds(PAD, 128), :] = pack[...].T

    def row(c, i, count):
        return columns[pl.ds(PAD + 4 * c + i, count), :]

    def returned(q, near, far):
        cx, cy, cz = VEL[q]
        step = (-PITCH * cz - cy) % 128
        value = row(26 - q, near, 8)
        value = pltpu.roll(value, step, 1) if step else value
        return jnp.where(row(WALL, far, 8) != 0.0, value, row(q, far, 8))[:1]

    for c in range(WALL + 1):
        cx = VEL[c][0] if c < 27 else 0
        if cx == 0:
            message[pl.ds(2 * c, 2), :] = row(c, 1, 2)
        elif cx > 0:
            message[pl.ds(2 * c, 1), :] = returned(c, 1, 0)
            message[pl.ds(2 * c + 1, 1), :] = row(c, 1, 1)
        else:
            message[pl.ds(2 * c, 1), :] = row(c, 2, 1)
            message[pl.ds(2 * c + 1, 1), :] = returned(c, 2, 3)


def block_kernel(full, post, walls):
    top = lax.axis_index("gz") == lax.axis_size("gz") - 1
    sponge = (lax.axis_index("gx") * NX + lane_ids()) < SPONGE
    for t in range(ROWS // 8):
        rows = pl.ds(8 * t, 8)
        flags = full[pl.ds(WALL * ROWS + 8 * t, 8), :]
        for cx in (-1, 0, 1):
            walls[cx + 1, rows, :] = pltpu.roll(flags, cx % 128, 1) if cx else flags
    for u in range(UNITS):
        cell = PAD + PITCH + 8 * u
        f = []
        solid = walls[1, pl.ds(cell, 8), :] != 0.0
        for q in range(27):
            cx, cy, cz = VEL[q]
            start = cell - PITCH * cz - cy
            value = full[pl.ds(q * ROWS + start, 8), :]
            if cx:
                value = pltpu.roll(value, cx % 128, 1)
            if q != 13:
                blocked = walls[cx + 1, pl.ds(start, 8), :] != 0.0
                value = jnp.where(blocked, full[pl.ds((26 - q) * ROWS + cell, 8), :], value)
            f.append(jnp.where(solid, WEIGHT[q], value))
        done = relaxed(f, sponge, full[pl.ds(AIM * ROWS + cell, 8), :])
        for q in range(27):
            post[q, pl.ds(8 * u, 8), :] = done[q]

    @pl.when(top)
    def _():
        for q in range(9):
            post[q, pl.ds((NZ + 1) * PITCH, PITCH), :] = post[q + 18, pl.ds(NZ * PITCH, PITCH), :]


def last_kernel(full, block, columns, x_one, x_two, out, west, east, column, walls, back, done, sems):
    here_x, size_x = lax.axis_index("gx"), lax.axis_size("gx")
    top = lax.axis_index("gz") == lax.axis_size("gz") - 1
    lanes, rows = lane_ids(), row_ids()

    if size_x == 2:

        def beside(side, start):
            first = min(max(start, 0), X_ROWS - 8)
            value = x_one[pl.ds(first, 8), :]
            return pltpu.roll(value, (first - start) % 8, 0) if first != start else value

    else:

        def spread(right, left):
            west[pl.ds(PAD, X_ROWS), :] = left[...]
            east[pl.ds(PAD, X_ROWS), :] = right[...]

        by_parity("gx", x_one, x_two, spread)

        def beside(side, start):
            return (west if side < 0 else east)[pl.ds(PAD + start, 8), :]

    def strip_at(c, shift):
        cx = VEL[c][0] if c < 27 else 0
        at = rows - shift
        first = PAD + 4 * c - shift
        value = jnp.where(at < 4, columns[pl.ds(first, 8), :], columns[pl.ds(first - 4, 8), :])
        if c <= WALL and cx >= 0:
            value = jnp.where(at < 2, beside(-1, 2 * c - (cx == 0) - shift), value)
        if c <= WALL and cx <= 0:
            value = jnp.where(at >= 6, beside(1, 2 * c - 6 + (cx == 0) - shift), value)
        if c == WALL:
            value = jnp.where((at == 0) | (at == 7), 0.0, value)
        return value

    strip = [strip_at(c, 0) for c in range(CHANNELS)]
    flags_at = {cx: strip_at(WALL, cx) if cx else strip[WALL] for cx in (-1, 0, 1)}

    def moved_along(value, q):
        cx, cy, cz = VEL[q]
        step = (PITCH * cz + cy) % 128
        return pltpu.roll(value, step, 1) if step else value

    moved = []
    for q in range(27):
        cx = VEL[q][0]
        value = moved_along(strip_at(q, cx) if cx else strip[q], q)
        if q != 13:
            value = jnp.where(moved_along(flags_at[cx], q) != 0.0, strip[26 - q], value)
        moved.append(jnp.where(strip[WALL] != 0.0, WEIGHT[q], value))
    place = here_x * NX + jnp.where(rows < 4, rows - 2, rows + (NX - 6))
    place = lax.rem(place + size_x * NX, size_x * NX)
    sides = relaxed(moved, place < SPONGE, strip[AIM])
    lid = top & (lanes >= (NZ + 2) * PITCH) & (lanes < (NZ + 3) * PITCH)
    for q in range(9):
        sides[q] = jnp.where(lid, pltpu.roll(sides[q + 18], PITCH, 1), sides[q])
    for q, side in enumerate(sides + [strip[WALL]]):
        column[pl.ds(PAD + 8 * q, 8), :] = side

    def picked(wanted):
        value = None
        for sublane, (q, row) in enumerate(wanted):
            moved = column[pl.ds(PAD + 8 * q + row - sublane, 8), :]
            value = moved if value is None else jnp.where(rows == sublane, moved, value)
        return value

    packed = []
    for k in range(9):
        a, b = 3 * k + 2, 3 * k
        packed.append(
            picked([(a, 5), (a, 2), (a, 1), (a, 2), (b, 5), (b, 2), (b, 5), (b, 6)])
        )
    rest = [(3 * k + 1, row) for k in range(9) for row in (5, 2)] + [(27, 1), (27, 6)]
    packed += [picked(rest[i : i + 8]) for i in range(0, len(rest), 8)]
    packed += [jnp.zeros((8, 128), F32)] * (16 - len(packed))
    back[...] = jnp.concatenate(packed, axis=0).T

    def column_at(place, lane, start):
        return pltpu.roll(back[pl.ds(start, 8), :], (lane - place) % 128, 1)

    rim = (lanes == 0) | (lanes == 127)

    def rimmed(q, start):
        k = q // 3
        ends = column_at((8 * k + 5, 73 + 2 * k, 8 * k + 1)[q % 3], 0, PITCH + start)
        return jnp.where(rim, ends, block[q, pl.ds(start, 8), :])

    for u in range(UNITS):
        flags = full[pl.ds(WALL * ROWS + PAD + PITCH + 8 * u, 8), :]
        walls[1, pl.ds(8 * u, 8), :] = flags
        for cx, edge, place in ((1, 0, 90), (-1, 127, 91)):
            walls[cx + 1, pl.ds(8 * u, 8), :] = jnp.where(
                lanes == edge, column_at(place, edge, PITCH + 8 * u), pltpu.roll(flags, cx % 128, 1)
            )

    cells = [(z + 1) * PITCH + 2 for z in range(NZ)]
    solids = [walls[1, pl.ds(cell, 8), :] != 0.0 for cell in cells]

    def streamed(q, z):
        cx, cy, cz = VEL[q]
        cell = cells[z]
        start = cell - PITCH * cz - cy
        if cx > 0:
            side = column_at(8 * (q // 3) + 2, 0, PITCH + start)
            value = jnp.where(lanes < 2, side, pltpu.roll(block[q, pl.ds(start, 8), :], 1, 1))
        elif cx < 0:
            side = column_at(8 * (q // 3) + 6, 126, PITCH + start)
            value = jnp.where(lanes > 125, side, pltpu.roll(block[q, pl.ds(start, 8), :], 127, 1))
        else:
            value = rimmed(q, start)
        if q != 13:
            blocked = walls[cx + 1, pl.ds(start, 8), :] != 0.0
            value = jnp.where(blocked, rimmed(26 - q, cell), value)
        return jnp.where(solids[z], WEIGHT[q], value)

    copies = []
    for first, count in ((0, 9), (9, 8), (17, 6), (23, 4)):
        for q in range(first, first + count):
            for z in range(NZ):
                done[q, z] = streamed(q, z)
        part = pl.ds(first, count)
        copies.append(pltpu.make_async_copy(done.at[part], out.at[part], sems.at[len(copies)]))
        copies[-1].start()
    for copy in copies:
        copy.wait()


def swap(value, axis, turn, wrap):
    size = lax.axis_size(axis)
    pairs = [(i, (i + 1) % size) for i in range(turn, size if wrap else size - 1, 2)]
    return lax.ppermute(value, axis, pairs + [(j, i) for i, j in pairs])


def shape(*dims):
    return jax.ShapeDtypeStruct(dims, F32)


def shards(pops, solid, profile_table, profile_index):
    own, y_two, y_one = pl.pallas_call(
        first_kernel,
        out_shape=[shape(CHANNELS * NZ * 8, 128), shape(Y_ROWS, 128), shape(Y_ROWS, 128)],
        in_specs=[HBM] * 4,
        out_specs=[VMEM] * 3,
        scratch_shapes=[
            pltpu.VMEM(pops.shape, F32),
            pltpu.VMEM(solid.shape, jnp.int32),
            pltpu.SMEM(profile_table.shape[::-1], F32),
            pltpu.SMEM(profile_index.shape, jnp.int32),
            pltpu.SemaphoreType.DMA((6,)),
        ],
        compiler_params=PARAMS,
        name="collide",
    )(*(pltpu.with_memory_space_constraint(a, pltpu.HBM) for a in (pops, solid, profile_table.T, profile_index)))
    y_two = swap(y_two, "gy", 1, True)
    y_one = swap(y_one, "gy", 0, True)
    own_two, own_one = pl.pallas_call(
        ahead_kernel,
        out_shape=[shape(Z_BLOCKS * 8, 128)] * 2,
        in_specs=[VMEM],
        out_specs=[VMEM] * 2,
        compiler_params=PARAMS,
        name="pack_own",
    )(own)
    own_two = swap(own_two, "gz", 1, False)
    own_one = swap(own_one, "gz", 0, False)
    z_one, z_two = pl.pallas_call(
        second_kernel,
        out_shape=[shape(Z_ROWS, 128)] * 2,
        in_specs=[VMEM] * 2,
        out_specs=[VMEM] * 2,
        scratch_shapes=[pltpu.VMEM((4 * NZ, 128), F32)] * 2,
        compiler_params=PARAMS,
        cost_estimate=pl.CostEstimate(flops=10**9, bytes_accessed=2**20, transcendentals=0),
        name="pack_z",
    )(y_two, y_one)
    z_one = swap(z_one, "gz", 0, False)
    z_two = swap(z_two, "gz", 1, False)
    part, packed = pl.pallas_call(
        fill_kernel,
        out_shape=[shape(SLABS * ROWS, 128), shape(128, 128)],
        in_specs=[VMEM] * 5,
        out_specs=[VMEM] * 2,
        scratch_shapes=[pltpu.VMEM((4 * NZ, 128), F32)] * 2,
        compiler_params=PARAMS,
        cost_estimate=pl.CostEstimate(flops=10**6, bytes_accessed=2**22, transcendentals=0),
        name="fill",
    )(own, y_two, y_one, own_two, own_one)
    full, packed, columns, message = pl.pallas_call(
        third_kernel,
        out_shape=[
            shape(SLABS * ROWS, 128),
            shape(128, 128),
            shape(PAD + 128 + PAD, 128),
            shape(X_ROWS, 128),
        ],
        in_specs=[VMEM] * 4,
        out_specs=[VMEM] * 4,
        input_output_aliases={0: 0, 1: 1},
        compiler_params=PARAMS,
        name="pack_x",
    )(part, packed, z_one, z_two)
    x_one = swap(message, "gx", 0, True)
    x_two = x_one if lax.axis_size("gx") == 2 else swap(message, "gx", 1, True)
    block = pl.pallas_call(
        block_kernel,
        out_shape=shape(27, UNITS * 8, 128),
        in_specs=[VMEM],
        out_specs=VMEM,
        scratch_shapes=[pltpu.VMEM((3, ROWS, 128), F32)],
        compiler_params=PARAMS,
        cost_estimate=pl.CostEstimate(
            flops=27 * 20 * UNITS * 1024, bytes_accessed=2**22, transcendentals=0
        ),
        name="block",
    )(full)
    return pl.pallas_call(
        last_kernel,
        out_shape=shape(27, NZ, NY, NX),
        in_specs=[VMEM] * 5,
        out_specs=HBM,
        scratch_shapes=[
            pltpu.VMEM((PAD + X_ROWS + PAD, 128), F32),
            pltpu.VMEM((PAD + X_ROWS + PAD, 128), F32),
            pltpu.VMEM((PAD + 28 * 8 + PAD, 128), F32),
            pltpu.VMEM((3, UNITS * 8, 128), F32),
            pltpu.VMEM((128, 128), F32),
            pltpu.VMEM((27, NZ, NY, NX), F32),
            pltpu.SemaphoreType.DMA((NZ,)),
        ],
        compiler_params=PARAMS,
        name="finish",
    )(full, block, columns, x_one, x_two)


def solution(mesh):
    return jax.shard_map(
        shards,
        mesh=mesh,
        in_specs=(P(None, "gz", "gy", "gx"), P("gz", "gy", "gx"), P(None, "gz"), P("gy")),
        out_specs=P(None, "gz", "gy", "gx"),
        check_vma=False,
    )
```

```python
import functools

import jax
import jax.numpy as jnp
import numpy as np
from jax import lax
from jax.experimental import pallas as pl
from jax.experimental.pallas import tpu as pltpu
from jax.sharding import PartitionSpec as P

SPONGE = 32
TAU = 0.52
SMAG = 18.0 * 1.4142135623730951 * 0.17 * 0.17

VEL = [(cx, cy, cz) for cz in (-1, 0, 1) for cy in (-1, 0, 1) for cx in (-1, 0, 1)]
WEIGHT = [
    float(np.array([8.0 / 27.0, 2.0 / 27.0, 1.0 / 54.0, 1.0 / 216.0])[cx * cx + cy * cy + cz * cz])
    for cx, cy, cz in VEL
]
WALL, AIM, CHANNELS = 27, 28, 29
NZ, NY, NX = 4, 8, 128
PITCH = NY + 4
FLAT = (NZ + 4) * PITCH
PAD = 8
ROWS = PAD + FLAT + PAD
SLABS = CHANNELS + 6
UNITS = (NZ + 2) * PITCH // 8

PARAMS = pltpu.CompilerParams(vmem_limit_bytes=12 * 2**20)
VMEM = pl.BlockSpec(memory_space=pltpu.VMEM)
HBM = pl.BlockSpec(memory_space=pltpu.HBM)
F32 = jnp.float32

MIXED = 24
Y_ROWS = (MIXED + 1 + 9) * NZ
Z_BLOCKS = CHANNELS + 10
Z_FAR = 2 * Z_BLOCKS
Z_ROWS = -(-(Z_FAR + 2 * 12) // 8) * 8

X_ROWS = 2 * (WALL + 1)


def relaxed(f, sponge, aim):
    quad = {}
    for cz in (-1, 0, 1):
        line = {}
        for cy in (-1, 0, 1):
            base = 9 * (cz + 1) + 3 * (cy + 1)
            both = f[base + 2] + f[base]
            line[cy] = (both + f[base + 1], f[base + 2] - f[base], both)
        s = line[1][0] + line[-1][0]
        sx = line[1][1] + line[-1][1]
        quad[cz] = dict(
            n=s + line[0][0],
            y=line[1][0] - line[-1][0],
            yy=s,
            x=sx + line[0][1],
            xy=line[1][1] - line[-1][1],
            xx=line[1][2] + line[-1][2] + line[0][2],
        )
    up, mid, down = quad[1], quad[0], quad[-1]
    zz = up["n"] + down["n"]
    rho = zz + mid["n"]
    jz = up["n"] - down["n"]
    jy = up["y"] + down["y"] + mid["y"]
    jx = up["x"] + down["x"] + mid["x"]
    inverse = 1.0 / rho
    ux, uy, uz = jx * inverse, jy * inverse, jz * inverse
    third = rho * (1.0 / 3.0)
    pxx = (up["xx"] + down["xx"] + mid["xx"]) - (third + jx * ux)
    pyy = (up["yy"] + down["yy"] + mid["yy"]) - (third + jy * uy)
    pzz = zz - (third + jz * uz)
    pxy = (up["xy"] + down["xy"] + mid["xy"]) - jx * uy
    pxz = (up["x"] - down["x"]) - jx * uz
    pyz = (up["y"] - down["y"]) - jy * uz
    strain = pxx * pxx + pyy * pyy + pzz * pzz + 2.0 * (pxy * pxy + pxz * pxz + pyz * pyz)
    size = jnp.sqrt(2.0 * strain)
    tau = 0.5 * (TAU + jnp.sqrt(TAU * TAU + SMAG * size * inverse))
    omega = 1.0 / tau
    keep = 1.0 - omega
    if sponge is not None:
        keep = jnp.where(sponge, 0.0, keep)
        omega = jnp.where(sponge, 1.0, omega)
        ux = jnp.where(sponge, aim, ux)
        uy = jnp.where(sponge, 0.0, uy)
        uz = jnp.where(sponge, 0.0, uz)
    square = 1.0 - 1.5 * (ux * ux + uy * uy + uz * uz)
    vx, vy, vz = 3.0 * ux, 3.0 * uy, 3.0 * uz
    share = rho * omega
    weighted = {w: share * w for w in sorted(set(WEIGHT))}
    post = [None] * 27
    for q in range(14):
        cx, cy, cz = VEL[q]
        along = None
        for c, v in ((cx, vx), (cy, vy), (cz, vz)):
            if c:
                along = (v if c > 0 else -v) if along is None else (along + v if c > 0 else along - v)
        scale = weighted[WEIGHT[q]]
        if along is None:
            post[q] = keep * f[q] + scale * square
            continue
        even = square + 0.5 * along * along
        post[q] = keep * f[q] + scale * (even + along)
        post[26 - q] = keep * f[26 - q] + scale * (even - along)
    return post


def lane_ids():
    return lax.broadcasted_iota(jnp.int32, (8, 128), 1)


def row_ids():
    return lax.broadcasted_iota(jnp.int32, (8, 128), 0)


def by_parity(axis, one, two, body):
    even = lax.rem(lax.axis_index(axis), 2) == 0
    pl.when(even)(lambda: body(one, two))
    pl.when(jnp.logical_not(even))(lambda: body(two, one))


def by_roles(first, second, body):
    even = lax.rem(lax.axis_index("gz"), 2) == 0
    pl.when(even)(lambda: by_parity("gy", second, first, body))
    pl.when(jnp.logical_not(even))(lambda: by_parity("gy", first, second, body))


def z_blocks(near, far, part):
    blocks = [(c, near) for c in range(CHANNELS)]
    return blocks + [(9 * part + k, far) for k in range(9)] + [(WALL, far)]


def first_kernel(pops_at, solid_at, table_at, index_at, own, first_out, second_out, *scratch):
    pops, solid, table, index, sems = scratch
    groups = [(pops_at.at[pl.ds(q, 9)], pops.at[pl.ds(q, 9)]) for q in (0, 9, 18)]
    small = [(table_at, table), (index_at, index)]
    copies = [
        pltpu.make_async_copy(source, target, sems.at[i])
        for i, (source, target) in enumerate([*small, *groups, (solid_at, solid)])
    ]
    for copy in copies:
        copy.start()
    for copy in copies[:2]:
        copy.wait()
    lanes, rows = lane_ids(), row_ids()
    sponge = (lax.axis_index("gx") * NX + lanes) < SPONGE
    profiles = [index[y] for y in range(NY)]
    aims = []
    for z in range(NZ):
        aim = jnp.zeros((8, 128), F32)
        for y, profile in enumerate(profiles):
            aim = jnp.where(rows == y, table[z, profile], aim)
        aims.append(aim)
    for copy in copies[2:-1]:
        copy.wait()
    for z, aim in enumerate(aims):
        post = relaxed([pops[q, z] for q in range(27)], sponge, aim)
        for q in range(27):
            own[pl.ds((q * NZ + z) * 8, 8), :] = post[q]
        own[pl.ds((AIM * NZ + z) * 8, 8), :] = aim
    copies[-1].wait()
    for z in range(NZ):
        own[pl.ds((WALL * NZ + z) * 8, 8), :] = solid[z].astype(F32)

    def pack(yup, ydown):
        inside = lax.rem(lanes, 4)
        for out, edge, second, part in ((yup, 7, 6, 6), (ydown, 0, 1, 0)):
            back = 15 - part
            for first, count, place in ((0, back, 0), (back + 3, 24 - back, back)):
                out[pl.ds(place * NZ, count * NZ), :] = own[
                    pl.ds(first * NZ * 8 + edge, count * NZ, stride=8), :
                ]
            for z in range(NZ):
                west, east, aim, flag = (
                    own[pl.ds((c * NZ + z) * 8, 8), :] for c in (back, back + 2, AIM, WALL)
                )
                mixed = jnp.where(inside < 2, jnp.where(inside == 0, west, aim), flag)
                mixed = jnp.where(inside == 3, east, mixed)
                out[pl.ds(MIXED * NZ + z, 1), :] = mixed[edge : edge + 1]
            for a in range(3):
                out[pl.ds((MIXED + 1 + 3 * a) * NZ, 3 * NZ), :] = own[
                    pl.ds((9 * a + part) * NZ * 8 + second, 3 * NZ, stride=8), :
                ]

    by_roles(first_out, second_out, pack)


def ahead_kernel(own, two, one):
    def pack(zup, zdown):
        for out, first, second, part in ((zup, NZ - 1, NZ - 2, 2), (zdown, 0, 1, 0)):
            for k, (c, z) in enumerate(z_blocks(first, second, part)):
                out[pl.ds(8 * k, 8), :] = own[pl.ds((c * NZ + z) * 8, 8), :]

    by_parity("gz", one, two, pack)


def y_runs(part):
    back = 15 - part
    return (0, back, 0), (back, 3, None), (back + 3, 24 - back, back)


def spread_mixed(below, above, flags, aims):
    flags[pl.ds(0, NZ), :] = below[pl.ds(MIXED * NZ, NZ), :]
    flags[pl.ds(NZ, NZ), :] = above[pl.ds(MIXED * NZ, NZ), :]
    mixed = flags[pl.ds(0, 2 * NZ), :]
    inside = lax.rem(lane_ids(), 4)
    moved = {k: pltpu.roll(mixed, k % 128, 1) if k else mixed for k in (-2, -1, 0, 1, 2)}

    def from_lane(source):
        value = moved[0]
        for lane in range(4):
            if lane != source:
                value = jnp.where(inside == lane, moved[lane - source], value)
        return value

    aims[pl.ds(0, 2 * NZ), :] = from_lane(1)
    flags[pl.ds(0, 2 * NZ), :] = from_lane(2)


def second_kernel(y_first, y_second, z_one, z_two, flags, aims):
    def pack(zup, zdown, above, below):
        spread_mixed(below, above, flags, aims)
        pack_planes(below, above, flags, aims, zup, zdown)

    even = lax.rem(lax.axis_index("gz"), 2) == 0
    ways = ((even, y_second, y_first, z_one, z_two), (~even, y_first, y_second, z_two, z_one))
    for here, one, two, zup, zdown in ways:
        pl.when(here)(
            functools.partial(by_parity, "gy", one, two, functools.partial(pack, zup, zdown))
        )


def pack_planes(below, above, flags, aims, zup, zdown):
    for out, first, second, part in ((zup, NZ - 1, NZ - 2, 2), (zdown, 0, 1, 0)):
        for side, (halo, inward) in enumerate(((below, 6), (above, 0))):
            near = side * Z_BLOCKS
            for channel, count, place in y_runs(inward):
                if place is None:
                    row = halo[pl.ds(MIXED * NZ + first, 1), :]
                    out[pl.ds(near + channel, 3), :] = jnp.broadcast_to(row, (3, 128))
                else:
                    out[pl.ds(near + channel, count), :] = halo[
                        pl.ds(place * NZ + first, count, stride=NZ), :
                    ]
            out[pl.ds(near + WALL, 1), :] = flags[pl.ds(side * NZ + first, 1), :]
            out[pl.ds(near + AIM, 1), :] = aims[pl.ds(side * NZ + first, 1), :]
            place = 15 if part else 0
            for k, count in ((0, 8), (8, 1)):
                out[pl.ds(near + CHANNELS + k, count), :] = halo[
                    pl.ds((place + k) * NZ + second, count, stride=NZ if count > 1 else 1), :
                ]
            out[pl.ds(near + Z_BLOCKS - 1, 1), :] = flags[pl.ds(side * NZ + second, 1), :]
            far = Z_FAR + 12 * side
            start = (MIXED + 1) * NZ
            out[pl.ds(far, 8), :] = halo[pl.ds(start + first, 8, stride=NZ), :]
            out[pl.ds(far + 8, 1), :] = halo[pl.ds(start + 8 * NZ + first, 1), :]
            for k in range(3):
                row = halo[pl.ds(start + (3 * part + k) * NZ + second, 1), :]
                out[pl.ds(far + 9 + k, 1), :] = row


def plane_at(z):
    return PAD + (z + 2) * PITCH


def add_rows(full, flags, aims, above, below):
    spread_mixed(below, above, flags, aims)

    def put(channel, row, source):
        full[pl.ds(channel * ROWS + plane_at(0) + row, NZ, stride=PITCH), :] = source

    sides = ((below, 1, 0, 6), (above, PITCH - 2, PITCH - 1, 0))
    for side, (halo, near, far, inward) in enumerate(sides):
        for first, count, place in y_runs(inward):
            for k in range(count):
                row = MIXED if place is None else place + k
                put(first + k, near, halo[pl.ds(row * NZ, NZ), :])
        flag = flags[pl.ds(side * NZ, NZ), :]
        put(WALL, near, flag)
        put(WALL, far, flag)
        put(AIM, near, aims[pl.ds(side * NZ, NZ), :])
        for k in range(9):
            q = 9 * (k // 3) + inward + k % 3
            put(q, far, halo[pl.ds((MIXED + 1 + k) * NZ, NZ), :])


def add_own_planes(full, ceiling, floor):
    for halo, near, far, part in ((floor, -1, -2, 2), (ceiling, NZ, NZ + 1, 0)):
        for k, (c, z) in enumerate(z_blocks(near, far, part)):
            full[pl.ds(c * ROWS + plane_at(z) + 2, 8), :] = halo[pl.ds(8 * k, 8), :]


def add_planes(full, ceiling, floor):
    def put(count, channel, z, row, source):
        start = channel * ROWS + plane_at(z) + row
        full[pl.ds(start, count, stride=ROWS), :] = source

    for halo, near, far, part in ((floor, -1, -2, 2), (ceiling, NZ, NZ + 1, 0)):
        for side, (row, beyond, group) in enumerate(((1, 0, 2), (PITCH - 2, PITCH - 1, 0))):
            start = side * Z_BLOCKS
            put(CHANNELS, 0, near, row, halo[pl.ds(start, CHANNELS), :])
            put(9, 9 * part, far, row, halo[pl.ds(start + CHANNELS, 9), :])
            first, second = (halo[pl.ds(start + k, 1), :] for k in (WALL, Z_BLOCKS - 1))
            put(1, WALL, far, row, second)
            start = Z_FAR + 12 * side
            for k in range(3):
                put(3, 9 * k + 3 * group, near, beyond, halo[pl.ds(start + 3 * k, 3), :])
            put(3, 9 * part + 3 * group, far, beyond, halo[pl.ds(start + 9, 3), :])
            put(1, WALL, near, beyond, first)
            put(1, WALL, far, beyond, second)


def pack_columns(full, pack, tiles):
    slot = lane_ids() // 4
    for t in tiles:
        packed = jnp.zeros((8, 128), F32)
        for c in range(CHANNELS):
            moved = pltpu.roll(full[pl.ds(c * ROWS + PAD + 8 * t, 8), :], (4 * c + 2) % 128, 1)
            packed = jnp.where(slot == c, moved, packed)
        pack[pl.ds(8 * t, 8), :] = packed


OWN_TILES = range(2 * PITCH // 8, (NZ + 2) * PITCH // 8)


def fill_kernel(own, y_first, y_second, two, one, full, pack, flags, aims):
    for c in range(CHANNELS):
        for z in range(NZ):
            full[pl.ds(c * ROWS + plane_at(z) + 2, 8), :] = own[pl.ds((c * NZ + z) * 8, 8), :]
    by_roles(y_first, y_second, functools.partial(add_rows, full, flags, aims))
    by_parity("gz", one, two, functools.partial(add_own_planes, full))
    pack_columns(full, pack, OWN_TILES)
    pack[pl.ds(FLAT, 128 - FLAT), :] = jnp.zeros((128 - FLAT, 128), F32)


def third_kernel(part, packed, z_one, z_two, full, pack, columns, message):
    last = lax.axis_size("gz") - 1
    here = lax.axis_index("gz")
    by_parity("gz", z_one, z_two, functools.partial(add_planes, full))

    @pl.when(here == 0)
    def _():
        full[pl.ds(WALL * ROWS + plane_at(-1), PITCH), :] = jnp.ones((PITCH, 128), F32)

    @pl.when(here == last)
    def _():
        for q in range(9):
            full[pl.ds(q * ROWS + plane_at(NZ), PITCH), :] = full[pl.ds((q + 18) * ROWS + plane_at(NZ - 1), PITCH), :]

    pack_columns(full, pack, [t for t in range(FLAT // 8) if t not in OWN_TILES])
    columns[pl.ds(PAD, 128), :] = pack[...].T

    def row(c, i, count):
        return columns[pl.ds(PAD + 4 * c + i, count), :]

    def returned(q, near, far):
        cx, cy, cz = VEL[q]
        step = (-PITCH * cz - cy) % 128
        value = row(26 - q, near, 8)
        value = pltpu.roll(value, step, 1) if step else value
        return jnp.where(row(WALL, far, 8) != 0.0, value, row(q, far, 8))[:1]

    for c in range(WALL + 1):
        cx = VEL[c][0] if c < 27 else 0
        if cx == 0:
            message[pl.ds(2 * c, 2), :] = row(c, 1, 2)
        elif cx > 0:
            message[pl.ds(2 * c, 1), :] = returned(c, 1, 0)
            message[pl.ds(2 * c + 1, 1), :] = row(c, 1, 1)
        else:
            message[pl.ds(2 * c, 1), :] = row(c, 2, 1)
            message[pl.ds(2 * c + 1, 1), :] = returned(c, 2, 3)


def block_kernel(full, post, walls):
    top = lax.axis_index("gz") == lax.axis_size("gz") - 1
    sponge = (lax.axis_index("gx") * NX + lane_ids()) < SPONGE
    for t in range(ROWS // 8):
        rows = pl.ds(8 * t, 8)
        flags = full[pl.ds(WALL * ROWS + 8 * t, 8), :]
        for cx in (-1, 0, 1):
            walls[cx + 1, rows, :] = pltpu.roll(flags, cx % 128, 1) if cx else flags
    for u in range(UNITS):
        cell = PAD + PITCH + 8 * u
        f = []
        solid = walls[1, pl.ds(cell, 8), :] != 0.0
        for q in range(27):
            cx, cy, cz = VEL[q]
            start = cell - PITCH * cz - cy
            value = full[pl.ds(q * ROWS + start, 8), :]
            if cx:
                value = pltpu.roll(value, cx % 128, 1)
            if q != 13:
                blocked = walls[cx + 1, pl.ds(start, 8), :] != 0.0
                value = jnp.where(blocked, full[pl.ds((26 - q) * ROWS + cell, 8), :], value)
            f.append(jnp.where(solid, WEIGHT[q], value))
        done = relaxed(f, sponge, full[pl.ds(AIM * ROWS + cell, 8), :])
        for q in range(27):
            post[q, pl.ds(8 * u, 8), :] = done[q]

    @pl.when(top)
    def _():
        for q in range(9):
            post[q, pl.ds((NZ + 1) * PITCH, PITCH), :] = post[q + 18, pl.ds(NZ * PITCH, PITCH), :]


def last_kernel(full, block, columns, x_one, x_two, out, west, east, column, walls, back, done, sems):
    here_x, size_x = lax.axis_index("gx"), lax.axis_size("gx")
    top = lax.axis_index("gz") == lax.axis_size("gz") - 1
    lanes, rows = lane_ids(), row_ids()

    if size_x == 2:

        def beside(side, start):
            first = min(max(start, 0), X_ROWS - 8)
            value = x_one[pl.ds(first, 8), :]
            return pltpu.roll(value, (first - start) % 8, 0) if first != start else value

    else:

        def spread(right, left):
            west[pl.ds(PAD, X_ROWS), :] = left[...]
            east[pl.ds(PAD, X_ROWS), :] = right[...]

        by_parity("gx", x_one, x_two, spread)

        def beside(side, start):
            return (west if side < 0 else east)[pl.ds(PAD + start, 8), :]

    def strip_at(c, shift):
        cx = VEL[c][0] if c < 27 else 0
        at = rows - shift
        first = PAD + 4 * c - shift
        value = jnp.where(at < 4, columns[pl.ds(first, 8), :], columns[pl.ds(first - 4, 8), :])
        if c <= WALL and cx >= 0:
            value = jnp.where(at < 2, beside(-1, 2 * c - (cx == 0) - shift), value)
        if c <= WALL and cx <= 0:
            value = jnp.where(at >= 6, beside(1, 2 * c - 6 + (cx == 0) - shift), value)
        if c == WALL:
            value = jnp.where((at == 0) | (at == 7), 0.0, value)
        return value

    strip = [strip_at(c, 0) for c in range(CHANNELS)]
    flags_at = {cx: strip_at(WALL, cx) if cx else strip[WALL] for cx in (-1, 0, 1)}

    def moved_along(value, q):
        cx, cy, cz = VEL[q]
        step = (PITCH * cz + cy) % 128
        return pltpu.roll(value, step, 1) if step else value

    moved = []
    for q in range(27):
        cx = VEL[q][0]
        value = moved_along(strip_at(q, cx) if cx else strip[q], q)
        if q != 13:
            value = jnp.where(moved_along(flags_at[cx], q) != 0.0, strip[26 - q], value)
        moved.append(jnp.where(strip[WALL] != 0.0, WEIGHT[q], value))
    place = here_x * NX + jnp.where(rows < 4, rows - 2, rows + (NX - 6))
    place = lax.rem(place + size_x * NX, size_x * NX)
    sides = relaxed(moved, place < SPONGE, strip[AIM])
    lid = top & (lanes >= (NZ + 2) * PITCH) & (lanes < (NZ + 3) * PITCH)
    for q in range(9):
        sides[q] = jnp.where(lid, pltpu.roll(sides[q + 18], PITCH, 1), sides[q])
    for q, side in enumerate(sides + [strip[WALL]]):
        column[pl.ds(PAD + 8 * q, 8), :] = side

    def picked(wanted):
        value = None
        for sublane, (q, row) in enumerate(wanted):
            moved = column[pl.ds(PAD + 8 * q + row - sublane, 8), :]
            value = moved if value is None else jnp.where(rows == sublane, moved, value)
        return value

    packed = []
    for k in range(9):
        a, b = 3 * k + 2, 3 * k
        packed.append(
            picked([(a, 5), (a, 2), (a, 1), (a, 2), (b, 5), (b, 2), (b, 5), (b, 6)])
        )
    rest = [(3 * k + 1, row) for k in range(9) for row in (5, 2)] + [(27, 1), (27, 6)]
    packed += [picked(rest[i : i + 8]) for i in range(0, len(rest), 8)]
    packed += [jnp.zeros((8, 128), F32)] * (16 - len(packed))
    back[...] = jnp.concatenate(packed, axis=0).T

    def column_at(place, lane, start):
        return pltpu.roll(back[pl.ds(start, 8), :], (lane - place) % 128, 1)

    rim = (lanes == 0) | (lanes == 127)

    def rimmed(q, start):
        k = q // 3
        ends = column_at((8 * k + 5, 73 + 2 * k, 8 * k + 1)[q % 3], 0, PITCH + start)
        return jnp.where(rim, ends, block[q, pl.ds(start, 8), :])

    for u in range(UNITS):
        flags = full[pl.ds(WALL * ROWS + PAD + PITCH + 8 * u, 8), :]
        walls[1, pl.ds(8 * u, 8), :] = flags
        for cx, edge, place in ((1, 0, 90), (-1, 127, 91)):
            walls[cx + 1, pl.ds(8 * u, 8), :] = jnp.where(
                lanes == edge, column_at(place, edge, PITCH + 8 * u), pltpu.roll(flags, cx % 128, 1)
            )

    cells = [(z + 1) * PITCH + 2 for z in range(NZ)]
    solids = [walls[1, pl.ds(cell, 8), :] != 0.0 for cell in cells]

    def streamed(q, z):
        cx, cy, cz = VEL[q]
        cell = cells[z]
        start = cell - PITCH * cz - cy
        if cx > 0:
            side = column_at(8 * (q // 3) + 2, 0, PITCH + start)
            value = jnp.where(lanes < 2, side, pltpu.roll(block[q, pl.ds(start, 8), :], 1, 1))
        elif cx < 0:
            side = column_at(8 * (q // 3) + 6, 126, PITCH + start)
            value = jnp.where(lanes > 125, side, pltpu.roll(block[q, pl.ds(start, 8), :], 127, 1))
        else:
            value = rimmed(q, start)
        if q != 13:
            blocked = walls[cx + 1, pl.ds(start, 8), :] != 0.0
            value = jnp.where(blocked, rimmed(26 - q, cell), value)
        return jnp.where(solids[z], WEIGHT[q], value)

    copies = []
    for first, count in ((0, 9), (9, 8), (17, 6), (23, 4)):
        for q in range(first, first + count):
            for z in range(NZ):
                done[q, z] = streamed(q, z)
        part = pl.ds(first, count)
        copies.append(pltpu.make_async_copy(done.at[part], out.at[part], sems.at[len(copies)]))
        copies[-1].start()
    for copy in copies:
        copy.wait()


def pairs(size, turn, wrap):
    ahead = [(i, (i + 1) % size) for i in range(turn, size if wrap else size - 1, 2)]
    return ahead + [(j, i) for i, j in ahead]


def swap(value, axis, turn, wrap):
    return lax.ppermute(value, axis, pairs(lax.axis_size(axis), turn, wrap))


def swap_mixed(value, turn):
    size, planes = lax.axis_size("gy"), lax.axis_size("gz")
    moves = []
    for k in range(planes):
        moves += [
            (i * planes + k, j * planes + k) for i, j in pairs(size, (turn + k) % 2, True)
        ]
    return lax.ppermute(value, ("gy", "gz"), moves)


def shape(*dims):
    return jax.ShapeDtypeStruct(dims, F32)


def shards(pops, solid, profile_table, profile_index):
    own, y_first, y_second = pl.pallas_call(
        first_kernel,
        out_shape=[shape(CHANNELS * NZ * 8, 128), shape(Y_ROWS, 128), shape(Y_ROWS, 128)],
        in_specs=[HBM] * 4,
        out_specs=[VMEM] * 3,
        scratch_shapes=[
            pltpu.VMEM(pops.shape, F32),
            pltpu.VMEM(solid.shape, jnp.int32),
            pltpu.SMEM(profile_table.shape[::-1], F32),
            pltpu.SMEM(profile_index.shape, jnp.int32),
            pltpu.SemaphoreType.DMA((6,)),
        ],
        compiler_params=PARAMS,
        name="collide",
    )(*(pltpu.with_memory_space_constraint(a, pltpu.HBM) for a in (pops, solid, profile_table.T, profile_index)))
    y_first = swap_mixed(y_first, 1)
    y_second = swap_mixed(y_second, 0)
    own_two, own_one = pl.pallas_call(
        ahead_kernel,
        out_shape=[shape(Z_BLOCKS * 8, 128)] * 2,
        in_specs=[VMEM],
        out_specs=[VMEM] * 2,
        compiler_params=PARAMS,
        name="pack_own",
    )(own)
    own_two = swap(own_two, "gz", 1, False)
    own_one = swap(own_one, "gz", 0, False)
    z_one, z_two = pl.pallas_call(
        second_kernel,
        out_shape=[shape(Z_ROWS, 128)] * 2,
        in_specs=[VMEM] * 2,
        out_specs=[VMEM] * 2,
        scratch_shapes=[pltpu.VMEM((4 * NZ, 128), F32)] * 2,
        compiler_params=PARAMS,
        cost_estimate=pl.CostEstimate(flops=10**9, bytes_accessed=2**20, transcendentals=0),
        name="pack_z",
    )(y_first, y_second)
    z_one = swap(z_one, "gz", 0, False)
    z_two = swap(z_two, "gz", 1, False)
    part, packed = pl.pallas_call(
        fill_kernel,
        out_shape=[shape(SLABS * ROWS, 128), shape(128, 128)],
        in_specs=[VMEM] * 5,
        out_specs=[VMEM] * 2,
        scratch_shapes=[pltpu.VMEM((4 * NZ, 128), F32)] * 2,
        compiler_params=PARAMS,
        cost_estimate=pl.CostEstimate(flops=10**6, bytes_accessed=2**22, transcendentals=0),
        name="fill",
    )(own, y_first, y_second, own_two, own_one)
    full, packed, columns, message = pl.pallas_call(
        third_kernel,
        out_shape=[
            shape(SLABS * ROWS, 128),
            shape(128, 128),
            shape(PAD + 128 + PAD, 128),
            shape(X_ROWS, 128),
        ],
        in_specs=[VMEM] * 4,
        out_specs=[VMEM] * 4,
        input_output_aliases={0: 0, 1: 1},
        compiler_params=PARAMS,
        name="pack_x",
    )(part, packed, z_one, z_two)
    x_one = swap(message, "gx", 0, True)
    x_two = x_one if lax.axis_size("gx") == 2 else swap(message, "gx", 1, True)
    block = pl.pallas_call(
        block_kernel,
        out_shape=shape(27, UNITS * 8, 128),
        in_specs=[VMEM],
        out_specs=VMEM,
        scratch_shapes=[pltpu.VMEM((3, ROWS, 128), F32)],
        compiler_params=PARAMS,
        cost_estimate=pl.CostEstimate(
            flops=27 * 20 * UNITS * 1024, bytes_accessed=2**22, transcendentals=0
        ),
        name="block",
    )(full)
    return pl.pallas_call(
        last_kernel,
        out_shape=shape(27, NZ, NY, NX),
        in_specs=[VMEM] * 5,
        out_specs=HBM,
        scratch_shapes=[
            pltpu.VMEM((PAD + X_ROWS + PAD, 128), F32),
            pltpu.VMEM((PAD + X_ROWS + PAD, 128), F32),
            pltpu.VMEM((PAD + 28 * 8 + PAD, 128), F32),
            pltpu.VMEM((3, UNITS * 8, 128), F32),
            pltpu.VMEM((128, 128), F32),
            pltpu.VMEM((27, NZ, NY, NX), F32),
            pltpu.SemaphoreType.DMA((NZ,)),
        ],
        compiler_params=PARAMS,
        name="finish",
    )(full, block, columns, x_one, x_two)


def solution(mesh):
    return jax.shard_map(
        shards,
        mesh=mesh,
        in_specs=(P(None, "gz", "gy", "gx"), P("gz", "gy", "gx"), P(None, "gz"), P("gy")),
        out_specs=P(None, "gz", "gy", "gx"),
        check_vma=False,
    )
```

```python
import functools

import jax
import jax.numpy as jnp
import numpy as np
from jax import lax
from jax.experimental import pallas as pl
from jax.experimental.pallas import tpu as pltpu
from jax.sharding import PartitionSpec as P

SPONGE = 32
TAU = 0.52
SMAG = 18.0 * 1.4142135623730951 * 0.17 * 0.17

VEL = [(cx, cy, cz) for cz in (-1, 0, 1) for cy in (-1, 0, 1) for cx in (-1, 0, 1)]
WEIGHT = [
    float(np.array([8.0 / 27.0, 2.0 / 27.0, 1.0 / 54.0, 1.0 / 216.0])[cx * cx + cy * cy + cz * cz])
    for cx, cy, cz in VEL
]
WALL, AIM, CHANNELS = 27, 28, 29
NZ, NY, NX = 4, 8, 128
PITCH = NY + 4
FLAT = (NZ + 4) * PITCH
PAD = 8
ROWS = PAD + FLAT + PAD
SLABS = CHANNELS + 6
UNITS = (NZ + 2) * PITCH // 8

PARAMS = pltpu.CompilerParams(vmem_limit_bytes=12 * 2**20)
VMEM = pl.BlockSpec(memory_space=pltpu.VMEM)
HBM = pl.BlockSpec(memory_space=pltpu.HBM)
F32 = jnp.float32

MIXED = 24
Y_ROWS = (MIXED + 1 + 9) * NZ
Z_BLOCKS = CHANNELS + 10
Z_FAR = 2 * Z_BLOCKS
Z_ROWS = -(-(Z_FAR + 2 * 12) // 8) * 8

X_ROWS = 2 * (WALL + 1)


def relaxed(f, sponge, aim):
    quad = {}
    for cz in (-1, 0, 1):
        line = {}
        for cy in (-1, 0, 1):
            base = 9 * (cz + 1) + 3 * (cy + 1)
            both = f[base + 2] + f[base]
            line[cy] = (both + f[base + 1], f[base + 2] - f[base], both)
        s = line[1][0] + line[-1][0]
        sx = line[1][1] + line[-1][1]
        quad[cz] = dict(
            n=s + line[0][0],
            y=line[1][0] - line[-1][0],
            yy=s,
            x=sx + line[0][1],
            xy=line[1][1] - line[-1][1],
            xx=line[1][2] + line[-1][2] + line[0][2],
        )
    up, mid, down = quad[1], quad[0], quad[-1]
    zz = up["n"] + down["n"]
    rho = zz + mid["n"]
    jz = up["n"] - down["n"]
    jy = up["y"] + down["y"] + mid["y"]
    jx = up["x"] + down["x"] + mid["x"]
    inverse = 1.0 / rho
    ux, uy, uz = jx * inverse, jy * inverse, jz * inverse
    third = rho * (1.0 / 3.0)
    pxx = (up["xx"] + down["xx"] + mid["xx"]) - (third + jx * ux)
    pyy = (up["yy"] + down["yy"] + mid["yy"]) - (third + jy * uy)
    pzz = zz - (third + jz * uz)
    pxy = (up["xy"] + down["xy"] + mid["xy"]) - jx * uy
    pxz = (up["x"] - down["x"]) - jx * uz
    pyz = (up["y"] - down["y"]) - jy * uz
    strain = pxx * pxx + pyy * pyy + pzz * pzz + 2.0 * (pxy * pxy + pxz * pxz + pyz * pyz)
    size = jnp.sqrt(2.0 * strain)
    tau = 0.5 * (TAU + jnp.sqrt(TAU * TAU + SMAG * size * inverse))
    omega = 1.0 / tau
    keep = 1.0 - omega
    if sponge is not None:
        keep = jnp.where(sponge, 0.0, keep)
        omega = jnp.where(sponge, 1.0, omega)
        ux = jnp.where(sponge, aim, ux)
        uy = jnp.where(sponge, 0.0, uy)
        uz = jnp.where(sponge, 0.0, uz)
    square = 1.0 - 1.5 * (ux * ux + uy * uy + uz * uz)
    vx, vy, vz = 3.0 * ux, 3.0 * uy, 3.0 * uz
    share = rho * omega
    weighted = {w: share * w for w in sorted(set(WEIGHT))}
    post = [None] * 27
    for q in range(14):
        cx, cy, cz = VEL[q]
        along = None
        for c, v in ((cx, vx), (cy, vy), (cz, vz)):
            if c:
                along = (v if c > 0 else -v) if along is None else (along + v if c > 0 else along - v)
        scale = weighted[WEIGHT[q]]
        if along is None:
            post[q] = keep * f[q] + scale * square
            continue
        even = square + 0.5 * along * along
        post[q] = keep * f[q] + scale * (even + along)
        post[26 - q] = keep * f[26 - q] + scale * (even - along)
    return post


def lane_ids():
    return lax.broadcasted_iota(jnp.int32, (8, 128), 1)


def row_ids():
    return lax.broadcasted_iota(jnp.int32, (8, 128), 0)


def by_parity(axis, one, two, body):
    even = lax.rem(lax.axis_index(axis), 2) == 0
    pl.when(even)(lambda: body(one, two))
    pl.when(jnp.logical_not(even))(lambda: body(two, one))


def by_roles(first, second, body):
    even = lax.rem(lax.axis_index("gz"), 2) == 0
    pl.when(even)(lambda: by_parity("gy", first, second, body))
    pl.when(jnp.logical_not(even))(lambda: by_parity("gy", second, first, body))


def z_blocks(near, far, part):
    blocks = [(c, near) for c in range(CHANNELS)]
    return blocks + [(9 * part + k, far) for k in range(9)] + [(WALL, far)]


def first_kernel(pops_at, solid_at, table_at, index_at, own, first_out, second_out, *scratch):
    pops, solid, table, index, sems = scratch
    groups = [(pops_at.at[pl.ds(q, 9)], pops.at[pl.ds(q, 9)]) for q in (0, 9, 18)]
    small = [(table_at, table), (index_at, index)]
    copies = [
        pltpu.make_async_copy(source, target, sems.at[i])
        for i, (source, target) in enumerate([*small, *groups, (solid_at, solid)])
    ]
    for copy in copies:
        copy.start()
    for copy in copies[:2]:
        copy.wait()
    lanes, rows = lane_ids(), row_ids()
    sponge = (lax.axis_index("gx") * NX + lanes) < SPONGE
    profiles = [index[y] for y in range(NY)]
    aims = []
    for z in range(NZ):
        aim = jnp.zeros((8, 128), F32)
        for y, profile in enumerate(profiles):
            aim = jnp.where(rows == y, table[z, profile], aim)
        aims.append(aim)
    for copy in copies[2:-1]:
        copy.wait()
    for z, aim in enumerate(aims):
        post = relaxed([pops[q, z] for q in range(27)], sponge, aim)
        for q in range(27):
            own[pl.ds((q * NZ + z) * 8, 8), :] = post[q]
        own[pl.ds((AIM * NZ + z) * 8, 8), :] = aim
    copies[-1].wait()
    for z in range(NZ):
        own[pl.ds((WALL * NZ + z) * 8, 8), :] = solid[z].astype(F32)

    def pack(yup, ydown):
        inside = lax.rem(lanes, 4)
        for out, edge, second, part in ((yup, 7, 6, 6), (ydown, 0, 1, 0)):
            back = 15 - part
            for first, count, place in ((0, back, 0), (back + 3, 24 - back, back)):
                out[pl.ds(place * NZ, count * NZ), :] = own[
                    pl.ds(first * NZ * 8 + edge, count * NZ, stride=8), :
                ]
            for z in range(NZ):
                west, east, aim, flag = (
                    own[pl.ds((c * NZ + z) * 8, 8), :] for c in (back, back + 2, AIM, WALL)
                )
                mixed = jnp.where(inside < 2, jnp.where(inside == 0, west, aim), flag)
                mixed = jnp.where(inside == 3, east, mixed)
                out[pl.ds(MIXED * NZ + z, 1), :] = mixed[edge : edge + 1]
            for a in range(3):
                out[pl.ds((MIXED + 1 + 3 * a) * NZ, 3 * NZ), :] = own[
                    pl.ds((9 * a + part) * NZ * 8 + second, 3 * NZ, stride=8), :
                ]

    by_roles(first_out, second_out, pack)


def ahead_kernel(own, two, one):
    def pack(zup, zdown):
        for out, first, second, part in ((zup, NZ - 1, NZ - 2, 2), (zdown, 0, 1, 0)):
            for k, (c, z) in enumerate(z_blocks(first, second, part)):
                out[pl.ds(8 * k, 8), :] = own[pl.ds((c * NZ + z) * 8, 8), :]

    by_parity("gz", one, two, pack)


def y_runs(part):
    back = 15 - part
    return (0, back, 0), (back, 3, None), (back + 3, 24 - back, back)


def spread_mixed(below, above, flags, aims):
    flags[pl.ds(0, NZ), :] = below[pl.ds(MIXED * NZ, NZ), :]
    flags[pl.ds(NZ, NZ), :] = above[pl.ds(MIXED * NZ, NZ), :]
    mixed = flags[pl.ds(0, 2 * NZ), :]
    inside = lax.rem(lane_ids(), 4)
    moved = {k: pltpu.roll(mixed, k % 128, 1) if k else mixed for k in (-2, -1, 0, 1, 2)}

    def from_lane(source):
        value = moved[0]
        for lane in range(4):
            if lane != source:
                value = jnp.where(inside == lane, moved[lane - source], value)
        return value

    aims[pl.ds(0, 2 * NZ), :] = from_lane(1)
    flags[pl.ds(0, 2 * NZ), :] = from_lane(2)


def second_kernel(y_first, y_second, z_one, z_two, flags, aims):
    def pack(zup, zdown, above, below):
        spread_mixed(below, above, flags, aims)
        pack_planes(below, above, flags, aims, zup, zdown)

    even = lax.rem(lax.axis_index("gz"), 2) == 0
    ways = ((even, y_first, y_second, z_one, z_two), (~even, y_second, y_first, z_two, z_one))
    for here, one, two, zup, zdown in ways:
        pl.when(here)(
            functools.partial(by_parity, "gy", one, two, functools.partial(pack, zup, zdown))
        )


def pack_planes(below, above, flags, aims, zup, zdown):
    for out, first, second, part in ((zup, NZ - 1, NZ - 2, 2), (zdown, 0, 1, 0)):
        for side, (halo, inward) in enumerate(((below, 6), (above, 0))):
            near = side * Z_BLOCKS
            for channel, count, place in y_runs(inward):
                if place is None:
                    row = halo[pl.ds(MIXED * NZ + first, 1), :]
                    out[pl.ds(near + channel, 3), :] = jnp.broadcast_to(row, (3, 128))
                else:
                    out[pl.ds(near + channel, count), :] = halo[
                        pl.ds(place * NZ + first, count, stride=NZ), :
                    ]
            out[pl.ds(near + WALL, 1), :] = flags[pl.ds(side * NZ + first, 1), :]
            out[pl.ds(near + AIM, 1), :] = aims[pl.ds(side * NZ + first, 1), :]
            place = 15 if part else 0
            for k, count in ((0, 8), (8, 1)):
                out[pl.ds(near + CHANNELS + k, count), :] = halo[
                    pl.ds((place + k) * NZ + second, count, stride=NZ if count > 1 else 1), :
                ]
            out[pl.ds(near + Z_BLOCKS - 1, 1), :] = flags[pl.ds(side * NZ + second, 1), :]
            far = Z_FAR + 12 * side
            start = (MIXED + 1) * NZ
            out[pl.ds(far, 8), :] = halo[pl.ds(start + first, 8, stride=NZ), :]
            out[pl.ds(far + 8, 1), :] = halo[pl.ds(start + 8 * NZ + first, 1), :]
            for k in range(3):
                row = halo[pl.ds(start + (3 * part + k) * NZ + second, 1), :]
                out[pl.ds(far + 9 + k, 1), :] = row


def plane_at(z):
    return PAD + (z + 2) * PITCH


def add_rows(full, flags, aims, above, below):
    spread_mixed(below, above, flags, aims)

    def put(channel, row, source):
        full[pl.ds(channel * ROWS + plane_at(0) + row, NZ, stride=PITCH), :] = source

    sides = ((below, 1, 0, 6), (above, PITCH - 2, PITCH - 1, 0))
    for side, (halo, near, far, inward) in enumerate(sides):
        for first, count, place in y_runs(inward):
            for k in range(count):
                row = MIXED if place is None else place + k
                put(first + k, near, halo[pl.ds(row * NZ, NZ), :])
        flag = flags[pl.ds(side * NZ, NZ), :]
        put(WALL, near, flag)
        put(WALL, far, flag)
        put(AIM, near, aims[pl.ds(side * NZ, NZ), :])
        for k in range(9):
            q = 9 * (k // 3) + inward + k % 3
            put(q, far, halo[pl.ds((MIXED + 1 + k) * NZ, NZ), :])


def add_own_planes(full, ceiling, floor):
    for halo, near, far, part in ((floor, -1, -2, 2), (ceiling, NZ, NZ + 1, 0)):
        for k, (c, z) in enumerate(z_blocks(near, far, part)):
            full[pl.ds(c * ROWS + plane_at(z) + 2, 8), :] = halo[pl.ds(8 * k, 8), :]


def add_planes(full, ceiling, floor):
    def put(count, channel, z, row, source):
        start = channel * ROWS + plane_at(z) + row
        full[pl.ds(start, count, stride=ROWS), :] = source

    for halo, near, far, part in ((floor, -1, -2, 2), (ceiling, NZ, NZ + 1, 0)):
        for side, (row, beyond, group) in enumerate(((1, 0, 2), (PITCH - 2, PITCH - 1, 0))):
            start = side * Z_BLOCKS
            put(CHANNELS, 0, near, row, halo[pl.ds(start, CHANNELS), :])
            put(9, 9 * part, far, row, halo[pl.ds(start + CHANNELS, 9), :])
            first, second = (halo[pl.ds(start + k, 1), :] for k in (WALL, Z_BLOCKS - 1))
            put(1, WALL, far, row, second)
            start = Z_FAR + 12 * side
            for k in range(3):
                put(3, 9 * k + 3 * group, near, beyond, halo[pl.ds(start + 3 * k, 3), :])
            put(3, 9 * part + 3 * group, far, beyond, halo[pl.ds(start + 9, 3), :])
            put(1, WALL, near, beyond, first)
            put(1, WALL, far, beyond, second)


def pack_columns(full, pack, tiles):
    slot = lane_ids() // 4
    for t in tiles:
        packed = jnp.zeros((8, 128), F32)
        for c in range(CHANNELS):
            moved = pltpu.roll(full[pl.ds(c * ROWS + PAD + 8 * t, 8), :], (4 * c + 2) % 128, 1)
            packed = jnp.where(slot == c, moved, packed)
        pack[pl.ds(8 * t, 8), :] = packed


OWN_TILES = range(2 * PITCH // 8, (NZ + 2) * PITCH // 8)


def fill_kernel(own, y_first, y_second, two, one, full, pack, flags, aims):
    for c in range(CHANNELS):
        for z in range(NZ):
            full[pl.ds(c * ROWS + plane_at(z) + 2, 8), :] = own[pl.ds((c * NZ + z) * 8, 8), :]
    by_roles(y_first, y_second, functools.partial(add_rows, full, flags, aims))
    by_parity("gz", one, two, functools.partial(add_own_planes, full))
    pack_columns(full, pack, OWN_TILES)
    pack[pl.ds(FLAT, 128 - FLAT), :] = jnp.zeros((128 - FLAT, 128), F32)


def third_kernel(part, packed, z_one, z_two, full, pack, columns, message):
    last = lax.axis_size("gz") - 1
    here = lax.axis_index("gz")
    by_parity("gz", z_one, z_two, functools.partial(add_planes, full))

    @pl.when(here == 0)
    def _():
        full[pl.ds(WALL * ROWS + plane_at(-1), PITCH), :] = jnp.ones((PITCH, 128), F32)

    @pl.when(here == last)
    def _():
        for q in range(9):
            full[pl.ds(q * ROWS + plane_at(NZ), PITCH), :] = full[pl.ds((q + 18) * ROWS + plane_at(NZ - 1), PITCH), :]

    pack_columns(full, pack, [t for t in range(FLAT // 8) if t not in OWN_TILES])
    columns[pl.ds(PAD, 128), :] = pack[...].T

    def row(c, i, count):
        return columns[pl.ds(PAD + 4 * c + i, count), :]

    def returned(q, near, far):
        cx, cy, cz = VEL[q]
        step = (-PITCH * cz - cy) % 128
        value = row(26 - q, near, 8)
        value = pltpu.roll(value, step, 1) if step else value
        return jnp.where(row(WALL, far, 8) != 0.0, value, row(q, far, 8))[:1]

    for c in range(WALL + 1):
        cx = VEL[c][0] if c < 27 else 0
        if cx == 0:
            message[pl.ds(2 * c, 2), :] = row(c, 1, 2)
        elif cx > 0:
            message[pl.ds(2 * c, 1), :] = returned(c, 1, 0)
            message[pl.ds(2 * c + 1, 1), :] = row(c, 1, 1)
        else:
            message[pl.ds(2 * c, 1), :] = row(c, 2, 1)
            message[pl.ds(2 * c + 1, 1), :] = returned(c, 2, 3)


def block_kernel(full, post, walls):
    top = lax.axis_index("gz") == lax.axis_size("gz") - 1
    sponge = (lax.axis_index("gx") * NX + lane_ids()) < SPONGE
    for t in range(ROWS // 8):
        rows = pl.ds(8 * t, 8)
        flags = full[pl.ds(WALL * ROWS + 8 * t, 8), :]
        for cx in (-1, 0, 1):
            walls[cx + 1, rows, :] = pltpu.roll(flags, cx % 128, 1) if cx else flags
    for u in range(UNITS):
        cell = PAD + PITCH + 8 * u
        f = []
        solid = walls[1, pl.ds(cell, 8), :] != 0.0
        for q in range(27):
            cx, cy, cz = VEL[q]
            start = cell - PITCH * cz - cy
            value = full[pl.ds(q * ROWS + start, 8), :]
            if cx:
                value = pltpu.roll(value, cx % 128, 1)
            if q != 13:
                blocked = walls[cx + 1, pl.ds(start, 8), :] != 0.0
                value = jnp.where(blocked, full[pl.ds((26 - q) * ROWS + cell, 8), :], value)
            f.append(jnp.where(solid, WEIGHT[q], value))
        done = relaxed(f, sponge, full[pl.ds(AIM * ROWS + cell, 8), :])
        for q in range(27):
            post[q, pl.ds(8 * u, 8), :] = done[q]

    @pl.when(top)
    def _():
        for q in range(9):
            post[q, pl.ds((NZ + 1) * PITCH, PITCH), :] = post[q + 18, pl.ds(NZ * PITCH, PITCH), :]


def last_kernel(full, block, columns, x_one, x_two, out, west, east, column, walls, back, done, sems):
    here_x, size_x = lax.axis_index("gx"), lax.axis_size("gx")
    top = lax.axis_index("gz") == lax.axis_size("gz") - 1
    lanes, rows = lane_ids(), row_ids()

    if size_x == 2:

        def beside(side, start):
            first = min(max(start, 0), X_ROWS - 8)
            value = x_one[pl.ds(first, 8), :]
            return pltpu.roll(value, (first - start) % 8, 0) if first != start else value

    else:

        def spread(right, left):
            west[pl.ds(PAD, X_ROWS), :] = left[...]
            east[pl.ds(PAD, X_ROWS), :] = right[...]

        by_parity("gx", x_one, x_two, spread)

        def beside(side, start):
            return (west if side < 0 else east)[pl.ds(PAD + start, 8), :]

    def strip_at(c, shift):
        cx = VEL[c][0] if c < 27 else 0
        at = rows - shift
        first = PAD + 4 * c - shift
        value = jnp.where(at < 4, columns[pl.ds(first, 8), :], columns[pl.ds(first - 4, 8), :])
        if c <= WALL and cx >= 0:
            value = jnp.where(at < 2, beside(-1, 2 * c - (cx == 0) - shift), value)
        if c <= WALL and cx <= 0:
            value = jnp.where(at >= 6, beside(1, 2 * c - 6 + (cx == 0) - shift), value)
        if c == WALL:
            value = jnp.where((at == 0) | (at == 7), 0.0, value)
        return value

    strip = [strip_at(c, 0) for c in range(CHANNELS)]
    flags_at = {cx: strip_at(WALL, cx) if cx else strip[WALL] for cx in (-1, 0, 1)}

    def moved_along(value, q):
        cx, cy, cz = VEL[q]
        step = (PITCH * cz + cy) % 128
        return pltpu.roll(value, step, 1) if step else value

    moved = []
    for q in range(27):
        cx = VEL[q][0]
        value = moved_along(strip_at(q, cx) if cx else strip[q], q)
        if q != 13:
            value = jnp.where(moved_along(flags_at[cx], q) != 0.0, strip[26 - q], value)
        moved.append(jnp.where(strip[WALL] != 0.0, WEIGHT[q], value))
    place = here_x * NX + jnp.where(rows < 4, rows - 2, rows + (NX - 6))
    place = lax.rem(place + size_x * NX, size_x * NX)
    sides = relaxed(moved, place < SPONGE, strip[AIM])
    lid = top & (lanes >= (NZ + 2) * PITCH) & (lanes < (NZ + 3) * PITCH)
    for q in range(9):
        sides[q] = jnp.where(lid, pltpu.roll(sides[q + 18], PITCH, 1), sides[q])
    for q, side in enumerate(sides + [strip[WALL]]):
        column[pl.ds(PAD + 8 * q, 8), :] = side

    def picked(wanted):
        value = None
        for sublane, (q, row) in enumerate(wanted):
            moved = column[pl.ds(PAD + 8 * q + row - sublane, 8), :]
            value = moved if value is None else jnp.where(rows == sublane, moved, value)
        return value

    packed = []
    for k in range(9):
        a, b = 3 * k + 2, 3 * k
        packed.append(
            picked([(a, 5), (a, 2), (a, 1), (a, 2), (b, 5), (b, 2), (b, 5), (b, 6)])
        )
    rest = [(3 * k + 1, row) for k in range(9) for row in (5, 2)] + [(27, 1), (27, 6)]
    packed += [picked(rest[i : i + 8]) for i in range(0, len(rest), 8)]
    packed += [jnp.zeros((8, 128), F32)] * (16 - len(packed))
    back[...] = jnp.concatenate(packed, axis=0).T

    def column_at(place, lane, start):
        return pltpu.roll(back[pl.ds(start, 8), :], (lane - place) % 128, 1)

    rim = (lanes == 0) | (lanes == 127)

    def rimmed(q, start):
        k = q // 3
        ends = column_at((8 * k + 5, 73 + 2 * k, 8 * k + 1)[q % 3], 0, PITCH + start)
        return jnp.where(rim, ends, block[q, pl.ds(start, 8), :])

    for u in range(UNITS):
        flags = full[pl.ds(WALL * ROWS + PAD + PITCH + 8 * u, 8), :]
        walls[1, pl.ds(8 * u, 8), :] = flags
        for cx, edge, place in ((1, 0, 90), (-1, 127, 91)):
            walls[cx + 1, pl.ds(8 * u, 8), :] = jnp.where(
                lanes == edge, column_at(place, edge, PITCH + 8 * u), pltpu.roll(flags, cx % 128, 1)
            )

    cells = [(z + 1) * PITCH + 2 for z in range(NZ)]
    solids = [walls[1, pl.ds(cell, 8), :] != 0.0 for cell in cells]

    def streamed(q, z):
        cx, cy, cz = VEL[q]
        cell = cells[z]
        start = cell - PITCH * cz - cy
        if cx > 0:
            side = column_at(8 * (q // 3) + 2, 0, PITCH + start)
            value = jnp.where(lanes < 2, side, pltpu.roll(block[q, pl.ds(start, 8), :], 1, 1))
        elif cx < 0:
            side = column_at(8 * (q // 3) + 6, 126, PITCH + start)
            value = jnp.where(lanes > 125, side, pltpu.roll(block[q, pl.ds(start, 8), :], 127, 1))
        else:
            value = rimmed(q, start)
        if q != 13:
            blocked = walls[cx + 1, pl.ds(start, 8), :] != 0.0
            value = jnp.where(blocked, rimmed(26 - q, cell), value)
        return jnp.where(solids[z], WEIGHT[q], value)

    copies = []
    for first, count in ((0, 9), (9, 8), (17, 6), (23, 4)):
        for q in range(first, first + count):
            for z in range(NZ):
                done[q, z] = streamed(q, z)
        part = pl.ds(first, count)
        copies.append(pltpu.make_async_copy(done.at[part], out.at[part], sems.at[len(copies)]))
        copies[-1].start()
    for copy in copies:
        copy.wait()


def pairs(size, turn, wrap):
    ahead = [(i, (i + 1) % size) for i in range(turn, size if wrap else size - 1, 2)]
    return ahead + [(j, i) for i, j in ahead]


def swap(value, axis, turn, wrap):
    return lax.ppermute(value, axis, pairs(lax.axis_size(axis), turn, wrap))


def swap_mixed(value, turn):
    size, planes = lax.axis_size("gy"), lax.axis_size("gz")
    moves = []
    for k in range(planes):
        moves += [
            (i * planes + k, j * planes + k) for i, j in pairs(size, (turn + k) % 2, True)
        ]
    return lax.ppermute(value, ("gy", "gz"), moves)


def shape(*dims):
    return jax.ShapeDtypeStruct(dims, F32)


def shards(pops, solid, profile_table, profile_index):
    own, y_first, y_second = pl.pallas_call(
        first_kernel,
        out_shape=[shape(CHANNELS * NZ * 8, 128), shape(Y_ROWS, 128), shape(Y_ROWS, 128)],
        in_specs=[HBM] * 4,
        out_specs=[VMEM] * 3,
        scratch_shapes=[
            pltpu.VMEM(pops.shape, F32),
            pltpu.VMEM(solid.shape, jnp.int32),
            pltpu.SMEM(profile_table.shape[::-1], F32),
            pltpu.SMEM(profile_index.shape, jnp.int32),
            pltpu.SemaphoreType.DMA((6,)),
        ],
        compiler_params=PARAMS,
        name="collide",
    )(*(pltpu.with_memory_space_constraint(a, pltpu.HBM) for a in (pops, solid, profile_table.T, profile_index)))
    y_first = swap_mixed(y_first, 0)
    y_second = swap_mixed(y_second, 1)
    own_two, own_one = pl.pallas_call(
        ahead_kernel,
        out_shape=[shape(Z_BLOCKS * 8, 128)] * 2,
        in_specs=[VMEM],
        out_specs=[VMEM] * 2,
        compiler_params=PARAMS,
        name="pack_own",
    )(own)
    own_two = swap(own_two, "gz", 1, False)
    own_one = swap(own_one, "gz", 0, False)
    z_one, z_two = pl.pallas_call(
        second_kernel,
        out_shape=[shape(Z_ROWS, 128)] * 2,
        in_specs=[VMEM] * 2,
        out_specs=[VMEM] * 2,
        scratch_shapes=[pltpu.VMEM((4 * NZ, 128), F32)] * 2,
        compiler_params=PARAMS,
        cost_estimate=pl.CostEstimate(flops=10**9, bytes_accessed=2**20, transcendentals=0),
        name="pack_z",
    )(y_first, y_second)
    z_one = swap(z_one, "gz", 0, False)
    z_two = swap(z_two, "gz", 1, False)
    part, packed = pl.pallas_call(
        fill_kernel,
        out_shape=[shape(SLABS * ROWS, 128), shape(128, 128)],
        in_specs=[VMEM] * 5,
        out_specs=[VMEM] * 2,
        scratch_shapes=[pltpu.VMEM((4 * NZ, 128), F32)] * 2,
        compiler_params=PARAMS,
        cost_estimate=pl.CostEstimate(flops=10**6, bytes_accessed=2**22, transcendentals=0),
        name="fill",
    )(own, y_first, y_second, own_two, own_one)
    full, packed, columns, message = pl.pallas_call(
        third_kernel,
        out_shape=[
            shape(SLABS * ROWS, 128),
            shape(128, 128),
            shape(PAD + 128 + PAD, 128),
            shape(X_ROWS, 128),
        ],
        in_specs=[VMEM] * 4,
        out_specs=[VMEM] * 4,
        input_output_aliases={0: 0, 1: 1},
        compiler_params=PARAMS,
        name="pack_x",
    )(part, packed, z_one, z_two)
    x_one = swap(message, "gx", 0, True)
    x_two = x_one if lax.axis_size("gx") == 2 else swap(message, "gx", 1, True)
    block = pl.pallas_call(
        block_kernel,
        out_shape=shape(27, UNITS * 8, 128),
        in_specs=[VMEM],
        out_specs=VMEM,
        scratch_shapes=[pltpu.VMEM((3, ROWS, 128), F32)],
        compiler_params=PARAMS,
        cost_estimate=pl.CostEstimate(
            flops=27 * 20 * UNITS * 1024, bytes_accessed=2**22, transcendentals=0
        ),
        name="block",
    )(full)
    return pl.pallas_call(
        last_kernel,
        out_shape=shape(27, NZ, NY, NX),
        in_specs=[VMEM] * 5,
        out_specs=HBM,
        scratch_shapes=[
            pltpu.VMEM((PAD + X_ROWS + PAD, 128), F32),
            pltpu.VMEM((PAD + X_ROWS + PAD, 128), F32),
            pltpu.VMEM((PAD + 28 * 8 + PAD, 128), F32),
            pltpu.VMEM((3, UNITS * 8, 128), F32),
            pltpu.VMEM((128, 128), F32),
            pltpu.VMEM((27, NZ, NY, NX), F32),
            pltpu.SemaphoreType.DMA((NZ,)),
        ],
        compiler_params=PARAMS,
        name="finish",
    )(full, block, columns, x_one, x_two)


def solution(mesh):
    return jax.shard_map(
        shards,
        mesh=mesh,
        in_specs=(P(None, "gz", "gy", "gx"), P("gz", "gy", "gx"), P(None, "gz"), P("gy")),
        out_specs=P(None, "gz", "gy", "gx"),
        check_vma=False,
    )
```

```python
import functools

import jax
import jax.numpy as jnp
import numpy as np
from jax import lax
from jax.experimental import pallas as pl
from jax.experimental.pallas import tpu as pltpu
from jax.sharding import PartitionSpec as P

SPONGE = 32
TAU = 0.52
SMAG = 18.0 * 1.4142135623730951 * 0.17 * 0.17

VEL = [(cx, cy, cz) for cz in (-1, 0, 1) for cy in (-1, 0, 1) for cx in (-1, 0, 1)]
WEIGHT = [
    float(np.array([8.0 / 27.0, 2.0 / 27.0, 1.0 / 54.0, 1.0 / 216.0])[cx * cx + cy * cy + cz * cz])
    for cx, cy, cz in VEL
]
WALL, AIM, CHANNELS = 27, 28, 29
NZ, NY, NX = 4, 8, 128
PITCH = NY + 4
FLAT = (NZ + 4) * PITCH
PAD = 8
ROWS = PAD + FLAT + PAD
SLABS = CHANNELS + 6
UNITS = (NZ + 2) * PITCH // 8

PARAMS = pltpu.CompilerParams(vmem_limit_bytes=12 * 2**20)
VMEM = pl.BlockSpec(memory_space=pltpu.VMEM)
HBM = pl.BlockSpec(memory_space=pltpu.HBM)
F32 = jnp.float32

MIXED = 24
Y_ROWS = (MIXED + 1 + 9) * NZ
Z_BLOCKS = CHANNELS + 10
Z_FAR = 2 * Z_BLOCKS
Z_ROWS = -(-(Z_FAR + 2 * 12) // 8) * 8

X_ROWS = 2 * (WALL + 1)


def relaxed(f, sponge, aim):
    quad = {}
    for cz in (-1, 0, 1):
        line = {}
        for cy in (-1, 0, 1):
            base = 9 * (cz + 1) + 3 * (cy + 1)
            both = f[base + 2] + f[base]
            line[cy] = (both + f[base + 1], f[base + 2] - f[base], both)
        s = line[1][0] + line[-1][0]
        sx = line[1][1] + line[-1][1]
        quad[cz] = dict(
            n=s + line[0][0],
            y=line[1][0] - line[-1][0],
            yy=s,
            x=sx + line[0][1],
            xy=line[1][1] - line[-1][1],
            xx=line[1][2] + line[-1][2] + line[0][2],
        )
    up, mid, down = quad[1], quad[0], quad[-1]
    zz = up["n"] + down["n"]
    rho = zz + mid["n"]
    jz = up["n"] - down["n"]
    jy = up["y"] + down["y"] + mid["y"]
    jx = up["x"] + down["x"] + mid["x"]
    inverse = 1.0 / rho
    ux, uy, uz = jx * inverse, jy * inverse, jz * inverse
    third = rho * (1.0 / 3.0)
    pxx = (up["xx"] + down["xx"] + mid["xx"]) - (third + jx * ux)
    pyy = (up["yy"] + down["yy"] + mid["yy"]) - (third + jy * uy)
    pzz = zz - (third + jz * uz)
    pxy = (up["xy"] + down["xy"] + mid["xy"]) - jx * uy
    pxz = (up["x"] - down["x"]) - jx * uz
    pyz = (up["y"] - down["y"]) - jy * uz
    strain = pxx * pxx + pyy * pyy + pzz * pzz + 2.0 * (pxy * pxy + pxz * pxz + pyz * pyz)
    size = jnp.sqrt(2.0 * strain)
    tau = 0.5 * (TAU + jnp.sqrt(TAU * TAU + SMAG * size * inverse))
    omega = 1.0 / tau
    keep = 1.0 - omega
    if sponge is not None:
        keep = jnp.where(sponge, 0.0, keep)
        omega = jnp.where(sponge, 1.0, omega)
        ux = jnp.where(sponge, aim, ux)
        uy = jnp.where(sponge, 0.0, uy)
        uz = jnp.where(sponge, 0.0, uz)
    square = 1.0 - 1.5 * (ux * ux + uy * uy + uz * uz)
    vx, vy, vz = 3.0 * ux, 3.0 * uy, 3.0 * uz
    share = rho * omega
    weighted = {w: share * w for w in sorted(set(WEIGHT))}
    post = [None] * 27
    for q in range(14):
        cx, cy, cz = VEL[q]
        along = None
        for c, v in ((cx, vx), (cy, vy), (cz, vz)):
            if c:
                along = (v if c > 0 else -v) if along is None else (along + v if c > 0 else along - v)
        scale = weighted[WEIGHT[q]]
        if along is None:
            post[q] = keep * f[q] + scale * square
            continue
        even = square + 0.5 * along * along
        post[q] = keep * f[q] + scale * (even + along)
        post[26 - q] = keep * f[26 - q] + scale * (even - along)
    return post


def lane_ids():
    return lax.broadcasted_iota(jnp.int32, (8, 128), 1)


def row_ids():
    return lax.broadcasted_iota(jnp.int32, (8, 128), 0)


def by_parity(axis, one, two, body):
    even = lax.rem(lax.axis_index(axis), 2) == 0
    pl.when(even)(lambda: body(one, two))
    pl.when(jnp.logical_not(even))(lambda: body(two, one))


def by_roles(first, second, body):
    inner = lax.rem((lax.axis_index("gz") + 1) // 2, 2) == 1
    pl.when(inner)(lambda: by_parity("gy", first, second, body))
    pl.when(jnp.logical_not(inner))(lambda: by_parity("gy", second, first, body))


def z_blocks(near, far, part):
    blocks = [(c, near) for c in range(CHANNELS)]
    return blocks + [(9 * part + k, far) for k in range(9)] + [(WALL, far)]


def first_kernel(pops_at, solid_at, table_at, index_at, own, first_out, second_out, *scratch):
    pops, solid, table, index, sems = scratch
    groups = [(pops_at.at[pl.ds(q, 9)], pops.at[pl.ds(q, 9)]) for q in (0, 9, 18)]
    small = [(table_at, table), (index_at, index)]
    copies = [
        pltpu.make_async_copy(source, target, sems.at[i])
        for i, (source, target) in enumerate([*small, *groups, (solid_at, solid)])
    ]
    for copy in copies:
        copy.start()
    for copy in copies[:2]:
        copy.wait()
    lanes, rows = lane_ids(), row_ids()
    sponge = (lax.axis_index("gx") * NX + lanes) < SPONGE
    profiles = [index[y] for y in range(NY)]
    aims = []
    for z in range(NZ):
        aim = jnp.zeros((8, 128), F32)
        for y, profile in enumerate(profiles):
            aim = jnp.where(rows == y, table[z, profile], aim)
        aims.append(aim)
    for copy in copies[2:-1]:
        copy.wait()
    for z, aim in enumerate(aims):
        post = relaxed([pops[q, z] for q in range(27)], sponge, aim)
        for q in range(27):
            own[pl.ds((q * NZ + z) * 8, 8), :] = post[q]
        own[pl.ds((AIM * NZ + z) * 8, 8), :] = aim
    copies[-1].wait()
    for z in range(NZ):
        own[pl.ds((WALL * NZ + z) * 8, 8), :] = solid[z].astype(F32)

    def pack(yup, ydown):
        inside = lax.rem(lanes, 4)
        for out, edge, second, part in ((yup, 7, 6, 6), (ydown, 0, 1, 0)):
            back = 15 - part
            for first, count, place in ((0, back, 0), (back + 3, 24 - back, back)):
                out[pl.ds(place * NZ, count * NZ), :] = own[
                    pl.ds(first * NZ * 8 + edge, count * NZ, stride=8), :
                ]
            for z in range(NZ):
                west, east, aim, flag = (
                    own[pl.ds((c * NZ + z) * 8, 8), :] for c in (back, back + 2, AIM, WALL)
                )
                mixed = jnp.where(inside < 2, jnp.where(inside == 0, west, aim), flag)
                mixed = jnp.where(inside == 3, east, mixed)
                out[pl.ds(MIXED * NZ + z, 1), :] = mixed[edge : edge + 1]
            for a in range(3):
                out[pl.ds((MIXED + 1 + 3 * a) * NZ, 3 * NZ), :] = own[
                    pl.ds((9 * a + part) * NZ * 8 + second, 3 * NZ, stride=8), :
                ]

    by_roles(first_out, second_out, pack)


def ahead_kernel(own, two, one):
    def pack(zup, zdown):
        for out, first, second, part in ((zup, NZ - 1, NZ - 2, 2), (zdown, 0, 1, 0)):
            for k, (c, z) in enumerate(z_blocks(first, second, part)):
                out[pl.ds(8 * k, 8), :] = own[pl.ds((c * NZ + z) * 8, 8), :]

    by_parity("gz", one, two, pack)


def y_runs(part):
    back = 15 - part
    return (0, back, 0), (back, 3, None), (back + 3, 24 - back, back)


def spread_mixed(below, above, flags, aims):
    flags[pl.ds(0, NZ), :] = below[pl.ds(MIXED * NZ, NZ), :]
    flags[pl.ds(NZ, NZ), :] = above[pl.ds(MIXED * NZ, NZ), :]
    mixed = flags[pl.ds(0, 2 * NZ), :]
    inside = lax.rem(lane_ids(), 4)
    moved = {k: pltpu.roll(mixed, k % 128, 1) if k else mixed for k in (-2, -1, 0, 1, 2)}

    def from_lane(source):
        value = moved[0]
        for lane in range(4):
            if lane != source:
                value = jnp.where(inside == lane, moved[lane - source], value)
        return value

    aims[pl.ds(0, 2 * NZ), :] = from_lane(1)
    flags[pl.ds(0, 2 * NZ), :] = from_lane(2)


def second_kernel(y_first, y_second, z_one, z_two, flags, aims):
    def pack(above, below):
        spread_mixed(below, above, flags, aims)
        by_parity(
            "gz",
            z_one,
            z_two,
            lambda zup, zdown: pack_planes(below, above, flags, aims, zup, zdown),
        )

    by_roles(y_first, y_second, pack)


def pack_planes(below, above, flags, aims, zup, zdown):
    for out, first, second, part in ((zup, NZ - 1, NZ - 2, 2), (zdown, 0, 1, 0)):
        for side, (halo, inward) in enumerate(((below, 6), (above, 0))):
            near = side * Z_BLOCKS
            for channel, count, place in y_runs(inward):
                if place is None:
                    row = halo[pl.ds(MIXED * NZ + first, 1), :]
                    out[pl.ds(near + channel, 3), :] = jnp.broadcast_to(row, (3, 128))
                else:
                    out[pl.ds(near + channel, count), :] = halo[
                        pl.ds(place * NZ + first, count, stride=NZ), :
                    ]
            out[pl.ds(near + WALL, 1), :] = flags[pl.ds(side * NZ + first, 1), :]
            out[pl.ds(near + AIM, 1), :] = aims[pl.ds(side * NZ + first, 1), :]
            place = 15 if part else 0
            for k, count in ((0, 8), (8, 1)):
                out[pl.ds(near + CHANNELS + k, count), :] = halo[
                    pl.ds((place + k) * NZ + second, count, stride=NZ if count > 1 else 1), :
                ]
            out[pl.ds(near + Z_BLOCKS - 1, 1), :] = flags[pl.ds(side * NZ + second, 1), :]
            far = Z_FAR + 12 * side
            start = (MIXED + 1) * NZ
            out[pl.ds(far, 8), :] = halo[pl.ds(start + first, 8, stride=NZ), :]
            out[pl.ds(far + 8, 1), :] = halo[pl.ds(start + 8 * NZ + first, 1), :]
            for k in range(3):
                row = halo[pl.ds(start + (3 * part + k) * NZ + second, 1), :]
                out[pl.ds(far + 9 + k, 1), :] = row


def plane_at(z):
    return PAD + (z + 2) * PITCH


def add_rows(full, flags, aims, above, below):
    spread_mixed(below, above, flags, aims)

    def put(channel, row, source):
        full[pl.ds(channel * ROWS + plane_at(0) + row, NZ, stride=PITCH), :] = source

    sides = ((below, 1, 0, 6), (above, PITCH - 2, PITCH - 1, 0))
    for side, (halo, near, far, inward) in enumerate(sides):
        for first, count, place in y_runs(inward):
            for k in range(count):
                row = MIXED if place is None else place + k
                put(first + k, near, halo[pl.ds(row * NZ, NZ), :])
        flag = flags[pl.ds(side * NZ, NZ), :]
        put(WALL, near, flag)
        put(WALL, far, flag)
        put(AIM, near, aims[pl.ds(side * NZ, NZ), :])
        for k in range(9):
            q = 9 * (k // 3) + inward + k % 3
            put(q, far, halo[pl.ds((MIXED + 1 + k) * NZ, NZ), :])


def add_own_planes(full, ceiling, floor):
    for halo, near, far, part in ((floor, -1, -2, 2), (ceiling, NZ, NZ + 1, 0)):
        for k, (c, z) in enumerate(z_blocks(near, far, part)):
            full[pl.ds(c * ROWS + plane_at(z) + 2, 8), :] = halo[pl.ds(8 * k, 8), :]


def add_planes(full, ceiling, floor):
    def put(count, channel, z, row, source):
        start = channel * ROWS + plane_at(z) + row
        full[pl.ds(start, count, stride=ROWS), :] = source

    for halo, near, far, part in ((floor, -1, -2, 2), (ceiling, NZ, NZ + 1, 0)):
        for side, (row, beyond, group) in enumerate(((1, 0, 2), (PITCH - 2, PITCH - 1, 0))):
            start = side * Z_BLOCKS
            put(CHANNELS, 0, near, row, halo[pl.ds(start, CHANNELS), :])
            put(9, 9 * part, far, row, halo[pl.ds(start + CHANNELS, 9), :])
            first, second = (halo[pl.ds(start + k, 1), :] for k in (WALL, Z_BLOCKS - 1))
            put(1, WALL, far, row, second)
            start = Z_FAR + 12 * side
            for k in range(3):
                put(3, 9 * k + 3 * group, near, beyond, halo[pl.ds(start + 3 * k, 3), :])
            put(3, 9 * part + 3 * group, far, beyond, halo[pl.ds(start + 9, 3), :])
            put(1, WALL, near, beyond, first)
            put(1, WALL, far, beyond, second)


def pack_columns(full, pack, tiles):
    slot = lane_ids() // 4
    for t in tiles:
        packed = jnp.zeros((8, 128), F32)
        for c in range(CHANNELS):
            moved = pltpu.roll(full[pl.ds(c * ROWS + PAD + 8 * t, 8), :], (4 * c + 2) % 128, 1)
            packed = jnp.where(slot == c, moved, packed)
        pack[pl.ds(8 * t, 8), :] = packed


OWN_TILES = range(2 * PITCH // 8, (NZ + 2) * PITCH // 8)


def fill_kernel(own, y_first, y_second, two, one, full, pack, flags, aims):
    for c in range(CHANNELS):
        for z in range(NZ):
            full[pl.ds(c * ROWS + plane_at(z) + 2, 8), :] = own[pl.ds((c * NZ + z) * 8, 8), :]
    by_roles(y_first, y_second, functools.partial(add_rows, full, flags, aims))
    by_parity("gz", one, two, functools.partial(add_own_planes, full))
    pack_columns(full, pack, OWN_TILES)
    pack[pl.ds(FLAT, 128 - FLAT), :] = jnp.zeros((128 - FLAT, 128), F32)


def third_kernel(part, packed, z_one, z_two, full, pack, columns, message):
    last = lax.axis_size("gz") - 1
    here = lax.axis_index("gz")
    by_parity("gz", z_one, z_two, functools.partial(add_planes, full))

    @pl.when(here == 0)
    def _():
        full[pl.ds(WALL * ROWS + plane_at(-1), PITCH), :] = jnp.ones((PITCH, 128), F32)

    @pl.when(here == last)
    def _():
        for q in range(9):
            full[pl.ds(q * ROWS + plane_at(NZ), PITCH), :] = full[pl.ds((q + 18) * ROWS + plane_at(NZ - 1), PITCH), :]

    pack_columns(full, pack, [t for t in range(FLAT // 8) if t not in OWN_TILES])
    columns[pl.ds(PAD, 128), :] = pack[...].T

    def row(c, i, count):
        return columns[pl.ds(PAD + 4 * c + i, count), :]

    def returned(q, near, far):
        cx, cy, cz = VEL[q]
        step = (-PITCH * cz - cy) % 128
        value = row(26 - q, near, 8)
        value = pltpu.roll(value, step, 1) if step else value
        return jnp.where(row(WALL, far, 8) != 0.0, value, row(q, far, 8))[:1]

    for c in range(WALL + 1):
        cx = VEL[c][0] if c < 27 else 0
        if cx == 0:
            message[pl.ds(2 * c, 2), :] = row(c, 1, 2)
        elif cx > 0:
            message[pl.ds(2 * c, 1), :] = returned(c, 1, 0)
            message[pl.ds(2 * c + 1, 1), :] = row(c, 1, 1)
        else:
            message[pl.ds(2 * c, 1), :] = row(c, 2, 1)
            message[pl.ds(2 * c + 1, 1), :] = returned(c, 2, 3)


def block_kernel(full, post, walls):
    top = lax.axis_index("gz") == lax.axis_size("gz") - 1
    sponge = (lax.axis_index("gx") * NX + lane_ids()) < SPONGE
    for t in range(ROWS // 8):
        rows = pl.ds(8 * t, 8)
        flags = full[pl.ds(WALL * ROWS + 8 * t, 8), :]
        for cx in (-1, 0, 1):
            walls[cx + 1, rows, :] = pltpu.roll(flags, cx % 128, 1) if cx else flags
    for u in range(UNITS):
        cell = PAD + PITCH + 8 * u
        f = []
        solid = walls[1, pl.ds(cell, 8), :] != 0.0
        for q in range(27):
            cx, cy, cz = VEL[q]
            start = cell - PITCH * cz - cy
            value = full[pl.ds(q * ROWS + start, 8), :]
            if cx:
                value = pltpu.roll(value, cx % 128, 1)
            if q != 13:
                blocked = walls[cx + 1, pl.ds(start, 8), :] != 0.0
                value = jnp.where(blocked, full[pl.ds((26 - q) * ROWS + cell, 8), :], value)
            f.append(jnp.where(solid, WEIGHT[q], value))
        done = relaxed(f, sponge, full[pl.ds(AIM * ROWS + cell, 8), :])
        for q in range(27):
            post[q, pl.ds(8 * u, 8), :] = done[q]

    @pl.when(top)
    def _():
        for q in range(9):
            post[q, pl.ds((NZ + 1) * PITCH, PITCH), :] = post[q + 18, pl.ds(NZ * PITCH, PITCH), :]


def last_kernel(full, block, columns, x_one, x_two, out, west, east, column, walls, back, done, sems):
    here_x, size_x = lax.axis_index("gx"), lax.axis_size("gx")
    top = lax.axis_index("gz") == lax.axis_size("gz") - 1
    lanes, rows = lane_ids(), row_ids()

    if size_x == 2:

        def beside(side, start):
            first = min(max(start, 0), X_ROWS - 8)
            value = x_one[pl.ds(first, 8), :]
            return pltpu.roll(value, (first - start) % 8, 0) if first != start else value

    else:

        def spread(right, left):
            west[pl.ds(PAD, X_ROWS), :] = left[...]
            east[pl.ds(PAD, X_ROWS), :] = right[...]

        by_parity("gx", x_one, x_two, spread)

        def beside(side, start):
            return (west if side < 0 else east)[pl.ds(PAD + start, 8), :]

    def strip_at(c, shift):
        cx = VEL[c][0] if c < 27 else 0
        at = rows - shift
        first = PAD + 4 * c - shift
        value = jnp.where(at < 4, columns[pl.ds(first, 8), :], columns[pl.ds(first - 4, 8), :])
        if c <= WALL and cx >= 0:
            value = jnp.where(at < 2, beside(-1, 2 * c - (cx == 0) - shift), value)
        if c <= WALL and cx <= 0:
            value = jnp.where(at >= 6, beside(1, 2 * c - 6 + (cx == 0) - shift), value)
        if c == WALL:
            value = jnp.where((at == 0) | (at == 7), 0.0, value)
        return value

    strip = [strip_at(c, 0) for c in range(CHANNELS)]
    flags_at = {cx: strip_at(WALL, cx) if cx else strip[WALL] for cx in (-1, 0, 1)}

    def moved_along(value, q):
        cx, cy, cz = VEL[q]
        step = (PITCH * cz + cy) % 128
        return pltpu.roll(value, step, 1) if step else value

    moved = []
    for q in range(27):
        cx = VEL[q][0]
        value = moved_along(strip_at(q, cx) if cx else strip[q], q)
        if q != 13:
            value = jnp.where(moved_along(flags_at[cx], q) != 0.0, strip[26 - q], value)
        moved.append(jnp.where(strip[WALL] != 0.0, WEIGHT[q], value))
    place = here_x * NX + jnp.where(rows < 4, rows - 2, rows + (NX - 6))
    place = lax.rem(place + size_x * NX, size_x * NX)
    sides = relaxed(moved, place < SPONGE, strip[AIM])
    lid = top & (lanes >= (NZ + 2) * PITCH) & (lanes < (NZ + 3) * PITCH)
    for q in range(9):
        sides[q] = jnp.where(lid, pltpu.roll(sides[q + 18], PITCH, 1), sides[q])
    for q, side in enumerate(sides + [strip[WALL]]):
        column[pl.ds(PAD + 8 * q, 8), :] = side

    def picked(wanted):
        value = None
        for sublane, (q, row) in enumerate(wanted):
            moved = column[pl.ds(PAD + 8 * q + row - sublane, 8), :]
            value = moved if value is None else jnp.where(rows == sublane, moved, value)
        return value

    packed = []
    for k in range(9):
        a, b = 3 * k + 2, 3 * k
        packed.append(
            picked([(a, 5), (a, 2), (a, 1), (a, 2), (b, 5), (b, 2), (b, 5), (b, 6)])
        )
    rest = [(3 * k + 1, row) for k in range(9) for row in (5, 2)] + [(27, 1), (27, 6)]
    packed += [picked(rest[i : i + 8]) for i in range(0, len(rest), 8)]
    packed += [jnp.zeros((8, 128), F32)] * (16 - len(packed))
    back[...] = jnp.concatenate(packed, axis=0).T

    def column_at(place, lane, start):
        return pltpu.roll(back[pl.ds(start, 8), :], (lane - place) % 128, 1)

    rim = (lanes == 0) | (lanes == 127)

    def rimmed(q, start):
        k = q // 3
        ends = column_at((8 * k + 5, 73 + 2 * k, 8 * k + 1)[q % 3], 0, PITCH + start)
        return jnp.where(rim, ends, block[q, pl.ds(start, 8), :])

    for u in range(UNITS):
        flags = full[pl.ds(WALL * ROWS + PAD + PITCH + 8 * u, 8), :]
        walls[1, pl.ds(8 * u, 8), :] = flags
        for cx, edge, place in ((1, 0, 90), (-1, 127, 91)):
            walls[cx + 1, pl.ds(8 * u, 8), :] = jnp.where(
                lanes == edge, column_at(place, edge, PITCH + 8 * u), pltpu.roll(flags, cx % 128, 1)
            )

    cells = [(z + 1) * PITCH + 2 for z in range(NZ)]
    solids = [walls[1, pl.ds(cell, 8), :] != 0.0 for cell in cells]

    def streamed(q, z):
        cx, cy, cz = VEL[q]
        cell = cells[z]
        start = cell - PITCH * cz - cy
        if cx > 0:
            side = column_at(8 * (q // 3) + 2, 0, PITCH + start)
            value = jnp.where(lanes < 2, side, pltpu.roll(block[q, pl.ds(start, 8), :], 1, 1))
        elif cx < 0:
            side = column_at(8 * (q // 3) + 6, 126, PITCH + start)
            value = jnp.where(lanes > 125, side, pltpu.roll(block[q, pl.ds(start, 8), :], 127, 1))
        else:
            value = rimmed(q, start)
        if q != 13:
            blocked = walls[cx + 1, pl.ds(start, 8), :] != 0.0
            value = jnp.where(blocked, rimmed(26 - q, cell), value)
        return jnp.where(solids[z], WEIGHT[q], value)

    copies = []
    for first, count in ((0, 9), (9, 8), (17, 6), (23, 4)):
        for q in range(first, first + count):
            for z in range(NZ):
                done[q, z] = streamed(q, z)
        part = pl.ds(first, count)
        copies.append(pltpu.make_async_copy(done.at[part], out.at[part], sems.at[len(copies)]))
        copies[-1].start()
    for copy in copies:
        copy.wait()


def pairs(size, turn, wrap):
    ahead = [(i, (i + 1) % size) for i in range(turn, size if wrap else size - 1, 2)]
    return ahead + [(j, i) for i, j in ahead]


def swap(value, axis, turn, wrap):
    return lax.ppermute(value, axis, pairs(lax.axis_size(axis), turn, wrap))


def swap_mixed(value, turn):
    size, planes = lax.axis_size("gy"), lax.axis_size("gz")
    moves = []
    for k in range(planes):
        moves += [
            (i * planes + k, j * planes + k)
            for i, j in pairs(size, (turn + (k + 1) // 2 + 1) % 2, True)
        ]
    return lax.ppermute(value, ("gy", "gz"), moves)


def shape(*dims):
    return jax.ShapeDtypeStruct(dims, F32)


def shards(pops, solid, profile_table, profile_index):
    own, y_first, y_second = pl.pallas_call(
        first_kernel,
        out_shape=[shape(CHANNELS * NZ * 8, 128), shape(Y_ROWS, 128), shape(Y_ROWS, 128)],
        in_specs=[HBM] * 4,
        out_specs=[VMEM] * 3,
        scratch_shapes=[
            pltpu.VMEM(pops.shape, F32),
            pltpu.VMEM(solid.shape, jnp.int32),
            pltpu.SMEM(profile_table.shape[::-1], F32),
            pltpu.SMEM(profile_index.shape, jnp.int32),
            pltpu.SemaphoreType.DMA((6,)),
        ],
        compiler_params=PARAMS,
        name="collide",
    )(*(pltpu.with_memory_space_constraint(a, pltpu.HBM) for a in (pops, solid, profile_table.T, profile_index)))
    y_first = swap_mixed(y_first, 0)
    y_second = swap_mixed(y_second, 1)
    own_two, own_one = pl.pallas_call(
        ahead_kernel,
        out_shape=[shape(Z_BLOCKS * 8, 128)] * 2,
        in_specs=[VMEM],
        out_specs=[VMEM] * 2,
        compiler_params=PARAMS,
        name="pack_own",
    )(own)
    own_two = swap(own_two, "gz", 1, False)
    own_one = swap(own_one, "gz", 0, False)
    z_one, z_two = pl.pallas_call(
        second_kernel,
        out_shape=[shape(Z_ROWS, 128)] * 2,
        in_specs=[VMEM] * 2,
        out_specs=[VMEM] * 2,
        scratch_shapes=[pltpu.VMEM((4 * NZ, 128), F32)] * 2,
        compiler_params=PARAMS,
        cost_estimate=pl.CostEstimate(flops=10**9, bytes_accessed=2**20, transcendentals=0),
        name="pack_z",
    )(y_first, y_second)
    z_one = swap(z_one, "gz", 0, False)
    z_two = swap(z_two, "gz", 1, False)
    part, packed = pl.pallas_call(
        fill_kernel,
        out_shape=[shape(SLABS * ROWS, 128), shape(128, 128)],
        in_specs=[VMEM] * 5,
        out_specs=[VMEM] * 2,
        scratch_shapes=[pltpu.VMEM((4 * NZ, 128), F32)] * 2,
        compiler_params=PARAMS,
        cost_estimate=pl.CostEstimate(flops=10**6, bytes_accessed=2**22, transcendentals=0),
        name="fill",
    )(own, y_first, y_second, own_two, own_one)
    full, packed, columns, message = pl.pallas_call(
        third_kernel,
        out_shape=[
            shape(SLABS * ROWS, 128),
            shape(128, 128),
            shape(PAD + 128 + PAD, 128),
            shape(X_ROWS, 128),
        ],
        in_specs=[VMEM] * 4,
        out_specs=[VMEM] * 4,
        input_output_aliases={0: 0, 1: 1},
        compiler_params=PARAMS,
        name="pack_x",
    )(part, packed, z_one, z_two)
    x_one = swap(message, "gx", 0, True)
    x_two = x_one if lax.axis_size("gx") == 2 else swap(message, "gx", 1, True)
    block = pl.pallas_call(
        block_kernel,
        out_shape=shape(27, UNITS * 8, 128),
        in_specs=[VMEM],
        out_specs=VMEM,
        scratch_shapes=[pltpu.VMEM((3, ROWS, 128), F32)],
        compiler_params=PARAMS,
        cost_estimate=pl.CostEstimate(
            flops=27 * 20 * UNITS * 1024, bytes_accessed=2**22, transcendentals=0
        ),
        name="block",
    )(full)
    return pl.pallas_call(
        last_kernel,
        out_shape=shape(27, NZ, NY, NX),
        in_specs=[VMEM] * 5,
        out_specs=HBM,
        scratch_shapes=[
            pltpu.VMEM((PAD + X_ROWS + PAD, 128), F32),
            pltpu.VMEM((PAD + X_ROWS + PAD, 128), F32),
            pltpu.VMEM((PAD + 28 * 8 + PAD, 128), F32),
            pltpu.VMEM((3, UNITS * 8, 128), F32),
            pltpu.VMEM((128, 128), F32),
            pltpu.VMEM((27, NZ, NY, NX), F32),
            pltpu.SemaphoreType.DMA((NZ,)),
        ],
        compiler_params=PARAMS,
        name="finish",
    )(full, block, columns, x_one, x_two)


def solution(mesh):
    return jax.shard_map(
        shards,
        mesh=mesh,
        in_specs=(P(None, "gz", "gy", "gx"), P("gz", "gy", "gx"), P(None, "gz"), P("gy")),
        out_specs=P(None, "gz", "gy", "gx"),
        check_vma=False,
    )
```

```python
import functools

import jax
import jax.numpy as jnp
import numpy as np
from jax import lax
from jax.experimental import pallas as pl
from jax.experimental.pallas import tpu as pltpu
from jax.sharding import PartitionSpec as P

SPONGE = 32
TAU = 0.52
SMAG = 18.0 * 1.4142135623730951 * 0.17 * 0.17

VEL = [(cx, cy, cz) for cz in (-1, 0, 1) for cy in (-1, 0, 1) for cx in (-1, 0, 1)]
WEIGHT = [
    float(np.array([8.0 / 27.0, 2.0 / 27.0, 1.0 / 54.0, 1.0 / 216.0])[cx * cx + cy * cy + cz * cz])
    for cx, cy, cz in VEL
]
WALL, AIM, CHANNELS = 27, 28, 29
NZ, NY, NX = 4, 8, 128
PITCH = NY + 4
FLAT = (NZ + 4) * PITCH
PAD = 8
ROWS = PAD + FLAT + PAD
SLABS = CHANNELS + 6
UNITS = (NZ + 2) * PITCH // 8

PARAMS = pltpu.CompilerParams(vmem_limit_bytes=12 * 2**20)
VMEM = pl.BlockSpec(memory_space=pltpu.VMEM)
HBM = pl.BlockSpec(memory_space=pltpu.HBM)
F32 = jnp.float32

MIXED = 24
Y_ROWS = (MIXED + 1 + 9) * NZ
Z_BLOCKS = CHANNELS + 10
Z_FAR = 2 * Z_BLOCKS
Z_ROWS = -(-(Z_FAR + 2 * 12) // 8) * 8

X_ROWS = 2 * (WALL + 1)


def relaxed(f, sponge, aim):
    quad = {}
    for cz in (-1, 0, 1):
        line = {}
        for cy in (-1, 0, 1):
            base = 9 * (cz + 1) + 3 * (cy + 1)
            both = f[base + 2] + f[base]
            line[cy] = (both + f[base + 1], f[base + 2] - f[base], both)
        s = line[1][0] + line[-1][0]
        sx = line[1][1] + line[-1][1]
        quad[cz] = dict(
            n=s + line[0][0],
            y=line[1][0] - line[-1][0],
            yy=s,
            x=sx + line[0][1],
            xy=line[1][1] - line[-1][1],
            xx=line[1][2] + line[-1][2] + line[0][2],
        )
    up, mid, down = quad[1], quad[0], quad[-1]
    zz = up["n"] + down["n"]
    rho = zz + mid["n"]
    jz = up["n"] - down["n"]
    jy = up["y"] + down["y"] + mid["y"]
    jx = up["x"] + down["x"] + mid["x"]
    inverse = 1.0 / rho
    ux, uy, uz = jx * inverse, jy * inverse, jz * inverse
    third = rho * (1.0 / 3.0)
    pxx = (up["xx"] + down["xx"] + mid["xx"]) - (third + jx * ux)
    pyy = (up["yy"] + down["yy"] + mid["yy"]) - (third + jy * uy)
    pzz = zz - (third + jz * uz)
    pxy = (up["xy"] + down["xy"] + mid["xy"]) - jx * uy
    pxz = (up["x"] - down["x"]) - jx * uz
    pyz = (up["y"] - down["y"]) - jy * uz
    strain = pxx * pxx + pyy * pyy + pzz * pzz + 2.0 * (pxy * pxy + pxz * pxz + pyz * pyz)
    size = jnp.sqrt(2.0 * strain)
    tau = 0.5 * (TAU + jnp.sqrt(TAU * TAU + SMAG * size * inverse))
    omega = 1.0 / tau
    keep = 1.0 - omega
    if sponge is not None:
        keep = jnp.where(sponge, 0.0, keep)
        omega = jnp.where(sponge, 1.0, omega)
        ux = jnp.where(sponge, aim, ux)
        uy = jnp.where(sponge, 0.0, uy)
        uz = jnp.where(sponge, 0.0, uz)
    square = 1.0 - 1.5 * (ux * ux + uy * uy + uz * uz)
    vx, vy, vz = 3.0 * ux, 3.0 * uy, 3.0 * uz
    share = rho * omega
    weighted = {w: share * w for w in sorted(set(WEIGHT))}
    post = [None] * 27
    for q in range(14):
        cx, cy, cz = VEL[q]
        along = None
        for c, v in ((cx, vx), (cy, vy), (cz, vz)):
            if c:
                along = (v if c > 0 else -v) if along is None else (along + v if c > 0 else along - v)
        scale = weighted[WEIGHT[q]]
        if along is None:
            post[q] = keep * f[q] + scale * square
            continue
        even = square + 0.5 * along * along
        post[q] = keep * f[q] + scale * (even + along)
        post[26 - q] = keep * f[26 - q] + scale * (even - along)
    return post


def lane_ids():
    return lax.broadcasted_iota(jnp.int32, (8, 128), 1)


def row_ids():
    return lax.broadcasted_iota(jnp.int32, (8, 128), 0)


def by_parity(axis, one, two, body):
    even = lax.rem(lax.axis_index(axis), 2) == 0
    pl.when(even)(lambda: body(one, two))
    pl.when(jnp.logical_not(even))(lambda: body(two, one))


def way(*axes):
    return lax.rem(sum(lax.axis_index(axis) for axis in axes), 2)


def by_roles(first, second, body):
    ahead = way("gz", "gy") == 0
    pl.when(ahead)(lambda: body(first, second))
    pl.when(jnp.logical_not(ahead))(lambda: body(second, first))


def z_blocks(near, far, part):
    blocks = [(c, near) for c in range(CHANNELS)]
    return blocks + [(9 * part + k, far) for k in range(9)] + [(WALL, far)]


def first_kernel(pops_at, solid_at, table_at, index_at, own, first_out, second_out, *scratch):
    pops, solid, table, index, messages, sems = scratch
    groups = [(pops_at.at[pl.ds(q, 9)], pops.at[pl.ds(q, 9)]) for q in (0, 9, 18)]
    small = [(table_at, table), (index_at, index)]
    copies = [
        pltpu.make_async_copy(source, target, sems.at[i])
        for i, (source, target) in enumerate([*small, *groups, (solid_at, solid)])
    ]
    for copy in copies:
        copy.start()
    for copy in copies[:2]:
        copy.wait()
    lanes, rows = lane_ids(), row_ids()
    sponge = (lax.axis_index("gx") * NX + lanes) < SPONGE
    profiles = [index[y] for y in range(NY)]
    aims = []
    for z in range(NZ):
        aim = jnp.zeros((8, 128), F32)
        for y, profile in enumerate(profiles):
            aim = jnp.where(rows == y, table[z, profile], aim)
        aims.append(aim)
    for copy in copies[2:-1]:
        copy.wait()
    for z, aim in enumerate(aims):
        post = relaxed([pops[q, z] for q in range(27)], sponge, aim)
        for q in range(27):
            own[pl.ds((q * NZ + z) * 8, 8), :] = post[q]
        own[pl.ds((AIM * NZ + z) * 8, 8), :] = aim
    copies[-1].wait()
    for z in range(NZ):
        own[pl.ds((WALL * NZ + z) * 8, 8), :] = solid[z].astype(F32)

    inside = lax.rem(lanes, 4)
    for out, edge, second, part in ((messages.at[0], 7, 6, 6), (messages.at[1], 0, 1, 0)):
        back = 15 - part
        for first, count, place in ((0, back, 0), (back + 3, 24 - back, back)):
            out[pl.ds(place * NZ, count * NZ), :] = own[
                pl.ds(first * NZ * 8 + edge, count * NZ, stride=8), :
            ]
        for z in range(NZ):
            west, east, aim, flag = (
                own[pl.ds((c * NZ + z) * 8, 8), :] for c in (back, back + 2, AIM, WALL)
            )
            mixed = jnp.where(inside < 2, jnp.where(inside == 0, west, aim), flag)
            mixed = jnp.where(inside == 3, east, mixed)
            out[pl.ds(MIXED * NZ + z, 1), :] = mixed[edge : edge + 1]
        for a in range(3):
            out[pl.ds((MIXED + 1 + 3 * a) * NZ, 3 * NZ), :] = own[
                pl.ds((9 * a + part) * NZ * 8 + second, 3 * NZ, stride=8), :
            ]

    ahead = way("gz", "gy")
    first_out[...] = messages[ahead]
    second_out[...] = messages[1 - ahead]


def ahead_kernel(own, two, one):
    def pack(zup, zdown):
        for out, first, second, part in ((zup, NZ - 1, NZ - 2, 2), (zdown, 0, 1, 0)):
            for k, (c, z) in enumerate(z_blocks(first, second, part)):
                out[pl.ds(8 * k, 8), :] = own[pl.ds((c * NZ + z) * 8, 8), :]

    by_parity("gz", one, two, pack)


def y_runs(part):
    back = 15 - part
    return (0, back, 0), (back, 3, None), (back + 3, 24 - back, back)


def spread_mixed(below, above, flags, aims):
    flags[pl.ds(0, NZ), :] = below[pl.ds(MIXED * NZ, NZ), :]
    flags[pl.ds(NZ, NZ), :] = above[pl.ds(MIXED * NZ, NZ), :]
    mixed = flags[pl.ds(0, 2 * NZ), :]
    inside = lax.rem(lane_ids(), 4)
    moved = {k: pltpu.roll(mixed, k % 128, 1) if k else mixed for k in (-2, -1, 0, 1, 2)}

    def from_lane(source):
        value = moved[0]
        for lane in range(4):
            if lane != source:
                value = jnp.where(inside == lane, moved[lane - source], value)
        return value

    aims[pl.ds(0, 2 * NZ), :] = from_lane(1)
    flags[pl.ds(0, 2 * NZ), :] = from_lane(2)


def second_kernel(y_first, y_second, z_one, z_two, flags, aims, halos, messages):
    ahead = way("gz", "gy")
    halos[ahead] = y_first[...]
    halos[1 - ahead] = y_second[...]
    above, below = halos.at[0], halos.at[1]
    spread_mixed(below, above, flags, aims)
    pack_planes(below, above, flags, aims, messages.at[0], messages.at[1])
    ahead = way("gz")
    z_one[...] = messages[ahead]
    z_two[...] = messages[1 - ahead]


def pack_planes(below, above, flags, aims, zup, zdown):
    for out, first, second, part in ((zup, NZ - 1, NZ - 2, 2), (zdown, 0, 1, 0)):
        for side, (halo, inward) in enumerate(((below, 6), (above, 0))):
            near = side * Z_BLOCKS
            for channel, count, place in y_runs(inward):
                if place is None:
                    row = halo[pl.ds(MIXED * NZ + first, 1), :]
                    out[pl.ds(near + channel, 3), :] = jnp.broadcast_to(row, (3, 128))
                else:
                    out[pl.ds(near + channel, count), :] = halo[
                        pl.ds(place * NZ + first, count, stride=NZ), :
                    ]
            out[pl.ds(near + WALL, 1), :] = flags[pl.ds(side * NZ + first, 1), :]
            out[pl.ds(near + AIM, 1), :] = aims[pl.ds(side * NZ + first, 1), :]
            place = 15 if part else 0
            for k, count in ((0, 8), (8, 1)):
                out[pl.ds(near + CHANNELS + k, count), :] = halo[
                    pl.ds((place + k) * NZ + second, count, stride=NZ if count > 1 else 1), :
                ]
            out[pl.ds(near + Z_BLOCKS - 1, 1), :] = flags[pl.ds(side * NZ + second, 1), :]
            far = Z_FAR + 12 * side
            start = (MIXED + 1) * NZ
            out[pl.ds(far, 8), :] = halo[pl.ds(start + first, 8, stride=NZ), :]
            out[pl.ds(far + 8, 1), :] = halo[pl.ds(start + 8 * NZ + first, 1), :]
            for k in range(3):
                row = halo[pl.ds(start + (3 * part + k) * NZ + second, 1), :]
                out[pl.ds(far + 9 + k, 1), :] = row


def plane_at(z):
    return PAD + (z + 2) * PITCH


def add_rows(full, flags, aims, above, below):
    spread_mixed(below, above, flags, aims)

    def put(channel, row, source):
        full[pl.ds(channel * ROWS + plane_at(0) + row, NZ, stride=PITCH), :] = source

    sides = ((below, 1, 0, 6), (above, PITCH - 2, PITCH - 1, 0))
    for side, (halo, near, far, inward) in enumerate(sides):
        for first, count, place in y_runs(inward):
            for k in range(count):
                row = MIXED if place is None else place + k
                put(first + k, near, halo[pl.ds(row * NZ, NZ), :])
        flag = flags[pl.ds(side * NZ, NZ), :]
        put(WALL, near, flag)
        put(WALL, far, flag)
        put(AIM, near, aims[pl.ds(side * NZ, NZ), :])
        for k in range(9):
            q = 9 * (k // 3) + inward + k % 3
            put(q, far, halo[pl.ds((MIXED + 1 + k) * NZ, NZ), :])


def add_own_planes(full, ceiling, floor):
    for halo, near, far, part in ((floor, -1, -2, 2), (ceiling, NZ, NZ + 1, 0)):
        for k, (c, z) in enumerate(z_blocks(near, far, part)):
            full[pl.ds(c * ROWS + plane_at(z) + 2, 8), :] = halo[pl.ds(8 * k, 8), :]


def add_planes(full, ceiling, floor):
    def put(count, channel, z, row, source):
        start = channel * ROWS + plane_at(z) + row
        full[pl.ds(start, count, stride=ROWS), :] = source

    for halo, near, far, part in ((floor, -1, -2, 2), (ceiling, NZ, NZ + 1, 0)):
        for side, (row, beyond, group) in enumerate(((1, 0, 2), (PITCH - 2, PITCH - 1, 0))):
            start = side * Z_BLOCKS
            put(CHANNELS, 0, near, row, halo[pl.ds(start, CHANNELS), :])
            put(9, 9 * part, far, row, halo[pl.ds(start + CHANNELS, 9), :])
            first, second = (halo[pl.ds(start + k, 1), :] for k in (WALL, Z_BLOCKS - 1))
            put(1, WALL, far, row, second)
            start = Z_FAR + 12 * side
            for k in range(3):
                put(3, 9 * k + 3 * group, near, beyond, halo[pl.ds(start + 3 * k, 3), :])
            put(3, 9 * part + 3 * group, far, beyond, halo[pl.ds(start + 9, 3), :])
            put(1, WALL, near, beyond, first)
            put(1, WALL, far, beyond, second)


def pack_columns(full, pack, tiles):
    slot = lane_ids() // 4
    for t in tiles:
        packed = jnp.zeros((8, 128), F32)
        for c in range(CHANNELS):
            moved = pltpu.roll(full[pl.ds(c * ROWS + PAD + 8 * t, 8), :], (4 * c + 2) % 128, 1)
            packed = jnp.where(slot == c, moved, packed)
        pack[pl.ds(8 * t, 8), :] = packed


OWN_TILES = range(2 * PITCH // 8, (NZ + 2) * PITCH // 8)


def fill_kernel(own, y_first, y_second, two, one, full, pack, flags, aims):
    for c in range(CHANNELS):
        for z in range(NZ):
            full[pl.ds(c * ROWS + plane_at(z) + 2, 8), :] = own[pl.ds((c * NZ + z) * 8, 8), :]
    by_roles(y_first, y_second, functools.partial(add_rows, full, flags, aims))
    by_parity("gz", one, two, functools.partial(add_own_planes, full))
    pack_columns(full, pack, OWN_TILES)
    pack[pl.ds(FLAT, 128 - FLAT), :] = jnp.zeros((128 - FLAT, 128), F32)


def third_kernel(part, packed, z_one, z_two, full, pack, columns, message, halos):
    here, last = lax.axis_index("gz"), lax.axis_size("gz") - 1
    ahead = way("gz")
    halos[ahead] = z_one[...]
    halos[1 - ahead] = z_two[...]
    add_planes(full, halos.at[0], halos.at[1])

    ground = pl.ds(WALL * ROWS + plane_at(-1), PITCH)
    full[ground, :] = jnp.where(here == 0, 1.0, full[ground, :])
    for q in range(9):
        above = pl.ds(q * ROWS + plane_at(NZ), PITCH)
        mirrored = full[pl.ds((q + 18) * ROWS + plane_at(NZ - 1), PITCH), :]
        full[above, :] = jnp.where(here == last, mirrored, full[above, :])

    pack_columns(full, pack, [t for t in range(FLAT // 8) if t not in OWN_TILES])
    columns[pl.ds(PAD, 128), :] = pack[...].T

    def row(c, i, count):
        return columns[pl.ds(PAD + 4 * c + i, count), :]

    def returned(q, near, far):
        cx, cy, cz = VEL[q]
        step = (-PITCH * cz - cy) % 128
        value = row(26 - q, near, 8)
        value = pltpu.roll(value, step, 1) if step else value
        return jnp.where(row(WALL, far, 8) != 0.0, value, row(q, far, 8))[:1]

    for c in range(WALL + 1):
        cx = VEL[c][0] if c < 27 else 0
        if cx == 0:
            message[pl.ds(2 * c, 2), :] = row(c, 1, 2)
        elif cx > 0:
            message[pl.ds(2 * c, 1), :] = returned(c, 1, 0)
            message[pl.ds(2 * c + 1, 1), :] = row(c, 1, 1)
        else:
            message[pl.ds(2 * c, 1), :] = row(c, 2, 1)
            message[pl.ds(2 * c + 1, 1), :] = returned(c, 2, 3)


def block_kernel(full, post, walls):
    top = lax.axis_index("gz") == lax.axis_size("gz") - 1
    sponge = (lax.axis_index("gx") * NX + lane_ids()) < SPONGE
    for t in range(ROWS // 8):
        rows = pl.ds(8 * t, 8)
        flags = full[pl.ds(WALL * ROWS + 8 * t, 8), :]
        for cx in (-1, 0, 1):
            walls[cx + 1, rows, :] = pltpu.roll(flags, cx % 128, 1) if cx else flags
    for u in range(UNITS):
        cell = PAD + PITCH + 8 * u
        f = []
        solid = walls[1, pl.ds(cell, 8), :] != 0.0
        for q in range(27):
            cx, cy, cz = VEL[q]
            start = cell - PITCH * cz - cy
            value = full[pl.ds(q * ROWS + start, 8), :]
            if cx:
                value = pltpu.roll(value, cx % 128, 1)
            if q != 13:
                blocked = walls[cx + 1, pl.ds(start, 8), :] != 0.0
                value = jnp.where(blocked, full[pl.ds((26 - q) * ROWS + cell, 8), :], value)
            f.append(jnp.where(solid, WEIGHT[q], value))
        done = relaxed(f, sponge, full[pl.ds(AIM * ROWS + cell, 8), :])
        for q in range(27):
            post[q, pl.ds(8 * u, 8), :] = done[q]

    @pl.when(top)
    def _():
        for q in range(9):
            post[q, pl.ds((NZ + 1) * PITCH, PITCH), :] = post[q + 18, pl.ds(NZ * PITCH, PITCH), :]


def last_kernel(full, block, columns, x_one, x_two, out, west, east, column, walls, back, done, sems):
    here_x, size_x = lax.axis_index("gx"), lax.axis_size("gx")
    top = lax.axis_index("gz") == lax.axis_size("gz") - 1
    lanes, rows = lane_ids(), row_ids()

    if size_x == 2:

        def beside(side, start):
            first = min(max(start, 0), X_ROWS - 8)
            value = x_one[pl.ds(first, 8), :]
            return pltpu.roll(value, (first - start) % 8, 0) if first != start else value

    else:

        def spread(right, left):
            west[pl.ds(PAD, X_ROWS), :] = left[...]
            east[pl.ds(PAD, X_ROWS), :] = right[...]

        by_parity("gx", x_one, x_two, spread)

        def beside(side, start):
            return (west if side < 0 else east)[pl.ds(PAD + start, 8), :]

    def strip_at(c, shift):
        cx = VEL[c][0] if c < 27 else 0
        at = rows - shift
        first = PAD + 4 * c - shift
        value = jnp.where(at < 4, columns[pl.ds(first, 8), :], columns[pl.ds(first - 4, 8), :])
        if c <= WALL and cx >= 0:
            value = jnp.where(at < 2, beside(-1, 2 * c - (cx == 0) - shift), value)
        if c <= WALL and cx <= 0:
            value = jnp.where(at >= 6, beside(1, 2 * c - 6 + (cx == 0) - shift), value)
        if c == WALL:
            value = jnp.where((at == 0) | (at == 7), 0.0, value)
        return value

    strip = [strip_at(c, 0) for c in range(CHANNELS)]
    flags_at = {cx: strip_at(WALL, cx) if cx else strip[WALL] for cx in (-1, 0, 1)}

    def moved_along(value, q):
        cx, cy, cz = VEL[q]
        step = (PITCH * cz + cy) % 128
        return pltpu.roll(value, step, 1) if step else value

    moved = []
    for q in range(27):
        cx = VEL[q][0]
        value = moved_along(strip_at(q, cx) if cx else strip[q], q)
        if q != 13:
            value = jnp.where(moved_along(flags_at[cx], q) != 0.0, strip[26 - q], value)
        moved.append(jnp.where(strip[WALL] != 0.0, WEIGHT[q], value))
    place = here_x * NX + jnp.where(rows < 4, rows - 2, rows + (NX - 6))
    place = lax.rem(place + size_x * NX, size_x * NX)
    sides = relaxed(moved, place < SPONGE, strip[AIM])
    lid = top & (lanes >= (NZ + 2) * PITCH) & (lanes < (NZ + 3) * PITCH)
    for q in range(9):
        sides[q] = jnp.where(lid, pltpu.roll(sides[q + 18], PITCH, 1), sides[q])
    for q, side in enumerate(sides + [strip[WALL]]):
        column[pl.ds(PAD + 8 * q, 8), :] = side

    def picked(wanted):
        value = None
        for sublane, (q, row) in enumerate(wanted):
            moved = column[pl.ds(PAD + 8 * q + row - sublane, 8), :]
            value = moved if value is None else jnp.where(rows == sublane, moved, value)
        return value

    packed = []
    for k in range(9):
        a, b = 3 * k + 2, 3 * k
        packed.append(
            picked([(a, 5), (a, 2), (a, 1), (a, 2), (b, 5), (b, 2), (b, 5), (b, 6)])
        )
    rest = [(3 * k + 1, row) for k in range(9) for row in (5, 2)] + [(27, 1), (27, 6)]
    packed += [picked(rest[i : i + 8]) for i in range(0, len(rest), 8)]
    packed += [jnp.zeros((8, 128), F32)] * (16 - len(packed))
    back[...] = jnp.concatenate(packed, axis=0).T

    def column_at(place, lane, start):
        return pltpu.roll(back[pl.ds(start, 8), :], (lane - place) % 128, 1)

    rim = (lanes == 0) | (lanes == 127)

    def rimmed(q, start):
        k = q // 3
        ends = column_at((8 * k + 5, 73 + 2 * k, 8 * k + 1)[q % 3], 0, PITCH + start)
        return jnp.where(rim, ends, block[q, pl.ds(start, 8), :])

    for u in range(UNITS):
        flags = full[pl.ds(WALL * ROWS + PAD + PITCH + 8 * u, 8), :]
        walls[1, pl.ds(8 * u, 8), :] = flags
        for cx, edge, place in ((1, 0, 90), (-1, 127, 91)):
            walls[cx + 1, pl.ds(8 * u, 8), :] = jnp.where(
                lanes == edge, column_at(place, edge, PITCH + 8 * u), pltpu.roll(flags, cx % 128, 1)
            )

    cells = [(z + 1) * PITCH + 2 for z in range(NZ)]
    solids = [walls[1, pl.ds(cell, 8), :] != 0.0 for cell in cells]

    def streamed(q, z):
        cx, cy, cz = VEL[q]
        cell = cells[z]
        start = cell - PITCH * cz - cy
        if cx > 0:
            side = column_at(8 * (q // 3) + 2, 0, PITCH + start)
            value = jnp.where(lanes < 2, side, pltpu.roll(block[q, pl.ds(start, 8), :], 1, 1))
        elif cx < 0:
            side = column_at(8 * (q // 3) + 6, 126, PITCH + start)
            value = jnp.where(lanes > 125, side, pltpu.roll(block[q, pl.ds(start, 8), :], 127, 1))
        else:
            value = rimmed(q, start)
        if q != 13:
            blocked = walls[cx + 1, pl.ds(start, 8), :] != 0.0
            value = jnp.where(blocked, rimmed(26 - q, cell), value)
        return jnp.where(solids[z], WEIGHT[q], value)

    copies = []
    for first, count in ((0, 9), (9, 8), (17, 6), (23, 4)):
        for q in range(first, first + count):
            for z in range(NZ):
                done[q, z] = streamed(q, z)
        part = pl.ds(first, count)
        copies.append(pltpu.make_async_copy(done.at[part], out.at[part], sems.at[len(copies)]))
        copies[-1].start()
    for copy in copies:
        copy.wait()


def pairs(size, turn, wrap):
    ahead = [(i, (i + 1) % size) for i in range(turn, size if wrap else size - 1, 2)]
    return ahead + [(j, i) for i, j in ahead]


def swap(value, axis, turn, wrap):
    return lax.ppermute(value, axis, pairs(lax.axis_size(axis), turn, wrap))


def swap_mixed(value, turn):
    size, planes = lax.axis_size("gy"), lax.axis_size("gz")
    moves = []
    for k in range(planes):
        moves += [
            (i * planes + k, j * planes + k) for i, j in pairs(size, (turn + k) % 2, True)
        ]
    return lax.ppermute(value, ("gy", "gz"), moves)


def shape(*dims):
    return jax.ShapeDtypeStruct(dims, F32)


def shards(pops, solid, profile_table, profile_index):
    own, y_first, y_second = pl.pallas_call(
        first_kernel,
        out_shape=[shape(CHANNELS * NZ * 8, 128), shape(Y_ROWS, 128), shape(Y_ROWS, 128)],
        in_specs=[HBM] * 4,
        out_specs=[VMEM] * 3,
        scratch_shapes=[
            pltpu.VMEM(pops.shape, F32),
            pltpu.VMEM(solid.shape, jnp.int32),
            pltpu.SMEM(profile_table.shape[::-1], F32),
            pltpu.SMEM(profile_index.shape, jnp.int32),
            pltpu.VMEM((2, Y_ROWS, 128), F32),
            pltpu.SemaphoreType.DMA((6,)),
        ],
        compiler_params=PARAMS,
        name="collide",
    )(*(pltpu.with_memory_space_constraint(a, pltpu.HBM) for a in (pops, solid, profile_table.T, profile_index)))
    y_first = swap_mixed(y_first, 0)
    y_second = swap_mixed(y_second, 1)
    own_two, own_one = pl.pallas_call(
        ahead_kernel,
        out_shape=[shape(Z_BLOCKS * 8, 128)] * 2,
        in_specs=[VMEM],
        out_specs=[VMEM] * 2,
        compiler_params=PARAMS,
        name="pack_own",
    )(own)
    own_two = swap(own_two, "gz", 1, False)
    own_one = swap(own_one, "gz", 0, False)
    z_one, z_two = pl.pallas_call(
        second_kernel,
        out_shape=[shape(Z_ROWS, 128)] * 2,
        in_specs=[VMEM] * 2,
        out_specs=[VMEM] * 2,
        scratch_shapes=[
            *[pltpu.VMEM((4 * NZ, 128), F32)] * 2,
            pltpu.VMEM((2, Y_ROWS, 128), F32),
            pltpu.VMEM((2, Z_ROWS, 128), F32),
        ],
        compiler_params=PARAMS,
        cost_estimate=pl.CostEstimate(flops=10**9, bytes_accessed=2**20, transcendentals=0),
        name="pack_z",
    )(y_first, y_second)
    z_one = swap(z_one, "gz", 0, False)
    z_two = swap(z_two, "gz", 1, False)
    part, packed = pl.pallas_call(
        fill_kernel,
        out_shape=[shape(SLABS * ROWS, 128), shape(128, 128)],
        in_specs=[VMEM] * 5,
        out_specs=[VMEM] * 2,
        scratch_shapes=[pltpu.VMEM((4 * NZ, 128), F32)] * 2,
        compiler_params=PARAMS,
        cost_estimate=pl.CostEstimate(flops=10**6, bytes_accessed=2**22, transcendentals=0),
        name="fill",
    )(own, y_first, y_second, own_two, own_one)
    full, packed, columns, message = pl.pallas_call(
        third_kernel,
        out_shape=[
            shape(SLABS * ROWS, 128),
            shape(128, 128),
            shape(PAD + 128 + PAD, 128),
            shape(X_ROWS, 128),
        ],
        in_specs=[VMEM] * 4,
        out_specs=[VMEM] * 4,
        scratch_shapes=[pltpu.VMEM((2, Z_ROWS, 128), F32)],
        input_output_aliases={0: 0, 1: 1},
        compiler_params=PARAMS,
        name="pack_x",
    )(part, packed, z_one, z_two)
    x_one = swap(message, "gx", 0, True)
    x_two = x_one if lax.axis_size("gx") == 2 else swap(message, "gx", 1, True)
    block = pl.pallas_call(
        block_kernel,
        out_shape=shape(27, UNITS * 8, 128),
        in_specs=[VMEM],
        out_specs=VMEM,
        scratch_shapes=[pltpu.VMEM((3, ROWS, 128), F32)],
        compiler_params=PARAMS,
        cost_estimate=pl.CostEstimate(
            flops=27 * 20 * UNITS * 1024, bytes_accessed=2**22, transcendentals=0
        ),
        name="block",
    )(full)
    return pl.pallas_call(
        last_kernel,
        out_shape=shape(27, NZ, NY, NX),
        in_specs=[VMEM] * 5,
        out_specs=HBM,
        scratch_shapes=[
            pltpu.VMEM((PAD + X_ROWS + PAD, 128), F32),
            pltpu.VMEM((PAD + X_ROWS + PAD, 128), F32),
            pltpu.VMEM((PAD + 28 * 8 + PAD, 128), F32),
            pltpu.VMEM((3, UNITS * 8, 128), F32),
            pltpu.VMEM((128, 128), F32),
            pltpu.VMEM((27, NZ, NY, NX), F32),
            pltpu.SemaphoreType.DMA((NZ,)),
        ],
        compiler_params=PARAMS,
        name="finish",
    )(full, block, columns, x_one, x_two)


def solution(mesh):
    return jax.shard_map(
        shards,
        mesh=mesh,
        in_specs=(P(None, "gz", "gy", "gx"), P("gz", "gy", "gx"), P(None, "gz"), P("gy")),
        out_specs=P(None, "gz", "gy", "gx"),
        check_vma=False,
    )
```

```python
import functools

import jax
import jax.numpy as jnp
import numpy as np
from jax import lax
from jax.experimental import pallas as pl
from jax.experimental.pallas import tpu as pltpu
from jax.sharding import PartitionSpec as P

SPONGE = 32
TAU = 0.52
SMAG = 18.0 * 1.4142135623730951 * 0.17 * 0.17

VEL = [(cx, cy, cz) for cz in (-1, 0, 1) for cy in (-1, 0, 1) for cx in (-1, 0, 1)]
WEIGHT = [
    float(np.array([8.0 / 27.0, 2.0 / 27.0, 1.0 / 54.0, 1.0 / 216.0])[cx * cx + cy * cy + cz * cz])
    for cx, cy, cz in VEL
]
WALL, AIM, CHANNELS = 27, 28, 29
NZ, NY, NX = 4, 8, 128
PITCH = NY + 4
FLAT = (NZ + 4) * PITCH
PAD = 8
ROWS = PAD + FLAT + PAD
SLABS = CHANNELS + 6
UNITS = (NZ + 2) * PITCH // 8

PARAMS = pltpu.CompilerParams(vmem_limit_bytes=12 * 2**20)
VMEM = pl.BlockSpec(memory_space=pltpu.VMEM)
HBM = pl.BlockSpec(memory_space=pltpu.HBM)
F32 = jnp.float32

MIXED = 24
Y_ROWS = (MIXED + 1 + 9) * NZ
Z_BLOCKS = CHANNELS + 10
Z_FAR = 2 * Z_BLOCKS
Z_ROWS = -(-(Z_FAR + 2 * 12) // 8) * 8

X_ROWS = 2 * (WALL + 1)


def relaxed(f, sponge, aim):
    quad = {}
    for cz in (-1, 0, 1):
        line = {}
        for cy in (-1, 0, 1):
            base = 9 * (cz + 1) + 3 * (cy + 1)
            both = f[base + 2] + f[base]
            line[cy] = (both + f[base + 1], f[base + 2] - f[base], both)
        s = line[1][0] + line[-1][0]
        sx = line[1][1] + line[-1][1]
        quad[cz] = dict(
            n=s + line[0][0],
            y=line[1][0] - line[-1][0],
            yy=s,
            x=sx + line[0][1],
            xy=line[1][1] - line[-1][1],
            xx=line[1][2] + line[-1][2] + line[0][2],
        )
    up, mid, down = quad[1], quad[0], quad[-1]
    zz = up["n"] + down["n"]
    rho = zz + mid["n"]
    jz = up["n"] - down["n"]
    jy = up["y"] + down["y"] + mid["y"]
    jx = up["x"] + down["x"] + mid["x"]
    inverse = 1.0 / rho
    ux, uy, uz = jx * inverse, jy * inverse, jz * inverse
    third = rho * (1.0 / 3.0)
    pxx = (up["xx"] + down["xx"] + mid["xx"]) - (third + jx * ux)
    pyy = (up["yy"] + down["yy"] + mid["yy"]) - (third + jy * uy)
    pzz = zz - (third + jz * uz)
    pxy = (up["xy"] + down["xy"] + mid["xy"]) - jx * uy
    pxz = (up["x"] - down["x"]) - jx * uz
    pyz = (up["y"] - down["y"]) - jy * uz
    strain = pxx * pxx + pyy * pyy + pzz * pzz + 2.0 * (pxy * pxy + pxz * pxz + pyz * pyz)
    size = jnp.sqrt(2.0 * strain)
    tau = 0.5 * (TAU + jnp.sqrt(TAU * TAU + SMAG * size * inverse))
    omega = 1.0 / tau
    keep = 1.0 - omega
    if sponge is not None:
        keep = jnp.where(sponge, 0.0, keep)
        omega = jnp.where(sponge, 1.0, omega)
        ux = jnp.where(sponge, aim, ux)
        uy = jnp.where(sponge, 0.0, uy)
        uz = jnp.where(sponge, 0.0, uz)
    square = 1.0 - 1.5 * (ux * ux + uy * uy + uz * uz)
    vx, vy, vz = 3.0 * ux, 3.0 * uy, 3.0 * uz
    share = rho * omega
    weighted = {w: share * w for w in sorted(set(WEIGHT))}
    post = [None] * 27
    for q in range(14):
        cx, cy, cz = VEL[q]
        along = None
        for c, v in ((cx, vx), (cy, vy), (cz, vz)):
            if c:
                along = (v if c > 0 else -v) if along is None else (along + v if c > 0 else along - v)
        scale = weighted[WEIGHT[q]]
        if along is None:
            post[q] = keep * f[q] + scale * square
            continue
        even = square + 0.5 * along * along
        post[q] = keep * f[q] + scale * (even + along)
        post[26 - q] = keep * f[26 - q] + scale * (even - along)
    return post


def lane_ids():
    return lax.broadcasted_iota(jnp.int32, (8, 128), 1)


def row_ids():
    return lax.broadcasted_iota(jnp.int32, (8, 128), 0)


def by_parity(axis, one, two, body):
    even = lax.rem(lax.axis_index(axis), 2) == 0
    pl.when(even)(lambda: body(one, two))
    pl.when(jnp.logical_not(even))(lambda: body(two, one))


def way(*axes):
    return lax.rem(sum(lax.axis_index(axis) for axis in axes), 2)


def by_roles(first, second, body):
    ahead = way("gz", "gy") == 0
    pl.when(ahead)(lambda: body(first, second))
    pl.when(jnp.logical_not(ahead))(lambda: body(second, first))


def z_blocks(near, far, part):
    blocks = [(c, near) for c in range(CHANNELS)]
    return blocks + [(9 * part + k, far) for k in range(9)] + [(WALL, far)]


def first_kernel(pops_at, solid_at, table_at, index_at, own, first_out, *scratch):
    pops, solid, table, index, sems = scratch
    groups = [(pops_at.at[pl.ds(q, 9)], pops.at[pl.ds(q, 9)]) for q in (0, 9, 18)]
    small = [(table_at, table), (index_at, index)]
    copies = [
        pltpu.make_async_copy(source, target, sems.at[i])
        for i, (source, target) in enumerate([*small, *groups, (solid_at, solid)])
    ]
    for copy in copies:
        copy.start()
    for copy in copies[:2]:
        copy.wait()
    lanes, rows = lane_ids(), row_ids()
    sponge = (lax.axis_index("gx") * NX + lanes) < SPONGE
    profiles = [index[y] for y in range(NY)]
    aims = []
    for z in range(NZ):
        aim = jnp.zeros((8, 128), F32)
        for y, profile in enumerate(profiles):
            aim = jnp.where(rows == y, table[z, profile], aim)
        aims.append(aim)
    for copy in copies[2:-1]:
        copy.wait()
    for z, aim in enumerate(aims):
        post = relaxed([pops[q, z] for q in range(27)], sponge, aim)
        for q in range(27):
            own[pl.ds((q * NZ + z) * 8, 8), :] = post[q]
        own[pl.ds((AIM * NZ + z) * 8, 8), :] = aim
    copies[-1].wait()
    for z in range(NZ):
        own[pl.ds((WALL * NZ + z) * 8, 8), :] = solid[z].astype(F32)

    ahead = way("gz", "gy") == 0
    pl.when(ahead)(lambda: pack_rows(own, first_out, True))
    pl.when(jnp.logical_not(ahead))(lambda: pack_rows(own, first_out, False))


def pack_rows(own, out, upward):
    inside = lax.rem(lane_ids(), 4)
    edge, second, part = (7, 6, 6) if upward else (0, 1, 0)
    back = 15 - part
    for first, count, place in ((0, back, 0), (back + 3, 24 - back, back)):
        out[pl.ds(place * NZ, count * NZ), :] = own[
            pl.ds(first * NZ * 8 + edge, count * NZ, stride=8), :
        ]
    for z in range(NZ):
        west, east, aim, flag = (
            own[pl.ds((c * NZ + z) * 8, 8), :] for c in (back, back + 2, AIM, WALL)
        )
        mixed = jnp.where(inside < 2, jnp.where(inside == 0, west, aim), flag)
        mixed = jnp.where(inside == 3, east, mixed)
        out[pl.ds(MIXED * NZ + z, 1), :] = mixed[edge : edge + 1]
    for a in range(3):
        out[pl.ds((MIXED + 1 + 3 * a) * NZ, 3 * NZ), :] = own[
            pl.ds((9 * a + part) * NZ * 8 + second, 3 * NZ, stride=8), :
        ]


def ahead_kernel(own, two, one, second_out):
    ahead = way("gz", "gy") == 0
    pl.when(ahead)(lambda: pack_rows(own, second_out, False))
    pl.when(jnp.logical_not(ahead))(lambda: pack_rows(own, second_out, True))

    def pack(zup, zdown):
        for out, first, second, part in ((zup, NZ - 1, NZ - 2, 2), (zdown, 0, 1, 0)):
            for k, (c, z) in enumerate(z_blocks(first, second, part)):
                out[pl.ds(8 * k, 8), :] = own[pl.ds((c * NZ + z) * 8, 8), :]

    by_parity("gz", one, two, pack)


def y_runs(part):
    back = 15 - part
    return (0, back, 0), (back, 3, None), (back + 3, 24 - back, back)


def spread_mixed(below, above, flags, aims):
    flags[pl.ds(0, NZ), :] = below[pl.ds(MIXED * NZ, NZ), :]
    flags[pl.ds(NZ, NZ), :] = above[pl.ds(MIXED * NZ, NZ), :]
    mixed = flags[pl.ds(0, 2 * NZ), :]
    inside = lax.rem(lane_ids(), 4)
    moved = {k: pltpu.roll(mixed, k % 128, 1) if k else mixed for k in (-2, -1, 0, 1, 2)}

    def from_lane(source):
        value = moved[0]
        for lane in range(4):
            if lane != source:
                value = jnp.where(inside == lane, moved[lane - source], value)
        return value

    aims[pl.ds(0, 2 * NZ), :] = from_lane(1)
    flags[pl.ds(0, 2 * NZ), :] = from_lane(2)


def second_kernel(y_first, y_second, z_one, z_two, flags, aims, halos, messages):
    ahead = way("gz", "gy")
    halos[ahead] = y_first[...]
    halos[1 - ahead] = y_second[...]
    above, below = halos.at[0], halos.at[1]
    spread_mixed(below, above, flags, aims)
    pack_planes(below, above, flags, aims, messages.at[0], messages.at[1])
    ahead = way("gz")
    z_one[...] = messages[ahead]
    z_two[...] = messages[1 - ahead]


def pack_planes(below, above, flags, aims, zup, zdown):
    for out, first, second, part in ((zup, NZ - 1, NZ - 2, 2), (zdown, 0, 1, 0)):
        for side, (halo, inward) in enumerate(((below, 6), (above, 0))):
            near = side * Z_BLOCKS
            for channel, count, place in y_runs(inward):
                if place is None:
                    row = halo[pl.ds(MIXED * NZ + first, 1), :]
                    out[pl.ds(near + channel, 3), :] = jnp.broadcast_to(row, (3, 128))
                else:
                    out[pl.ds(near + channel, count), :] = halo[
                        pl.ds(place * NZ + first, count, stride=NZ), :
                    ]
            out[pl.ds(near + WALL, 1), :] = flags[pl.ds(side * NZ + first, 1), :]
            out[pl.ds(near + AIM, 1), :] = aims[pl.ds(side * NZ + first, 1), :]
            place = 15 if part else 0
            for k, count in ((0, 8), (8, 1)):
                out[pl.ds(near + CHANNELS + k, count), :] = halo[
                    pl.ds((place + k) * NZ + second, count, stride=NZ if count > 1 else 1), :
                ]
            out[pl.ds(near + Z_BLOCKS - 1, 1), :] = flags[pl.ds(side * NZ + second, 1), :]
            far = Z_FAR + 12 * side
            start = (MIXED + 1) * NZ
            out[pl.ds(far, 8), :] = halo[pl.ds(start + first, 8, stride=NZ), :]
            out[pl.ds(far + 8, 1), :] = halo[pl.ds(start + 8 * NZ + first, 1), :]
            for k in range(3):
                row = halo[pl.ds(start + (3 * part + k) * NZ + second, 1), :]
                out[pl.ds(far + 9 + k, 1), :] = row


def plane_at(z):
    return PAD + (z + 2) * PITCH


def add_rows(full, flags, aims, above, below):
    spread_mixed(below, above, flags, aims)

    def put(channel, row, source):
        full[pl.ds(channel * ROWS + plane_at(0) + row, NZ, stride=PITCH), :] = source

    sides = ((below, 1, 0, 6), (above, PITCH - 2, PITCH - 1, 0))
    for side, (halo, near, far, inward) in enumerate(sides):
        for first, count, place in y_runs(inward):
            for k in range(count):
                row = MIXED if place is None else place + k
                put(first + k, near, halo[pl.ds(row * NZ, NZ), :])
        flag = flags[pl.ds(side * NZ, NZ), :]
        put(WALL, near, flag)
        put(WALL, far, flag)
        put(AIM, near, aims[pl.ds(side * NZ, NZ), :])
        for k in range(9):
            q = 9 * (k // 3) + inward + k % 3
            put(q, far, halo[pl.ds((MIXED + 1 + k) * NZ, NZ), :])


def add_own_planes(full, ceiling, floor):
    for halo, near, far, part in ((floor, -1, -2, 2), (ceiling, NZ, NZ + 1, 0)):
        for k, (c, z) in enumerate(z_blocks(near, far, part)):
            full[pl.ds(c * ROWS + plane_at(z) + 2, 8), :] = halo[pl.ds(8 * k, 8), :]


def add_planes(full, ceiling, floor):
    def put(count, channel, z, row, source):
        start = channel * ROWS + plane_at(z) + row
        full[pl.ds(start, count, stride=ROWS), :] = source

    for halo, near, far, part in ((floor, -1, -2, 2), (ceiling, NZ, NZ + 1, 0)):
        for side, (row, beyond, group) in enumerate(((1, 0, 2), (PITCH - 2, PITCH - 1, 0))):
            start = side * Z_BLOCKS
            put(CHANNELS, 0, near, row, halo[pl.ds(start, CHANNELS), :])
            put(9, 9 * part, far, row, halo[pl.ds(start + CHANNELS, 9), :])
            first, second = (halo[pl.ds(start + k, 1), :] for k in (WALL, Z_BLOCKS - 1))
            put(1, WALL, far, row, second)
            start = Z_FAR + 12 * side
            for k in range(3):
                put(3, 9 * k + 3 * group, near, beyond, halo[pl.ds(start + 3 * k, 3), :])
            put(3, 9 * part + 3 * group, far, beyond, halo[pl.ds(start + 9, 3), :])
            put(1, WALL, near, beyond, first)
            put(1, WALL, far, beyond, second)


def pack_columns(full, pack, tiles):
    slot = lane_ids() // 4
    for t in tiles:
        packed = jnp.zeros((8, 128), F32)
        for c in range(CHANNELS):
            moved = pltpu.roll(full[pl.ds(c * ROWS + PAD + 8 * t, 8), :], (4 * c + 2) % 128, 1)
            packed = jnp.where(slot == c, moved, packed)
        pack[pl.ds(8 * t, 8), :] = packed


OWN_TILES = range(2 * PITCH // 8, (NZ + 2) * PITCH // 8)


def fill_kernel(own, y_first, y_second, two, one, full, pack, flags, aims):
    for c in range(CHANNELS):
        for z in range(NZ):
            full[pl.ds(c * ROWS + plane_at(z) + 2, 8), :] = own[pl.ds((c * NZ + z) * 8, 8), :]
    by_roles(y_first, y_second, functools.partial(add_rows, full, flags, aims))
    by_parity("gz", one, two, functools.partial(add_own_planes, full))
    pack_columns(full, pack, OWN_TILES)
    pack[pl.ds(FLAT, 128 - FLAT), :] = jnp.zeros((128 - FLAT, 128), F32)


def third_kernel(part, packed, z_one, z_two, full, pack, columns, message, halos):
    here, last = lax.axis_index("gz"), lax.axis_size("gz") - 1
    ahead = way("gz")
    halos[ahead] = z_one[...]
    halos[1 - ahead] = z_two[...]
    add_planes(full, halos.at[0], halos.at[1])

    ground = pl.ds(WALL * ROWS + plane_at(-1), PITCH)
    full[ground, :] = jnp.where(here == 0, 1.0, full[ground, :])
    for q in range(9):
        above = pl.ds(q * ROWS + plane_at(NZ), PITCH)
        mirrored = full[pl.ds((q + 18) * ROWS + plane_at(NZ - 1), PITCH), :]
        full[above, :] = jnp.where(here == last, mirrored, full[above, :])

    pack_columns(full, pack, [t for t in range(FLAT // 8) if t not in OWN_TILES])
    columns[pl.ds(PAD, 128), :] = pack[...].T

    def row(c, i, count):
        return columns[pl.ds(PAD + 4 * c + i, count), :]

    def returned(q, near, far):
        cx, cy, cz = VEL[q]
        step = (-PITCH * cz - cy) % 128
        value = row(26 - q, near, 8)
        value = pltpu.roll(value, step, 1) if step else value
        return jnp.where(row(WALL, far, 8) != 0.0, value, row(q, far, 8))[:1]

    for c in range(WALL + 1):
        cx = VEL[c][0] if c < 27 else 0
        if cx == 0:
            message[pl.ds(2 * c, 2), :] = row(c, 1, 2)
        elif cx > 0:
            message[pl.ds(2 * c, 1), :] = returned(c, 1, 0)
            message[pl.ds(2 * c + 1, 1), :] = row(c, 1, 1)
        else:
            message[pl.ds(2 * c, 1), :] = row(c, 2, 1)
            message[pl.ds(2 * c + 1, 1), :] = returned(c, 2, 3)


def block_kernel(full, post, walls):
    top = lax.axis_index("gz") == lax.axis_size("gz") - 1
    sponge = (lax.axis_index("gx") * NX + lane_ids()) < SPONGE
    for t in range(ROWS // 8):
        rows = pl.ds(8 * t, 8)
        flags = full[pl.ds(WALL * ROWS + 8 * t, 8), :]
        for cx in (-1, 0, 1):
            walls[cx + 1, rows, :] = pltpu.roll(flags, cx % 128, 1) if cx else flags
    for u in range(UNITS):
        cell = PAD + PITCH + 8 * u
        f = []
        solid = walls[1, pl.ds(cell, 8), :] != 0.0
        for q in range(27):
            cx, cy, cz = VEL[q]
            start = cell - PITCH * cz - cy
            value = full[pl.ds(q * ROWS + start, 8), :]
            if cx:
                value = pltpu.roll(value, cx % 128, 1)
            if q != 13:
                blocked = walls[cx + 1, pl.ds(start, 8), :] != 0.0
                value = jnp.where(blocked, full[pl.ds((26 - q) * ROWS + cell, 8), :], value)
            f.append(jnp.where(solid, WEIGHT[q], value))
        done = relaxed(f, sponge, full[pl.ds(AIM * ROWS + cell, 8), :])
        for q in range(27):
            post[q, pl.ds(8 * u, 8), :] = done[q]

    @pl.when(top)
    def _():
        for q in range(9):
            post[q, pl.ds((NZ + 1) * PITCH, PITCH), :] = post[q + 18, pl.ds(NZ * PITCH, PITCH), :]


def last_kernel(full, block, columns, x_one, x_two, out, west, east, column, walls, back, done, sems):
    here_x, size_x = lax.axis_index("gx"), lax.axis_size("gx")
    top = lax.axis_index("gz") == lax.axis_size("gz") - 1
    lanes, rows = lane_ids(), row_ids()

    if size_x == 2:

        def beside(side, start):
            first = min(max(start, 0), X_ROWS - 8)
            value = x_one[pl.ds(first, 8), :]
            return pltpu.roll(value, (first - start) % 8, 0) if first != start else value

    else:

        def spread(right, left):
            west[pl.ds(PAD, X_ROWS), :] = left[...]
            east[pl.ds(PAD, X_ROWS), :] = right[...]

        by_parity("gx", x_one, x_two, spread)

        def beside(side, start):
            return (west if side < 0 else east)[pl.ds(PAD + start, 8), :]

    def strip_at(c, shift):
        cx = VEL[c][0] if c < 27 else 0
        at = rows - shift
        first = PAD + 4 * c - shift
        value = jnp.where(at < 4, columns[pl.ds(first, 8), :], columns[pl.ds(first - 4, 8), :])
        if c <= WALL and cx >= 0:
            value = jnp.where(at < 2, beside(-1, 2 * c - (cx == 0) - shift), value)
        if c <= WALL and cx <= 0:
            value = jnp.where(at >= 6, beside(1, 2 * c - 6 + (cx == 0) - shift), value)
        if c == WALL:
            value = jnp.where((at == 0) | (at == 7), 0.0, value)
        return value

    strip = [strip_at(c, 0) for c in range(CHANNELS)]
    flags_at = {cx: strip_at(WALL, cx) if cx else strip[WALL] for cx in (-1, 0, 1)}

    def moved_along(value, q):
        cx, cy, cz = VEL[q]
        step = (PITCH * cz + cy) % 128
        return pltpu.roll(value, step, 1) if step else value

    moved = []
    for q in range(27):
        cx = VEL[q][0]
        value = moved_along(strip_at(q, cx) if cx else strip[q], q)
        if q != 13:
            value = jnp.where(moved_along(flags_at[cx], q) != 0.0, strip[26 - q], value)
        moved.append(jnp.where(strip[WALL] != 0.0, WEIGHT[q], value))
    place = here_x * NX + jnp.where(rows < 4, rows - 2, rows + (NX - 6))
    place = lax.rem(place + size_x * NX, size_x * NX)
    sides = relaxed(moved, place < SPONGE, strip[AIM])
    lid = top & (lanes >= (NZ + 2) * PITCH) & (lanes < (NZ + 3) * PITCH)
    for q in range(9):
        sides[q] = jnp.where(lid, pltpu.roll(sides[q + 18], PITCH, 1), sides[q])
    for q, side in enumerate(sides + [strip[WALL]]):
        column[pl.ds(PAD + 8 * q, 8), :] = side

    def picked(wanted):
        value = None
        for sublane, (q, row) in enumerate(wanted):
            moved = column[pl.ds(PAD + 8 * q + row - sublane, 8), :]
            value = moved if value is None else jnp.where(rows == sublane, moved, value)
        return value

    packed = []
    for k in range(9):
        a, b = 3 * k + 2, 3 * k
        packed.append(
            picked([(a, 5), (a, 2), (a, 1), (a, 2), (b, 5), (b, 2), (b, 5), (b, 6)])
        )
    rest = [(3 * k + 1, row) for k in range(9) for row in (5, 2)] + [(27, 1), (27, 6)]
    packed += [picked(rest[i : i + 8]) for i in range(0, len(rest), 8)]
    packed += [jnp.zeros((8, 128), F32)] * (16 - len(packed))
    back[...] = jnp.concatenate(packed, axis=0).T

    def column_at(place, lane, start):
        return pltpu.roll(back[pl.ds(start, 8), :], (lane - place) % 128, 1)

    rim = (lanes == 0) | (lanes == 127)

    def rimmed(q, start):
        k = q // 3
        ends = column_at((8 * k + 5, 73 + 2 * k, 8 * k + 1)[q % 3], 0, PITCH + start)
        return jnp.where(rim, ends, block[q, pl.ds(start, 8), :])

    for u in range(UNITS):
        flags = full[pl.ds(WALL * ROWS + PAD + PITCH + 8 * u, 8), :]
        walls[1, pl.ds(8 * u, 8), :] = flags
        for cx, edge, place in ((1, 0, 90), (-1, 127, 91)):
            walls[cx + 1, pl.ds(8 * u, 8), :] = jnp.where(
                lanes == edge, column_at(place, edge, PITCH + 8 * u), pltpu.roll(flags, cx % 128, 1)
            )

    cells = [(z + 1) * PITCH + 2 for z in range(NZ)]
    solids = [walls[1, pl.ds(cell, 8), :] != 0.0 for cell in cells]

    def streamed(q, z):
        cx, cy, cz = VEL[q]
        cell = cells[z]
        start = cell - PITCH * cz - cy
        if cx > 0:
            side = column_at(8 * (q // 3) + 2, 0, PITCH + start)
            value = jnp.where(lanes < 2, side, pltpu.roll(block[q, pl.ds(start, 8), :], 1, 1))
        elif cx < 0:
            side = column_at(8 * (q // 3) + 6, 126, PITCH + start)
            value = jnp.where(lanes > 125, side, pltpu.roll(block[q, pl.ds(start, 8), :], 127, 1))
        else:
            value = rimmed(q, start)
        if q != 13:
            blocked = walls[cx + 1, pl.ds(start, 8), :] != 0.0
            value = jnp.where(blocked, rimmed(26 - q, cell), value)
        return jnp.where(solids[z], WEIGHT[q], value)

    copies = []
    for first, count in ((0, 9), (9, 8), (17, 6), (23, 4)):
        for q in range(first, first + count):
            for z in range(NZ):
                done[q, z] = streamed(q, z)
        part = pl.ds(first, count)
        copies.append(pltpu.make_async_copy(done.at[part], out.at[part], sems.at[len(copies)]))
        copies[-1].start()
    for copy in copies:
        copy.wait()


def pairs(size, turn, wrap):
    ahead = [(i, (i + 1) % size) for i in range(turn, size if wrap else size - 1, 2)]
    return ahead + [(j, i) for i, j in ahead]


def swap(value, axis, turn, wrap):
    return lax.ppermute(value, axis, pairs(lax.axis_size(axis), turn, wrap))


def swap_mixed(value, turn):
    size, planes = lax.axis_size("gy"), lax.axis_size("gz")
    moves = []
    for k in range(planes):
        moves += [
            (i * planes + k, j * planes + k) for i, j in pairs(size, (turn + k) % 2, True)
        ]
    return lax.ppermute(value, ("gy", "gz"), moves)


def shape(*dims):
    return jax.ShapeDtypeStruct(dims, F32)


def shards(pops, solid, profile_table, profile_index):
    own, y_first = pl.pallas_call(
        first_kernel,
        out_shape=[shape(CHANNELS * NZ * 8, 128), shape(Y_ROWS, 128)],
        in_specs=[HBM] * 4,
        out_specs=[VMEM] * 2,
        scratch_shapes=[
            pltpu.VMEM(pops.shape, F32),
            pltpu.VMEM(solid.shape, jnp.int32),
            pltpu.SMEM(profile_table.shape[::-1], F32),
            pltpu.SMEM(profile_index.shape, jnp.int32),
            pltpu.SemaphoreType.DMA((6,)),
        ],
        compiler_params=PARAMS,
        name="collide",
    )(*(pltpu.with_memory_space_constraint(a, pltpu.HBM) for a in (pops, solid, profile_table.T, profile_index)))
    y_first = swap_mixed(y_first, 0)
    own_two, own_one, y_second = pl.pallas_call(
        ahead_kernel,
        out_shape=[*[shape(Z_BLOCKS * 8, 128)] * 2, shape(Y_ROWS, 128)],
        in_specs=[VMEM],
        out_specs=[VMEM] * 3,
        compiler_params=PARAMS,
        name="pack_own",
    )(own)
    own_two = swap(own_two, "gz", 1, False)
    own_one = swap(own_one, "gz", 0, False)
    y_second = swap_mixed(y_second, 1)
    z_one, z_two = pl.pallas_call(
        second_kernel,
        out_shape=[shape(Z_ROWS, 128)] * 2,
        in_specs=[VMEM] * 2,
        out_specs=[VMEM] * 2,
        scratch_shapes=[
            *[pltpu.VMEM((4 * NZ, 128), F32)] * 2,
            pltpu.VMEM((2, Y_ROWS, 128), F32),
            pltpu.VMEM((2, Z_ROWS, 128), F32),
        ],
        compiler_params=PARAMS,
        cost_estimate=pl.CostEstimate(flops=10**9, bytes_accessed=2**20, transcendentals=0),
        name="pack_z",
    )(y_first, y_second)
    z_one = swap(z_one, "gz", 0, False)
    z_two = swap(z_two, "gz", 1, False)
    part, packed = pl.pallas_call(
        fill_kernel,
        out_shape=[shape(SLABS * ROWS, 128), shape(128, 128)],
        in_specs=[VMEM] * 5,
        out_specs=[VMEM] * 2,
        scratch_shapes=[pltpu.VMEM((4 * NZ, 128), F32)] * 2,
        compiler_params=PARAMS,
        cost_estimate=pl.CostEstimate(flops=10**6, bytes_accessed=2**22, transcendentals=0),
        name="fill",
    )(own, y_first, y_second, own_two, own_one)
    full, packed, columns, message = pl.pallas_call(
        third_kernel,
        out_shape=[
            shape(SLABS * ROWS, 128),
            shape(128, 128),
            shape(PAD + 128 + PAD, 128),
            shape(X_ROWS, 128),
        ],
        in_specs=[VMEM] * 4,
        out_specs=[VMEM] * 4,
        scratch_shapes=[pltpu.VMEM((2, Z_ROWS, 128), F32)],
        input_output_aliases={0: 0, 1: 1},
        compiler_params=PARAMS,
        name="pack_x",
    )(part, packed, z_one, z_two)
    x_one = swap(message, "gx", 0, True)
    x_two = x_one if lax.axis_size("gx") == 2 else swap(message, "gx", 1, True)
    block = pl.pallas_call(
        block_kernel,
        out_shape=shape(27, UNITS * 8, 128),
        in_specs=[VMEM],
        out_specs=VMEM,
        scratch_shapes=[pltpu.VMEM((3, ROWS, 128), F32)],
        compiler_params=PARAMS,
        cost_estimate=pl.CostEstimate(
            flops=27 * 20 * UNITS * 1024, bytes_accessed=2**22, transcendentals=0
        ),
        name="block",
    )(full)
    return pl.pallas_call(
        last_kernel,
        out_shape=shape(27, NZ, NY, NX),
        in_specs=[VMEM] * 5,
        out_specs=HBM,
        scratch_shapes=[
            pltpu.VMEM((PAD + X_ROWS + PAD, 128), F32),
            pltpu.VMEM((PAD + X_ROWS + PAD, 128), F32),
            pltpu.VMEM((PAD + 28 * 8 + PAD, 128), F32),
            pltpu.VMEM((3, UNITS * 8, 128), F32),
            pltpu.VMEM((128, 128), F32),
            pltpu.VMEM((27, NZ, NY, NX), F32),
            pltpu.SemaphoreType.DMA((NZ,)),
        ],
        compiler_params=PARAMS,
        name="finish",
    )(full, block, columns, x_one, x_two)


def solution(mesh):
    return jax.shard_map(
        shards,
        mesh=mesh,
        in_specs=(P(None, "gz", "gy", "gx"), P("gz", "gy", "gx"), P(None, "gz"), P("gy")),
        out_specs=P(None, "gz", "gy", "gx"),
        check_vma=False,
    )
```

```python
import functools

import jax
import jax.numpy as jnp
import numpy as np
from jax import lax
from jax.experimental import pallas as pl
from jax.experimental.pallas import tpu as pltpu
from jax.sharding import PartitionSpec as P

SPONGE = 32
TAU = 0.52
SMAG = 18.0 * 1.4142135623730951 * 0.17 * 0.17

VEL = [(cx, cy, cz) for cz in (-1, 0, 1) for cy in (-1, 0, 1) for cx in (-1, 0, 1)]
WEIGHT = [
    float(np.array([8.0 / 27.0, 2.0 / 27.0, 1.0 / 54.0, 1.0 / 216.0])[cx * cx + cy * cy + cz * cz])
    for cx, cy, cz in VEL
]
WALL, AIM, CHANNELS = 27, 28, 29
NZ, NY, NX = 4, 8, 128
PITCH = NY + 4
FLAT = (NZ + 4) * PITCH
PAD = 8
ROWS = PAD + FLAT + PAD
SLABS = CHANNELS + 6
UNITS = (NZ + 2) * PITCH // 8

PARAMS = pltpu.CompilerParams(vmem_limit_bytes=12 * 2**20)
VMEM = pl.BlockSpec(memory_space=pltpu.VMEM)
HBM = pl.BlockSpec(memory_space=pltpu.HBM)
F32 = jnp.float32

MIXED = 24
Y_ROWS = (MIXED + 1 + 9) * NZ
Z_BLOCKS = CHANNELS + 10
Z_FAR = 2 * Z_BLOCKS
Z_ROWS = -(-(Z_FAR + 2 * 12) // 8) * 8

X_ROWS = 2 * (WALL + 1)


def relaxed(f, sponge, aim):
    quad = {}
    for cz in (-1, 0, 1):
        line = {}
        for cy in (-1, 0, 1):
            base = 9 * (cz + 1) + 3 * (cy + 1)
            both = f[base + 2] + f[base]
            line[cy] = (both + f[base + 1], f[base + 2] - f[base], both)
        s = line[1][0] + line[-1][0]
        sx = line[1][1] + line[-1][1]
        quad[cz] = dict(
            n=s + line[0][0],
            y=line[1][0] - line[-1][0],
            yy=s,
            x=sx + line[0][1],
            xy=line[1][1] - line[-1][1],
            xx=line[1][2] + line[-1][2] + line[0][2],
        )
    up, mid, down = quad[1], quad[0], quad[-1]
    zz = up["n"] + down["n"]
    rho = zz + mid["n"]
    jz = up["n"] - down["n"]
    jy = up["y"] + down["y"] + mid["y"]
    jx = up["x"] + down["x"] + mid["x"]
    inverse = 1.0 / rho
    ux, uy, uz = jx * inverse, jy * inverse, jz * inverse
    third = rho * (1.0 / 3.0)
    pxx = (up["xx"] + down["xx"] + mid["xx"]) - (third + jx * ux)
    pyy = (up["yy"] + down["yy"] + mid["yy"]) - (third + jy * uy)
    pzz = zz - (third + jz * uz)
    pxy = (up["xy"] + down["xy"] + mid["xy"]) - jx * uy
    pxz = (up["x"] - down["x"]) - jx * uz
    pyz = (up["y"] - down["y"]) - jy * uz
    strain = pxx * pxx + pyy * pyy + pzz * pzz + 2.0 * (pxy * pxy + pxz * pxz + pyz * pyz)
    size = jnp.sqrt(2.0 * strain)
    tau = 0.5 * (TAU + jnp.sqrt(TAU * TAU + SMAG * size * inverse))
    omega = 1.0 / tau
    keep = 1.0 - omega
    if sponge is not None:
        keep = jnp.where(sponge, 0.0, keep)
        omega = jnp.where(sponge, 1.0, omega)
        ux = jnp.where(sponge, aim, ux)
        uy = jnp.where(sponge, 0.0, uy)
        uz = jnp.where(sponge, 0.0, uz)
    square = 1.0 - 1.5 * (ux * ux + uy * uy + uz * uz)
    vx, vy, vz = 3.0 * ux, 3.0 * uy, 3.0 * uz
    share = rho * omega
    weighted = {w: share * w for w in sorted(set(WEIGHT))}
    post = [None] * 27
    for q in range(14):
        cx, cy, cz = VEL[q]
        along = None
        for c, v in ((cx, vx), (cy, vy), (cz, vz)):
            if c:
                along = (v if c > 0 else -v) if along is None else (along + v if c > 0 else along - v)
        scale = weighted[WEIGHT[q]]
        if along is None:
            post[q] = keep * f[q] + scale * square
            continue
        even = square + 0.5 * along * along
        post[q] = keep * f[q] + scale * (even + along)
        post[26 - q] = keep * f[26 - q] + scale * (even - along)
    return post


def lane_ids():
    return lax.broadcasted_iota(jnp.int32, (8, 128), 1)


def row_ids():
    return lax.broadcasted_iota(jnp.int32, (8, 128), 0)


def by_parity(axis, one, two, body):
    even = lax.rem(lax.axis_index(axis), 2) == 0
    pl.when(even)(lambda: body(one, two))
    pl.when(jnp.logical_not(even))(lambda: body(two, one))


def way(*axes):
    return lax.rem(sum(lax.axis_index(axis) for axis in axes), 2)


def by_roles(first, second, body):
    ahead = way("gz", "gy") == 0
    pl.when(ahead)(lambda: body(first, second))
    pl.when(jnp.logical_not(ahead))(lambda: body(second, first))


def z_blocks(near, far, part):
    blocks = [(c, near) for c in range(CHANNELS)]
    return blocks + [(9 * part + k, far) for k in range(9)] + [(WALL, far)]


def first_kernel(pops_at, solid_at, table_at, index_at, own, first_out, second_out, *scratch):
    pops, solid, table, index, messages, sems = scratch
    groups = [(pops_at.at[pl.ds(q, 9)], pops.at[pl.ds(q, 9)]) for q in (0, 9, 18)]
    small = [(table_at, table), (index_at, index)]
    copies = [
        pltpu.make_async_copy(source, target, sems.at[i])
        for i, (source, target) in enumerate([*small, *groups, (solid_at, solid)])
    ]
    for copy in copies:
        copy.start()
    for copy in copies[:2]:
        copy.wait()
    lanes, rows = lane_ids(), row_ids()
    sponge = (lax.axis_index("gx") * NX + lanes) < SPONGE
    profiles = [index[y] for y in range(NY)]
    aims = []
    for z in range(NZ):
        aim = jnp.zeros((8, 128), F32)
        for y, profile in enumerate(profiles):
            aim = jnp.where(rows == y, table[z, profile], aim)
        aims.append(aim)
    for copy in copies[2:-1]:
        copy.wait()
    for z, aim in enumerate(aims):
        post = relaxed([pops[q, z] for q in range(27)], sponge, aim)
        for q in range(27):
            own[pl.ds((q * NZ + z) * 8, 8), :] = post[q]
        own[pl.ds((AIM * NZ + z) * 8, 8), :] = aim
    copies[-1].wait()
    for z in range(NZ):
        own[pl.ds((WALL * NZ + z) * 8, 8), :] = solid[z].astype(F32)

    inside = lax.rem(lanes, 4)
    for out, edge, second, part in ((messages.at[0], 7, 6, 6), (messages.at[1], 0, 1, 0)):
        back = 15 - part
        for first, count, place in ((0, back, 0), (back + 3, 24 - back, back)):
            out[pl.ds(place * NZ, count * NZ), :] = own[
                pl.ds(first * NZ * 8 + edge, count * NZ, stride=8), :
            ]
        for z in range(NZ):
            west, east, aim, flag = (
                own[pl.ds((c * NZ + z) * 8, 8), :] for c in (back, back + 2, AIM, WALL)
            )
            mixed = jnp.where(inside < 2, jnp.where(inside == 0, west, aim), flag)
            mixed = jnp.where(inside == 3, east, mixed)
            out[pl.ds(MIXED * NZ + z, 1), :] = mixed[edge : edge + 1]
        for a in range(3):
            out[pl.ds((MIXED + 1 + 3 * a) * NZ, 3 * NZ), :] = own[
                pl.ds((9 * a + part) * NZ * 8 + second, 3 * NZ, stride=8), :
            ]

    ahead = way("gz", "gy")
    first_out[...] = messages[ahead]
    second_out[...] = messages[1 - ahead]


def ahead_kernel(own, two, one):
    def pack(zup, zdown):
        for out, first, second, part in ((zup, NZ - 1, NZ - 2, 2), (zdown, 0, 1, 0)):
            for k, (c, z) in enumerate(z_blocks(first, second, part)):
                out[pl.ds(8 * k, 8), :] = own[pl.ds((c * NZ + z) * 8, 8), :]

    by_parity("gz", one, two, pack)


def y_runs(part):
    back = 15 - part
    return (0, back, 0), (back, 3, None), (back + 3, 24 - back, back)


def spread_mixed(below, above, flags, aims):
    flags[pl.ds(0, NZ), :] = below[pl.ds(MIXED * NZ, NZ), :]
    flags[pl.ds(NZ, NZ), :] = above[pl.ds(MIXED * NZ, NZ), :]
    mixed = flags[pl.ds(0, 2 * NZ), :]
    inside = lax.rem(lane_ids(), 4)
    moved = {k: pltpu.roll(mixed, k % 128, 1) if k else mixed for k in (-2, -1, 0, 1, 2)}

    def from_lane(source):
        value = moved[0]
        for lane in range(4):
            if lane != source:
                value = jnp.where(inside == lane, moved[lane - source], value)
        return value

    aims[pl.ds(0, 2 * NZ), :] = from_lane(1)
    flags[pl.ds(0, 2 * NZ), :] = from_lane(2)


def second_kernel(y_first, y_second, z_one, z_two, flags, aims, halos, messages):
    ahead = way("gz", "gy")
    halos[ahead] = y_first[...]
    halos[1 - ahead] = y_second[...]
    above, below = halos.at[0], halos.at[1]
    spread_mixed(below, above, flags, aims)
    pack_planes(below, above, flags, aims, messages.at[0], messages.at[1])
    ahead = way("gz")
    z_one[...] = messages[ahead]
    z_two[...] = messages[1 - ahead]


def pack_planes(below, above, flags, aims, zup, zdown):
    for out, first, second, part in ((zup, NZ - 1, NZ - 2, 2), (zdown, 0, 1, 0)):
        for side, (halo, inward) in enumerate(((below, 6), (above, 0))):
            near = side * Z_BLOCKS
            for channel, count, place in y_runs(inward):
                if place is None:
                    row = halo[pl.ds(MIXED * NZ + first, 1), :]
                    out[pl.ds(near + channel, 3), :] = jnp.broadcast_to(row, (3, 128))
                else:
                    out[pl.ds(near + channel, count), :] = halo[
                        pl.ds(place * NZ + first, count, stride=NZ), :
                    ]
            out[pl.ds(near + WALL, 1), :] = flags[pl.ds(side * NZ + first, 1), :]
            out[pl.ds(near + AIM, 1), :] = aims[pl.ds(side * NZ + first, 1), :]
            place = 15 if part else 0
            for k, count in ((0, 8), (8, 1)):
                out[pl.ds(near + CHANNELS + k, count), :] = halo[
                    pl.ds((place + k) * NZ + second, count, stride=NZ if count > 1 else 1), :
                ]
            out[pl.ds(near + Z_BLOCKS - 1, 1), :] = flags[pl.ds(side * NZ + second, 1), :]
            far = Z_FAR + 12 * side
            start = (MIXED + 1) * NZ
            out[pl.ds(far, 8), :] = halo[pl.ds(start + first, 8, stride=NZ), :]
            out[pl.ds(far + 8, 1), :] = halo[pl.ds(start + 8 * NZ + first, 1), :]
            for k in range(3):
                row = halo[pl.ds(start + (3 * part + k) * NZ + second, 1), :]
                out[pl.ds(far + 9 + k, 1), :] = row


def plane_at(z):
    return PAD + (z + 2) * PITCH


def add_rows(full, flags, aims, above, below):
    spread_mixed(below, above, flags, aims)

    def put(channel, row, source):
        full[pl.ds(channel * ROWS + plane_at(0) + row, NZ, stride=PITCH), :] = source

    sides = ((below, 1, 0, 6), (above, PITCH - 2, PITCH - 1, 0))
    for side, (halo, near, far, inward) in enumerate(sides):
        for first, count, place in y_runs(inward):
            for k in range(count):
                row = MIXED if place is None else place + k
                put(first + k, near, halo[pl.ds(row * NZ, NZ), :])
        flag = flags[pl.ds(side * NZ, NZ), :]
        put(WALL, near, flag)
        put(WALL, far, flag)
        put(AIM, near, aims[pl.ds(side * NZ, NZ), :])
        for k in range(9):
            q = 9 * (k // 3) + inward + k % 3
            put(q, far, halo[pl.ds((MIXED + 1 + k) * NZ, NZ), :])


def add_own_planes(full, ceiling, floor):
    for halo, near, far, part in ((floor, -1, -2, 2), (ceiling, NZ, NZ + 1, 0)):
        for k, (c, z) in enumerate(z_blocks(near, far, part)):
            full[pl.ds(c * ROWS + plane_at(z) + 2, 8), :] = halo[pl.ds(8 * k, 8), :]


def add_planes(full, ceiling, floor):
    def put(count, channel, z, row, source):
        start = channel * ROWS + plane_at(z) + row
        full[pl.ds(start, count, stride=ROWS), :] = source

    for halo, near, far, part in ((floor, -1, -2, 2), (ceiling, NZ, NZ + 1, 0)):
        for side, (row, beyond, group) in enumerate(((1, 0, 2), (PITCH - 2, PITCH - 1, 0))):
            start = side * Z_BLOCKS
            put(CHANNELS, 0, near, row, halo[pl.ds(start, CHANNELS), :])
            put(9, 9 * part, far, row, halo[pl.ds(start + CHANNELS, 9), :])
            first, second = (halo[pl.ds(start + k, 1), :] for k in (WALL, Z_BLOCKS - 1))
            put(1, WALL, far, row, second)
            start = Z_FAR + 12 * side
            for k in range(3):
                put(3, 9 * k + 3 * group, near, beyond, halo[pl.ds(start + 3 * k, 3), :])
            put(3, 9 * part + 3 * group, far, beyond, halo[pl.ds(start + 9, 3), :])
            put(1, WALL, near, beyond, first)
            put(1, WALL, far, beyond, second)


def pack_columns(full, pack, tiles):
    slot = lane_ids() // 4
    for t in tiles:
        packed = jnp.zeros((8, 128), F32)
        for c in range(CHANNELS):
            moved = pltpu.roll(full[pl.ds(c * ROWS + PAD + 8 * t, 8), :], (4 * c + 2) % 128, 1)
            packed = jnp.where(slot == c, moved, packed)
        pack[pl.ds(8 * t, 8), :] = packed


def pack_rim(full, pack, first):
    slot, rows = lane_ids() // 4, row_ids()
    parts = (rows < 2, (rows >= 2) & (rows < 6), rows >= 6)
    packed = jnp.zeros((8, 128), F32)
    for c in range(CHANNELS):
        a, b, d = (full[pl.ds(c * ROWS + PAD + 8 * (first + t), 8), :] for t in range(3))
        rim = jnp.where(parts[0], a, jnp.where(parts[1], b, d))
        packed = jnp.where(slot == c, pltpu.roll(rim, (4 * c + 2) % 128, 1), packed)
    for t, part in enumerate(parts):
        tile = pl.ds(8 * (first + t), 8)
        pack[tile, :] = jnp.where(part, packed, pack[tile, :])


def bound_planes(full):
    here, last = lax.axis_index("gz"), lax.axis_size("gz") - 1
    ground = pl.ds(WALL * ROWS + plane_at(-1), PITCH)
    full[ground, :] = jnp.where(here == 0, 1.0, full[ground, :])
    for q in range(9):
        above = pl.ds(q * ROWS + plane_at(NZ), PITCH)
        mirrored = full[pl.ds((q + 18) * ROWS + plane_at(NZ - 1), PITCH), :]
        full[above, :] = jnp.where(here == last, mirrored, full[above, :])


def fill_kernel(own, y_first, y_second, two, one, full, pack, flags, aims):
    for c in range(CHANNELS):
        for z in range(NZ):
            full[pl.ds(c * ROWS + plane_at(z) + 2, 8), :] = own[pl.ds((c * NZ + z) * 8, 8), :]
    by_roles(y_first, y_second, functools.partial(add_rows, full, flags, aims))
    by_parity("gz", one, two, functools.partial(add_own_planes, full))
    bound_planes(full)
    pack_columns(full, pack, range(FLAT // 8))
    pack[pl.ds(FLAT, 128 - FLAT), :] = jnp.zeros((128 - FLAT, 128), F32)


def third_kernel(part, packed, z_one, z_two, full, pack, columns, message, halos):
    ahead = way("gz")
    halos[ahead] = z_one[...]
    halos[1 - ahead] = z_two[...]
    add_planes(full, halos.at[0], halos.at[1])
    bound_planes(full)
    for first in (0, (NZ + 2) * PITCH // 8):
        pack_rim(full, pack, first)
    columns[pl.ds(PAD, 128), :] = pack[...].T

    def row(c, i, count):
        return columns[pl.ds(PAD + 4 * c + i, count), :]

    def returned(q, near, far):
        cx, cy, cz = VEL[q]
        step = (-PITCH * cz - cy) % 128
        value = row(26 - q, near, 8)
        value = pltpu.roll(value, step, 1) if step else value
        return jnp.where(row(WALL, far, 8) != 0.0, value, row(q, far, 8))[:1]

    for c in range(WALL + 1):
        cx = VEL[c][0] if c < 27 else 0
        if cx == 0:
            message[pl.ds(2 * c, 2), :] = row(c, 1, 2)
        elif cx > 0:
            message[pl.ds(2 * c, 1), :] = returned(c, 1, 0)
            message[pl.ds(2 * c + 1, 1), :] = row(c, 1, 1)
        else:
            message[pl.ds(2 * c, 1), :] = row(c, 2, 1)
            message[pl.ds(2 * c + 1, 1), :] = returned(c, 2, 3)


def block_kernel(full, post, walls):
    top = lax.axis_index("gz") == lax.axis_size("gz") - 1
    sponge = (lax.axis_index("gx") * NX + lane_ids()) < SPONGE
    for t in range(ROWS // 8):
        rows = pl.ds(8 * t, 8)
        flags = full[pl.ds(WALL * ROWS + 8 * t, 8), :]
        for cx in (-1, 0, 1):
            walls[cx + 1, rows, :] = pltpu.roll(flags, cx % 128, 1) if cx else flags
    for u in range(UNITS):
        cell = PAD + PITCH + 8 * u
        f = []
        solid = walls[1, pl.ds(cell, 8), :] != 0.0
        for q in range(27):
            cx, cy, cz = VEL[q]
            start = cell - PITCH * cz - cy
            value = full[pl.ds(q * ROWS + start, 8), :]
            if cx:
                value = pltpu.roll(value, cx % 128, 1)
            if q != 13:
                blocked = walls[cx + 1, pl.ds(start, 8), :] != 0.0
                value = jnp.where(blocked, full[pl.ds((26 - q) * ROWS + cell, 8), :], value)
            f.append(jnp.where(solid, WEIGHT[q], value))
        done = relaxed(f, sponge, full[pl.ds(AIM * ROWS + cell, 8), :])
        for q in range(27):
            post[q, pl.ds(8 * u, 8), :] = done[q]

    @pl.when(top)
    def _():
        for q in range(9):
            post[q, pl.ds((NZ + 1) * PITCH, PITCH), :] = post[q + 18, pl.ds(NZ * PITCH, PITCH), :]


def last_kernel(full, block, columns, x_one, x_two, out, west, east, column, walls, back, done, sems):
    here_x, size_x = lax.axis_index("gx"), lax.axis_size("gx")
    top = lax.axis_index("gz") == lax.axis_size("gz") - 1
    lanes, rows = lane_ids(), row_ids()

    if size_x == 2:

        def beside(side, start):
            first = min(max(start, 0), X_ROWS - 8)
            value = x_one[pl.ds(first, 8), :]
            return pltpu.roll(value, (first - start) % 8, 0) if first != start else value

    else:

        def spread(right, left):
            west[pl.ds(PAD, X_ROWS), :] = left[...]
            east[pl.ds(PAD, X_ROWS), :] = right[...]

        by_parity("gx", x_one, x_two, spread)

        def beside(side, start):
            return (west if side < 0 else east)[pl.ds(PAD + start, 8), :]

    def strip_at(c, shift):
        cx = VEL[c][0] if c < 27 else 0
        at = rows - shift
        first = PAD + 4 * c - shift
        value = jnp.where(at < 4, columns[pl.ds(first, 8), :], columns[pl.ds(first - 4, 8), :])
        if c <= WALL and cx >= 0:
            value = jnp.where(at < 2, beside(-1, 2 * c - (cx == 0) - shift), value)
        if c <= WALL and cx <= 0:
            value = jnp.where(at >= 6, beside(1, 2 * c - 6 + (cx == 0) - shift), value)
        if c == WALL:
            value = jnp.where((at == 0) | (at == 7), 0.0, value)
        return value

    strip = [strip_at(c, 0) for c in range(CHANNELS)]
    flags_at = {cx: strip_at(WALL, cx) if cx else strip[WALL] for cx in (-1, 0, 1)}

    def moved_along(value, q):
        cx, cy, cz = VEL[q]
        step = (PITCH * cz + cy) % 128
        return pltpu.roll(value, step, 1) if step else value

    moved = []
    for q in range(27):
        cx = VEL[q][0]
        value = moved_along(strip_at(q, cx) if cx else strip[q], q)
        if q != 13:
            value = jnp.where(moved_along(flags_at[cx], q) != 0.0, strip[26 - q], value)
        moved.append(jnp.where(strip[WALL] != 0.0, WEIGHT[q], value))
    place = here_x * NX + jnp.where(rows < 4, rows - 2, rows + (NX - 6))
    place = lax.rem(place + size_x * NX, size_x * NX)
    sides = relaxed(moved, place < SPONGE, strip[AIM])
    lid = top & (lanes >= (NZ + 2) * PITCH) & (lanes < (NZ + 3) * PITCH)
    for q in range(9):
        sides[q] = jnp.where(lid, pltpu.roll(sides[q + 18], PITCH, 1), sides[q])
    for q, side in enumerate(sides + [strip[WALL]]):
        column[pl.ds(PAD + 8 * q, 8), :] = side

    def picked(wanted):
        value = None
        for sublane, (q, row) in enumerate(wanted):
            moved = column[pl.ds(PAD + 8 * q + row - sublane, 8), :]
            value = moved if value is None else jnp.where(rows == sublane, moved, value)
        return value

    packed = []
    for k in range(9):
        a, b = 3 * k + 2, 3 * k
        packed.append(
            picked([(a, 5), (a, 2), (a, 1), (a, 2), (b, 5), (b, 2), (b, 5), (b, 6)])
        )
    rest = [(3 * k + 1, row) for k in range(9) for row in (5, 2)] + [(27, 1), (27, 6)]
    packed += [picked(rest[i : i + 8]) for i in range(0, len(rest), 8)]
    packed += [jnp.zeros((8, 128), F32)] * (16 - len(packed))
    back[...] = jnp.concatenate(packed, axis=0).T

    def column_at(place, lane, start):
        return pltpu.roll(back[pl.ds(start, 8), :], (lane - place) % 128, 1)

    rim = (lanes == 0) | (lanes == 127)

    def rimmed(q, start):
        k = q // 3
        ends = column_at((8 * k + 5, 73 + 2 * k, 8 * k + 1)[q % 3], 0, PITCH + start)
        return jnp.where(rim, ends, block[q, pl.ds(start, 8), :])

    for u in range(UNITS):
        flags = full[pl.ds(WALL * ROWS + PAD + PITCH + 8 * u, 8), :]
        walls[1, pl.ds(8 * u, 8), :] = flags
        for cx, edge, place in ((1, 0, 90), (-1, 127, 91)):
            walls[cx + 1, pl.ds(8 * u, 8), :] = jnp.where(
                lanes == edge, column_at(place, edge, PITCH + 8 * u), pltpu.roll(flags, cx % 128, 1)
            )

    cells = [(z + 1) * PITCH + 2 for z in range(NZ)]
    solids = [walls[1, pl.ds(cell, 8), :] != 0.0 for cell in cells]

    def streamed(q, z):
        cx, cy, cz = VEL[q]
        cell = cells[z]
        start = cell - PITCH * cz - cy
        if cx > 0:
            side = column_at(8 * (q // 3) + 2, 0, PITCH + start)
            value = jnp.where(lanes < 2, side, pltpu.roll(block[q, pl.ds(start, 8), :], 1, 1))
        elif cx < 0:
            side = column_at(8 * (q // 3) + 6, 126, PITCH + start)
            value = jnp.where(lanes > 125, side, pltpu.roll(block[q, pl.ds(start, 8), :], 127, 1))
        else:
            value = rimmed(q, start)
        if q != 13:
            blocked = walls[cx + 1, pl.ds(start, 8), :] != 0.0
            value = jnp.where(blocked, rimmed(26 - q, cell), value)
        return jnp.where(solids[z], WEIGHT[q], value)

    copies = []
    for first, count in ((0, 9), (9, 8), (17, 6), (23, 4)):
        for q in range(first, first + count):
            for z in range(NZ):
                done[q, z] = streamed(q, z)
        part = pl.ds(first, count)
        copies.append(pltpu.make_async_copy(done.at[part], out.at[part], sems.at[len(copies)]))
        copies[-1].start()
    for copy in copies:
        copy.wait()


def pairs(size, turn, wrap):
    ahead = [(i, (i + 1) % size) for i in range(turn, size if wrap else size - 1, 2)]
    return ahead + [(j, i) for i, j in ahead]


def swap(value, axis, turn, wrap):
    return lax.ppermute(value, axis, pairs(lax.axis_size(axis), turn, wrap))


def swap_mixed(value, turn):
    size, planes = lax.axis_size("gy"), lax.axis_size("gz")
    moves = []
    for k in range(planes):
        moves += [
            (i * planes + k, j * planes + k) for i, j in pairs(size, (turn + k) % 2, True)
        ]
    return lax.ppermute(value, ("gy", "gz"), moves)


def shape(*dims):
    return jax.ShapeDtypeStruct(dims, F32)


def shards(pops, solid, profile_table, profile_index):
    own, y_first, y_second = pl.pallas_call(
        first_kernel,
        out_shape=[shape(CHANNELS * NZ * 8, 128), shape(Y_ROWS, 128), shape(Y_ROWS, 128)],
        in_specs=[HBM] * 4,
        out_specs=[VMEM] * 3,
        scratch_shapes=[
            pltpu.VMEM(pops.shape, F32),
            pltpu.VMEM(solid.shape, jnp.int32),
            pltpu.SMEM(profile_table.shape[::-1], F32),
            pltpu.SMEM(profile_index.shape, jnp.int32),
            pltpu.VMEM((2, Y_ROWS, 128), F32),
            pltpu.SemaphoreType.DMA((6,)),
        ],
        compiler_params=PARAMS,
        name="collide",
    )(*(pltpu.with_memory_space_constraint(a, pltpu.HBM) for a in (pops, solid, profile_table.T, profile_index)))
    y_first = swap_mixed(y_first, 0)
    y_second = swap_mixed(y_second, 1)
    own_two, own_one = pl.pallas_call(
        ahead_kernel,
        out_shape=[shape(Z_BLOCKS * 8, 128)] * 2,
        in_specs=[VMEM],
        out_specs=[VMEM] * 2,
        compiler_params=PARAMS,
        name="pack_own",
    )(own)
    own_two = swap(own_two, "gz", 1, False)
    own_one = swap(own_one, "gz", 0, False)
    z_one, z_two = pl.pallas_call(
        second_kernel,
        out_shape=[shape(Z_ROWS, 128)] * 2,
        in_specs=[VMEM] * 2,
        out_specs=[VMEM] * 2,
        scratch_shapes=[
            *[pltpu.VMEM((4 * NZ, 128), F32)] * 2,
            pltpu.VMEM((2, Y_ROWS, 128), F32),
            pltpu.VMEM((2, Z_ROWS, 128), F32),
        ],
        compiler_params=PARAMS,
        cost_estimate=pl.CostEstimate(flops=10**9, bytes_accessed=2**20, transcendentals=0),
        name="pack_z",
    )(y_first, y_second)
    z_one = swap(z_one, "gz", 0, False)
    z_two = swap(z_two, "gz", 1, False)
    part, packed = pl.pallas_call(
        fill_kernel,
        out_shape=[shape(SLABS * ROWS, 128), shape(128, 128)],
        in_specs=[VMEM] * 5,
        out_specs=[VMEM] * 2,
        scratch_shapes=[pltpu.VMEM((4 * NZ, 128), F32)] * 2,
        compiler_params=PARAMS,
        cost_estimate=pl.CostEstimate(flops=10**6, bytes_accessed=2**22, transcendentals=0),
        name="fill",
    )(own, y_first, y_second, own_two, own_one)
    full, packed, columns, message = pl.pallas_call(
        third_kernel,
        out_shape=[
            shape(SLABS * ROWS, 128),
            shape(128, 128),
            shape(PAD + 128 + PAD, 128),
            shape(X_ROWS, 128),
        ],
        in_specs=[VMEM] * 4,
        out_specs=[VMEM] * 4,
        scratch_shapes=[pltpu.VMEM((2, Z_ROWS, 128), F32)],
        input_output_aliases={0: 0, 1: 1},
        compiler_params=PARAMS,
        name="pack_x",
    )(part, packed, z_one, z_two)
    x_one = swap(message, "gx", 0, True)
    x_two = x_one if lax.axis_size("gx") == 2 else swap(message, "gx", 1, True)
    block = pl.pallas_call(
        block_kernel,
        out_shape=shape(27, UNITS * 8, 128),
        in_specs=[VMEM],
        out_specs=VMEM,
        scratch_shapes=[pltpu.VMEM((3, ROWS, 128), F32)],
        compiler_params=PARAMS,
        cost_estimate=pl.CostEstimate(
            flops=27 * 20 * UNITS * 1024, bytes_accessed=2**22, transcendentals=0
        ),
        name="block",
    )(full)
    return pl.pallas_call(
        last_kernel,
        out_shape=shape(27, NZ, NY, NX),
        in_specs=[VMEM] * 5,
        out_specs=HBM,
        scratch_shapes=[
            pltpu.VMEM((PAD + X_ROWS + PAD, 128), F32),
            pltpu.VMEM((PAD + X_ROWS + PAD, 128), F32),
            pltpu.VMEM((PAD + 28 * 8 + PAD, 128), F32),
            pltpu.VMEM((3, UNITS * 8, 128), F32),
            pltpu.VMEM((128, 128), F32),
            pltpu.VMEM((27, NZ, NY, NX), F32),
            pltpu.SemaphoreType.DMA((NZ,)),
        ],
        compiler_params=PARAMS,
        name="finish",
    )(full, block, columns, x_one, x_two)


def solution(mesh):
    return jax.shard_map(
        shards,
        mesh=mesh,
        in_specs=(P(None, "gz", "gy", "gx"), P("gz", "gy", "gx"), P(None, "gz"), P("gy")),
        out_specs=P(None, "gz", "gy", "gx"),
        check_vma=False,
    )
```

```python
import functools

import jax
import jax.numpy as jnp
import numpy as np
from jax import lax
from jax.experimental import pallas as pl
from jax.experimental.pallas import tpu as pltpu
from jax.sharding import PartitionSpec as P

SPONGE = 32
TAU = 0.52
SMAG = 18.0 * 1.4142135623730951 * 0.17 * 0.17

VEL = [(cx, cy, cz) for cz in (-1, 0, 1) for cy in (-1, 0, 1) for cx in (-1, 0, 1)]
WEIGHT = [
    float(np.array([8.0 / 27.0, 2.0 / 27.0, 1.0 / 54.0, 1.0 / 216.0])[cx * cx + cy * cy + cz * cz])
    for cx, cy, cz in VEL
]
WALL, AIM, CHANNELS = 27, 28, 29
NZ, NY, NX = 4, 8, 128
PITCH = NY + 4
FLAT = (NZ + 4) * PITCH
PAD = 8
ROWS = PAD + FLAT + PAD
SLABS = CHANNELS + 6
UNITS = (NZ + 2) * PITCH // 8

PARAMS = pltpu.CompilerParams(vmem_limit_bytes=12 * 2**20)
VMEM = pl.BlockSpec(memory_space=pltpu.VMEM)
HBM = pl.BlockSpec(memory_space=pltpu.HBM)
F32 = jnp.float32

MIXED = 24
Y_ROWS = (MIXED + 1 + 9) * NZ
Z_BLOCKS = CHANNELS + 10
Z_FAR = 2 * Z_BLOCKS
Z_ROWS = -(-(Z_FAR + 2 * 12) // 8) * 8

X_ROWS = 2 * (WALL + 1)


def relaxed(f, sponge, aim):
    quad = {}
    for cz in (-1, 0, 1):
        line = {}
        for cy in (-1, 0, 1):
            base = 9 * (cz + 1) + 3 * (cy + 1)
            both = f[base + 2] + f[base]
            line[cy] = (both + f[base + 1], f[base + 2] - f[base], both)
        s = line[1][0] + line[-1][0]
        sx = line[1][1] + line[-1][1]
        quad[cz] = dict(
            n=s + line[0][0],
            y=line[1][0] - line[-1][0],
            yy=s,
            x=sx + line[0][1],
            xy=line[1][1] - line[-1][1],
            xx=line[1][2] + line[-1][2] + line[0][2],
        )
    up, mid, down = quad[1], quad[0], quad[-1]
    zz = up["n"] + down["n"]
    rho = zz + mid["n"]
    jz = up["n"] - down["n"]
    jy = up["y"] + down["y"] + mid["y"]
    jx = up["x"] + down["x"] + mid["x"]
    inverse = 1.0 / rho
    ux, uy, uz = jx * inverse, jy * inverse, jz * inverse
    third = rho * (1.0 / 3.0)
    pxx = (up["xx"] + down["xx"] + mid["xx"]) - (third + jx * ux)
    pyy = (up["yy"] + down["yy"] + mid["yy"]) - (third + jy * uy)
    pzz = zz - (third + jz * uz)
    pxy = (up["xy"] + down["xy"] + mid["xy"]) - jx * uy
    pxz = (up["x"] - down["x"]) - jx * uz
    pyz = (up["y"] - down["y"]) - jy * uz
    strain = pxx * pxx + pyy * pyy + pzz * pzz + 2.0 * (pxy * pxy + pxz * pxz + pyz * pyz)
    size = jnp.sqrt(2.0 * strain)
    tau = 0.5 * (TAU + jnp.sqrt(TAU * TAU + SMAG * size * inverse))
    omega = 1.0 / tau
    keep = 1.0 - omega
    if sponge is not None:
        keep = jnp.where(sponge, 0.0, keep)
        omega = jnp.where(sponge, 1.0, omega)
        ux = jnp.where(sponge, aim, ux)
        uy = jnp.where(sponge, 0.0, uy)
        uz = jnp.where(sponge, 0.0, uz)
    square = 1.0 - 1.5 * (ux * ux + uy * uy + uz * uz)
    vx, vy, vz = 3.0 * ux, 3.0 * uy, 3.0 * uz
    share = rho * omega
    weighted = {w: share * w for w in sorted(set(WEIGHT))}
    post = [None] * 27
    for q in range(14):
        cx, cy, cz = VEL[q]
        along = None
        for c, v in ((cx, vx), (cy, vy), (cz, vz)):
            if c:
                along = (v if c > 0 else -v) if along is None else (along + v if c > 0 else along - v)
        scale = weighted[WEIGHT[q]]
        if along is None:
            post[q] = keep * f[q] + scale * square
            continue
        even = square + 0.5 * along * along
        post[q] = keep * f[q] + scale * (even + along)
        post[26 - q] = keep * f[26 - q] + scale * (even - along)
    return post


def lane_ids():
    return lax.broadcasted_iota(jnp.int32, (8, 128), 1)


def row_ids():
    return lax.broadcasted_iota(jnp.int32, (8, 128), 0)


def by_parity(axis, one, two, body):
    even = lax.rem(lax.axis_index(axis), 2) == 0
    pl.when(even)(lambda: body(one, two))
    pl.when(jnp.logical_not(even))(lambda: body(two, one))


def way(*axes):
    return lax.rem(sum(lax.axis_index(axis) for axis in axes), 2)


def by_roles(first, second, body):
    ahead = way("gz", "gy") == 0
    pl.when(ahead)(lambda: body(first, second))
    pl.when(jnp.logical_not(ahead))(lambda: body(second, first))


def z_blocks(near, far, part):
    blocks = [(c, near) for c in range(CHANNELS)]
    return blocks + [(9 * part + k, far) for k in range(9)] + [(WALL, far)]


def first_kernel(pops_at, solid_at, table_at, index_at, own, first_out, second_out, *scratch):
    pops, solid, table, index, messages, sems = scratch
    groups = [(pops_at.at[pl.ds(q, 9)], pops.at[pl.ds(q, 9)]) for q in (0, 9, 18)]
    small = [(table_at, table), (index_at, index)]
    copies = [
        pltpu.make_async_copy(source, target, sems.at[i])
        for i, (source, target) in enumerate([*small, *groups, (solid_at, solid)])
    ]
    for copy in copies:
        copy.start()
    for copy in copies[:2]:
        copy.wait()
    lanes, rows = lane_ids(), row_ids()
    sponge = (lax.axis_index("gx") * NX + lanes) < SPONGE
    profiles = [index[y] for y in range(NY)]
    aims = []
    for z in range(NZ):
        aim = jnp.zeros((8, 128), F32)
        for y, profile in enumerate(profiles):
            aim = jnp.where(rows == y, table[z, profile], aim)
        aims.append(aim)
    for copy in copies[2:-1]:
        copy.wait()
    for z, aim in enumerate(aims):
        post = relaxed([pops[q, z] for q in range(27)], sponge, aim)
        for q in range(27):
            own[pl.ds((q * NZ + z) * 8, 8), :] = post[q]
        own[pl.ds((AIM * NZ + z) * 8, 8), :] = aim
    copies[-1].wait()
    for z in range(NZ):
        own[pl.ds((WALL * NZ + z) * 8, 8), :] = solid[z].astype(F32)

    inside = lax.rem(lanes, 4)
    for out, edge, second, part in ((messages.at[0], 7, 6, 6), (messages.at[1], 0, 1, 0)):
        back = 15 - part
        for first, count, place in ((0, back, 0), (back + 3, 24 - back, back)):
            out[pl.ds(place * NZ, count * NZ), :] = own[
                pl.ds(first * NZ * 8 + edge, count * NZ, stride=8), :
            ]
        for z in range(NZ):
            west, east, aim, flag = (
                own[pl.ds((c * NZ + z) * 8, 8), :] for c in (back, back + 2, AIM, WALL)
            )
            mixed = jnp.where(inside < 2, jnp.where(inside == 0, west, aim), flag)
            mixed = jnp.where(inside == 3, east, mixed)
            out[pl.ds(MIXED * NZ + z, 1), :] = mixed[edge : edge + 1]
        for a in range(3):
            out[pl.ds((MIXED + 1 + 3 * a) * NZ, 3 * NZ), :] = own[
                pl.ds((9 * a + part) * NZ * 8 + second, 3 * NZ, stride=8), :
            ]

    ahead = way("gz", "gy")
    first_out[...] = messages[ahead]
    second_out[...] = messages[1 - ahead]


def ahead_kernel(own, two, one):
    def pack(zup, zdown):
        for out, first, second, part in ((zup, NZ - 1, NZ - 2, 2), (zdown, 0, 1, 0)):
            for k, (c, z) in enumerate(z_blocks(first, second, part)):
                out[pl.ds(8 * k, 8), :] = own[pl.ds((c * NZ + z) * 8, 8), :]

    by_parity("gz", one, two, pack)


def y_runs(part):
    back = 15 - part
    return (0, back, 0), (back, 3, None), (back + 3, 24 - back, back)


def spread_mixed(below, above, flags, aims):
    flags[pl.ds(0, NZ), :] = below[pl.ds(MIXED * NZ, NZ), :]
    flags[pl.ds(NZ, NZ), :] = above[pl.ds(MIXED * NZ, NZ), :]
    mixed = flags[pl.ds(0, 2 * NZ), :]
    inside = lax.rem(lane_ids(), 4)
    moved = {k: pltpu.roll(mixed, k % 128, 1) if k else mixed for k in (-2, -1, 0, 1, 2)}

    def from_lane(source):
        value = moved[0]
        for lane in range(4):
            if lane != source:
                value = jnp.where(inside == lane, moved[lane - source], value)
        return value

    aims[pl.ds(0, 2 * NZ), :] = from_lane(1)
    flags[pl.ds(0, 2 * NZ), :] = from_lane(2)


def second_kernel(y_first, y_second, z_one, z_two, flags, aims, halos, messages):
    ahead = way("gz", "gy")
    halos[ahead] = y_first[...]
    halos[1 - ahead] = y_second[...]
    above, below = halos.at[0], halos.at[1]
    spread_mixed(below, above, flags, aims)
    pack_planes(below, above, flags, aims, messages.at[0], messages.at[1])
    ahead = way("gz")
    z_one[...] = messages[ahead]
    z_two[...] = messages[1 - ahead]


def pack_planes(below, above, flags, aims, zup, zdown):
    for out, first, second, part in ((zup, NZ - 1, NZ - 2, 2), (zdown, 0, 1, 0)):
        for side, (halo, inward) in enumerate(((below, 6), (above, 0))):
            near = side * Z_BLOCKS
            for channel, count, place in y_runs(inward):
                if place is None:
                    row = halo[pl.ds(MIXED * NZ + first, 1), :]
                    out[pl.ds(near + channel, 3), :] = jnp.broadcast_to(row, (3, 128))
                else:
                    out[pl.ds(near + channel, count), :] = halo[
                        pl.ds(place * NZ + first, count, stride=NZ), :
                    ]
            out[pl.ds(near + WALL, 1), :] = flags[pl.ds(side * NZ + first, 1), :]
            out[pl.ds(near + AIM, 1), :] = aims[pl.ds(side * NZ + first, 1), :]
            place = 15 if part else 0
            for k, count in ((0, 8), (8, 1)):
                out[pl.ds(near + CHANNELS + k, count), :] = halo[
                    pl.ds((place + k) * NZ + second, count, stride=NZ if count > 1 else 1), :
                ]
            out[pl.ds(near + Z_BLOCKS - 1, 1), :] = flags[pl.ds(side * NZ + second, 1), :]
            far = Z_FAR + 12 * side
            start = (MIXED + 1) * NZ
            out[pl.ds(far, 8), :] = halo[pl.ds(start + first, 8, stride=NZ), :]
            out[pl.ds(far + 8, 1), :] = halo[pl.ds(start + 8 * NZ + first, 1), :]
            for k in range(3):
                row = halo[pl.ds(start + (3 * part + k) * NZ + second, 1), :]
                out[pl.ds(far + 9 + k, 1), :] = row


def plane_at(z):
    return PAD + (z + 2) * PITCH


def add_rows(full, flags, aims, above, below):
    spread_mixed(below, above, flags, aims)

    def put(channel, row, source):
        full[pl.ds(channel * ROWS + plane_at(0) + row, NZ, stride=PITCH), :] = source

    sides = ((below, 1, 0, 6), (above, PITCH - 2, PITCH - 1, 0))
    for side, (halo, near, far, inward) in enumerate(sides):
        for first, count, place in y_runs(inward):
            for k in range(count):
                row = MIXED if place is None else place + k
                put(first + k, near, halo[pl.ds(row * NZ, NZ), :])
        flag = flags[pl.ds(side * NZ, NZ), :]
        put(WALL, near, flag)
        put(WALL, far, flag)
        put(AIM, near, aims[pl.ds(side * NZ, NZ), :])
        for k in range(9):
            q = 9 * (k // 3) + inward + k % 3
            put(q, far, halo[pl.ds((MIXED + 1 + k) * NZ, NZ), :])


def add_own_planes(full, ceiling, floor):
    for halo, near, far, part in ((floor, -1, -2, 2), (ceiling, NZ, NZ + 1, 0)):
        for k, (c, z) in enumerate(z_blocks(near, far, part)):
            full[pl.ds(c * ROWS + plane_at(z) + 2, 8), :] = halo[pl.ds(8 * k, 8), :]


def add_planes(full, ceiling, floor):
    def put(count, channel, z, row, source):
        start = channel * ROWS + plane_at(z) + row
        full[pl.ds(start, count, stride=ROWS), :] = source

    for halo, near, far, part in ((floor, -1, -2, 2), (ceiling, NZ, NZ + 1, 0)):
        for side, (row, beyond, group) in enumerate(((1, 0, 2), (PITCH - 2, PITCH - 1, 0))):
            start = side * Z_BLOCKS
            put(CHANNELS, 0, near, row, halo[pl.ds(start, CHANNELS), :])
            put(9, 9 * part, far, row, halo[pl.ds(start + CHANNELS, 9), :])
            first, second = (halo[pl.ds(start + k, 1), :] for k in (WALL, Z_BLOCKS - 1))
            put(1, WALL, far, row, second)
            start = Z_FAR + 12 * side
            for k in range(3):
                put(3, 9 * k + 3 * group, near, beyond, halo[pl.ds(start + 3 * k, 3), :])
            put(3, 9 * part + 3 * group, far, beyond, halo[pl.ds(start + 9, 3), :])
            put(1, WALL, near, beyond, first)
            put(1, WALL, far, beyond, second)


def pack_columns(full, pack, tiles):
    slot = lane_ids() // 4
    for t in tiles:
        packed = jnp.zeros((8, 128), F32)
        for c in range(CHANNELS):
            moved = pltpu.roll(full[pl.ds(c * ROWS + PAD + 8 * t, 8), :], (4 * c + 2) % 128, 1)
            packed = jnp.where(slot == c, moved, packed)
        pack[pl.ds(8 * t, 8), :] = packed


def pack_rim(full, pack, first):
    slot, rows = lane_ids() // 4, row_ids()
    parts = (rows < 2, (rows >= 2) & (rows < 6), rows >= 6)
    packed = jnp.zeros((8, 128), F32)
    for c in range(CHANNELS):
        a, b, d = (full[pl.ds(c * ROWS + PAD + 8 * (first + t), 8), :] for t in range(3))
        rim = jnp.where(parts[0], a, jnp.where(parts[1], b, d))
        packed = jnp.where(slot == c, pltpu.roll(rim, (4 * c + 2) % 128, 1), packed)
    for t, part in enumerate(parts):
        tile = pl.ds(8 * (first + t), 8)
        pack[tile, :] = jnp.where(part, packed, pack[tile, :])


def bound_planes(full):
    here, last = lax.axis_index("gz"), lax.axis_size("gz") - 1
    ground = pl.ds(WALL * ROWS + plane_at(-1), PITCH)
    full[ground, :] = jnp.where(here == 0, 1.0, full[ground, :])
    for q in range(9):
        above = pl.ds(q * ROWS + plane_at(NZ), PITCH)
        mirrored = full[pl.ds((q + 18) * ROWS + plane_at(NZ - 1), PITCH), :]
        full[above, :] = jnp.where(here == last, mirrored, full[above, :])


def fill_kernel(own, y_first, y_second, two, one, full, pack, flags, aims):
    for c in range(CHANNELS):
        for z in range(NZ):
            full[pl.ds(c * ROWS + plane_at(z) + 2, 8), :] = own[pl.ds((c * NZ + z) * 8, 8), :]
    by_roles(y_first, y_second, functools.partial(add_rows, full, flags, aims))
    by_parity("gz", one, two, functools.partial(add_own_planes, full))
    bound_planes(full)
    pack_columns(full, pack, range(FLAT // 8))
    pack[pl.ds(FLAT, 128 - FLAT), :] = jnp.zeros((128 - FLAT, 128), F32)


def third_kernel(part, packed, z_one, z_two, full, pack, columns, message, halos):
    ahead = way("gz")
    halos[ahead] = z_one[...]
    halos[1 - ahead] = z_two[...]
    add_planes(full, halos.at[0], halos.at[1])
    bound_planes(full)
    for first in (0, (NZ + 2) * PITCH // 8):
        pack_rim(full, pack, first)
    columns[pl.ds(PAD, 128), :] = pack[...].T

    def row(c, i, count):
        return columns[pl.ds(PAD + 4 * c + i, count), :]

    def returned(q, near, far):
        cx, cy, cz = VEL[q]
        step = (-PITCH * cz - cy) % 128
        value = row(26 - q, near, 8)
        value = pltpu.roll(value, step, 1) if step else value
        return jnp.where(row(WALL, far, 8) != 0.0, value, row(q, far, 8))[:1]

    for c in range(WALL + 1):
        cx = VEL[c][0] if c < 27 else 0
        if cx == 0:
            message[pl.ds(2 * c, 2), :] = row(c, 1, 2)
        elif cx > 0:
            message[pl.ds(2 * c, 1), :] = returned(c, 1, 0)
            message[pl.ds(2 * c + 1, 1), :] = row(c, 1, 1)
        else:
            message[pl.ds(2 * c, 1), :] = row(c, 2, 1)
            message[pl.ds(2 * c + 1, 1), :] = returned(c, 2, 3)


def block_kernel(full, base, post, walls):
    top = lax.axis_index("gz") == lax.axis_size("gz") - 1
    sponge = (lax.axis_index("gx") * NX + lane_ids()) < SPONGE
    for t in range(ROWS // 8):
        rows = pl.ds(8 * t, 8)
        flags = full[pl.ds(WALL * ROWS + 8 * t, 8), :]
        for cx in (-1, 0, 1):
            walls[cx + 1, rows, :] = pltpu.roll(flags, cx % 128, 1) if cx else flags
    for u in range(UNITS):
        cell = PAD + PITCH + 8 * u
        f = []
        solid = walls[1, pl.ds(cell, 8), :] != 0.0
        for q in range(27):
            cx, cy, cz = VEL[q]
            start = cell - PITCH * cz - cy
            value = full[pl.ds(q * ROWS + start, 8), :]
            if cx:
                value = pltpu.roll(value, cx % 128, 1)
            if q != 13:
                blocked = walls[cx + 1, pl.ds(start, 8), :] != 0.0
                value = jnp.where(blocked, full[pl.ds((26 - q) * ROWS + cell, 8), :], value)
            f.append(jnp.where(solid, WEIGHT[q], value))
        done = relaxed(f, sponge, full[pl.ds(AIM * ROWS + cell, 8), :])
        for q in range(27):
            post[q, pl.ds(8 * u, 8), :] = done[q]

    @pl.when(top)
    def _():
        for q in range(9):
            post[q, pl.ds((NZ + 1) * PITCH, PITCH), :] = post[q + 18, pl.ds(NZ * PITCH, PITCH), :]

    for z in range(NZ):
        cell = (z + 1) * PITCH + 2
        for q in range(27):
            cx, cy, cz = VEL[q]
            start = cell - PITCH * cz - cy
            value = post[q, pl.ds(start, 8), :]
            if cx:
                value = pltpu.roll(value, cx % 128, 1)
            if q != 13:
                blocked = walls[cx + 1, pl.ds(PAD + PITCH + start, 8), :] != 0.0
                value = jnp.where(blocked, post[26 - q, pl.ds(cell, 8), :], value)
            base[q, z] = value


def last_kernel(full, base, columns, x_one, x_two, out, west, east, column, walls, back, done, sems):
    here_x, size_x = lax.axis_index("gx"), lax.axis_size("gx")
    top = lax.axis_index("gz") == lax.axis_size("gz") - 1
    lanes, rows = lane_ids(), row_ids()

    if size_x == 2:

        def beside(side, start):
            first = min(max(start, 0), X_ROWS - 8)
            value = x_one[pl.ds(first, 8), :]
            return pltpu.roll(value, (first - start) % 8, 0) if first != start else value

    else:

        def spread(right, left):
            west[pl.ds(PAD, X_ROWS), :] = left[...]
            east[pl.ds(PAD, X_ROWS), :] = right[...]

        by_parity("gx", x_one, x_two, spread)

        def beside(side, start):
            return (west if side < 0 else east)[pl.ds(PAD + start, 8), :]

    def strip_at(c, shift):
        cx = VEL[c][0] if c < 27 else 0
        at = rows - shift
        first = PAD + 4 * c - shift
        value = jnp.where(at < 4, columns[pl.ds(first, 8), :], columns[pl.ds(first - 4, 8), :])
        if c <= WALL and cx >= 0:
            value = jnp.where(at < 2, beside(-1, 2 * c - (cx == 0) - shift), value)
        if c <= WALL and cx <= 0:
            value = jnp.where(at >= 6, beside(1, 2 * c - 6 + (cx == 0) - shift), value)
        if c == WALL:
            value = jnp.where((at == 0) | (at == 7), 0.0, value)
        return value

    strip = [strip_at(c, 0) for c in range(CHANNELS)]
    flags_at = {cx: strip_at(WALL, cx) if cx else strip[WALL] for cx in (-1, 0, 1)}

    def moved_along(value, q):
        cx, cy, cz = VEL[q]
        step = (PITCH * cz + cy) % 128
        return pltpu.roll(value, step, 1) if step else value

    moved = []
    for q in range(27):
        cx = VEL[q][0]
        value = moved_along(strip_at(q, cx) if cx else strip[q], q)
        if q != 13:
            value = jnp.where(moved_along(flags_at[cx], q) != 0.0, strip[26 - q], value)
        moved.append(jnp.where(strip[WALL] != 0.0, WEIGHT[q], value))
    place = here_x * NX + jnp.where(rows < 4, rows - 2, rows + (NX - 6))
    place = lax.rem(place + size_x * NX, size_x * NX)
    sides = relaxed(moved, place < SPONGE, strip[AIM])
    lid = top & (lanes >= (NZ + 2) * PITCH) & (lanes < (NZ + 3) * PITCH)
    for q in range(9):
        sides[q] = jnp.where(lid, pltpu.roll(sides[q + 18], PITCH, 1), sides[q])
    for q, side in enumerate(sides + [strip[WALL]]):
        column[pl.ds(PAD + 8 * q, 8), :] = side

    def picked(wanted):
        value = None
        for sublane, (q, row) in enumerate(wanted):
            moved = column[pl.ds(PAD + 8 * q + row - sublane, 8), :]
            value = moved if value is None else jnp.where(rows == sublane, moved, value)
        return value

    packed = []
    for k in range(9):
        a, b = 3 * k + 2, 3 * k
        packed.append(
            picked([(a, 5), (a, 2), (a, 1), (a, 2), (b, 5), (b, 2), (b, 5), (b, 6)])
        )
    rest = [(3 * k + 1, row) for k in range(9) for row in (5, 2)] + [(27, 1), (27, 6)]
    packed += [picked(rest[i : i + 8]) for i in range(0, len(rest), 8)]
    packed += [jnp.zeros((8, 128), F32)] * (16 - len(packed))
    back[...] = jnp.concatenate(packed, axis=0).T

    def column_at(place, lane, start):
        return pltpu.roll(back[pl.ds(start, 8), :], (lane - place) % 128, 1)

    rim = (lanes == 0) | (lanes == 127)

    def ends_at(q, start):
        k = q // 3
        return column_at((8 * k + 5, 73 + 2 * k, 8 * k + 1)[q % 3], 0, PITCH + start)

    for u in range(UNITS):
        flags = full[pl.ds(WALL * ROWS + PAD + PITCH + 8 * u, 8), :]
        walls[1, pl.ds(8 * u, 8), :] = flags
        for cx, edge, place in ((1, 0, 90), (-1, 127, 91)):
            walls[cx + 1, pl.ds(8 * u, 8), :] = jnp.where(
                lanes == edge, column_at(place, edge, PITCH + 8 * u), pltpu.roll(flags, cx % 128, 1)
            )

    cells = [(z + 1) * PITCH + 2 for z in range(NZ)]
    solids = [walls[1, pl.ds(cell, 8), :] != 0.0 for cell in cells]

    def streamed(q, z):
        cx, cy, cz = VEL[q]
        cell = cells[z]
        start = cell - PITCH * cz - cy
        if cx > 0:
            side, reach = column_at(8 * (q // 3) + 2, 0, PITCH + start), lanes < 2
        elif cx < 0:
            side, reach = column_at(8 * (q // 3) + 6, 126, PITCH + start), lanes > 125
        else:
            side, reach = ends_at(q, start), rim
        if q != 13:
            blocked = walls[cx + 1, pl.ds(start, 8), :] != 0.0
            side = jnp.where(blocked, ends_at(26 - q, cell), side)
            reach = (blocked & rim) | (jnp.logical_not(blocked) & reach)
        value = jnp.where(reach, side, base[q, z])
        return jnp.where(solids[z], WEIGHT[q], value)

    copies = []
    for first, count in ((0, 9), (9, 8), (17, 6), (23, 4)):
        for q in range(first, first + count):
            for z in range(NZ):
                done[q, z] = streamed(q, z)
        part = pl.ds(first, count)
        copies.append(pltpu.make_async_copy(done.at[part], out.at[part], sems.at[len(copies)]))
        copies[-1].start()
    for copy in copies:
        copy.wait()


def pairs(size, turn, wrap):
    ahead = [(i, (i + 1) % size) for i in range(turn, size if wrap else size - 1, 2)]
    return ahead + [(j, i) for i, j in ahead]


def swap(value, axis, turn, wrap):
    return lax.ppermute(value, axis, pairs(lax.axis_size(axis), turn, wrap))


def swap_mixed(value, turn):
    size, planes = lax.axis_size("gy"), lax.axis_size("gz")
    moves = []
    for k in range(planes):
        moves += [
            (i * planes + k, j * planes + k) for i, j in pairs(size, (turn + k) % 2, True)
        ]
    return lax.ppermute(value, ("gy", "gz"), moves)


def shape(*dims):
    return jax.ShapeDtypeStruct(dims, F32)


def shards(pops, solid, profile_table, profile_index):
    own, y_first, y_second = pl.pallas_call(
        first_kernel,
        out_shape=[shape(CHANNELS * NZ * 8, 128), shape(Y_ROWS, 128), shape(Y_ROWS, 128)],
        in_specs=[HBM] * 4,
        out_specs=[VMEM] * 3,
        scratch_shapes=[
            pltpu.VMEM(pops.shape, F32),
            pltpu.VMEM(solid.shape, jnp.int32),
            pltpu.SMEM(profile_table.shape[::-1], F32),
            pltpu.SMEM(profile_index.shape, jnp.int32),
            pltpu.VMEM((2, Y_ROWS, 128), F32),
            pltpu.SemaphoreType.DMA((6,)),
        ],
        compiler_params=PARAMS,
        name="collide",
    )(*(pltpu.with_memory_space_constraint(a, pltpu.HBM) for a in (pops, solid, profile_table.T, profile_index)))
    y_first = swap_mixed(y_first, 0)
    y_second = swap_mixed(y_second, 1)
    own_two, own_one = pl.pallas_call(
        ahead_kernel,
        out_shape=[shape(Z_BLOCKS * 8, 128)] * 2,
        in_specs=[VMEM],
        out_specs=[VMEM] * 2,
        compiler_params=PARAMS,
        name="pack_own",
    )(own)
    own_two = swap(own_two, "gz", 1, False)
    own_one = swap(own_one, "gz", 0, False)
    z_one, z_two = pl.pallas_call(
        second_kernel,
        out_shape=[shape(Z_ROWS, 128)] * 2,
        in_specs=[VMEM] * 2,
        out_specs=[VMEM] * 2,
        scratch_shapes=[
            *[pltpu.VMEM((4 * NZ, 128), F32)] * 2,
            pltpu.VMEM((2, Y_ROWS, 128), F32),
            pltpu.VMEM((2, Z_ROWS, 128), F32),
        ],
        compiler_params=PARAMS,
        cost_estimate=pl.CostEstimate(flops=10**9, bytes_accessed=2**20, transcendentals=0),
        name="pack_z",
    )(y_first, y_second)
    z_one = swap(z_one, "gz", 0, False)
    z_two = swap(z_two, "gz", 1, False)
    part, packed = pl.pallas_call(
        fill_kernel,
        out_shape=[shape(SLABS * ROWS, 128), shape(128, 128)],
        in_specs=[VMEM] * 5,
        out_specs=[VMEM] * 2,
        scratch_shapes=[pltpu.VMEM((4 * NZ, 128), F32)] * 2,
        compiler_params=PARAMS,
        cost_estimate=pl.CostEstimate(flops=10**6, bytes_accessed=2**22, transcendentals=0),
        name="fill",
    )(own, y_first, y_second, own_two, own_one)
    full, packed, columns, message = pl.pallas_call(
        third_kernel,
        out_shape=[
            shape(SLABS * ROWS, 128),
            shape(128, 128),
            shape(PAD + 128 + PAD, 128),
            shape(X_ROWS, 128),
        ],
        in_specs=[VMEM] * 4,
        out_specs=[VMEM] * 4,
        scratch_shapes=[pltpu.VMEM((2, Z_ROWS, 128), F32)],
        input_output_aliases={0: 0, 1: 1},
        compiler_params=PARAMS,
        name="pack_x",
    )(part, packed, z_one, z_two)
    x_one = swap(message, "gx", 0, True)
    x_two = x_one if lax.axis_size("gx") == 2 else swap(message, "gx", 1, True)
    base = pl.pallas_call(
        block_kernel,
        out_shape=shape(27, NZ, NY, NX),
        in_specs=[VMEM],
        out_specs=VMEM,
        scratch_shapes=[pltpu.VMEM((27, UNITS * 8, 128), F32), pltpu.VMEM((3, ROWS, 128), F32)],
        compiler_params=PARAMS,
        cost_estimate=pl.CostEstimate(
            flops=27 * 20 * UNITS * 1024, bytes_accessed=2**22, transcendentals=0
        ),
        name="block",
    )(full)
    return pl.pallas_call(
        last_kernel,
        out_shape=shape(27, NZ, NY, NX),
        in_specs=[VMEM] * 5,
        out_specs=HBM,
        scratch_shapes=[
            pltpu.VMEM((PAD + X_ROWS + PAD, 128), F32),
            pltpu.VMEM((PAD + X_ROWS + PAD, 128), F32),
            pltpu.VMEM((PAD + 28 * 8 + PAD, 128), F32),
            pltpu.VMEM((3, UNITS * 8, 128), F32),
            pltpu.VMEM((128, 128), F32),
            pltpu.VMEM((27, NZ, NY, NX), F32),
            pltpu.SemaphoreType.DMA((NZ,)),
        ],
        compiler_params=PARAMS,
        name="finish",
    )(full, base, columns, x_one, x_two)


def solution(mesh):
    return jax.shard_map(
        shards,
        mesh=mesh,
        in_specs=(P(None, "gz", "gy", "gx"), P("gz", "gy", "gx"), P(None, "gz"), P("gy")),
        out_specs=P(None, "gz", "gy", "gx"),
        check_vma=False,
    )
```

```python
import functools

import jax
import jax.numpy as jnp
import numpy as np
from jax import lax
from jax.experimental import pallas as pl
from jax.experimental.pallas import tpu as pltpu
from jax.sharding import PartitionSpec as P

SPONGE = 32
TAU = 0.52
SMAG = 18.0 * 1.4142135623730951 * 0.17 * 0.17

VEL = [(cx, cy, cz) for cz in (-1, 0, 1) for cy in (-1, 0, 1) for cx in (-1, 0, 1)]
WEIGHT = [
    float(np.array([8.0 / 27.0, 2.0 / 27.0, 1.0 / 54.0, 1.0 / 216.0])[cx * cx + cy * cy + cz * cz])
    for cx, cy, cz in VEL
]
WALL, AIM, CHANNELS = 27, 28, 29
NZ, NY, NX = 4, 8, 128
PITCH = NY + 4
FLAT = (NZ + 4) * PITCH
PAD = 8
ROWS = PAD + FLAT + PAD
SLABS = CHANNELS + 6
UNITS = (NZ + 2) * PITCH // 8

PARAMS = pltpu.CompilerParams(vmem_limit_bytes=12 * 2**20)
VMEM = pl.BlockSpec(memory_space=pltpu.VMEM)
HBM = pl.BlockSpec(memory_space=pltpu.HBM)
F32 = jnp.float32

MIXED = 24
Y_ROWS = (MIXED + 1 + 9) * NZ
Z_BLOCKS = CHANNELS + 10
Z_FAR = 2 * Z_BLOCKS
Z_ROWS = -(-(Z_FAR + 2 * 12) // 8) * 8

X_ROWS = 2 * (WALL + 1)


def relaxed(f, sponge, aim):
    quad = {}
    for cz in (-1, 0, 1):
        line = {}
        for cy in (-1, 0, 1):
            base = 9 * (cz + 1) + 3 * (cy + 1)
            both = f[base + 2] + f[base]
            line[cy] = (both + f[base + 1], f[base + 2] - f[base], both)
        s = line[1][0] + line[-1][0]
        sx = line[1][1] + line[-1][1]
        quad[cz] = dict(
            n=s + line[0][0],
            y=line[1][0] - line[-1][0],
            yy=s,
            x=sx + line[0][1],
            xy=line[1][1] - line[-1][1],
            xx=line[1][2] + line[-1][2] + line[0][2],
        )
    up, mid, down = quad[1], quad[0], quad[-1]
    zz = up["n"] + down["n"]
    rho = zz + mid["n"]
    jz = up["n"] - down["n"]
    jy = up["y"] + down["y"] + mid["y"]
    jx = up["x"] + down["x"] + mid["x"]
    inverse = 1.0 / rho
    ux, uy, uz = jx * inverse, jy * inverse, jz * inverse
    third = rho * (1.0 / 3.0)
    pxx = (up["xx"] + down["xx"] + mid["xx"]) - (third + jx * ux)
    pyy = (up["yy"] + down["yy"] + mid["yy"]) - (third + jy * uy)
    pzz = zz - (third + jz * uz)
    pxy = (up["xy"] + down["xy"] + mid["xy"]) - jx * uy
    pxz = (up["x"] - down["x"]) - jx * uz
    pyz = (up["y"] - down["y"]) - jy * uz
    strain = pxx * pxx + pyy * pyy + pzz * pzz + 2.0 * (pxy * pxy + pxz * pxz + pyz * pyz)
    size = jnp.sqrt(2.0 * strain)
    tau = 0.5 * (TAU + jnp.sqrt(TAU * TAU + SMAG * size * inverse))
    omega = 1.0 / tau
    keep = 1.0 - omega
    if sponge is not None:
        keep = jnp.where(sponge, 0.0, keep)
        omega = jnp.where(sponge, 1.0, omega)
        ux = jnp.where(sponge, aim, ux)
        uy = jnp.where(sponge, 0.0, uy)
        uz = jnp.where(sponge, 0.0, uz)
    square = 1.0 - 1.5 * (ux * ux + uy * uy + uz * uz)
    vx, vy, vz = 3.0 * ux, 3.0 * uy, 3.0 * uz
    share = rho * omega
    weighted = {w: share * w for w in sorted(set(WEIGHT))}
    post = [None] * 27
    for q in range(14):
        cx, cy, cz = VEL[q]
        along = None
        for c, v in ((cx, vx), (cy, vy), (cz, vz)):
            if c:
                along = (v if c > 0 else -v) if along is None else (along + v if c > 0 else along - v)
        scale = weighted[WEIGHT[q]]
        if along is None:
            post[q] = keep * f[q] + scale * square
            continue
        even = square + 0.5 * along * along
        post[q] = keep * f[q] + scale * (even + along)
        post[26 - q] = keep * f[26 - q] + scale * (even - along)
    return post


def lane_ids():
    return lax.broadcasted_iota(jnp.int32, (8, 128), 1)


def row_ids():
    return lax.broadcasted_iota(jnp.int32, (8, 128), 0)


def by_parity(axis, one, two, body):
    even = lax.rem(lax.axis_index(axis), 2) == 0
    pl.when(even)(lambda: body(one, two))
    pl.when(jnp.logical_not(even))(lambda: body(two, one))


def way(*axes):
    return lax.rem(sum(lax.axis_index(axis) for axis in axes), 2)


def by_roles(first, second, body):
    ahead = way("gz", "gy") == 0
    pl.when(ahead)(lambda: body(first, second))
    pl.when(jnp.logical_not(ahead))(lambda: body(second, first))


def z_blocks(near, far, part):
    blocks = [(c, near) for c in range(CHANNELS)]
    return blocks + [(9 * part + k, far) for k in range(9)] + [(WALL, far)]


def first_kernel(pops_at, solid_at, table_at, index_at, own, first_out, second_out, *scratch):
    pops, solid, table, index, messages, sems = scratch
    groups = [(pops_at.at[pl.ds(q, 9)], pops.at[pl.ds(q, 9)]) for q in (0, 9, 18)]
    small = [(table_at, table), (index_at, index)]
    copies = [
        pltpu.make_async_copy(source, target, sems.at[i])
        for i, (source, target) in enumerate([*small, *groups, (solid_at, solid)])
    ]
    for copy in copies:
        copy.start()
    for copy in copies[:2]:
        copy.wait()
    lanes, rows = lane_ids(), row_ids()
    sponge = (lax.axis_index("gx") * NX + lanes) < SPONGE
    profiles = [index[y] for y in range(NY)]
    aims = []
    for z in range(NZ):
        aim = jnp.zeros((8, 128), F32)
        for y, profile in enumerate(profiles):
            aim = jnp.where(rows == y, table[z, profile], aim)
        aims.append(aim)
    for copy in copies[2:-1]:
        copy.wait()
    for z, aim in enumerate(aims):
        post = relaxed([pops[q, z] for q in range(27)], sponge, aim)
        for q in range(27):
            own[pl.ds((q * NZ + z) * 8, 8), :] = post[q]
        own[pl.ds((AIM * NZ + z) * 8, 8), :] = aim
    copies[-1].wait()
    for z in range(NZ):
        own[pl.ds((WALL * NZ + z) * 8, 8), :] = solid[z].astype(F32)

    inside = lax.rem(lanes, 4)
    for out, edge, second, part in ((messages.at[0], 7, 6, 6), (messages.at[1], 0, 1, 0)):
        back = 15 - part
        for first, count, place in ((0, back, 0), (back + 3, 24 - back, back)):
            out[pl.ds(place * NZ, count * NZ), :] = own[
                pl.ds(first * NZ * 8 + edge, count * NZ, stride=8), :
            ]
        for z in range(NZ):
            west, east, aim, flag = (
                own[pl.ds((c * NZ + z) * 8, 8), :] for c in (back, back + 2, AIM, WALL)
            )
            mixed = jnp.where(inside < 2, jnp.where(inside == 0, west, aim), flag)
            mixed = jnp.where(inside == 3, east, mixed)
            out[pl.ds(MIXED * NZ + z, 1), :] = mixed[edge : edge + 1]
        for a in range(3):
            out[pl.ds((MIXED + 1 + 3 * a) * NZ, 3 * NZ), :] = own[
                pl.ds((9 * a + part) * NZ * 8 + second, 3 * NZ, stride=8), :
            ]

    ahead = way("gz", "gy")
    first_out[...] = messages[ahead]
    second_out[...] = messages[1 - ahead]


def ahead_kernel(own, two, one):
    def pack(zup, zdown):
        for out, first, second, part in ((zup, NZ - 1, NZ - 2, 2), (zdown, 0, 1, 0)):
            for k, (c, z) in enumerate(z_blocks(first, second, part)):
                out[pl.ds(8 * k, 8), :] = own[pl.ds((c * NZ + z) * 8, 8), :]

    by_parity("gz", one, two, pack)


def y_runs(part):
    back = 15 - part
    return (0, back, 0), (back, 3, None), (back + 3, 24 - back, back)


def spread_mixed(below, above, flags, aims):
    flags[pl.ds(0, NZ), :] = below[pl.ds(MIXED * NZ, NZ), :]
    flags[pl.ds(NZ, NZ), :] = above[pl.ds(MIXED * NZ, NZ), :]
    mixed = flags[pl.ds(0, 2 * NZ), :]
    inside = lax.rem(lane_ids(), 4)
    moved = {k: pltpu.roll(mixed, k % 128, 1) if k else mixed for k in (-2, -1, 0, 1, 2)}

    def from_lane(source):
        value = moved[0]
        for lane in range(4):
            if lane != source:
                value = jnp.where(inside == lane, moved[lane - source], value)
        return value

    aims[pl.ds(0, 2 * NZ), :] = from_lane(1)
    flags[pl.ds(0, 2 * NZ), :] = from_lane(2)


def second_kernel(y_first, y_second, z_one, z_two, flags, aims, halos, messages):
    ahead = way("gz", "gy")
    halos[ahead] = y_first[...]
    halos[1 - ahead] = y_second[...]
    above, below = halos.at[0], halos.at[1]
    spread_mixed(below, above, flags, aims)
    pack_planes(below, above, flags, aims, messages.at[0], messages.at[1])
    ahead = way("gz")
    z_one[...] = messages[ahead]
    z_two[...] = messages[1 - ahead]


def pack_planes(below, above, flags, aims, zup, zdown):
    for out, first, second, part in ((zup, NZ - 1, NZ - 2, 2), (zdown, 0, 1, 0)):
        for side, (halo, inward) in enumerate(((below, 6), (above, 0))):
            near = side * Z_BLOCKS
            for channel, count, place in y_runs(inward):
                if place is None:
                    row = halo[pl.ds(MIXED * NZ + first, 1), :]
                    out[pl.ds(near + channel, 3), :] = jnp.broadcast_to(row, (3, 128))
                else:
                    out[pl.ds(near + channel, count), :] = halo[
                        pl.ds(place * NZ + first, count, stride=NZ), :
                    ]
            out[pl.ds(near + WALL, 1), :] = flags[pl.ds(side * NZ + first, 1), :]
            out[pl.ds(near + AIM, 1), :] = aims[pl.ds(side * NZ + first, 1), :]
            place = 15 if part else 0
            for k, count in ((0, 8), (8, 1)):
                out[pl.ds(near + CHANNELS + k, count), :] = halo[
                    pl.ds((place + k) * NZ + second, count, stride=NZ if count > 1 else 1), :
                ]
            out[pl.ds(near + Z_BLOCKS - 1, 1), :] = flags[pl.ds(side * NZ + second, 1), :]
            far = Z_FAR + 12 * side
            start = (MIXED + 1) * NZ
            out[pl.ds(far, 8), :] = halo[pl.ds(start + first, 8, stride=NZ), :]
            out[pl.ds(far + 8, 1), :] = halo[pl.ds(start + 8 * NZ + first, 1), :]
            for k in range(3):
                row = halo[pl.ds(start + (3 * part + k) * NZ + second, 1), :]
                out[pl.ds(far + 9 + k, 1), :] = row


def plane_at(z):
    return PAD + (z + 2) * PITCH


def add_rows(full, flags, aims, above, below):
    spread_mixed(below, above, flags, aims)

    def put(channel, row, source):
        full[pl.ds(channel * ROWS + plane_at(0) + row, NZ, stride=PITCH), :] = source

    sides = ((below, 1, 0, 6), (above, PITCH - 2, PITCH - 1, 0))
    for side, (halo, near, far, inward) in enumerate(sides):
        for first, count, place in y_runs(inward):
            for k in range(count):
                row = MIXED if place is None else place + k
                put(first + k, near, halo[pl.ds(row * NZ, NZ), :])
        flag = flags[pl.ds(side * NZ, NZ), :]
        put(WALL, near, flag)
        put(WALL, far, flag)
        put(AIM, near, aims[pl.ds(side * NZ, NZ), :])
        for k in range(9):
            q = 9 * (k // 3) + inward + k % 3
            put(q, far, halo[pl.ds((MIXED + 1 + k) * NZ, NZ), :])


def add_own_planes(full, ceiling, floor):
    for halo, near, far, part in ((floor, -1, -2, 2), (ceiling, NZ, NZ + 1, 0)):
        for k, (c, z) in enumerate(z_blocks(near, far, part)):
            full[pl.ds(c * ROWS + plane_at(z) + 2, 8), :] = halo[pl.ds(8 * k, 8), :]


def add_planes(full, ceiling, floor):
    def put(count, channel, z, row, source):
        start = channel * ROWS + plane_at(z) + row
        full[pl.ds(start, count, stride=ROWS), :] = source

    for halo, near, far, part in ((floor, -1, -2, 2), (ceiling, NZ, NZ + 1, 0)):
        for side, (row, beyond, group) in enumerate(((1, 0, 2), (PITCH - 2, PITCH - 1, 0))):
            start = side * Z_BLOCKS
            put(CHANNELS, 0, near, row, halo[pl.ds(start, CHANNELS), :])
            put(9, 9 * part, far, row, halo[pl.ds(start + CHANNELS, 9), :])
            first, second = (halo[pl.ds(start + k, 1), :] for k in (WALL, Z_BLOCKS - 1))
            put(1, WALL, far, row, second)
            start = Z_FAR + 12 * side
            for k in range(3):
                put(3, 9 * k + 3 * group, near, beyond, halo[pl.ds(start + 3 * k, 3), :])
            put(3, 9 * part + 3 * group, far, beyond, halo[pl.ds(start + 9, 3), :])
            put(1, WALL, near, beyond, first)
            put(1, WALL, far, beyond, second)


def pack_columns(full, pack, tiles):
    slot = lane_ids() // 4
    for t in tiles:
        packed = jnp.zeros((8, 128), F32)
        for c in range(CHANNELS):
            moved = pltpu.roll(full[pl.ds(c * ROWS + PAD + 8 * t, 8), :], (4 * c + 2) % 128, 1)
            packed = jnp.where(slot == c, moved, packed)
        pack[pl.ds(8 * t, 8), :] = packed


def pack_rim(full, pack, first):
    slot, rows = lane_ids() // 4, row_ids()
    parts = (rows < 2, (rows >= 2) & (rows < 6), rows >= 6)
    packed = jnp.zeros((8, 128), F32)
    for c in range(CHANNELS):
        a, b, d = (full[pl.ds(c * ROWS + PAD + 8 * (first + t), 8), :] for t in range(3))
        rim = jnp.where(parts[0], a, jnp.where(parts[1], b, d))
        packed = jnp.where(slot == c, pltpu.roll(rim, (4 * c + 2) % 128, 1), packed)
    for t, part in enumerate(parts):
        tile = pl.ds(8 * (first + t), 8)
        pack[tile, :] = jnp.where(part, packed, pack[tile, :])


def bound_planes(full):
    here, last = lax.axis_index("gz"), lax.axis_size("gz") - 1
    ground = pl.ds(WALL * ROWS + plane_at(-1), PITCH)
    full[ground, :] = jnp.where(here == 0, 1.0, full[ground, :])
    for q in range(9):
        above = pl.ds(q * ROWS + plane_at(NZ), PITCH)
        mirrored = full[pl.ds((q + 18) * ROWS + plane_at(NZ - 1), PITCH), :]
        full[above, :] = jnp.where(here == last, mirrored, full[above, :])


def fill_kernel(own, y_first, y_second, two, one, full, pack, flags, aims):
    for c in range(CHANNELS):
        for z in range(NZ):
            full[pl.ds(c * ROWS + plane_at(z) + 2, 8), :] = own[pl.ds((c * NZ + z) * 8, 8), :]
    by_roles(y_first, y_second, functools.partial(add_rows, full, flags, aims))
    by_parity("gz", one, two, functools.partial(add_own_planes, full))
    bound_planes(full)
    pack_columns(full, pack, range(FLAT // 8))
    pack[pl.ds(FLAT, 128 - FLAT), :] = jnp.zeros((128 - FLAT, 128), F32)


def third_kernel(part, packed, z_one, z_two, full, pack, columns, message, halos):
    ahead = way("gz")
    halos[ahead] = z_one[...]
    halos[1 - ahead] = z_two[...]
    add_planes(full, halos.at[0], halos.at[1])
    bound_planes(full)
    for first in (0, (NZ + 2) * PITCH // 8):
        pack_rim(full, pack, first)
    columns[pl.ds(PAD, 128), :] = pack[...].T

    def row(c, i, count):
        return columns[pl.ds(PAD + 4 * c + i, count), :]

    def returned(q, near, far):
        cx, cy, cz = VEL[q]
        step = (-PITCH * cz - cy) % 128
        value = row(26 - q, near, 8)
        value = pltpu.roll(value, step, 1) if step else value
        return jnp.where(row(WALL, far, 8) != 0.0, value, row(q, far, 8))[:1]

    for c in range(WALL + 1):
        cx = VEL[c][0] if c < 27 else 0
        if cx == 0:
            message[pl.ds(2 * c, 2), :] = row(c, 1, 2)
        elif cx > 0:
            message[pl.ds(2 * c, 1), :] = returned(c, 1, 0)
            message[pl.ds(2 * c + 1, 1), :] = row(c, 1, 1)
        else:
            message[pl.ds(2 * c, 1), :] = row(c, 2, 1)
            message[pl.ds(2 * c + 1, 1), :] = returned(c, 2, 3)


def block_kernel(full, post, walls):
    top = lax.axis_index("gz") == lax.axis_size("gz") - 1
    sponge = (lax.axis_index("gx") * NX + lane_ids()) < SPONGE
    for t in range(ROWS // 8):
        rows = pl.ds(8 * t, 8)
        flags = full[pl.ds(WALL * ROWS + 8 * t, 8), :]
        for cx in (-1, 0, 1):
            walls[cx + 1, rows, :] = pltpu.roll(flags, cx % 128, 1) if cx else flags
    for u in range(UNITS):
        cell = PAD + PITCH + 8 * u
        f = []
        solid = walls[1, pl.ds(cell, 8), :] != 0.0
        for q in range(27):
            cx, cy, cz = VEL[q]
            start = cell - PITCH * cz - cy
            value = full[pl.ds(q * ROWS + start, 8), :]
            if cx:
                value = pltpu.roll(value, cx % 128, 1)
            if q != 13:
                blocked = walls[cx + 1, pl.ds(start, 8), :] != 0.0
                value = jnp.where(blocked, full[pl.ds((26 - q) * ROWS + cell, 8), :], value)
            f.append(jnp.where(solid, WEIGHT[q], value))
        done = relaxed(f, sponge, full[pl.ds(AIM * ROWS + cell, 8), :])
        for q in range(27):
            post[q, pl.ds(8 * u, 8), :] = done[q]

    @pl.when(top)
    def _():
        for q in range(9):
            post[q, pl.ds((NZ + 1) * PITCH, PITCH), :] = post[q + 18, pl.ds(NZ * PITCH, PITCH), :]


def last_kernel(full, block, columns, x_one, x_two, out, west, east, column, walls, back, done, sems):
    here_x, size_x = lax.axis_index("gx"), lax.axis_size("gx")
    top = lax.axis_index("gz") == lax.axis_size("gz") - 1
    lanes, rows = lane_ids(), row_ids()

    if size_x == 2:

        def beside(side, start):
            first = min(max(start, 0), X_ROWS - 8)
            value = x_one[pl.ds(first, 8), :]
            return pltpu.roll(value, (first - start) % 8, 0) if first != start else value

    else:

        def spread(right, left):
            west[pl.ds(PAD, X_ROWS), :] = left[...]
            east[pl.ds(PAD, X_ROWS), :] = right[...]

        by_parity("gx", x_one, x_two, spread)

        def beside(side, start):
            return (west if side < 0 else east)[pl.ds(PAD + start, 8), :]

    def strip_at(c, shift):
        cx = VEL[c][0] if c < 27 else 0
        at = rows - shift
        first = PAD + 4 * c - shift
        value = jnp.where(at < 4, columns[pl.ds(first, 8), :], columns[pl.ds(first - 4, 8), :])
        if c <= WALL and cx >= 0:
            value = jnp.where(at < 2, beside(-1, 2 * c - (cx == 0) - shift), value)
        if c <= WALL and cx <= 0:
            value = jnp.where(at >= 6, beside(1, 2 * c - 6 + (cx == 0) - shift), value)
        if c == WALL:
            value = jnp.where((at == 0) | (at == 7), 0.0, value)
        return value

    strip = [strip_at(c, 0) for c in range(CHANNELS)]
    flags_at = {cx: strip_at(WALL, cx) if cx else strip[WALL] for cx in (-1, 0, 1)}

    def moved_along(value, q):
        cx, cy, cz = VEL[q]
        step = (PITCH * cz + cy) % 128
        return pltpu.roll(value, step, 1) if step else value

    moved = []
    for q in range(27):
        cx = VEL[q][0]
        value = moved_along(strip_at(q, cx) if cx else strip[q], q)
        if q != 13:
            value = jnp.where(moved_along(flags_at[cx], q) != 0.0, strip[26 - q], value)
        moved.append(jnp.where(strip[WALL] != 0.0, WEIGHT[q], value))
    place = here_x * NX + jnp.where(rows < 4, rows - 2, rows + (NX - 6))
    place = lax.rem(place + size_x * NX, size_x * NX)
    sides = relaxed(moved, place < SPONGE, strip[AIM])
    for q, side in enumerate(sides + [strip[WALL]]):
        column[pl.ds(PAD + 8 * q, 8), :] = side

    def picked(wanted):
        value = None
        for sublane, (q, row) in enumerate(wanted):
            moved = column[pl.ds(PAD + 8 * q + row - sublane, 8), :]
            value = moved if value is None else jnp.where(rows == sublane, moved, value)
        return value

    packed = []
    for k in range(9):
        a, b = 3 * k + 2, 3 * k
        packed.append(
            picked([(a, 5), (a, 2), (a, 1), (a, 2), (b, 5), (b, 2), (b, 5), (b, 6)])
        )
    rest = [(3 * k + 1, row) for k in range(9) for row in (5, 2)] + [(27, 1), (27, 6)]
    packed += [picked(rest[i : i + 8]) for i in range(0, len(rest), 8)]
    packed += [jnp.zeros((8, 128), F32)] * (16 - len(packed))
    back[...] = jnp.concatenate(packed, axis=0).T

    def column_at(place, lane, start):
        return pltpu.roll(back[pl.ds(start, 8), :], (lane - place) % 128, 1)

    rim = (lanes == 0) | (lanes == 127)

    def edge_of(q, z, start, base, lane):
        place = 72 + 2 * (q // 3) + base if q % 3 == 1 else 8 * (q // 3) + base
        value = column_at(place, lane, PITCH + start)
        if z == NZ - 1 and VEL[q][2] < 0:
            value = jnp.where(top, column_at(place + (12 if q % 3 == 1 else 48), lane, start), value)
        return value

    def rimmed(q, z, start):
        ends = edge_of(q, z, start, (5, 1, 1)[q % 3], 0)
        return jnp.where(rim, ends, block[q, pl.ds(start, 8), :])

    for u in range(UNITS):
        flags = full[pl.ds(WALL * ROWS + PAD + PITCH + 8 * u, 8), :]
        walls[1, pl.ds(8 * u, 8), :] = flags
        for cx, edge, place in ((1, 0, 90), (-1, 127, 91)):
            walls[cx + 1, pl.ds(8 * u, 8), :] = jnp.where(
                lanes == edge, column_at(place, edge, PITCH + 8 * u), pltpu.roll(flags, cx % 128, 1)
            )

    cells = [(z + 1) * PITCH + 2 for z in range(NZ)]
    solids = [walls[1, pl.ds(cell, 8), :] != 0.0 for cell in cells]

    def streamed(q, z):
        cx, cy, cz = VEL[q]
        cell = cells[z]
        start = cell - PITCH * cz - cy
        if cx > 0:
            side = edge_of(q, z, start, 2, 0)
            value = jnp.where(lanes < 2, side, pltpu.roll(block[q, pl.ds(start, 8), :], 1, 1))
        elif cx < 0:
            side = edge_of(q, z, start, 6, 126)
            value = jnp.where(lanes > 125, side, pltpu.roll(block[q, pl.ds(start, 8), :], 127, 1))
        else:
            value = rimmed(q, z, start)
        if q != 13:
            blocked = walls[cx + 1, pl.ds(start, 8), :] != 0.0
            value = jnp.where(blocked, rimmed(26 - q, None, cell), value)
        return jnp.where(solids[z], WEIGHT[q], value)

    copies = []
    for first, count in ((0, 9), (9, 8), (17, 6), (23, 4)):
        for q in range(first, first + count):
            for z in range(NZ):
                done[q, z] = streamed(q, z)
        part = pl.ds(first, count)
        copies.append(pltpu.make_async_copy(done.at[part], out.at[part], sems.at[len(copies)]))
        copies[-1].start()
    for copy in copies:
        copy.wait()


def pairs(size, turn, wrap):
    ahead = [(i, (i + 1) % size) for i in range(turn, size if wrap else size - 1, 2)]
    return ahead + [(j, i) for i, j in ahead]


def swap(value, axis, turn, wrap):
    return lax.ppermute(value, axis, pairs(lax.axis_size(axis), turn, wrap))


def swap_mixed(value, turn):
    size, planes = lax.axis_size("gy"), lax.axis_size("gz")
    moves = []
    for k in range(planes):
        moves += [
            (i * planes + k, j * planes + k) for i, j in pairs(size, (turn + k) % 2, True)
        ]
    return lax.ppermute(value, ("gy", "gz"), moves)


def shape(*dims):
    return jax.ShapeDtypeStruct(dims, F32)


def shards(pops, solid, profile_table, profile_index):
    own, y_first, y_second = pl.pallas_call(
        first_kernel,
        out_shape=[shape(CHANNELS * NZ * 8, 128), shape(Y_ROWS, 128), shape(Y_ROWS, 128)],
        in_specs=[HBM] * 4,
        out_specs=[VMEM] * 3,
        scratch_shapes=[
            pltpu.VMEM(pops.shape, F32),
            pltpu.VMEM(solid.shape, jnp.int32),
            pltpu.SMEM(profile_table.shape[::-1], F32),
            pltpu.SMEM(profile_index.shape, jnp.int32),
            pltpu.VMEM((2, Y_ROWS, 128), F32),
            pltpu.SemaphoreType.DMA((6,)),
        ],
        compiler_params=PARAMS,
        name="collide",
    )(*(pltpu.with_memory_space_constraint(a, pltpu.HBM) for a in (pops, solid, profile_table.T, profile_index)))
    y_first = swap_mixed(y_first, 0)
    y_second = swap_mixed(y_second, 1)
    own_two, own_one = pl.pallas_call(
        ahead_kernel,
        out_shape=[shape(Z_BLOCKS * 8, 128)] * 2,
        in_specs=[VMEM],
        out_specs=[VMEM] * 2,
        compiler_params=PARAMS,
        name="pack_own",
    )(own)
    own_two = swap(own_two, "gz", 1, False)
    own_one = swap(own_one, "gz", 0, False)
    z_one, z_two = pl.pallas_call(
        second_kernel,
        out_shape=[shape(Z_ROWS, 128)] * 2,
        in_specs=[VMEM] * 2,
        out_specs=[VMEM] * 2,
        scratch_shapes=[
            *[pltpu.VMEM((4 * NZ, 128), F32)] * 2,
            pltpu.VMEM((2, Y_ROWS, 128), F32),
            pltpu.VMEM((2, Z_ROWS, 128), F32),
        ],
        compiler_params=PARAMS,
        cost_estimate=pl.CostEstimate(flops=10**9, bytes_accessed=2**20, transcendentals=0),
        name="pack_z",
    )(y_first, y_second)
    z_one = swap(z_one, "gz", 0, False)
    z_two = swap(z_two, "gz", 1, False)
    part, packed = pl.pallas_call(
        fill_kernel,
        out_shape=[shape(SLABS * ROWS, 128), shape(128, 128)],
        in_specs=[VMEM] * 5,
        out_specs=[VMEM] * 2,
        scratch_shapes=[pltpu.VMEM((4 * NZ, 128), F32)] * 2,
        compiler_params=PARAMS,
        cost_estimate=pl.CostEstimate(flops=10**6, bytes_accessed=2**22, transcendentals=0),
        name="fill",
    )(own, y_first, y_second, own_two, own_one)
    full, packed, columns, message = pl.pallas_call(
        third_kernel,
        out_shape=[
            shape(SLABS * ROWS, 128),
            shape(128, 128),
            shape(PAD + 128 + PAD, 128),
            shape(X_ROWS, 128),
        ],
        in_specs=[VMEM] * 4,
        out_specs=[VMEM] * 4,
        scratch_shapes=[pltpu.VMEM((2, Z_ROWS, 128), F32)],
        input_output_aliases={0: 0, 1: 1},
        compiler_params=PARAMS,
        name="pack_x",
    )(part, packed, z_one, z_two)
    x_one = swap(message, "gx", 0, True)
    x_two = x_one if lax.axis_size("gx") == 2 else swap(message, "gx", 1, True)
    block = pl.pallas_call(
        block_kernel,
        out_shape=shape(27, UNITS * 8, 128),
        in_specs=[VMEM],
        out_specs=VMEM,
        scratch_shapes=[pltpu.VMEM((3, ROWS, 128), F32)],
        compiler_params=PARAMS,
        cost_estimate=pl.CostEstimate(
            flops=27 * 20 * UNITS * 1024, bytes_accessed=2**22, transcendentals=0
        ),
        name="block",
    )(full)
    return pl.pallas_call(
        last_kernel,
        out_shape=shape(27, NZ, NY, NX),
        in_specs=[VMEM] * 5,
        out_specs=HBM,
        scratch_shapes=[
            pltpu.VMEM((PAD + X_ROWS + PAD, 128), F32),
            pltpu.VMEM((PAD + X_ROWS + PAD, 128), F32),
            pltpu.VMEM((PAD + 28 * 8 + PAD, 128), F32),
            pltpu.VMEM((3, UNITS * 8, 128), F32),
            pltpu.VMEM((128, 128), F32),
            pltpu.VMEM((27, NZ, NY, NX), F32),
            pltpu.SemaphoreType.DMA((NZ,)),
        ],
        compiler_params=PARAMS,
        name="finish",
    )(full, block, columns, x_one, x_two)


def solution(mesh):
    return jax.shard_map(
        shards,
        mesh=mesh,
        in_specs=(P(None, "gz", "gy", "gx"), P("gz", "gy", "gx"), P(None, "gz"), P("gy")),
        out_specs=P(None, "gz", "gy", "gx"),
        check_vma=False,
    )
```

```python
import functools

import jax
import jax.numpy as jnp
import numpy as np
from jax import lax
from jax.experimental import pallas as pl
from jax.experimental.pallas import tpu as pltpu
from jax.sharding import PartitionSpec as P

SPONGE = 32
TAU = 0.52
SMAG = 18.0 * 1.4142135623730951 * 0.17 * 0.17

VEL = [(cx, cy, cz) for cz in (-1, 0, 1) for cy in (-1, 0, 1) for cx in (-1, 0, 1)]
WEIGHT = [
    float(np.array([8.0 / 27.0, 2.0 / 27.0, 1.0 / 54.0, 1.0 / 216.0])[cx * cx + cy * cy + cz * cz])
    for cx, cy, cz in VEL
]
WALL, AIM, CHANNELS = 27, 28, 29
NZ, NY, NX = 4, 8, 128
PITCH = NY + 4
FLAT = (NZ + 4) * PITCH
PAD = 8
ROWS = PAD + FLAT + PAD
SLABS = CHANNELS + 6
UNITS = (NZ + 2) * PITCH // 8

PARAMS = pltpu.CompilerParams(vmem_limit_bytes=12 * 2**20)
VMEM = pl.BlockSpec(memory_space=pltpu.VMEM)
HBM = pl.BlockSpec(memory_space=pltpu.HBM)
F32 = jnp.float32

MIXED = 24
Y_ROWS = (MIXED + 1 + 9) * NZ
Z_BLOCKS = CHANNELS + 10
Z_FAR = 2 * Z_BLOCKS
Z_ROWS = -(-(Z_FAR + 2 * 12) // 8) * 8

X_ROWS = 2 * (WALL + 1)


def relaxed(f, sponge, aim):
    quad = {}
    for cz in (-1, 0, 1):
        line = {}
        for cy in (-1, 0, 1):
            base = 9 * (cz + 1) + 3 * (cy + 1)
            both = f[base + 2] + f[base]
            line[cy] = (both + f[base + 1], f[base + 2] - f[base], both)
        s = line[1][0] + line[-1][0]
        sx = line[1][1] + line[-1][1]
        quad[cz] = dict(
            n=s + line[0][0],
            y=line[1][0] - line[-1][0],
            yy=s,
            x=sx + line[0][1],
            xy=line[1][1] - line[-1][1],
            xx=line[1][2] + line[-1][2] + line[0][2],
        )
    up, mid, down = quad[1], quad[0], quad[-1]
    zz = up["n"] + down["n"]
    rho = zz + mid["n"]
    jz = up["n"] - down["n"]
    jy = up["y"] + down["y"] + mid["y"]
    jx = up["x"] + down["x"] + mid["x"]
    inverse = 1.0 / rho
    ux, uy, uz = jx * inverse, jy * inverse, jz * inverse
    third = rho * (1.0 / 3.0)
    pxx = (up["xx"] + down["xx"] + mid["xx"]) - (third + jx * ux)
    pyy = (up["yy"] + down["yy"] + mid["yy"]) - (third + jy * uy)
    pzz = zz - (third + jz * uz)
    pxy = (up["xy"] + down["xy"] + mid["xy"]) - jx * uy
    pxz = (up["x"] - down["x"]) - jx * uz
    pyz = (up["y"] - down["y"]) - jy * uz
    strain = pxx * pxx + pyy * pyy + pzz * pzz + 2.0 * (pxy * pxy + pxz * pxz + pyz * pyz)
    size = jnp.sqrt(2.0 * strain)
    tau = 0.5 * (TAU + jnp.sqrt(TAU * TAU + SMAG * size * inverse))
    omega = 1.0 / tau
    keep = 1.0 - omega
    if sponge is not None:
        keep = jnp.where(sponge, 0.0, keep)
        omega = jnp.where(sponge, 1.0, omega)
        ux = jnp.where(sponge, aim, ux)
        uy = jnp.where(sponge, 0.0, uy)
        uz = jnp.where(sponge, 0.0, uz)
    square = 1.0 - 1.5 * (ux * ux + uy * uy + uz * uz)
    vx, vy, vz = 3.0 * ux, 3.0 * uy, 3.0 * uz
    share = rho * omega
    weighted = {w: share * w for w in sorted(set(WEIGHT))}
    post = [None] * 27
    for q in range(14):
        cx, cy, cz = VEL[q]
        along = None
        for c, v in ((cx, vx), (cy, vy), (cz, vz)):
            if c:
                along = (v if c > 0 else -v) if along is None else (along + v if c > 0 else along - v)
        scale = weighted[WEIGHT[q]]
        if along is None:
            post[q] = keep * f[q] + scale * square
            continue
        even = square + 0.5 * along * along
        post[q] = keep * f[q] + scale * (even + along)
        post[26 - q] = keep * f[26 - q] + scale * (even - along)
    return post


def lane_ids():
    return lax.broadcasted_iota(jnp.int32, (8, 128), 1)


def row_ids():
    return lax.broadcasted_iota(jnp.int32, (8, 128), 0)


def by_parity(axis, one, two, body):
    even = lax.rem(lax.axis_index(axis), 2) == 0
    pl.when(even)(lambda: body(one, two))
    pl.when(jnp.logical_not(even))(lambda: body(two, one))


def way(*axes):
    return lax.rem(sum(lax.axis_index(axis) for axis in axes), 2)


def by_roles(first, second, body):
    ahead = way("gz", "gy") == 0
    pl.when(ahead)(lambda: body(first, second))
    pl.when(jnp.logical_not(ahead))(lambda: body(second, first))


def z_blocks(near, far, part):
    blocks = [(c, near) for c in range(CHANNELS)]
    return blocks + [(9 * part + k, far) for k in range(9)] + [(WALL, far)]


def first_kernel(pops_at, solid_at, table_at, index_at, own, first_out, second_out, *scratch):
    pops, solid, table, index, messages, sems = scratch
    groups = [(pops_at.at[pl.ds(q, 9)], pops.at[pl.ds(q, 9)]) for q in (0, 9, 18)]
    small = [(table_at, table), (index_at, index)]
    copies = [
        pltpu.make_async_copy(source, target, sems.at[i])
        for i, (source, target) in enumerate([*small, *groups, (solid_at, solid)])
    ]
    for copy in copies:
        copy.start()
    for copy in copies[:2]:
        copy.wait()
    lanes, rows = lane_ids(), row_ids()
    sponge = (lax.axis_index("gx") * NX + lanes) < SPONGE
    profiles = [index[y] for y in range(NY)]
    aims = []
    for z in range(NZ):
        aim = jnp.zeros((8, 128), F32)
        for y, profile in enumerate(profiles):
            aim = jnp.where(rows == y, table[z, profile], aim)
        aims.append(aim)
    for copy in copies[2:-1]:
        copy.wait()
    for z, aim in enumerate(aims):
        post = relaxed([pops[q, z] for q in range(27)], sponge, aim)
        for q in range(27):
            own[pl.ds((q * NZ + z) * 8, 8), :] = post[q]
        own[pl.ds((AIM * NZ + z) * 8, 8), :] = aim
    copies[-1].wait()
    for z in range(NZ):
        own[pl.ds((WALL * NZ + z) * 8, 8), :] = solid[z].astype(F32)

    inside = lax.rem(lanes, 4)
    for out, edge, second, part in ((messages.at[0], 7, 6, 6), (messages.at[1], 0, 1, 0)):
        back = 15 - part
        for first, count, place in ((0, back, 0), (back + 3, 24 - back, back)):
            out[pl.ds(place * NZ, count * NZ), :] = own[
                pl.ds(first * NZ * 8 + edge, count * NZ, stride=8), :
            ]
        for z in range(NZ):
            west, east, aim, flag = (
                own[pl.ds((c * NZ + z) * 8, 8), :] for c in (back, back + 2, AIM, WALL)
            )
            mixed = jnp.where(inside < 2, jnp.where(inside == 0, west, aim), flag)
            mixed = jnp.where(inside == 3, east, mixed)
            out[pl.ds(MIXED * NZ + z, 1), :] = mixed[edge : edge + 1]
        for a in range(3):
            out[pl.ds((MIXED + 1 + 3 * a) * NZ, 3 * NZ), :] = own[
                pl.ds((9 * a + part) * NZ * 8 + second, 3 * NZ, stride=8), :
            ]

    ahead = way("gz", "gy")
    first_out[...] = messages[ahead]
    second_out[...] = messages[1 - ahead]


def ahead_kernel(own, two, one):
    def pack(zup, zdown):
        for out, first, second, part in ((zup, NZ - 1, NZ - 2, 2), (zdown, 0, 1, 0)):
            for k, (c, z) in enumerate(z_blocks(first, second, part)):
                out[pl.ds(8 * k, 8), :] = own[pl.ds((c * NZ + z) * 8, 8), :]

    by_parity("gz", one, two, pack)


def y_runs(part):
    back = 15 - part
    return (0, back, 0), (back, 3, None), (back + 3, 24 - back, back)


def spread_mixed(below, above, flags, aims):
    flags[pl.ds(0, NZ), :] = below[pl.ds(MIXED * NZ, NZ), :]
    flags[pl.ds(NZ, NZ), :] = above[pl.ds(MIXED * NZ, NZ), :]
    mixed = flags[pl.ds(0, 2 * NZ), :]
    inside = lax.rem(lane_ids(), 4)
    moved = {k: pltpu.roll(mixed, k % 128, 1) if k else mixed for k in (-2, -1, 0, 1, 2)}

    def from_lane(source):
        value = moved[0]
        for lane in range(4):
            if lane != source:
                value = jnp.where(inside == lane, moved[lane - source], value)
        return value

    aims[pl.ds(0, 2 * NZ), :] = from_lane(1)
    flags[pl.ds(0, 2 * NZ), :] = from_lane(2)


def second_kernel(y_first, y_second, z_one, z_two, flags, aims, halos, messages):
    ahead = way("gz", "gy")
    halos[ahead] = y_first[...]
    halos[1 - ahead] = y_second[...]
    above, below = halos.at[0], halos.at[1]
    spread_mixed(below, above, flags, aims)
    pack_planes(below, above, flags, aims, messages.at[0], messages.at[1])
    ahead = way("gz")
    z_one[...] = messages[ahead]
    z_two[...] = messages[1 - ahead]


def pack_planes(below, above, flags, aims, zup, zdown):
    for out, first, second, part in ((zup, NZ - 1, NZ - 2, 2), (zdown, 0, 1, 0)):
        for side, (halo, inward) in enumerate(((below, 6), (above, 0))):
            near = side * Z_BLOCKS
            for channel, count, place in y_runs(inward):
                if place is None:
                    row = halo[pl.ds(MIXED * NZ + first, 1), :]
                    out[pl.ds(near + channel, 3), :] = jnp.broadcast_to(row, (3, 128))
                else:
                    out[pl.ds(near + channel, count), :] = halo[
                        pl.ds(place * NZ + first, count, stride=NZ), :
                    ]
            out[pl.ds(near + WALL, 1), :] = flags[pl.ds(side * NZ + first, 1), :]
            out[pl.ds(near + AIM, 1), :] = aims[pl.ds(side * NZ + first, 1), :]
            place = 15 if part else 0
            for k, count in ((0, 8), (8, 1)):
                out[pl.ds(near + CHANNELS + k, count), :] = halo[
                    pl.ds((place + k) * NZ + second, count, stride=NZ if count > 1 else 1), :
                ]
            out[pl.ds(near + Z_BLOCKS - 1, 1), :] = flags[pl.ds(side * NZ + second, 1), :]
            far = Z_FAR + 12 * side
            start = (MIXED + 1) * NZ
            out[pl.ds(far, 8), :] = halo[pl.ds(start + first, 8, stride=NZ), :]
            out[pl.ds(far + 8, 1), :] = halo[pl.ds(start + 8 * NZ + first, 1), :]
            for k in range(3):
                row = halo[pl.ds(start + (3 * part + k) * NZ + second, 1), :]
                out[pl.ds(far + 9 + k, 1), :] = row


def plane_at(z):
    return PAD + (z + 2) * PITCH


def add_rows(full, flags, aims, above, below):
    spread_mixed(below, above, flags, aims)

    def put(channel, row, source):
        full[pl.ds(channel * ROWS + plane_at(0) + row, NZ, stride=PITCH), :] = source

    sides = ((below, 1, 0, 6), (above, PITCH - 2, PITCH - 1, 0))
    for side, (halo, near, far, inward) in enumerate(sides):
        for first, count, place in y_runs(inward):
            for k in range(count):
                row = MIXED if place is None else place + k
                put(first + k, near, halo[pl.ds(row * NZ, NZ), :])
        flag = flags[pl.ds(side * NZ, NZ), :]
        put(WALL, near, flag)
        put(WALL, far, flag)
        put(AIM, near, aims[pl.ds(side * NZ, NZ), :])
        for k in range(9):
            q = 9 * (k // 3) + inward + k % 3
            put(q, far, halo[pl.ds((MIXED + 1 + k) * NZ, NZ), :])


def add_own_planes(full, ceiling, floor):
    for halo, near, far, part in ((floor, -1, -2, 2), (ceiling, NZ, NZ + 1, 0)):
        for k, (c, z) in enumerate(z_blocks(near, far, part)):
            full[pl.ds(c * ROWS + plane_at(z) + 2, 8), :] = halo[pl.ds(8 * k, 8), :]


def add_planes(full, ceiling, floor):
    def put(count, channel, z, row, source):
        start = channel * ROWS + plane_at(z) + row
        full[pl.ds(start, count, stride=ROWS), :] = source

    for halo, near, far, part in ((floor, -1, -2, 2), (ceiling, NZ, NZ + 1, 0)):
        for side, (row, beyond, group) in enumerate(((1, 0, 2), (PITCH - 2, PITCH - 1, 0))):
            start = side * Z_BLOCKS
            put(CHANNELS, 0, near, row, halo[pl.ds(start, CHANNELS), :])
            put(9, 9 * part, far, row, halo[pl.ds(start + CHANNELS, 9), :])
            first, second = (halo[pl.ds(start + k, 1), :] for k in (WALL, Z_BLOCKS - 1))
            put(1, WALL, far, row, second)
            start = Z_FAR + 12 * side
            for k in range(3):
                put(3, 9 * k + 3 * group, near, beyond, halo[pl.ds(start + 3 * k, 3), :])
            put(3, 9 * part + 3 * group, far, beyond, halo[pl.ds(start + 9, 3), :])
            put(1, WALL, near, beyond, first)
            put(1, WALL, far, beyond, second)


def pack_columns(full, pack, tiles):
    slot = lane_ids() // 4
    for t in tiles:
        packed = jnp.zeros((8, 128), F32)
        for c in range(CHANNELS):
            moved = pltpu.roll(full[pl.ds(c * ROWS + PAD + 8 * t, 8), :], (4 * c + 2) % 128, 1)
            packed = jnp.where(slot == c, moved, packed)
        pack[pl.ds(8 * t, 8), :] = packed


def pack_rim(full, pack, first):
    slot, rows = lane_ids() // 4, row_ids()
    parts = (rows < 2, (rows >= 2) & (rows < 6), rows >= 6)
    chains = []
    for base in range(0, CHANNELS, 8):
        chain = None
        for c in range(base, min(base + 8, CHANNELS)):
            a, b, d = (full[pl.ds(c * ROWS + PAD + 8 * (first + t), 8), :] for t in range(3))
            rim = jnp.where(parts[0], a, jnp.where(parts[1], b, d))
            moved = pltpu.roll(rim, (4 * c + 2) % 128, 1)
            chain = moved if chain is None else jnp.where(slot == c, moved, chain)
        chains.append(chain)
    packed = jnp.where(
        slot < 16,
        jnp.where(slot < 8, chains[0], chains[1]),
        jnp.where(slot < 24, chains[2], chains[3]),
    )
    for t, part in enumerate(parts):
        tile = pl.ds(8 * (first + t), 8)
        pack[tile, :] = jnp.where(part, packed, pack[tile, :])


def bound_planes(full):
    here, last = lax.axis_index("gz"), lax.axis_size("gz") - 1
    ground = pl.ds(WALL * ROWS + plane_at(-1), PITCH)
    full[ground, :] = jnp.where(here == 0, 1.0, full[ground, :])
    for q in range(9):
        above = pl.ds(q * ROWS + plane_at(NZ), PITCH)
        mirrored = full[pl.ds((q + 18) * ROWS + plane_at(NZ - 1), PITCH), :]
        full[above, :] = jnp.where(here == last, mirrored, full[above, :])


def fill_kernel(own, y_first, y_second, two, one, full, pack, flags, aims):
    for c in range(CHANNELS):
        for z in range(NZ):
            full[pl.ds(c * ROWS + plane_at(z) + 2, 8), :] = own[pl.ds((c * NZ + z) * 8, 8), :]
    by_roles(y_first, y_second, functools.partial(add_rows, full, flags, aims))
    by_parity("gz", one, two, functools.partial(add_own_planes, full))
    bound_planes(full)
    pack_columns(full, pack, range(FLAT // 8))
    pack[pl.ds(FLAT, 128 - FLAT), :] = jnp.zeros((128 - FLAT, 128), F32)


def third_kernel(part, packed, z_one, z_two, full, pack, columns, message, halos):
    ahead = way("gz")
    halos[ahead] = z_one[...]
    halos[1 - ahead] = z_two[...]
    add_planes(full, halos.at[0], halos.at[1])
    bound_planes(full)
    for first in (0, (NZ + 2) * PITCH // 8):
        pack_rim(full, pack, first)
    columns[pl.ds(PAD, 128), :] = pack[...].T

    def row(c, i, count):
        return columns[pl.ds(PAD + 4 * c + i, count), :]

    def returned(q, near, far):
        cx, cy, cz = VEL[q]
        step = (-PITCH * cz - cy) % 128
        value = row(26 - q, near, 8)
        value = pltpu.roll(value, step, 1) if step else value
        return jnp.where(row(WALL, far, 8) != 0.0, value, row(q, far, 8))[:1]

    for c in range(WALL + 1):
        cx = VEL[c][0] if c < 27 else 0
        if cx == 0:
            message[pl.ds(2 * c, 2), :] = row(c, 1, 2)
        elif cx > 0:
            message[pl.ds(2 * c, 1), :] = returned(c, 1, 0)
            message[pl.ds(2 * c + 1, 1), :] = row(c, 1, 1)
        else:
            message[pl.ds(2 * c, 1), :] = row(c, 2, 1)
            message[pl.ds(2 * c + 1, 1), :] = returned(c, 2, 3)


def block_kernel(full, post, walls):
    top = lax.axis_index("gz") == lax.axis_size("gz") - 1
    sponge = (lax.axis_index("gx") * NX + lane_ids()) < SPONGE
    for t in range(ROWS // 8):
        rows = pl.ds(8 * t, 8)
        flags = full[pl.ds(WALL * ROWS + 8 * t, 8), :]
        for cx in (-1, 0, 1):
            walls[cx + 1, rows, :] = pltpu.roll(flags, cx % 128, 1) if cx else flags
    for u in range(UNITS):
        cell = PAD + PITCH + 8 * u
        f = []
        solid = walls[1, pl.ds(cell, 8), :] != 0.0
        for q in range(27):
            cx, cy, cz = VEL[q]
            start = cell - PITCH * cz - cy
            value = full[pl.ds(q * ROWS + start, 8), :]
            if cx:
                value = pltpu.roll(value, cx % 128, 1)
            if q != 13:
                blocked = walls[cx + 1, pl.ds(start, 8), :] != 0.0
                value = jnp.where(blocked, full[pl.ds((26 - q) * ROWS + cell, 8), :], value)
            f.append(jnp.where(solid, WEIGHT[q], value))
        done = relaxed(f, sponge, full[pl.ds(AIM * ROWS + cell, 8), :])
        for q in range(27):
            post[q, pl.ds(8 * u, 8), :] = done[q]

    @pl.when(top)
    def _():
        for q in range(9):
            post[q, pl.ds((NZ + 1) * PITCH, PITCH), :] = post[q + 18, pl.ds(NZ * PITCH, PITCH), :]


def last_kernel(full, block, columns, x_one, x_two, out, west, east, column, walls, back, done, sems):
    here_x, size_x = lax.axis_index("gx"), lax.axis_size("gx")
    top = lax.axis_index("gz") == lax.axis_size("gz") - 1
    lanes, rows = lane_ids(), row_ids()

    if size_x == 2:

        def beside(side, start):
            first = min(max(start, 0), X_ROWS - 8)
            value = x_one[pl.ds(first, 8), :]
            return pltpu.roll(value, (first - start) % 8, 0) if first != start else value

    else:

        def spread(right, left):
            west[pl.ds(PAD, X_ROWS), :] = left[...]
            east[pl.ds(PAD, X_ROWS), :] = right[...]

        by_parity("gx", x_one, x_two, spread)

        def beside(side, start):
            return (west if side < 0 else east)[pl.ds(PAD + start, 8), :]

    def strip_at(c, shift):
        cx = VEL[c][0] if c < 27 else 0
        at = rows - shift
        first = PAD + 4 * c - shift
        value = jnp.where(at < 4, columns[pl.ds(first, 8), :], columns[pl.ds(first - 4, 8), :])
        if c <= WALL and cx >= 0:
            value = jnp.where(at < 2, beside(-1, 2 * c - (cx == 0) - shift), value)
        if c <= WALL and cx <= 0:
            value = jnp.where(at >= 6, beside(1, 2 * c - 6 + (cx == 0) - shift), value)
        if c == WALL:
            value = jnp.where((at == 0) | (at == 7), 0.0, value)
        return value

    strip = [strip_at(c, 0) for c in range(CHANNELS)]
    flags_at = {cx: strip_at(WALL, cx) if cx else strip[WALL] for cx in (-1, 0, 1)}

    def moved_along(value, q):
        cx, cy, cz = VEL[q]
        step = (PITCH * cz + cy) % 128
        return pltpu.roll(value, step, 1) if step else value

    moved = []
    for q in range(27):
        cx = VEL[q][0]
        value = moved_along(strip_at(q, cx) if cx else strip[q], q)
        if q != 13:
            value = jnp.where(moved_along(flags_at[cx], q) != 0.0, strip[26 - q], value)
        moved.append(jnp.where(strip[WALL] != 0.0, WEIGHT[q], value))
    place = here_x * NX + jnp.where(rows < 4, rows - 2, rows + (NX - 6))
    place = lax.rem(place + size_x * NX, size_x * NX)
    sides = relaxed(moved, place < SPONGE, strip[AIM])
    for q, side in enumerate(sides + [strip[WALL]]):
        column[pl.ds(PAD + 8 * q, 8), :] = side

    def picked(wanted):
        value = None
        for sublane, (q, row) in enumerate(wanted):
            moved = column[pl.ds(PAD + 8 * q + row - sublane, 8), :]
            value = moved if value is None else jnp.where(rows == sublane, moved, value)
        return value

    packed = []
    for k in range(9):
        a, b = 3 * k + 2, 3 * k
        packed.append(
            picked([(a, 5), (a, 2), (a, 1), (a, 2), (b, 5), (b, 2), (b, 5), (b, 6)])
        )
    rest = [(3 * k + 1, row) for k in range(9) for row in (5, 2)] + [(27, 1), (27, 6)]
    packed += [picked(rest[i : i + 8]) for i in range(0, len(rest), 8)]
    packed += [jnp.zeros((8, 128), F32)] * (16 - len(packed))
    back[...] = jnp.concatenate(packed, axis=0).T

    def column_at(place, lane, start):
        return pltpu.roll(back[pl.ds(start, 8), :], (lane - place) % 128, 1)

    rim = (lanes == 0) | (lanes == 127)

    def edge_of(q, z, start, base, lane):
        place = 72 + 2 * (q // 3) + base if q % 3 == 1 else 8 * (q // 3) + base
        value = column_at(place, lane, PITCH + start)
        if z == NZ - 1 and VEL[q][2] < 0:
            value = jnp.where(top, column_at(place + (12 if q % 3 == 1 else 48), lane, start), value)
        return value

    def rimmed(q, z, start):
        ends = edge_of(q, z, start, (5, 1, 1)[q % 3], 0)
        return jnp.where(rim, ends, block[q, pl.ds(start, 8), :])

    for u in range(UNITS):
        flags = full[pl.ds(WALL * ROWS + PAD + PITCH + 8 * u, 8), :]
        walls[1, pl.ds(8 * u, 8), :] = flags
        for cx, edge, place in ((1, 0, 90), (-1, 127, 91)):
            walls[cx + 1, pl.ds(8 * u, 8), :] = jnp.where(
                lanes == edge, column_at(place, edge, PITCH + 8 * u), pltpu.roll(flags, cx % 128, 1)
            )

    cells = [(z + 1) * PITCH + 2 for z in range(NZ)]
    solids = [walls[1, pl.ds(cell, 8), :] != 0.0 for cell in cells]

    def streamed(q, z):
        cx, cy, cz = VEL[q]
        cell = cells[z]
        start = cell - PITCH * cz - cy
        if cx > 0:
            side = edge_of(q, z, start, 2, 0)
            value = jnp.where(lanes < 2, side, pltpu.roll(block[q, pl.ds(start, 8), :], 1, 1))
        elif cx < 0:
            side = edge_of(q, z, start, 6, 126)
            value = jnp.where(lanes > 125, side, pltpu.roll(block[q, pl.ds(start, 8), :], 127, 1))
        else:
            value = rimmed(q, z, start)
        if q != 13:
            blocked = walls[cx + 1, pl.ds(start, 8), :] != 0.0
            value = jnp.where(blocked, rimmed(26 - q, None, cell), value)
        return jnp.where(solids[z], WEIGHT[q], value)

    copies = []
    for first, count in ((0, 9), (9, 8), (17, 6), (23, 4)):
        for q in range(first, first + count):
            for z in range(NZ):
                done[q, z] = streamed(q, z)
        part = pl.ds(first, count)
        copies.append(pltpu.make_async_copy(done.at[part], out.at[part], sems.at[len(copies)]))
        copies[-1].start()
    for copy in copies:
        copy.wait()


def pairs(size, turn, wrap):
    ahead = [(i, (i + 1) % size) for i in range(turn, size if wrap else size - 1, 2)]
    return ahead + [(j, i) for i, j in ahead]


def swap(value, axis, turn, wrap):
    return lax.ppermute(value, axis, pairs(lax.axis_size(axis), turn, wrap))


def swap_mixed(value, turn):
    size, planes = lax.axis_size("gy"), lax.axis_size("gz")
    moves = []
    for k in range(planes):
        moves += [
            (i * planes + k, j * planes + k) for i, j in pairs(size, (turn + k) % 2, True)
        ]
    return lax.ppermute(value, ("gy", "gz"), moves)


def shape(*dims):
    return jax.ShapeDtypeStruct(dims, F32)


def shards(pops, solid, profile_table, profile_index):
    own, y_first, y_second = pl.pallas_call(
        first_kernel,
        out_shape=[shape(CHANNELS * NZ * 8, 128), shape(Y_ROWS, 128), shape(Y_ROWS, 128)],
        in_specs=[HBM] * 4,
        out_specs=[VMEM] * 3,
        scratch_shapes=[
            pltpu.VMEM(pops.shape, F32),
            pltpu.VMEM(solid.shape, jnp.int32),
            pltpu.SMEM(profile_table.shape[::-1], F32),
            pltpu.SMEM(profile_index.shape, jnp.int32),
            pltpu.VMEM((2, Y_ROWS, 128), F32),
            pltpu.SemaphoreType.DMA((6,)),
        ],
        compiler_params=PARAMS,
        name="collide",
    )(*(pltpu.with_memory_space_constraint(a, pltpu.HBM) for a in (pops, solid, profile_table.T, profile_index)))
    y_first = swap_mixed(y_first, 0)
    y_second = swap_mixed(y_second, 1)
    own_two, own_one = pl.pallas_call(
        ahead_kernel,
        out_shape=[shape(Z_BLOCKS * 8, 128)] * 2,
        in_specs=[VMEM],
        out_specs=[VMEM] * 2,
        compiler_params=PARAMS,
        name="pack_own",
    )(own)
    own_two = swap(own_two, "gz", 1, False)
    own_one = swap(own_one, "gz", 0, False)
    z_one, z_two = pl.pallas_call(
        second_kernel,
        out_shape=[shape(Z_ROWS, 128)] * 2,
        in_specs=[VMEM] * 2,
        out_specs=[VMEM] * 2,
        scratch_shapes=[
            *[pltpu.VMEM((4 * NZ, 128), F32)] * 2,
            pltpu.VMEM((2, Y_ROWS, 128), F32),
            pltpu.VMEM((2, Z_ROWS, 128), F32),
        ],
        compiler_params=PARAMS,
        cost_estimate=pl.CostEstimate(flops=10**9, bytes_accessed=2**20, transcendentals=0),
        name="pack_z",
    )(y_first, y_second)
    z_one = swap(z_one, "gz", 0, False)
    z_two = swap(z_two, "gz", 1, False)
    part, packed = pl.pallas_call(
        fill_kernel,
        out_shape=[shape(SLABS * ROWS, 128), shape(128, 128)],
        in_specs=[VMEM] * 5,
        out_specs=[VMEM] * 2,
        scratch_shapes=[pltpu.VMEM((4 * NZ, 128), F32)] * 2,
        compiler_params=PARAMS,
        cost_estimate=pl.CostEstimate(flops=10**6, bytes_accessed=2**22, transcendentals=0),
        name="fill",
    )(own, y_first, y_second, own_two, own_one)
    full, packed, columns, message = pl.pallas_call(
        third_kernel,
        out_shape=[
            shape(SLABS * ROWS, 128),
            shape(128, 128),
            shape(PAD + 128 + PAD, 128),
            shape(X_ROWS, 128),
        ],
        in_specs=[VMEM] * 4,
        out_specs=[VMEM] * 4,
        scratch_shapes=[pltpu.VMEM((2, Z_ROWS, 128), F32)],
        input_output_aliases={0: 0, 1: 1},
        compiler_params=PARAMS,
        name="pack_x",
    )(part, packed, z_one, z_two)
    x_one = swap(message, "gx", 0, True)
    x_two = x_one if lax.axis_size("gx") == 2 else swap(message, "gx", 1, True)
    block = pl.pallas_call(
        block_kernel,
        out_shape=shape(27, UNITS * 8, 128),
        in_specs=[VMEM],
        out_specs=VMEM,
        scratch_shapes=[pltpu.VMEM((3, ROWS, 128), F32)],
        compiler_params=PARAMS,
        cost_estimate=pl.CostEstimate(
            flops=27 * 20 * UNITS * 1024, bytes_accessed=2**22, transcendentals=0
        ),
        name="block",
    )(full)
    return pl.pallas_call(
        last_kernel,
        out_shape=shape(27, NZ, NY, NX),
        in_specs=[VMEM] * 5,
        out_specs=HBM,
        scratch_shapes=[
            pltpu.VMEM((PAD + X_ROWS + PAD, 128), F32),
            pltpu.VMEM((PAD + X_ROWS + PAD, 128), F32),
            pltpu.VMEM((PAD + 28 * 8 + PAD, 128), F32),
            pltpu.VMEM((3, UNITS * 8, 128), F32),
            pltpu.VMEM((128, 128), F32),
            pltpu.VMEM((27, NZ, NY, NX), F32),
            pltpu.SemaphoreType.DMA((NZ,)),
        ],
        compiler_params=PARAMS,
        name="finish",
    )(full, block, columns, x_one, x_two)


def solution(mesh):
    return jax.shard_map(
        shards,
        mesh=mesh,
        in_specs=(P(None, "gz", "gy", "gx"), P("gz", "gy", "gx"), P(None, "gz"), P("gy")),
        out_specs=P(None, "gz", "gy", "gx"),
        check_vma=False,
    )
```
